32 devices in a mesh: row: 8 (over y, x, core), col: 4 (over z).
Axes of the slice: x: 2, y: 2, z: 4, core: 2. Of those that a mesh axis runs over, the one named last changes fastest.
Arguments:
- hidden: bfloat16 [64, 2048], P('row', 'col'), may hold values from -60 to 60
- queries: bfloat16 [64, 4096], P('row'), may hold values from -6 to 6
- new_kv: bfloat16 [64, 2, 2048], P('row'), may hold values from -12 to 12
- prompt_kv: bfloat16 [8, 2, 1024, 2048], P('row', None, 'col'), may hold values from -180 to 180
- suffix_kv: bfloat16 [64, 2, 128, 2048], P('row', None, 'col'), may hold values from -12 to 12
- lengths: int32 [64], P('row'), may hold values from 1 to 128, as said below
- w_out: bfloat16 [4096, 2048], P(None, 'col'), may hold values from -0.375 to 0.375
- moe_gain: bfloat16 [2048], P('col'), may hold values from 0.099609375 to 1.8984375
- w_router: bfloat16 [2048, 8], P('col'), may hold values from -0.5 to 0.5
- expert_weights: bfloat16 [8, 5632, 3, 2048], P(None, 'row', None, 'col'), may hold values from -0.25 to 0.25
- old_lines: int32 [8, 5632], replicated, may hold values from 0 to 5631, as said below
- new_lines: int32 [8, 5632], replicated, may hold values from 0 to 5631, as said below
- routes: int32 [64, 2], replicated, may hold values from 0 to 7, all different within a row
Outputs:
- layer_out: float32 [64, 2048], P('row', 'col')
- moved_weights: bfloat16 [8, 5632, 3, 2048], P(None, 'row', None, 'col')
The draws below stay inside these ranges and needn't reach their ends.
Inputs may be any that keep to these rules, and one draw needn't show every extreme that they name: `lengths`: some sequence has all 128 slots filled. `old_lines`: each row is a permutation of the hidden units of one expert; stored lines [j * 704, (j + 1) * 704) lie on row index j. `new_lines`: each row is a permutation of the hidden units of one expert. Counting all experts together, exactly 704 of the lines that one row index holds under old_lines are held by each row index under new_lines. `routes`: the two experts of a token differ.
All inputs are finite; a program needn't handle non-finite values.
Results may differ from the reference program's by a relative error of at most 0.04.
Values may be sent and summed in bfloat16 or wider, within the bound.
No kernel may reach another device: no remote copies, remote signals or barrier semaphores. Data moves between devices by JAX's collectives and lax.ppermute only.
A program may use at most 128 MiB of HBM per device.

```python
import jax
import jax.numpy as jnp
from jax import lax

D = 2048
HEADS = 32
KVH = 16
HD = 128
E = 8
FF = 5632
TOPK = 2
SEQ_G = 8
PROMPT = 1024
SUF = 128
G = 8
REP = 2
TOKENS = 64


def draw_hidden(key, part):
    key_values = jax.random.fold_in(key, 0)
    feature_ramp = 1.0 + 2.0 * jnp.arange(D, dtype=jnp.float32) / (D - 1)
    values_base = 0.3 * jnp.clip(jax.random.normal(key_values, (TOKENS, D), jnp.float32), -6.0, 6.0)
    return (values_base * feature_ramp[None, :]).astype(jnp.bfloat16)


def draw_prompt_kv(key, part):
    key_values = jax.random.fold_in(key, 0)
    shape_all = (G, 2, PROMPT, KVH * HD)
    return (2.0 * jnp.clip(jax.random.normal(key_values, shape_all, jnp.float32), -6.0, 6.0)).astype(jnp.bfloat16)


def draw_lengths(key, part):
    key_values, key_spot = jax.random.split(key)
    filled = jax.random.randint(key_values, (TOKENS,), 1, SUF + 1)
    spot_index = jax.random.randint(key_spot, (), 0, TOKENS)
    return jnp.where(jnp.arange(TOKENS) == spot_index, SUF, filled).astype(jnp.int32)


def line_tables(key):
    base_key = jax.random.fold_in(key, 4242)
    key_old, key_shuffle, key_order = jax.random.split(base_key, 3)
    line_count = FF // G
    old_table = jax.vmap(lambda item_key: jax.random.permutation(item_key, FF))(jax.random.split(key_old, E)).astype(jnp.int32)
    source_ids = jnp.arange(G, dtype=jnp.int32)[:, None, None]
    target_ids = jnp.arange(G, dtype=jnp.int32)[None, :, None]
    expert_ids = jnp.arange(E, dtype=jnp.int32)[None, None, :]
    extra_one = jnp.where(line_count % G > 0, ((source_ids + target_ids + expert_ids) % 2 == 0).astype(jnp.int32), 0)
    counts = line_count // G + extra_one
    bounds = jnp.transpose(jnp.cumsum(counts, axis=1), (0, 2, 1))
    slot_ids = jnp.arange(line_count, dtype=jnp.int32)
    target = jnp.sum((bounds[:, :, None, :] <= slot_ids[None, None, :, None]).astype(jnp.int32), axis=-1)
    shuffles = jax.vmap(lambda item_key: jax.random.permutation(item_key, line_count))(jax.random.split(key_shuffle, G * E))
    shuffles = shuffles.reshape(G, E, line_count).astype(jnp.int32)
    stored = source_ids * line_count + shuffles
    stored_by_expert = jnp.transpose(stored, (1, 0, 2)).reshape(E, FF)
    target_by_expert = jnp.transpose(target, (1, 0, 2)).reshape(E, FF)
    tie_break = jax.vmap(lambda item_key: jax.random.permutation(item_key, FF))(jax.random.split(key_order, E)).astype(jnp.int32)
    sort_order = jnp.argsort(target_by_expert * FF + tie_break, axis=1)
    chosen = jnp.take_along_axis(stored_by_expert, sort_order, axis=1)
    new_table = jnp.take_along_axis(old_table, chosen, axis=1)
    return (old_table.astype(jnp.int32), new_table.astype(jnp.int32))


def draw_old_lines(key, part):
    return line_tables(key)[0]


def draw_new_lines(key, part):
    return line_tables(key)[1]


def level_of(own_key, shape, shards, low, top_value):
    gain, own = 1.0, jax.random.fold_in(own_key, 6)
    for axis_at, blocks in shards:
        heights = jnp.exp(jax.random.uniform(jax.random.fold_in(own, axis_at), (blocks,), jnp.float32, low / len(shards), top_value / len(shards)))
        gain = gain * jnp.repeat(heights, shape[axis_at] // blocks).reshape([-1 if axis == axis_at else 1 for axis in range(len(shape))])
    return gain


def different_ones(own_key, rows, amount, top, lift):
    sequence = jax.random.permutation(jax.random.fold_in(own_key, 1), amount)
    favour = sequence
    for power in range(3):
        favour = favour * favour // amount
    favour = favour * lift // amount
    tickets = jax.random.randint(jax.random.fold_in(own_key, 2), (rows, amount), 0, 4096) + favour
    sure = jax.random.permutation(jax.random.fold_in(own_key, 3), rows)[jnp.arange(amount) % rows]
    tickets = jnp.where(jnp.arange(rows)[:, None] == sure[None, :], 1 << 14, tickets)
    priority = tickets * amount + jnp.arange(amount)
    return lax.top_k(priority.astype(jnp.int32), top)[1].astype(jnp.int32)


def scatter_about(rng, shape, scale, bound, cuts=(), held_as=jnp.bfloat16):
    gain = level_of(rng, shape, cuts, -0.22, 0.18) if cuts else 1.0
    array = jax.random.normal(rng, shape, jnp.float32) * scale * gain
    return jnp.minimum(jnp.maximum(array, -bound), bound).astype(held_as)


def setup_inputs(seed: int = 0) -> dict:
    splits = jax.random.split(jax.random.key(seed), 14)
    hidden = draw_hidden(jax.random.fold_in(splits[13], 71), 0)
    queries = scatter_about(splits[1], (TOKENS, HEADS * HD), 1.0, 6.0, ((0, 8),))
    new_kv = scatter_about(splits[2], (TOKENS, 2, KVH * HD), 2.0, 12.0, ((0, 8),))
    prompt_kv = draw_prompt_kv(jax.random.fold_in(splits[13], 71), 0)
    suffix_kv = scatter_about(splits[4], (TOKENS, 2, SUF, KVH * HD), 2.0, 12.0, ((0, 8), (2, 4)))
    lengths = draw_lengths(jax.random.fold_in(splits[13], 71), 0)
    w_out = scatter_about(splits[6], (HEADS * HD, D), (HEADS * HD // 16) ** -0.5, 0.375, ((1, 4),))
    moe_gain = jnp.clip(1.0 + 0.18 * jax.random.normal(splits[7], (D,), jnp.float32), 0.099609375, 1.8984375).astype(jnp.bfloat16)
    w_router = scatter_about(splits[8], (D, E), (D // 16) ** -0.5, 0.5, ((0, 4),))
    expert_weights = scatter_about(splits[9], (E, FF, 3, D), (D // 4) ** -0.5, 0.25, ((1, 8), (3, 4)))
    old_lines = draw_old_lines(jax.random.fold_in(splits[13], 71), 0)
    new_lines = draw_new_lines(jax.random.fold_in(splits[13], 71), 0)
    routes = different_ones(splits[12], TOKENS, E, TOPK, 4096)
    return {"hidden": hidden, "queries": queries, "new_kv": new_kv, "prompt_kv": prompt_kv, "suffix_kv": suffix_kv, "lengths": lengths, "w_out": w_out, "moe_gain": moe_gain, "w_router": w_router, "expert_weights": expert_weights, "old_lines": old_lines, "new_lines": new_lines, "routes": routes}


norm_eps = 1e-06
neg_big = -1e+30

def round_trip(values):
    return lax.optimization_barrier(values.astype(jnp.bfloat16)).astype(jnp.float32)

def group_attention(queries, new_kv, prompt_kv, suffix_kv, lengths, group_index):
    first_row = (group_index * SEQ_G).astype(jnp.int32)
    query_rows = lax.dynamic_slice_in_dim(queries, first_row, SEQ_G, 0).astype(jnp.float32)
    query_heads = query_rows.reshape(SEQ_G, KVH, REP, HD)
    own_pairs = lax.dynamic_slice_in_dim(new_kv, first_row, SEQ_G, 0).astype(jnp.float32)
    own_keys = own_pairs[:, 0].reshape(SEQ_G, KVH, HD)
    own_values = own_pairs[:, 1].reshape(SEQ_G, KVH, HD)
    prompt_pair = lax.dynamic_index_in_dim(prompt_kv, group_index, 0, keepdims=False).astype(jnp.float32)
    prompt_keys = prompt_pair[0].reshape(PROMPT, KVH, HD)
    prompt_values = prompt_pair[1].reshape(PROMPT, KVH, HD)
    suffix_pair = lax.dynamic_slice_in_dim(suffix_kv, first_row, SEQ_G, 0).astype(jnp.float32)
    suffix_keys = suffix_pair[:, 0].reshape(SEQ_G, SUF, KVH, HD)
    suffix_values = suffix_pair[:, 1].reshape(SEQ_G, SUF, KVH, HD)
    seq_lengths = lax.dynamic_slice_in_dim(lengths, first_row, SEQ_G, 0)
    score_scale = HD ** (-0.5)
    prompt_scores = jnp.einsum('skgd,pkd->skgp', query_heads, prompt_keys) * score_scale
    suffix_scores = jnp.einsum('skgd,spkd->skgp', query_heads, suffix_keys) * score_scale
    own_scores = jnp.einsum('skgd,skd->skg', query_heads, own_keys) * score_scale
    live_slots = (jnp.arange(SUF, dtype=jnp.int32)[None, :] < seq_lengths[:, None])[:, None, None, :]
    suffix_scores = jnp.where(live_slots, suffix_scores, neg_big)
    highest = jnp.maximum(jnp.maximum(lax.optimization_barrier(jnp.max(prompt_scores, axis=-1)), lax.optimization_barrier(jnp.max(suffix_scores, axis=-1))), own_scores)
    prompt_weights = jnp.exp(prompt_scores - highest[..., None])
    suffix_weights = jnp.where(live_slots, jnp.exp(suffix_scores - highest[..., None]), 0.0)
    own_weights = jnp.exp(own_scores - highest)
    totals = lax.optimization_barrier(jnp.sum(prompt_weights, axis=-1)) + lax.optimization_barrier(jnp.sum(suffix_weights, axis=-1)) + own_weights
    mixture = jnp.einsum('skgp,pkd->skgd', round_trip(prompt_weights), prompt_values)
    mixture = mixture + jnp.einsum('skgp,spkd->skgd', round_trip(suffix_weights), suffix_values)
    mixture = mixture + round_trip(own_weights)[..., None] * own_values[:, :, None, :]
    return (mixture / totals[..., None]).astype(jnp.bfloat16).reshape(SEQ_G, HEADS * HD)

def reference(hidden, queries, new_kv, prompt_kv, suffix_kv, lengths, w_out, moe_gain, w_router, expert_weights, old_lines, new_lines, routes):

    def one_group(group_index):
        return group_attention(queries, new_kv, prompt_kv, suffix_kv, lengths, group_index)
    attended = lax.map(one_group, jnp.arange(G, dtype=jnp.int32)).reshape(TOKENS, HEADS * HD)
    projected = jnp.dot(attended, w_out, preferred_element_type=jnp.float32)
    h_mid = (hidden.astype(jnp.float32) + projected).astype(jnp.bfloat16)
    h_float = h_mid.astype(jnp.float32)
    scaled = (h_float * moe_gain.astype(jnp.float32)[None, :]).astype(jnp.bfloat16)
    inverse_rms = lax.rsqrt(lax.optimization_barrier(jnp.mean(h_float * h_float, axis=1)) + norm_eps)
    logits = jnp.dot(scaled, w_router, preferred_element_type=jnp.float32) * inverse_rms[:, None]
    selected = jnp.take_along_axis(logits, routes, axis=1)
    gates = jax.nn.softmax(selected, axis=-1)
    expert_ids = jnp.arange(E, dtype=jnp.int32)
    coefficient = lax.optimization_barrier(jnp.sum(jnp.where(routes[:, :, None] == expert_ids[None, None, :], gates[:, :, None], 0.0), axis=1))
    coefficient_rows = jnp.transpose(coefficient)

    def expert_step(running, expert_index):
        lines = lax.dynamic_index_in_dim(expert_weights, expert_index, 0, keepdims=False)
        gate_part = jnp.dot(scaled, jnp.transpose(lines[:, 0, :]), preferred_element_type=jnp.float32) * inverse_rms[:, None]
        up_part = jnp.dot(scaled, jnp.transpose(lines[:, 1, :]), preferred_element_type=jnp.float32) * inverse_rms[:, None]
        activated = (jax.nn.silu(gate_part) * up_part).astype(jnp.bfloat16)
        produced = jnp.dot(activated, lines[:, 2, :], preferred_element_type=jnp.float32)
        weight_col = lax.dynamic_index_in_dim(coefficient_rows, expert_index, 0, keepdims=False)
        return (running + weight_col[:, None] * produced, None)
    mixed, unused_stack = lax.scan(expert_step, jnp.zeros((TOKENS, D), jnp.float32), expert_ids)
    layer_out = h_float + mixed
    positions = jnp.argsort(old_lines, axis=1).astype(jnp.int32)
    source_lines = jnp.take_along_axis(positions, new_lines, axis=1).astype(jnp.int32)
    moved_weights = expert_weights[expert_ids[:, None], source_lines]
    return (layer_out, moved_weights)
```

```python
import functools

import jax
import jax.numpy as jnp
from jax import lax
from jax.experimental import pallas as pl
from jax.experimental.pallas import tpu as pltpu
from jax.sharding import PartitionSpec as P

KVH = 16
HD = 128
REP = 2
TILE = 16
LANES = 128

norm_eps = 1e-06
neg_big = -1e30
VMEM_LIMIT = 48 * 1024 * 1024


def up_to(value, unit):
    return -(-value // unit) * unit


def iota(shape, axis):
    return lax.broadcasted_iota(jnp.int32, shape, axis)


def ones_where(mask):
    return jnp.where(mask, 1.0, 0.0).astype(jnp.bfloat16)


def params():
    return pltpu.CompilerParams(vmem_limit_bytes=VMEM_LIMIT)


def find_slots(table_row, id_row):
    full = table_row.shape[1]
    ids = id_row.shape[1]
    high_count = up_to(-(-full // 64), 16)
    table_high = ones_where(iota((high_count, full), 0) == (table_row >> 6))
    half = iota((LANES, full), 0)
    slot = iota((LANES, full), 1)
    value = jnp.where(half < 64, slot >> 7, slot & 127).astype(jnp.float32)
    table_low = jnp.where((half & 63) == (table_row & 63), value, 0.0).astype(jnp.bfloat16)
    square = lax.dot_general(
        table_low, table_high, (((1,), (1,)), ((), ())), preferred_element_type=jnp.float32
    )
    id_high = ones_where(iota((high_count, ids), 0) == (id_row >> 6))
    spread = jnp.dot(square.astype(jnp.bfloat16), id_high, preferred_element_type=jnp.float32)
    chosen = jnp.where((iota((LANES, ids), 0) & 63) == (id_row & 63), spread, 0.0)
    high = jnp.sum(chosen[:64], axis=0, keepdims=True)
    low = jnp.sum(chosen[64:], axis=0, keepdims=True)
    return high * 128.0 + low


def segment_plan(counts, experts, rows):
    starts = []
    running = jnp.zeros((rows, LANES), jnp.float32)
    for e in range(experts):
        starts.append(running)
        running = running + counts[e * rows : (e + 1) * rows]
    start = jnp.concatenate(starts, axis=0)
    lead = jnp.floor(start * (1.0 / TILE))
    tail = jnp.floor((start + counts + (TILE - 1.0)) * (1.0 / TILE))
    tiles = jnp.where(counts > 0.0, tail - lead, 0.0)
    pairs = experts * rows
    line = iota((pairs, pairs), 0)
    column = iota((pairs, pairs), 1)
    earlier = ones_where((line // rows == column // rows) & (column < line))
    base = jnp.dot(earlier, tiles.astype(jnp.bfloat16), preferred_element_type=jnp.float32)
    return start, lead, tiles, base


def write_plan(plan_ref, start, lead, tiles, base):
    shared = start - lead * TILE
    for n, part in enumerate((lead, tiles, base, shared)):
        plan_ref[n] = part.astype(jnp.int32)


def outgoing_kernel(lines, rows, new_ref, held_ref, stack_ref, plan_ref):
    experts = new_ref.shape[0]
    width = held_ref.shape[1]
    real = iota((1, width), 1) < lines
    hits = []
    for e in range(experts):
        slots = find_slots(new_ref[e : e + 1, :], held_ref[e : e + 1, :])
        peer = jnp.floor((slots + 0.5) * (1.0 / lines)).astype(jnp.int32)
        hits.append(jnp.where((iota((rows, width), 0) == peer) & real, 1.0, 0.0))
    hits = jnp.concatenate(hits, axis=0)
    until = ones_where(iota((width, width), 0) <= iota((width, width), 1))
    ranks = jnp.dot(hits.astype(jnp.bfloat16), until, preferred_element_type=jnp.float32)
    counts = jnp.broadcast_to(jnp.sum(hits, axis=1, keepdims=True), (experts * rows, LANES))
    start, lead, tiles, base = segment_plan(counts, experts, rows)
    write_plan(plan_ref, start, lead, tiles, base)
    offset = (base * TILE + start - lead * TILE - 1.0)[:, :1]
    placed = hits * (ranks + offset)
    for e in range(experts):
        row = jnp.sum(placed[e * rows : (e + 1) * rows], axis=0, keepdims=True)
        stack_ref[e] = jnp.where(real, row, -1.0).astype(jnp.int32)


def incoming_kernel(lines, rows, old_ref, wanted_ref, stack_ref, plan_ref):
    experts = old_ref.shape[0]
    width = wanted_ref.shape[1]
    real = iota((1, width), 1) < lines
    held_at = []
    hits = []
    for e in range(experts):
        slots = find_slots(old_ref[e : e + 1, :], wanted_ref[e : e + 1, :])
        held_at.append(jnp.where(real, slots, 1e9))
        peer = jnp.floor((slots + 0.5) * (1.0 / lines)).astype(jnp.int32)
        hits.append(jnp.where((iota((rows, width), 0) == peer) & real, 1.0, 0.0))
    hits = jnp.concatenate(hits, axis=0)
    counts = jnp.broadcast_to(jnp.sum(hits, axis=1, keepdims=True), (experts * rows, LANES))
    start, lead, tiles, base = segment_plan(counts, experts, rows)
    write_plan(plan_ref, start, lead, tiles, base)
    blank = jnp.zeros((LANES - experts, width), jnp.float32)
    columns = jnp.transpose(jnp.concatenate(held_at + [blank], axis=0))
    rows_out = []
    for e in range(experts):
        mine = slice(e * rows, (e + 1) * rows)
        before = jnp.where(columns[:, e : e + 1] < held_at[e], 1.0, 0.0)
        rank = jnp.sum(before, axis=0, keepdims=True)
        ahead = jnp.zeros((1, LANES), jnp.float32)
        firsts = []
        for r in range(rows):
            firsts.append(ahead)
            ahead = ahead + counts[e * rows + r : e * rows + r + 1]
        first = jnp.concatenate(firsts, axis=0)
        offset = (base[mine] * TILE + start[mine] - lead[mine] * TILE - first)[:, :1]
        rows_out.append(jnp.sum(hits[mine] * (rank + offset), axis=0, keepdims=True))
    stack_ref[...] = jnp.transpose(jnp.concatenate(rows_out + [blank], axis=0))


def pack_kernel(rows, plan_ref, place_ref, lines_ref, out_ref, stage_ref):
    e = pl.program_id(0)
    pairs = pl.num_programs(0) * rows
    deep, _ = stage_ref.shape
    lines = lines_ref.shape[2]
    place = place_ref[0][:, :lines]
    onehot = ones_where(iota((deep, lines), 0) == place)
    stage_ref[...] = jnp.dot(
        onehot, lines_ref[0, 0], preferred_element_type=jnp.float32
    ).astype(jnp.bfloat16)

    def one_peer(d, carry):
        k = e * rows + d
        lead = plan_ref[k]
        tiles = plan_ref[pairs + k]
        base = plan_ref[2 * pairs + k]
        shared = plan_ref[3 * pairs + k] > 0

        def source(t):
            return stage_ref[pl.ds(pl.multiple_of((base + t) * TILE, TILE), TILE), :]

        def target(t):
            return pl.ds(pl.multiple_of((lead + t) * TILE, TILE), TILE)

        @pl.when((tiles > 0) & shared)
        def _():
            out_ref[d, target(0), :] = out_ref[d, target(0), :] + source(0)

        @pl.when((tiles > 0) & jnp.logical_not(shared))
        def _():
            out_ref[d, target(0), :] = source(0)

        def put(t, c):
            out_ref[d, target(t), :] = source(t)
            return c

        return lax.fori_loop(1, tiles, put, carry)

    lax.fori_loop(0, rows, one_peer, 0)


def unpack_kernel(rows, plan_ref, place_ref, block_ref, *rest):
    out_ref, stage_ref = rest[-2:]
    e = pl.program_id(0)
    pairs = pl.num_programs(0) * rows
    deep, _ = stage_ref.shape
    lines = out_ref.shape[2]

    @pl.when(e == 0)
    def _():
        stage_ref[...] = jnp.zeros_like(stage_ref)

    def one_peer(s, carry):
        k = e * rows + s
        lead = plan_ref[k]
        tiles = plan_ref[pairs + k]
        base = plan_ref[2 * pairs + k]

        def put(t, c):
            here = pl.ds(pl.multiple_of((base + t) * TILE, TILE), TILE)
            there = pl.ds(pl.multiple_of((lead + t) * TILE, TILE), TILE)
            stage_ref[here, :] = block_ref[s, there, :]
            return c

        return lax.fori_loop(0, tiles, put, carry)

    lax.fori_loop(0, rows, one_peer, 0)
    place = jnp.where(iota((lines, LANES), 1) == e, place_ref[:lines, :], 0.0)
    place = jnp.sum(place, axis=1, keepdims=True).astype(jnp.int32)
    onehot = ones_where(iota((lines, deep), 1) == place)
    out_ref[0, 0] = jnp.dot(
        onehot, stage_ref[...], preferred_element_type=jnp.float32
    ).astype(jnp.bfloat16)


def call_plan(kernel, name, table, ids, lines, rows, transposed):
    experts, width = ids.shape
    stack = (
        jax.ShapeDtypeStruct((width, LANES), jnp.float32)
        if transposed
        else jax.ShapeDtypeStruct((experts, 1, width), jnp.int32)
    )
    stack, plan = pl.pallas_call(
        functools.partial(kernel, lines, rows),
        out_shape=(stack, jax.ShapeDtypeStruct((4, experts * rows, LANES), jnp.int32)),
        compiler_params=params(),
        cost_estimate=pl.CostEstimate(
            flops=20 * experts * table.shape[1] * 256,
            bytes_accessed=8 * table.size,
            transcendentals=0,
        ),
        name=name,
    )(table, ids)
    return stack, plan[:, :, 0].reshape(-1)


def pack(expert_lines, place, plan, part, rows, block_rows, deep):
    experts, _, lines, width = expert_lines.shape
    return pl.pallas_call(
        functools.partial(pack_kernel, rows),
        grid_spec=pltpu.PrefetchScalarGridSpec(
            num_scalar_prefetch=1,
            grid=(experts,),
            in_specs=[
                pl.BlockSpec((1, 1, place.shape[2]), lambda e, plan: (e, 0, 0)),
                pl.BlockSpec((1, 1, lines, width), lambda e, plan: (e, part, 0, 0)),
            ],
            out_specs=pl.BlockSpec((rows, block_rows, width), lambda e, plan: (0, 0, 0)),
            scratch_shapes=[pltpu.VMEM((deep, width), jnp.bfloat16)],
        ),
        out_shape=jax.ShapeDtypeStruct((rows, block_rows, width), jnp.bfloat16),
        compiler_params=params(),
        cost_estimate=pl.CostEstimate(
            flops=2 * experts * deep * lines * width,
            bytes_accessed=4 * experts * lines * width,
            transcendentals=0,
        ),
        name="pack_lines",
    )(plan, place, expert_lines)


def unpack(arrived, place, plan, part, shape, deep, previous):
    experts, _, lines, width = shape
    rows, block_rows, _ = arrived.shape
    in_specs = [
        pl.BlockSpec(place.shape, lambda e, plan: (0, 0)),
        pl.BlockSpec((rows, block_rows, width), lambda e, plan: (0, 0, 0)),
    ]
    operands = [plan, place, arrived]
    aliases = {}
    if previous is not None:
        in_specs.append(pl.BlockSpec(memory_space=pl.ANY))
        operands.append(previous)
        aliases = {3: 0}
    return pl.pallas_call(
        functools.partial(unpack_kernel, rows),
        grid_spec=pltpu.PrefetchScalarGridSpec(
            num_scalar_prefetch=1,
            grid=(experts,),
            in_specs=in_specs,
            out_specs=pl.BlockSpec((1, 1, lines, width), lambda e, plan: (e, part, 0, 0)),
            scratch_shapes=[pltpu.VMEM((deep, width), jnp.bfloat16)],
        ),
        out_shape=jax.ShapeDtypeStruct(shape, jnp.bfloat16),
        input_output_aliases=aliases,
        compiler_params=params(),
        cost_estimate=pl.CostEstimate(
            flops=2 * experts * deep * lines * width,
            bytes_accessed=4 * experts * lines * width,
            transcendentals=0,
        ),
        name="unpack_lines",
    )(*operands)


def own_ids(table, lines, width):
    mine = lax.dynamic_slice_in_dim(table, lax.axis_index("row") * lines, lines, 1)
    return jnp.pad(mine, ((0, 0), (0, width - lines)), constant_values=-1)


def migrate(expert_lines, old_lines, new_lines):
    rows = lax.axis_size("row")
    experts, parts, lines, width = expert_lines.shape
    padded = up_to(lines, LANES)
    block_rows = up_to(experts * lines // rows, TILE)
    deep = up_to(lines + 2 * (TILE - 1) * rows, TILE)
    out_place, out_plan = call_plan(
        outgoing_kernel, "outgoing_plan", new_lines, own_ids(old_lines, lines, padded),
        lines, rows, False,
    )
    in_place, in_plan = call_plan(
        incoming_kernel, "incoming_plan", old_lines, own_ids(new_lines, lines, padded),
        lines, rows, True,
    )
    moved = None
    packed = [
        pack(expert_lines, out_place, out_plan, part, rows, block_rows, deep)
        for part in range(parts)
    ]
    arrived = [lax.all_to_all(block, "row", split_axis=0, concat_axis=0, tiled=True) for block in packed]
    for part in range(parts):
        moved = unpack(
            arrived[part], in_place, in_plan, part, expert_lines.shape, up_to(deep, LANES), moved
        )
    return moved


def from_peer(block, axis, offset):
    size = lax.axis_size(axis)
    return lax.ppermute(block, axis, [(i, i ^ offset) for i in range(size)])


def attend(queries, new_kv, prompt_kv, suffix_kv, lengths):
    seq_count = queries.shape[0]
    prompt_rows = prompt_kv.shape[2]
    suffix_rows = suffix_kv.shape[2]
    col_index = lax.axis_index("col")
    query_heads = queries.reshape(seq_count, KVH, REP, HD)
    prompt_keys = prompt_kv[0, 0].reshape(prompt_rows, KVH, HD)
    prompt_values = prompt_kv[0, 1].reshape(prompt_rows, KVH, HD)
    suffix_keys = suffix_kv[:, 0].reshape(seq_count, suffix_rows, KVH, HD)
    suffix_values = suffix_kv[:, 1].reshape(seq_count, suffix_rows, KVH, HD)
    own_keys = new_kv[:, 0].reshape(seq_count, KVH, HD)
    own_values = new_kv[:, 1].reshape(seq_count, KVH, HD)
    score_scale = HD ** (-0.5)
    prompt_scores = (
        jnp.einsum("skgd,pkd->skgp", query_heads, prompt_keys, preferred_element_type=jnp.float32)
        * score_scale
    )
    suffix_scores = (
        jnp.einsum("skgd,spkd->skgp", query_heads, suffix_keys, preferred_element_type=jnp.float32)
        * score_scale
    )
    own_scores = (
        jnp.einsum("skgd,skd->skg", query_heads, own_keys, preferred_element_type=jnp.float32)
        * score_scale
    )
    positions = col_index * suffix_rows + jnp.arange(suffix_rows, dtype=jnp.int32)
    live_slots = (positions[None, :] < lengths[:, None])[:, None, None, :]
    holder = col_index == 0
    suffix_scores = jnp.where(live_slots, suffix_scores, neg_big)
    own_scores = jnp.where(holder, own_scores, neg_big)
    highest = jnp.maximum(
        jnp.maximum(jnp.max(prompt_scores, axis=-1), jnp.max(suffix_scores, axis=-1)), own_scores
    )
    prompt_weights = jnp.exp(prompt_scores - highest[..., None])
    suffix_weights = jnp.where(live_slots, jnp.exp(suffix_scores - highest[..., None]), 0.0)
    own_weights = jnp.where(holder, jnp.exp(own_scores - highest), 0.0)
    totals = jnp.sum(prompt_weights, axis=-1) + jnp.sum(suffix_weights, axis=-1) + own_weights
    mixture = jnp.einsum(
        "skgp,pkd->skgd",
        prompt_weights.astype(jnp.bfloat16),
        prompt_values,
        preferred_element_type=jnp.float32,
    )
    mixture = mixture + jnp.einsum(
        "skgp,spkd->skgd",
        suffix_weights.astype(jnp.bfloat16),
        suffix_values,
        preferred_element_type=jnp.float32,
    )
    own_rounded = lax.optimization_barrier(own_weights.astype(jnp.bfloat16)).astype(jnp.float32)
    mixture = mixture + own_rounded[..., None] * own_values.astype(jnp.float32)[:, :, None, :]
    heads = KVH * REP
    bundle = jnp.concatenate(
        [
            mixture.reshape(seq_count, heads * HD),
            highest.reshape(seq_count, heads),
            totals.reshape(seq_count, heads),
            jnp.zeros((seq_count, LANES - 2 * heads), jnp.float32),
        ],
        axis=1,
    )
    bundles = [bundle] + [from_peer(bundle, "col", o) for o in range(1, lax.axis_size("col"))]
    every = jnp.stack(bundles)
    mixtures = every[:, :, : heads * HD].reshape(-1, seq_count, heads, HD)
    peaks = every[:, :, heads * HD : heads * HD + heads]
    sums = every[:, :, heads * HD + heads : heads * HD + 2 * heads]
    factors = jnp.exp(peaks - jnp.max(peaks, axis=0))
    total = jnp.sum(sums * factors, axis=0)
    mixed = jnp.sum(mixtures * factors[..., None], axis=0)
    return (mixed / total[..., None]).astype(jnp.bfloat16).reshape(seq_count, heads * HD)


def gate_up_kernel(me_ref, h_ref, gain_ref, router_ref, routes_ref, gate_ref, up_ref, out_ref, acc_ref):
    e = pl.program_id(0)
    tokens = h_ref.shape[0]
    lines = gate_ref.shape[2]
    padded = out_ref.shape[3]
    h = h_ref[...].astype(jnp.float32)
    scaled = (h * gain_ref[...].astype(jnp.float32)).astype(jnp.bfloat16)

    @pl.when(e == 0)
    def _():
        acc_ref[...] = jnp.zeros_like(acc_ref)

    against = (((1,), (1,)), ((), ()))
    gate = lax.dot_general(scaled, gate_ref[0, 0], against, preferred_element_type=jnp.float32)
    up = lax.dot_general(scaled, up_ref[0, 0], against, preferred_element_type=jnp.float32)
    for k in range(routes_ref.shape[1]):
        chosen = routes_ref[:, k : k + 1] == e
        acc_ref[2 * k, :, :lines] += jnp.where(chosen, gate, 0.0)
        acc_ref[2 * k + 1, :, :lines] += jnp.where(chosen, up, 0.0)

    @pl.when(e == pl.num_programs(0) - 1)
    def _():
        last = padded - LANES
        shift = lines - last
        experts = pl.num_programs(0)
        extra = jnp.dot(scaled, router_ref[...], preferred_element_type=jnp.float32)
        lane = iota((tokens, LANES), 1)
        square = jnp.sum(h * h, axis=1, keepdims=True)
        extra = jnp.where(lane == shift + experts, square, extra)
        high = extra.astype(jnp.bfloat16).astype(jnp.float32)
        low = extra - high
        acc_ref[0, :, last:] += jnp.where(lane >= shift, high, 0.0)
        acc_ref[1, :, last:] += jnp.where(lane >= shift, low, 0.0)
        peers, _, share, _ = out_ref.shape
        me = me_ref[0]
        for o in range(peers):
            begin = pl.multiple_of((me ^ o) * share, share)
            out_ref[o] = acc_ref[:, pl.ds(begin, share), :].astype(jnp.bfloat16)


def activate_kernel(lines, experts, model_width, routes_ref, *refs):
    out_ref = refs[-1]
    summed = refs[0][...].astype(jnp.float32)
    for ref in refs[1:-1]:
        summed = summed + ref[...].astype(jnp.float32)
    _, share, padded = summed.shape
    last = padded - LANES
    shift = lines - last
    extra = summed[0, :, last:] + summed[1, :, last:]
    lane = iota((share, LANES), 1)
    square = jnp.sum(jnp.where(lane == shift + experts, extra, 0.0), axis=1, keepdims=True)
    inverse_rms = lax.rsqrt(square / model_width + norm_eps)
    logits = []
    for k in range(out_ref.shape[0]):
        wanted = lane == routes_ref[:, k : k + 1] + shift
        logits.append(jnp.sum(jnp.where(wanted, extra, 0.0), axis=1, keepdims=True) * inverse_rms)
    peak = functools.reduce(jnp.maximum, logits)
    shares = [jnp.exp(v - peak) for v in logits]
    total = functools.reduce(jnp.add, shares)
    inside = iota((share, padded), 1) < lines
    for k in range(out_ref.shape[0]):
        gate = summed[2 * k] * inverse_rms
        up = summed[2 * k + 1] * inverse_rms
        act = gate / (1.0 + jnp.exp(-gate)) * up
        out_ref[k] = jnp.where(inside, act * (shares[k] / total), 0.0).astype(jnp.bfloat16)


def down_kernel(me_ref, routes_ref, *refs):
    down_ref, out_ref, act_ref = refs[-3:]
    chunks = refs[:-3]
    e = pl.program_id(0)
    topk, share, _ = chunks[0].shape
    lines = down_ref.shape[2]

    @pl.when(e == 0)
    def _():
        me = me_ref[0]
        out_ref[...] = jnp.zeros_like(out_ref)
        for o, chunk in enumerate(chunks):
            begin = pl.multiple_of((me ^ o) * share, share)
            act_ref[:, pl.ds(begin, share), :] = chunk[...]

    mine = jnp.zeros((act_ref.shape[1], lines), jnp.float32)
    for k in range(topk):
        chosen = routes_ref[:, k : k + 1] == e
        mine = mine + jnp.where(chosen, act_ref[k, :, :lines].astype(jnp.float32), 0.0)
    out_ref[...] += jnp.dot(
        mine.astype(jnp.bfloat16), down_ref[0, 0], preferred_element_type=jnp.float32
    )


def experts_part(h_mid, moe_gain, w_router, expert_lines, routes):
    rows = lax.axis_size("row")
    cols = lax.axis_size("col")
    row_index = lax.axis_index("row")
    col_index = lax.axis_index("col")
    experts, _, lines, width = expert_lines.shape
    own, _ = h_mid.shape
    tokens = own * rows
    topk = routes.shape[1]
    share = tokens // cols
    padded = up_to(lines + experts + 1, LANES)
    shift = lines - (padded - LANES)
    me = col_index.astype(jnp.int32).reshape(1)

    order = row_index ^ jnp.arange(rows, dtype=jnp.int32)
    routes = routes.reshape(rows, own, topk)[order].reshape(tokens, topk)
    my_routes = lax.dynamic_slice_in_dim(routes, col_index * share, share, 0)
    router = jnp.pad(w_router, ((0, 0), (shift, LANES - shift - experts)))
    every_h = jnp.concatenate(
        [h_mid] + [from_peer(h_mid, "row", o) for o in range(1, rows)], axis=0
    )
    part_spec = lambda part: pl.BlockSpec((1, 1, lines, width), lambda e, me: (e, part, 0, 0))
    whole = lambda a: pl.BlockSpec(a.shape, lambda e, me: (0,) * a.ndim)
    gain = moe_gain.reshape(1, width)
    partial = pl.pallas_call(
        gate_up_kernel,
        grid_spec=pltpu.PrefetchScalarGridSpec(
            num_scalar_prefetch=1,
            grid=(experts,),
            in_specs=[whole(every_h), whole(gain), whole(router), whole(routes)]
            + [part_spec(0), part_spec(1)],
            out_specs=pl.BlockSpec((cols, 2 * topk, share, padded), lambda e, me: (0, 0, 0, 0)),
            scratch_shapes=[pltpu.VMEM((2 * topk, tokens, padded), jnp.float32)],
        ),
        out_shape=jax.ShapeDtypeStruct((cols, 2 * topk, share, padded), jnp.bfloat16),
        compiler_params=params(),
        cost_estimate=pl.CostEstimate(
            flops=4 * experts * tokens * lines * width,
            bytes_accessed=4 * experts * lines * width,
            transcendentals=0,
        ),
        name="gate_up",
    )(me, every_h, gain, router, routes, expert_lines, expert_lines)
    gathered = [partial[0]] + [from_peer(partial[o], "col", o) for o in range(1, cols)]
    activated = pl.pallas_call(
        functools.partial(activate_kernel, lines, experts, width * cols),
        out_shape=jax.ShapeDtypeStruct((topk, share, padded), jnp.bfloat16),
        compiler_params=params(),
        name="activate",
    )(my_routes, *gathered)
    chunks = [activated] + [from_peer(activated, "col", o) for o in range(1, cols)]
    produced = pl.pallas_call(
        down_kernel,
        grid_spec=pltpu.PrefetchScalarGridSpec(
            num_scalar_prefetch=1,
            grid=(experts,),
            in_specs=[whole(routes)] + [whole(c) for c in chunks] + [part_spec(2)],
            out_specs=pl.BlockSpec((tokens, width), lambda e, me: (0, 0)),
            scratch_shapes=[pltpu.VMEM((topk, tokens, padded), jnp.bfloat16)],
        ),
        out_shape=jax.ShapeDtypeStruct((tokens, width), jnp.float32),
        compiler_params=params(),
        cost_estimate=pl.CostEstimate(
            flops=2 * experts * tokens * lines * width,
            bytes_accessed=2 * experts * lines * width,
            transcendentals=0,
        ),
        name="down",
    )(me, routes, *chunks, expert_lines)
    blocks = produced.reshape(rows, own, width)
    mixed = blocks[0]
    for o in range(1, rows):
        mixed = mixed + from_peer(blocks[o], "row", o)
    return mixed


def local(
    hidden,
    queries,
    new_kv,
    prompt_kv,
    suffix_kv,
    lengths,
    w_out,
    moe_gain,
    w_router,
    expert_weights,
    old_lines,
    new_lines,
    routes,
):
    expert_lines = jnp.transpose(expert_weights, (0, 2, 1, 3))
    moved = migrate(expert_lines, old_lines, new_lines)
    attended = attend(queries, new_kv, prompt_kv, suffix_kv, lengths)
    projected = jnp.dot(attended, w_out, preferred_element_type=jnp.float32)
    h_mid = (hidden.astype(jnp.float32) + projected).astype(jnp.bfloat16)
    mixed = experts_part(h_mid, moe_gain, w_router, expert_lines, routes)
    return (h_mid.astype(jnp.float32) + mixed, jnp.transpose(moved, (0, 2, 1, 3)))


def solution(mesh):
    return jax.shard_map(
        local,
        mesh=mesh,
        in_specs=(
            P("row", "col"),
            P("row", None),
            P("row", None, None),
            P("row", None, "col", None),
            P("row", None, "col", None),
            P("row"),
            P(None, "col"),
            P("col"),
            P("col", None),
            P(None, "row", None, "col"),
            P(),
            P(),
            P(),
        ),
        out_specs=(P("row", "col"), P(None, "row", None, "col")),
        check_vma=False,
    )
```

```python
import functools

import jax
import jax.numpy as jnp
from jax import lax
from jax.experimental import pallas as pl
from jax.experimental.pallas import tpu as pltpu
from jax.sharding import PartitionSpec as P

KVH = 16
HD = 128
REP = 2
TILE = 16
LANES = 128

norm_eps = 1e-06
neg_big = -1e30
VMEM_LIMIT = 48 * 1024 * 1024


def up_to(value, unit):
    return -(-value // unit) * unit


def iota(shape, axis):
    return lax.broadcasted_iota(jnp.int32, shape, axis)


def ones_where(mask):
    return jnp.where(mask, 1.0, 0.0).astype(jnp.bfloat16)


def params():
    return pltpu.CompilerParams(vmem_limit_bytes=VMEM_LIMIT)


def find_slots(table_row, id_row):
    full = table_row.shape[1]
    ids = id_row.shape[1]
    high_count = up_to(-(-full // 64), 16)
    table_high = ones_where(iota((high_count, full), 0) == (table_row >> 6))
    half = iota((LANES, full), 0)
    slot = iota((LANES, full), 1)
    value = jnp.where(half < 64, slot >> 7, slot & 127).astype(jnp.float32)
    table_low = jnp.where((half & 63) == (table_row & 63), value, 0.0).astype(jnp.bfloat16)
    square = lax.dot_general(
        table_low, table_high, (((1,), (1,)), ((), ())), preferred_element_type=jnp.float32
    )
    id_high = ones_where(iota((high_count, ids), 0) == (id_row >> 6))
    spread = jnp.dot(square.astype(jnp.bfloat16), id_high, preferred_element_type=jnp.float32)
    chosen = jnp.where((iota((LANES, ids), 0) & 63) == (id_row & 63), spread, 0.0)
    high = jnp.sum(chosen[:64], axis=0, keepdims=True)
    low = jnp.sum(chosen[64:], axis=0, keepdims=True)
    return high * 128.0 + low


def segment_plan(counts, experts, rows):
    starts = []
    running = jnp.zeros((rows, LANES), jnp.float32)
    for e in range(experts):
        starts.append(running)
        running = running + counts[e * rows : (e + 1) * rows]
    start = jnp.concatenate(starts, axis=0)
    lead = jnp.floor(start * (1.0 / TILE))
    tail = jnp.floor((start + counts + (TILE - 1.0)) * (1.0 / TILE))
    tiles = jnp.where(counts > 0.0, tail - lead, 0.0)
    pairs = experts * rows
    line = iota((pairs, pairs), 0)
    column = iota((pairs, pairs), 1)
    earlier = ones_where((line // rows == column // rows) & (column < line))
    base = jnp.dot(earlier, tiles.astype(jnp.bfloat16), preferred_element_type=jnp.float32)
    return start, lead, tiles, base


def write_plan(plan_ref, start, lead, tiles, base):
    shared = start - lead * TILE
    for n, part in enumerate((lead, tiles, base, shared)):
        plan_ref[n] = part.astype(jnp.int32)


def outgoing_kernel(lines, rows, new_ref, held_ref, stack_ref, plan_ref):
    experts = new_ref.shape[0]
    width = held_ref.shape[1]
    real = iota((1, width), 1) < lines
    hits = []
    for e in range(experts):
        slots = find_slots(new_ref[e : e + 1, :], held_ref[e : e + 1, :])
        peer = jnp.floor((slots + 0.5) * (1.0 / lines)).astype(jnp.int32)
        hits.append(jnp.where((iota((rows, width), 0) == peer) & real, 1.0, 0.0))
    hits = jnp.concatenate(hits, axis=0)
    until = ones_where(iota((width, width), 0) <= iota((width, width), 1))
    ranks = jnp.dot(hits.astype(jnp.bfloat16), until, preferred_element_type=jnp.float32)
    counts = jnp.broadcast_to(jnp.sum(hits, axis=1, keepdims=True), (experts * rows, LANES))
    start, lead, tiles, base = segment_plan(counts, experts, rows)
    write_plan(plan_ref, start, lead, tiles, base)
    offset = (base * TILE + start - lead * TILE - 1.0)[:, :1]
    placed = hits * (ranks + offset)
    for e in range(experts):
        row = jnp.sum(placed[e * rows : (e + 1) * rows], axis=0, keepdims=True)
        stack_ref[e] = jnp.where(real, row, -1.0).astype(jnp.int32)


def incoming_kernel(lines, rows, old_ref, wanted_ref, stack_ref, plan_ref):
    experts = old_ref.shape[0]
    width = wanted_ref.shape[1]
    real = iota((1, width), 1) < lines
    held_at = []
    hits = []
    for e in range(experts):
        slots = find_slots(old_ref[e : e + 1, :], wanted_ref[e : e + 1, :])
        held_at.append(jnp.where(real, slots, 1e9))
        peer = jnp.floor((slots + 0.5) * (1.0 / lines)).astype(jnp.int32)
        hits.append(jnp.where((iota((rows, width), 0) == peer) & real, 1.0, 0.0))
    hits = jnp.concatenate(hits, axis=0)
    counts = jnp.broadcast_to(jnp.sum(hits, axis=1, keepdims=True), (experts * rows, LANES))
    start, lead, tiles, base = segment_plan(counts, experts, rows)
    write_plan(plan_ref, start, lead, tiles, base)
    blank = jnp.zeros((LANES - experts, width), jnp.float32)
    columns = jnp.transpose(jnp.concatenate(held_at + [blank], axis=0))
    rows_out = []
    for e in range(experts):
        mine = slice(e * rows, (e + 1) * rows)
        before = jnp.where(columns[:, e : e + 1] < held_at[e], 1.0, 0.0)
        rank = jnp.sum(before, axis=0, keepdims=True)
        ahead = jnp.zeros((1, LANES), jnp.float32)
        firsts = []
        for r in range(rows):
            firsts.append(ahead)
            ahead = ahead + counts[e * rows + r : e * rows + r + 1]
        first = jnp.concatenate(firsts, axis=0)
        offset = (base[mine] * TILE + start[mine] - lead[mine] * TILE - first)[:, :1]
        rows_out.append(jnp.sum(hits[mine] * (rank + offset), axis=0, keepdims=True))
    stack_ref[...] = jnp.transpose(jnp.concatenate(rows_out + [blank], axis=0))


def pack_kernel(rows, plan_ref, place_ref, lines_ref, out_ref, stage_ref):
    e = pl.program_id(0)
    pairs = pl.num_programs(0) * rows
    deep, _ = stage_ref.shape
    lines = lines_ref.shape[2]
    place = place_ref[0][:, :lines]
    onehot = ones_where(iota((deep, lines), 0) == place)
    stage_ref[...] = jnp.dot(
        onehot, lines_ref[0, 0], preferred_element_type=jnp.float32
    ).astype(jnp.bfloat16)

    def one_peer(d, carry):
        k = e * rows + d
        lead = plan_ref[k]
        tiles = plan_ref[pairs + k]
        base = plan_ref[2 * pairs + k]
        shared = plan_ref[3 * pairs + k] > 0

        def source(t):
            return stage_ref[pl.ds(pl.multiple_of((base + t) * TILE, TILE), TILE), :]

        def target(t):
            return pl.ds(pl.multiple_of((lead + t) * TILE, TILE), TILE)

        @pl.when((tiles > 0) & shared)
        def _():
            out_ref[d, target(0), :] = out_ref[d, target(0), :] + source(0)

        @pl.when((tiles > 0) & jnp.logical_not(shared))
        def _():
            out_ref[d, target(0), :] = source(0)

        def put(t, c):
            out_ref[d, target(t), :] = source(t)
            return c

        return lax.fori_loop(1, tiles, put, carry)

    lax.fori_loop(0, rows, one_peer, 0)


def unpack_kernel(rows, plan_ref, place_ref, block_ref, *rest):
    out_ref, stage_ref = rest[-2:]
    e = pl.program_id(0)
    pairs = pl.num_programs(0) * rows
    deep, _ = stage_ref.shape
    lines = out_ref.shape[2]

    @pl.when(e == 0)
    def _():
        stage_ref[...] = jnp.zeros_like(stage_ref)

    def one_peer(s, carry):
        k = e * rows + s
        lead = plan_ref[k]
        tiles = plan_ref[pairs + k]
        base = plan_ref[2 * pairs + k]

        def put(t, c):
            here = pl.ds(pl.multiple_of((base + t) * TILE, TILE), TILE)
            there = pl.ds(pl.multiple_of((lead + t) * TILE, TILE), TILE)
            stage_ref[here, :] = block_ref[s, there, :]
            return c

        return lax.fori_loop(0, tiles, put, carry)

    lax.fori_loop(0, rows, one_peer, 0)
    place = jnp.where(iota((lines, LANES), 1) == e, place_ref[:lines, :], 0.0)
    place = jnp.sum(place, axis=1, keepdims=True).astype(jnp.int32)
    onehot = ones_where(iota((lines, deep), 1) == place)
    out_ref[0, 0] = jnp.dot(
        onehot, stage_ref[...], preferred_element_type=jnp.float32
    ).astype(jnp.bfloat16)


def call_plan(kernel, name, table, ids, lines, rows, transposed):
    experts, width = ids.shape
    stack = (
        jax.ShapeDtypeStruct((width, LANES), jnp.float32)
        if transposed
        else jax.ShapeDtypeStruct((experts, 1, width), jnp.int32)
    )
    stack, plan = pl.pallas_call(
        functools.partial(kernel, lines, rows),
        out_shape=(stack, jax.ShapeDtypeStruct((4, experts * rows, LANES), jnp.int32)),
        compiler_params=params(),
        cost_estimate=pl.CostEstimate(
            flops=20 * experts * table.shape[1] * 256,
            bytes_accessed=8 * table.size,
            transcendentals=0,
        ),
        name=name,
    )(table, ids)
    return stack, plan[:, :, 0].reshape(-1)


def pack(expert_lines, place, plan, part, rows, block_rows, deep):
    experts, _, lines, width = expert_lines.shape
    return pl.pallas_call(
        functools.partial(pack_kernel, rows),
        grid_spec=pltpu.PrefetchScalarGridSpec(
            num_scalar_prefetch=1,
            grid=(experts,),
            in_specs=[
                pl.BlockSpec((1, 1, place.shape[2]), lambda e, plan: (e, 0, 0)),
                pl.BlockSpec((1, 1, lines, width), lambda e, plan: (e, part, 0, 0)),
            ],
            out_specs=pl.BlockSpec((rows, block_rows, width), lambda e, plan: (0, 0, 0)),
            scratch_shapes=[pltpu.VMEM((deep, width), jnp.bfloat16)],
        ),
        out_shape=jax.ShapeDtypeStruct((rows, block_rows, width), jnp.bfloat16),
        compiler_params=params(),
        cost_estimate=pl.CostEstimate(
            flops=2 * experts * deep * lines * width,
            bytes_accessed=4 * experts * lines * width,
            transcendentals=0,
        ),
        name="pack_lines",
    )(plan, place, expert_lines)


def unpack(arrived, place, plan, part, shape, deep, previous):
    experts, _, lines, width = shape
    rows, block_rows, _ = arrived.shape
    in_specs = [
        pl.BlockSpec(place.shape, lambda e, plan: (0, 0)),
        pl.BlockSpec((rows, block_rows, width), lambda e, plan: (0, 0, 0)),
    ]
    operands = [plan, place, arrived]
    aliases = {}
    if previous is not None:
        in_specs.append(pl.BlockSpec(memory_space=pl.ANY))
        operands.append(previous)
        aliases = {3: 0}
    return pl.pallas_call(
        functools.partial(unpack_kernel, rows),
        grid_spec=pltpu.PrefetchScalarGridSpec(
            num_scalar_prefetch=1,
            grid=(experts,),
            in_specs=in_specs,
            out_specs=pl.BlockSpec((1, 1, lines, width), lambda e, plan: (e, part, 0, 0)),
            scratch_shapes=[pltpu.VMEM((deep, width), jnp.bfloat16)],
        ),
        out_shape=jax.ShapeDtypeStruct(shape, jnp.bfloat16),
        input_output_aliases=aliases,
        compiler_params=params(),
        cost_estimate=pl.CostEstimate(
            flops=2 * experts * deep * lines * width,
            bytes_accessed=4 * experts * lines * width,
            transcendentals=0,
        ),
        name="unpack_lines",
    )(*operands)


def after_kernel(*refs):
    del refs


def after(values, signals):
    anywhere = pl.BlockSpec(memory_space=pl.ANY)
    return pl.pallas_call(
        after_kernel,
        in_specs=[anywhere] * (len(values) + len(signals)),
        out_specs=[anywhere] * len(values),
        out_shape=[jax.ShapeDtypeStruct(v.shape, v.dtype) for v in values],
        input_output_aliases={n: n for n in range(len(values))},
        name="after",
    )(*values, *signals)


def own_ids(table, lines, width):
    mine = lax.dynamic_slice_in_dim(table, lax.axis_index("row") * lines, lines, 1)
    return jnp.pad(mine, ((0, 0), (0, width - lines)), constant_values=-1)


def from_peer(block, axis, offset):
    size = lax.axis_size(axis)
    return lax.ppermute(block, axis, [(i, i ^ offset) for i in range(size)])


class Migration:
    def __init__(self, expert_lines, old_lines, new_lines):
        rows = lax.axis_size("row")
        experts, self.parts, lines, _ = expert_lines.shape
        padded = up_to(lines, LANES)
        block_rows = up_to(experts * lines // rows, TILE)
        self.deep = up_to(lines + 2 * (TILE - 1) * rows, TILE)
        self.shape = expert_lines.shape
        out_place, out_plan = call_plan(
            outgoing_kernel, "outgoing_plan", new_lines, own_ids(old_lines, lines, padded),
            lines, rows, False,
        )
        self.in_place, self.in_plan = call_plan(
            incoming_kernel, "incoming_plan", old_lines, own_ids(new_lines, lines, padded),
            lines, rows, True,
        )
        self.packed = [
            pack(expert_lines, out_place, out_plan, part, rows, block_rows, self.deep)
            for part in range(self.parts)
        ]
        self.arrived = []

    def send(self, part, signals=()):
        block = self.packed[part]
        if signals:
            (block,) = after([block], signals)
        self.arrived.append(
            lax.all_to_all(block, "row", split_axis=0, concat_axis=0, tiled=True)
        )

    def finish(self):
        moved = None
        for part in range(self.parts):
            moved = unpack(
                self.arrived[part], self.in_place, self.in_plan, part, self.shape,
                up_to(self.deep, LANES), moved,
            )
        return moved


def attend(queries, new_kv, prompt_kv, suffix_kv, lengths):
    seq_count = queries.shape[0]
    prompt_rows = prompt_kv.shape[2]
    suffix_rows = suffix_kv.shape[2]
    col_index = lax.axis_index("col")
    query_heads = queries.reshape(seq_count, KVH, REP, HD)
    prompt_keys = prompt_kv[0, 0].reshape(prompt_rows, KVH, HD)
    prompt_values = prompt_kv[0, 1].reshape(prompt_rows, KVH, HD)
    suffix_keys = suffix_kv[:, 0].reshape(seq_count, suffix_rows, KVH, HD)
    suffix_values = suffix_kv[:, 1].reshape(seq_count, suffix_rows, KVH, HD)
    own_keys = new_kv[:, 0].reshape(seq_count, KVH, HD)
    own_values = new_kv[:, 1].reshape(seq_count, KVH, HD)
    score_scale = HD ** (-0.5)
    prompt_scores = (
        jnp.einsum("skgd,pkd->skgp", query_heads, prompt_keys, preferred_element_type=jnp.float32)
        * score_scale
    )
    suffix_scores = (
        jnp.einsum("skgd,spkd->skgp", query_heads, suffix_keys, preferred_element_type=jnp.float32)
        * score_scale
    )
    own_scores = (
        jnp.einsum("skgd,skd->skg", query_heads, own_keys, preferred_element_type=jnp.float32)
        * score_scale
    )
    positions = col_index * suffix_rows + jnp.arange(suffix_rows, dtype=jnp.int32)
    live_slots = (positions[None, :] < lengths[:, None])[:, None, None, :]
    holder = col_index == 0
    suffix_scores = jnp.where(live_slots, suffix_scores, neg_big)
    own_scores = jnp.where(holder, own_scores, neg_big)
    highest = jnp.maximum(
        jnp.maximum(jnp.max(prompt_scores, axis=-1), jnp.max(suffix_scores, axis=-1)), own_scores
    )
    prompt_weights = jnp.exp(prompt_scores - highest[..., None])
    suffix_weights = jnp.where(live_slots, jnp.exp(suffix_scores - highest[..., None]), 0.0)
    own_weights = jnp.where(holder, jnp.exp(own_scores - highest), 0.0)
    totals = jnp.sum(prompt_weights, axis=-1) + jnp.sum(suffix_weights, axis=-1) + own_weights
    mixture = jnp.einsum(
        "skgp,pkd->skgd",
        prompt_weights.astype(jnp.bfloat16),
        prompt_values,
        preferred_element_type=jnp.float32,
    )
    mixture = mixture + jnp.einsum(
        "skgp,spkd->skgd",
        suffix_weights.astype(jnp.bfloat16),
        suffix_values,
        preferred_element_type=jnp.float32,
    )
    own_rounded = lax.optimization_barrier(own_weights.astype(jnp.bfloat16)).astype(jnp.float32)
    mixture = mixture + own_rounded[..., None] * own_values.astype(jnp.float32)[:, :, None, :]
    heads = KVH * REP
    bundle = jnp.concatenate(
        [
            mixture.reshape(seq_count, heads * HD),
            highest.reshape(seq_count, heads),
            totals.reshape(seq_count, heads),
            jnp.zeros((seq_count, LANES - 2 * heads), jnp.float32),
        ],
        axis=1,
    )
    bundles = [bundle] + [from_peer(bundle, "col", o) for o in range(1, lax.axis_size("col"))]
    every = jnp.stack(bundles)
    mixtures = every[:, :, : heads * HD].reshape(-1, seq_count, heads, HD)
    peaks = every[:, :, heads * HD : heads * HD + heads]
    sums = every[:, :, heads * HD + heads : heads * HD + 2 * heads]
    factors = jnp.exp(peaks - jnp.max(peaks, axis=0))
    total = jnp.sum(sums * factors, axis=0)
    mixed = jnp.sum(mixtures * factors[..., None], axis=0)
    return (mixed / total[..., None]).astype(jnp.bfloat16).reshape(seq_count, heads * HD)


def gate_up_kernel(me_ref, h_ref, gain_ref, router_ref, routes_ref, gate_ref, up_ref, out_ref, acc_ref):
    e = pl.program_id(0)
    tokens = h_ref.shape[0]
    lines = gate_ref.shape[2]
    padded = out_ref.shape[3]
    h = h_ref[...].astype(jnp.float32)
    scaled = (h * gain_ref[...].astype(jnp.float32)).astype(jnp.bfloat16)

    @pl.when(e == 0)
    def _():
        acc_ref[...] = jnp.zeros_like(acc_ref)

    against = (((1,), (1,)), ((), ()))
    gate = lax.dot_general(scaled, gate_ref[0, 0], against, preferred_element_type=jnp.float32)
    up = lax.dot_general(scaled, up_ref[0, 0], against, preferred_element_type=jnp.float32)
    for k in range(routes_ref.shape[1]):
        chosen = routes_ref[:, k : k + 1] == e
        acc_ref[2 * k, :, :lines] += jnp.where(chosen, gate, 0.0)
        acc_ref[2 * k + 1, :, :lines] += jnp.where(chosen, up, 0.0)

    @pl.when(e == pl.num_programs(0) - 1)
    def _():
        last = padded - LANES
        shift = lines - last
        experts = pl.num_programs(0)
        extra = jnp.dot(scaled, router_ref[...], preferred_element_type=jnp.float32)
        lane = iota((tokens, LANES), 1)
        square = jnp.sum(h * h, axis=1, keepdims=True)
        extra = jnp.where(lane == shift + experts, square, extra)
        high = extra.astype(jnp.bfloat16).astype(jnp.float32)
        low = extra - high
        acc_ref[0, :, last:] += jnp.where(lane >= shift, high, 0.0)
        acc_ref[1, :, last:] += jnp.where(lane >= shift, low, 0.0)
        peers, _, share, _ = out_ref.shape
        me = me_ref[0]
        for o in range(peers):
            begin = pl.multiple_of((me ^ o) * share, share)
            out_ref[o] = acc_ref[:, pl.ds(begin, share), :].astype(jnp.bfloat16)


def activate_kernel(lines, experts, model_width, routes_ref, *refs):
    out_ref = refs[-1]
    summed = refs[0][...].astype(jnp.float32)
    for ref in refs[1:-1]:
        summed = summed + ref[...].astype(jnp.float32)
    _, share, padded = summed.shape
    last = padded - LANES
    shift = lines - last
    extra = summed[0, :, last:] + summed[1, :, last:]
    lane = iota((share, LANES), 1)
    square = jnp.sum(jnp.where(lane == shift + experts, extra, 0.0), axis=1, keepdims=True)
    inverse_rms = lax.rsqrt(square / model_width + norm_eps)
    logits = []
    for k in range(out_ref.shape[0]):
        wanted = lane == routes_ref[:, k : k + 1] + shift
        logits.append(jnp.sum(jnp.where(wanted, extra, 0.0), axis=1, keepdims=True) * inverse_rms)
    peak = functools.reduce(jnp.maximum, logits)
    shares = [jnp.exp(v - peak) for v in logits]
    total = functools.reduce(jnp.add, shares)
    inside = iota((share, padded), 1) < lines
    for k in range(out_ref.shape[0]):
        gate = summed[2 * k] * inverse_rms
        up = summed[2 * k + 1] * inverse_rms
        act = gate / (1.0 + jnp.exp(-gate)) * up
        out_ref[k] = jnp.where(inside, act * (shares[k] / total), 0.0).astype(jnp.bfloat16)


def down_kernel(me_ref, routes_ref, *refs):
    down_ref, out_ref, act_ref = refs[-3:]
    chunks = refs[:-3]
    e = pl.program_id(0)
    topk, share, _ = chunks[0].shape
    lines = down_ref.shape[2]

    @pl.when(e == 0)
    def _():
        me = me_ref[0]
        out_ref[...] = jnp.zeros_like(out_ref)
        for o, chunk in enumerate(chunks):
            begin = pl.multiple_of((me ^ o) * share, share)
            act_ref[:, pl.ds(begin, share), :] = chunk[...]

    mine = jnp.zeros((act_ref.shape[1], lines), jnp.float32)
    for k in range(topk):
        chosen = routes_ref[:, k : k + 1] == e
        mine = mine + jnp.where(chosen, act_ref[k, :, :lines].astype(jnp.float32), 0.0)
    out_ref[...] += jnp.dot(
        mine.astype(jnp.bfloat16), down_ref[0, 0], preferred_element_type=jnp.float32
    )


def experts_part(h_mid, moe_gain, w_router, expert_lines, routes, migration):
    rows = lax.axis_size("row")
    cols = lax.axis_size("col")
    row_index = lax.axis_index("row")
    col_index = lax.axis_index("col")
    experts, _, lines, width = expert_lines.shape
    own, _ = h_mid.shape
    tokens = own * rows
    topk = routes.shape[1]
    share = tokens // cols
    padded = up_to(lines + experts + 1, LANES)
    shift = lines - (padded - LANES)
    me = col_index.astype(jnp.int32).reshape(1)

    order = row_index ^ jnp.arange(rows, dtype=jnp.int32)
    routes = routes.reshape(rows, own, topk)[order].reshape(tokens, topk)
    my_routes = lax.dynamic_slice_in_dim(routes, col_index * share, share, 0)
    router = jnp.pad(w_router, ((0, 0), (shift, LANES - shift - experts)))
    every_h = jnp.concatenate(
        [h_mid] + [from_peer(h_mid, "row", o) for o in range(1, rows)], axis=0
    )
    migration.send(1, [every_h])
    part_spec = lambda part: pl.BlockSpec((1, 1, lines, width), lambda e, me: (e, part, 0, 0))
    whole = lambda a: pl.BlockSpec(a.shape, lambda e, me: (0,) * a.ndim)
    gain = moe_gain.reshape(1, width)
    partial = pl.pallas_call(
        gate_up_kernel,
        grid_spec=pltpu.PrefetchScalarGridSpec(
            num_scalar_prefetch=1,
            grid=(experts,),
            in_specs=[whole(every_h), whole(gain), whole(router), whole(routes)]
            + [part_spec(0), part_spec(1)],
            out_specs=pl.BlockSpec((cols, 2 * topk, share, padded), lambda e, me: (0, 0, 0, 0)),
            scratch_shapes=[pltpu.VMEM((2 * topk, tokens, padded), jnp.float32)],
        ),
        out_shape=jax.ShapeDtypeStruct((cols, 2 * topk, share, padded), jnp.bfloat16),
        compiler_params=params(),
        cost_estimate=pl.CostEstimate(
            flops=4 * experts * tokens * lines * width,
            bytes_accessed=4 * experts * lines * width,
            transcendentals=0,
        ),
        name="gate_up",
    )(me, every_h, gain, router, routes, expert_lines, expert_lines)
    gathered = [partial[0]] + [from_peer(partial[o], "col", o) for o in range(1, cols)]
    activated = pl.pallas_call(
        functools.partial(activate_kernel, lines, experts, width * cols),
        out_shape=jax.ShapeDtypeStruct((topk, share, padded), jnp.bfloat16),
        compiler_params=params(),
        name="activate",
    )(my_routes, *gathered)
    chunks = [activated] + [from_peer(activated, "col", o) for o in range(1, cols)]
    produced = pl.pallas_call(
        down_kernel,
        grid_spec=pltpu.PrefetchScalarGridSpec(
            num_scalar_prefetch=1,
            grid=(experts,),
            in_specs=[whole(routes)] + [whole(c) for c in chunks] + [part_spec(2)],
            out_specs=pl.BlockSpec((tokens, width), lambda e, me: (0, 0)),
            scratch_shapes=[pltpu.VMEM((topk, tokens, padded), jnp.bfloat16)],
        ),
        out_shape=jax.ShapeDtypeStruct((tokens, width), jnp.float32),
        compiler_params=params(),
        cost_estimate=pl.CostEstimate(
            flops=2 * experts * tokens * lines * width,
            bytes_accessed=2 * experts * lines * width,
            transcendentals=0,
        ),
        name="down",
    )(me, routes, *chunks, expert_lines)
    blocks = produced.reshape(rows, own, width)
    mixed = blocks[0]
    for o in range(1, rows):
        mixed = mixed + from_peer(blocks[o], "row", o)
    return mixed


def local(
    hidden,
    queries,
    new_kv,
    prompt_kv,
    suffix_kv,
    lengths,
    w_out,
    moe_gain,
    w_router,
    expert_weights,
    old_lines,
    new_lines,
    routes,
):
    expert_lines = jnp.transpose(expert_weights, (0, 2, 1, 3))
    migration = Migration(expert_lines, old_lines, new_lines)
    migration.send(0)
    attended = attend(queries, new_kv, prompt_kv, suffix_kv, lengths)
    projected = jnp.dot(attended, w_out, preferred_element_type=jnp.float32)
    h_mid = (hidden.astype(jnp.float32) + projected).astype(jnp.bfloat16)
    mixed = experts_part(h_mid, moe_gain, w_router, expert_lines, routes, migration)
    migration.send(2, [mixed])
    moved = migration.finish()
    return (h_mid.astype(jnp.float32) + mixed, jnp.transpose(moved, (0, 2, 1, 3)))


def solution(mesh):
    return jax.shard_map(
        local,
        mesh=mesh,
        in_specs=(
            P("row", "col"),
            P("row", None),
            P("row", None, None),
            P("row", None, "col", None),
            P("row", None, "col", None),
            P("row"),
            P(None, "col"),
            P("col"),
            P("col", None),
            P(None, "row", None, "col"),
            P(),
            P(),
            P(),
        ),
        out_specs=(P("row", "col"), P(None, "row", None, "col")),
        check_vma=False,
    )
```

```python
import functools

import jax
import jax.numpy as jnp
from jax import lax
from jax.experimental import pallas as pl
from jax.experimental.pallas import tpu as pltpu
from jax.sharding import PartitionSpec as P

KVH = 16
HD = 128
REP = 2
TILE = 16
LANES = 128

norm_eps = 1e-06
neg_big = -1e30
VMEM_LIMIT = 48 * 1024 * 1024


def up_to(value, unit):
    return -(-value // unit) * unit


def iota(shape, axis):
    return lax.broadcasted_iota(jnp.int32, shape, axis)


def ones_where(mask):
    return jnp.where(mask, 1.0, 0.0).astype(jnp.bfloat16)


def params():
    return pltpu.CompilerParams(vmem_limit_bytes=VMEM_LIMIT)


def counting(shape, axis):
    return iota(shape, axis).astype(jnp.float32).astype(jnp.bfloat16)


def as_bf16(values):
    return values.astype(jnp.float32).astype(jnp.bfloat16)


def equal_ones(left, right):
    one = jnp.ones((), jnp.bfloat16)
    return jnp.where(left == right, one, jnp.zeros((), jnp.bfloat16))


def within(place, block):
    place = place - 256 * block
    return as_bf16(jnp.where((place >= 0) & (place < 256), place, -1))


def find_slots(table_row, id_row, numbers, values):
    full = table_row.shape[1]
    ids = id_row.shape[1]
    high_count = up_to(-(-full // 64), 16)
    table_high = equal_ones(numbers[:high_count], as_bf16(table_row >> 6))
    low = as_bf16(table_row & 63)
    zero = jnp.zeros((), jnp.bfloat16)
    table_low = jnp.concatenate(
        [jnp.where(numbers[:64] == low, part, zero) for part in values], axis=0
    )
    square = lax.dot_general(
        table_low, table_high, (((1,), (1,)), ((), ())), preferred_element_type=jnp.float32
    )
    id_high = equal_ones(numbers[:high_count, :ids], as_bf16(id_row >> 6))
    spread = jnp.dot(square.astype(jnp.bfloat16), id_high, preferred_element_type=jnp.float32)
    chosen = jnp.where((iota((LANES, ids), 0) & 63) == (id_row & 63), spread, 0.0)
    high = jnp.sum(chosen[:64], axis=0, keepdims=True)
    low = jnp.sum(chosen[64:], axis=0, keepdims=True)
    return high * 128.0 + low


def slot_parts(full):
    high_count = up_to(-(-full // 64), 16)
    numbers = counting((max(high_count, 64), full), 0)
    slot = iota((64, full), 1)
    return numbers, (as_bf16(slot >> 7), as_bf16(slot & 127))


def segment_plan(counts, experts, rows):
    starts = []
    running = jnp.zeros((rows, LANES), jnp.float32)
    for e in range(experts):
        starts.append(running)
        running = running + counts[e * rows : (e + 1) * rows]
    start = jnp.concatenate(starts, axis=0)
    lead = jnp.floor(start * (1.0 / TILE))
    tail = jnp.floor((start + counts + (TILE - 1.0)) * (1.0 / TILE))
    tiles = jnp.where(counts > 0.0, tail - lead, 0.0)
    pairs = experts * rows
    line = iota((pairs, pairs), 0)
    column = iota((pairs, pairs), 1)
    earlier = ones_where((line // rows == column // rows) & (column < line))
    base = jnp.dot(earlier, tiles.astype(jnp.bfloat16), preferred_element_type=jnp.float32)
    return start, lead, tiles, base


def write_plan(plan_ref, start, lead, tiles, base):
    shared = start - lead * TILE
    for n, part in enumerate((lead, tiles, base, shared)):
        plan_ref[n] = part.astype(jnp.int32)


def outgoing_kernel(lines, rows, new_ref, held_ref, stack_ref, plan_ref):
    experts = new_ref.shape[0]
    width = held_ref.shape[1]
    real = iota((1, width), 1) < lines
    hits = []
    numbers, values = slot_parts(new_ref.shape[1])
    for e in range(experts):
        slots = find_slots(new_ref[e : e + 1, :], held_ref[e : e + 1, :], numbers, values)
        peer = jnp.floor((slots + 0.5) * (1.0 / lines)).astype(jnp.int32)
        hits.append(jnp.where((iota((rows, width), 0) == peer) & real, 1.0, 0.0))
    hits = jnp.concatenate(hits, axis=0)
    until = ones_where(iota((width, width), 0) <= iota((width, width), 1))
    ranks = jnp.dot(hits.astype(jnp.bfloat16), until, preferred_element_type=jnp.float32)
    counts = jnp.broadcast_to(jnp.sum(hits, axis=1, keepdims=True), (experts * rows, LANES))
    start, lead, tiles, base = segment_plan(counts, experts, rows)
    write_plan(plan_ref, start, lead, tiles, base)
    offset = (base * TILE + start - lead * TILE - 1.0)[:, :1]
    placed = hits * (ranks + offset)
    for e in range(experts):
        row = jnp.sum(placed[e * rows : (e + 1) * rows], axis=0, keepdims=True)
        stack_ref[e] = jnp.where(real, row, -1.0).astype(jnp.int32)


def incoming_kernel(lines, rows, old_ref, wanted_ref, stack_ref, plan_ref):
    experts = old_ref.shape[0]
    width = wanted_ref.shape[1]
    real = iota((1, width), 1) < lines
    held_at = []
    hits = []
    numbers, values = slot_parts(old_ref.shape[1])
    for e in range(experts):
        slots = find_slots(old_ref[e : e + 1, :], wanted_ref[e : e + 1, :], numbers, values)
        held_at.append(jnp.where(real, slots, 1e9))
        peer = jnp.floor((slots + 0.5) * (1.0 / lines)).astype(jnp.int32)
        hits.append(jnp.where((iota((rows, width), 0) == peer) & real, 1.0, 0.0))
    hits = jnp.concatenate(hits, axis=0)
    counts = jnp.broadcast_to(jnp.sum(hits, axis=1, keepdims=True), (experts * rows, LANES))
    start, lead, tiles, base = segment_plan(counts, experts, rows)
    write_plan(plan_ref, start, lead, tiles, base)
    blank = jnp.zeros((LANES - experts, width), jnp.float32)
    columns = jnp.transpose(jnp.concatenate(held_at + [blank], axis=0))
    rows_out = []
    for e in range(experts):
        mine = slice(e * rows, (e + 1) * rows)
        before = jnp.where(columns[:, e : e + 1] < held_at[e], 1.0, 0.0)
        rank = jnp.sum(before, axis=0, keepdims=True)
        ahead = jnp.zeros((1, LANES), jnp.float32)
        firsts = []
        for r in range(rows):
            firsts.append(ahead)
            ahead = ahead + counts[e * rows + r : e * rows + r + 1]
        first = jnp.concatenate(firsts, axis=0)
        offset = (base[mine] * TILE + start[mine] - lead[mine] * TILE - first)[:, :1]
        rows_out.append(jnp.sum(hits[mine] * (rank + offset), axis=0, keepdims=True))
    stack_ref[...] = jnp.transpose(jnp.concatenate(rows_out + [blank], axis=0))


def pack_kernel(rows, plan_ref, place_ref, lines_ref, out_ref, stage_ref):
    e = pl.program_id(0)
    pairs = pl.num_programs(0) * rows
    deep, _ = stage_ref.shape
    lines = lines_ref.shape[2]
    place = place_ref[0][:, :lines]
    source_lines = lines_ref[0, 0]
    for first in range(0, deep, 256):
        count = min(256, deep - first)
        onehot = equal_ones(counting((count, lines), 0), within(place, first // 256))
        stage_ref[first : first + count] = jnp.dot(
            onehot, source_lines, preferred_element_type=jnp.float32
        ).astype(jnp.bfloat16)

    def one_peer(d, carry):
        k = e * rows + d
        lead = plan_ref[k]
        tiles = plan_ref[pairs + k]
        base = plan_ref[2 * pairs + k]
        shared = plan_ref[3 * pairs + k] > 0

        def source(t):
            return stage_ref[pl.ds(pl.multiple_of((base + t) * TILE, TILE), TILE), :]

        def target(t):
            return pl.ds(pl.multiple_of((lead + t) * TILE, TILE), TILE)

        @pl.when((tiles > 0) & shared)
        def _():
            out_ref[d, target(0), :] = out_ref[d, target(0), :] + source(0)

        @pl.when((tiles > 0) & jnp.logical_not(shared))
        def _():
            out_ref[d, target(0), :] = source(0)

        def put(t, c):
            out_ref[d, target(t), :] = source(t)
            return c

        return lax.fori_loop(1, tiles, put, carry)

    lax.fori_loop(0, rows, one_peer, 0)


def unpack_kernel(rows, plan_ref, place_ref, block_ref, *rest):
    out_ref, stage_ref = rest[-2:]
    e = pl.program_id(0)
    pairs = pl.num_programs(0) * rows
    deep, _ = stage_ref.shape
    lines = out_ref.shape[2]

    @pl.when(e == 0)
    def _():
        stage_ref[...] = jnp.zeros_like(stage_ref)

    def one_peer(s, carry):
        k = e * rows + s
        lead = plan_ref[k]
        tiles = plan_ref[pairs + k]
        base = plan_ref[2 * pairs + k]

        def put(t, c):
            here = pl.ds(pl.multiple_of((base + t) * TILE, TILE), TILE)
            there = pl.ds(pl.multiple_of((lead + t) * TILE, TILE), TILE)
            stage_ref[here, :] = block_ref[s, there, :]
            return c

        return lax.fori_loop(0, tiles, put, carry)

    lax.fori_loop(0, rows, one_peer, 0)
    place = jnp.where(iota((lines, LANES), 1) == e, place_ref[:lines, :], 0.0)
    place = jnp.sum(place, axis=1, keepdims=True).astype(jnp.int32)
    number = counting((lines, 256), 1)
    onehot = jnp.concatenate(
        [equal_ones(number, within(place, block)) for block in range(deep // 256)], axis=1
    )
    out_ref[0, 0] = jnp.dot(
        onehot, stage_ref[...], preferred_element_type=jnp.float32
    ).astype(jnp.bfloat16)


def call_plan(kernel, name, table, ids, lines, rows, transposed):
    experts, width = ids.shape
    stack = (
        jax.ShapeDtypeStruct((width, LANES), jnp.float32)
        if transposed
        else jax.ShapeDtypeStruct((experts, 1, width), jnp.int32)
    )
    stack, plan = pl.pallas_call(
        functools.partial(kernel, lines, rows),
        out_shape=(stack, jax.ShapeDtypeStruct((4, experts * rows, LANES), jnp.int32)),
        compiler_params=params(),
        cost_estimate=pl.CostEstimate(
            flops=20 * experts * table.shape[1] * 256,
            bytes_accessed=8 * table.size,
            transcendentals=0,
        ),
        name=name,
    )(table, ids)
    return stack, plan[:, :, 0].reshape(-1)


def pack(expert_lines, place, plan, piece, rows, block_rows, deep):
    experts, _, lines, _ = expert_lines.shape
    part, column, width = piece
    return pl.pallas_call(
        functools.partial(pack_kernel, rows),
        grid_spec=pltpu.PrefetchScalarGridSpec(
            num_scalar_prefetch=1,
            grid=(experts,),
            in_specs=[
                pl.BlockSpec((1, 1, place.shape[2]), lambda e, plan: (e, 0, 0)),
                pl.BlockSpec((1, 1, lines, width), lambda e, plan: (e, part, 0, column)),
            ],
            out_specs=pl.BlockSpec((rows, block_rows, width), lambda e, plan: (0, 0, 0)),
            scratch_shapes=[pltpu.VMEM((deep, width), jnp.bfloat16)],
        ),
        out_shape=jax.ShapeDtypeStruct((rows, block_rows, width), jnp.bfloat16),
        compiler_params=params(),
        cost_estimate=pl.CostEstimate(
            flops=2 * experts * deep * lines * width,
            bytes_accessed=4 * experts * lines * width,
            transcendentals=0,
        ),
        name="pack_lines",
    )(plan, place, expert_lines)


def unpack(arrived, place, plan, piece, shape, deep, previous):
    experts, _, lines, _ = shape
    part, column, width = piece
    rows, block_rows, _ = arrived.shape
    in_specs = [
        pl.BlockSpec(place.shape, lambda e, plan: (0, 0)),
        pl.BlockSpec((rows, block_rows, width), lambda e, plan: (0, 0, 0)),
    ]
    operands = [plan, place, arrived]
    aliases = {}
    if previous is not None:
        in_specs.append(pl.BlockSpec(memory_space=pl.ANY))
        operands.append(previous)
        aliases = {3: 0}
    return pl.pallas_call(
        functools.partial(unpack_kernel, rows),
        grid_spec=pltpu.PrefetchScalarGridSpec(
            num_scalar_prefetch=1,
            grid=(experts,),
            in_specs=in_specs,
            out_specs=pl.BlockSpec((1, 1, lines, width), lambda e, plan: (e, part, 0, column)),
            scratch_shapes=[pltpu.VMEM((deep, width), jnp.bfloat16)],
        ),
        out_shape=jax.ShapeDtypeStruct(shape, jnp.bfloat16),
        input_output_aliases=aliases,
        compiler_params=params(),
        cost_estimate=pl.CostEstimate(
            flops=2 * experts * deep * lines * width,
            bytes_accessed=4 * experts * lines * width,
            transcendentals=0,
        ),
        name="unpack_lines",
    )(*operands)


def after_kernel(*refs):
    del refs


def after(values, signals):
    anywhere = pl.BlockSpec(memory_space=pl.ANY)
    return pl.pallas_call(
        after_kernel,
        in_specs=[anywhere] * (len(values) + len(signals)),
        out_specs=[anywhere] * len(values),
        out_shape=[jax.ShapeDtypeStruct(v.shape, v.dtype) for v in values],
        input_output_aliases={n: n for n in range(len(values))},
        name="after",
    )(*values, *signals)


def own_ids(table, lines, width):
    mine = lax.dynamic_slice_in_dim(table, lax.axis_index("row") * lines, lines, 1)
    return jnp.pad(mine, ((0, 0), (0, width - lines)), constant_values=-1)


def from_peer(block, axis, offset):
    size = lax.axis_size(axis)
    return lax.ppermute(block, axis, [(i, i ^ offset) for i in range(size)])


def bulk_pieces(parts, width):
    if width % (2 * LANES):
        return [(part, 0, width) for part in range(parts)]
    half = width // 2
    return [(0, 0, half)] + [(part, 0, width) for part in range(1, parts)] + [(0, 1, half)]


class Migration:
    def __init__(self, expert_lines, old_lines, new_lines):
        rows = lax.axis_size("row")
        experts, parts, lines, width = expert_lines.shape
        padded = up_to(lines, LANES)
        block_rows = up_to(experts * lines // rows, TILE)
        self.deep = up_to(lines + 2 * (TILE - 1) * rows, TILE)
        self.shape = expert_lines.shape
        self.pieces = bulk_pieces(parts, width)
        out_place, out_plan = call_plan(
            outgoing_kernel, "outgoing_plan", new_lines, own_ids(old_lines, lines, padded),
            lines, rows, False,
        )
        self.in_place, self.in_plan = call_plan(
            incoming_kernel, "incoming_plan", old_lines, own_ids(new_lines, lines, padded),
            lines, rows, True,
        )
        self.packed = [
            pack(expert_lines, out_place, out_plan, piece, rows, block_rows, self.deep)
            for piece in self.pieces
        ]
        self.arrived = []

    def send(self, signals=()):
        block = self.packed[len(self.arrived)]
        if signals:
            (block,) = after([block], signals)
        self.arrived.append(
            lax.all_to_all(block, "row", split_axis=0, concat_axis=0, tiled=True)
        )

    def finish(self):
        moved = None
        for piece, arrived in zip(self.pieces, self.arrived):
            moved = unpack(
                arrived, self.in_place, self.in_plan, piece, self.shape,
                up_to(self.deep, 256), moved,
            )
        return moved


def attend(queries, new_kv, prompt_kv, suffix_kv, lengths):
    seq_count = queries.shape[0]
    prompt_rows = prompt_kv.shape[2]
    suffix_rows = suffix_kv.shape[2]
    col_index = lax.axis_index("col")
    query_heads = queries.reshape(seq_count, KVH, REP, HD)
    prompt_keys = prompt_kv[0, 0].reshape(prompt_rows, KVH, HD)
    prompt_values = prompt_kv[0, 1].reshape(prompt_rows, KVH, HD)
    suffix_keys = suffix_kv[:, 0].reshape(seq_count, suffix_rows, KVH, HD)
    suffix_values = suffix_kv[:, 1].reshape(seq_count, suffix_rows, KVH, HD)
    own_keys = new_kv[:, 0].reshape(seq_count, KVH, HD)
    own_values = new_kv[:, 1].reshape(seq_count, KVH, HD)
    score_scale = HD ** (-0.5)
    prompt_scores = (
        jnp.einsum("skgd,pkd->skgp", query_heads, prompt_keys, preferred_element_type=jnp.float32)
        * score_scale
    )
    suffix_scores = (
        jnp.einsum("skgd,spkd->skgp", query_heads, suffix_keys, preferred_element_type=jnp.float32)
        * score_scale
    )
    own_scores = (
        jnp.einsum("skgd,skd->skg", query_heads, own_keys, preferred_element_type=jnp.float32)
        * score_scale
    )
    positions = col_index * suffix_rows + jnp.arange(suffix_rows, dtype=jnp.int32)
    live_slots = (positions[None, :] < lengths[:, None])[:, None, None, :]
    holder = col_index == 0
    suffix_scores = jnp.where(live_slots, suffix_scores, neg_big)
    own_scores = jnp.where(holder, own_scores, neg_big)
    highest = jnp.maximum(
        jnp.maximum(jnp.max(prompt_scores, axis=-1), jnp.max(suffix_scores, axis=-1)), own_scores
    )
    prompt_weights = jnp.exp(prompt_scores - highest[..., None])
    suffix_weights = jnp.where(live_slots, jnp.exp(suffix_scores - highest[..., None]), 0.0)
    own_weights = jnp.where(holder, jnp.exp(own_scores - highest), 0.0)
    totals = jnp.sum(prompt_weights, axis=-1) + jnp.sum(suffix_weights, axis=-1) + own_weights
    mixture = jnp.einsum(
        "skgp,pkd->skgd",
        prompt_weights.astype(jnp.bfloat16),
        prompt_values,
        preferred_element_type=jnp.float32,
    )
    mixture = mixture + jnp.einsum(
        "skgp,spkd->skgd",
        suffix_weights.astype(jnp.bfloat16),
        suffix_values,
        preferred_element_type=jnp.float32,
    )
    own_rounded = lax.optimization_barrier(own_weights.astype(jnp.bfloat16)).astype(jnp.float32)
    mixture = mixture + own_rounded[..., None] * own_values.astype(jnp.float32)[:, :, None, :]
    heads = KVH * REP
    bundle = jnp.concatenate(
        [
            mixture.reshape(seq_count, heads * HD),
            highest.reshape(seq_count, heads),
            totals.reshape(seq_count, heads),
            jnp.zeros((seq_count, LANES - 2 * heads), jnp.float32),
        ],
        axis=1,
    )
    bundles = [bundle] + [from_peer(bundle, "col", o) for o in range(1, lax.axis_size("col"))]
    every = jnp.stack(bundles)
    mixtures = every[:, :, : heads * HD].reshape(-1, seq_count, heads, HD)
    peaks = every[:, :, heads * HD : heads * HD + heads]
    sums = every[:, :, heads * HD + heads : heads * HD + 2 * heads]
    factors = jnp.exp(peaks - jnp.max(peaks, axis=0))
    total = jnp.sum(sums * factors, axis=0)
    mixed = jnp.sum(mixtures * factors[..., None], axis=0)
    return (mixed / total[..., None]).astype(jnp.bfloat16).reshape(seq_count, heads * HD)


def gate_up_kernel(me_ref, h_ref, gain_ref, router_ref, routes_ref, gate_ref, up_ref, out_ref, acc_ref):
    e = pl.program_id(0)
    tokens = h_ref.shape[0]
    lines = gate_ref.shape[2]
    padded = out_ref.shape[3]
    h = h_ref[...].astype(jnp.float32)
    scaled = (h * gain_ref[...].astype(jnp.float32)).astype(jnp.bfloat16)

    @pl.when(e == 0)
    def _():
        acc_ref[...] = jnp.zeros_like(acc_ref)

    against = (((1,), (1,)), ((), ()))
    gate = lax.dot_general(scaled, gate_ref[0, 0], against, preferred_element_type=jnp.float32)
    up = lax.dot_general(scaled, up_ref[0, 0], against, preferred_element_type=jnp.float32)
    for k in range(routes_ref.shape[1]):
        chosen = routes_ref[:, k : k + 1] == e
        acc_ref[2 * k, :, :lines] += jnp.where(chosen, gate, 0.0)
        acc_ref[2 * k + 1, :, :lines] += jnp.where(chosen, up, 0.0)

    @pl.when(e == pl.num_programs(0) - 1)
    def _():
        last = padded - LANES
        shift = lines - last
        experts = pl.num_programs(0)
        extra = jnp.dot(scaled, router_ref[...], preferred_element_type=jnp.float32)
        lane = iota((tokens, LANES), 1)
        square = jnp.sum(h * h, axis=1, keepdims=True)
        extra = jnp.where(lane == shift + experts, square, extra)
        high = extra.astype(jnp.bfloat16).astype(jnp.float32)
        low = extra - high
        acc_ref[0, :, last:] += jnp.where(lane >= shift, high, 0.0)
        acc_ref[1, :, last:] += jnp.where(lane >= shift, low, 0.0)
        peers, _, share, _ = out_ref.shape
        me = me_ref[0]
        for o in range(peers):
            begin = pl.multiple_of((me ^ o) * share, share)
            out_ref[o] = acc_ref[:, pl.ds(begin, share), :].astype(jnp.bfloat16)


def activate_kernel(lines, experts, model_width, routes_ref, *refs):
    out_ref = refs[-1]
    summed = refs[0][...].astype(jnp.float32)
    for ref in refs[1:-1]:
        summed = summed + ref[...].astype(jnp.float32)
    _, share, padded = summed.shape
    last = padded - LANES
    shift = lines - last
    extra = summed[0, :, last:] + summed[1, :, last:]
    lane = iota((share, LANES), 1)
    square = jnp.sum(jnp.where(lane == shift + experts, extra, 0.0), axis=1, keepdims=True)
    inverse_rms = lax.rsqrt(square / model_width + norm_eps)
    logits = []
    for k in range(out_ref.shape[0]):
        wanted = lane == routes_ref[:, k : k + 1] + shift
        logits.append(jnp.sum(jnp.where(wanted, extra, 0.0), axis=1, keepdims=True) * inverse_rms)
    peak = functools.reduce(jnp.maximum, logits)
    shares = [jnp.exp(v - peak) for v in logits]
    total = functools.reduce(jnp.add, shares)
    inside = iota((share, padded), 1) < lines
    for k in range(out_ref.shape[0]):
        gate = summed[2 * k] * inverse_rms
        up = summed[2 * k + 1] * inverse_rms
        act = gate / (1.0 + jnp.exp(-gate)) * up
        out_ref[k] = jnp.where(inside, act * (shares[k] / total), 0.0).astype(jnp.bfloat16)


def down_kernel(me_ref, routes_ref, *refs):
    down_ref, out_ref, act_ref = refs[-3:]
    chunks = refs[:-3]
    e = pl.program_id(0)
    topk, share, _ = chunks[0].shape
    lines = down_ref.shape[2]

    @pl.when(e == 0)
    def _():
        me = me_ref[0]
        out_ref[...] = jnp.zeros_like(out_ref)
        for o, chunk in enumerate(chunks):
            begin = pl.multiple_of((me ^ o) * share, share)
            act_ref[:, pl.ds(begin, share), :] = chunk[...]

    mine = jnp.zeros((act_ref.shape[1], lines), jnp.float32)
    for k in range(topk):
        chosen = routes_ref[:, k : k + 1] == e
        mine = mine + jnp.where(chosen, act_ref[k, :, :lines].astype(jnp.float32), 0.0)
    out_ref[...] += jnp.dot(
        mine.astype(jnp.bfloat16), down_ref[0, 0], preferred_element_type=jnp.float32
    )


def experts_part(h_mid, moe_gain, w_router, expert_lines, routes, migration):
    rows = lax.axis_size("row")
    cols = lax.axis_size("col")
    row_index = lax.axis_index("row")
    col_index = lax.axis_index("col")
    experts, _, lines, width = expert_lines.shape
    own, _ = h_mid.shape
    tokens = own * rows
    topk = routes.shape[1]
    share = tokens // cols
    padded = up_to(lines + experts + 1, LANES)
    shift = lines - (padded - LANES)
    me = col_index.astype(jnp.int32).reshape(1)

    order = row_index ^ jnp.arange(rows, dtype=jnp.int32)
    routes = routes.reshape(rows, own, topk)[order].reshape(tokens, topk)
    my_routes = lax.dynamic_slice_in_dim(routes, col_index * share, share, 0)
    router = jnp.pad(w_router, ((0, 0), (shift, LANES - shift - experts)))
    every_h = jnp.concatenate(
        [h_mid] + [from_peer(h_mid, "row", o) for o in range(1, rows)], axis=0
    )
    migration.send([every_h])
    part_spec = lambda part: pl.BlockSpec((1, 1, lines, width), lambda e, me: (e, part, 0, 0))
    whole = lambda a: pl.BlockSpec(a.shape, lambda e, me: (0,) * a.ndim)
    gain = moe_gain.reshape(1, width)
    partial = pl.pallas_call(
        gate_up_kernel,
        grid_spec=pltpu.PrefetchScalarGridSpec(
            num_scalar_prefetch=1,
            grid=(experts,),
            in_specs=[whole(every_h), whole(gain), whole(router), whole(routes)]
            + [part_spec(0), part_spec(1)],
            out_specs=pl.BlockSpec((cols, 2 * topk, share, padded), lambda e, me: (0, 0, 0, 0)),
            scratch_shapes=[pltpu.VMEM((2 * topk, tokens, padded), jnp.float32)],
        ),
        out_shape=jax.ShapeDtypeStruct((cols, 2 * topk, share, padded), jnp.bfloat16),
        compiler_params=params(),
        cost_estimate=pl.CostEstimate(
            flops=4 * experts * tokens * lines * width,
            bytes_accessed=4 * experts * lines * width,
            transcendentals=0,
        ),
        name="gate_up",
    )(me, every_h, gain, router, routes, expert_lines, expert_lines)
    gathered = [partial[0]] + [from_peer(partial[o], "col", o) for o in range(1, cols)]
    activated = pl.pallas_call(
        functools.partial(activate_kernel, lines, experts, width * cols),
        out_shape=jax.ShapeDtypeStruct((topk, share, padded), jnp.bfloat16),
        compiler_params=params(),
        name="activate",
    )(my_routes, *gathered)
    chunks = [activated] + [from_peer(activated, "col", o) for o in range(1, cols)]
    produced = pl.pallas_call(
        down_kernel,
        grid_spec=pltpu.PrefetchScalarGridSpec(
            num_scalar_prefetch=1,
            grid=(experts,),
            in_specs=[whole(routes)] + [whole(c) for c in chunks] + [part_spec(2)],
            out_specs=pl.BlockSpec((tokens, width), lambda e, me: (0, 0)),
            scratch_shapes=[pltpu.VMEM((topk, tokens, padded), jnp.bfloat16)],
        ),
        out_shape=jax.ShapeDtypeStruct((tokens, width), jnp.float32),
        compiler_params=params(),
        cost_estimate=pl.CostEstimate(
            flops=2 * experts * tokens * lines * width,
            bytes_accessed=2 * experts * lines * width,
            transcendentals=0,
        ),
        name="down",
    )(me, routes, *chunks, expert_lines)
    blocks = produced.reshape(rows, own, width)
    mixed = blocks[0]
    for o in range(1, rows):
        mixed = mixed + from_peer(blocks[o], "row", o)
    return mixed


def local(
    hidden,
    queries,
    new_kv,
    prompt_kv,
    suffix_kv,
    lengths,
    w_out,
    moe_gain,
    w_router,
    expert_weights,
    old_lines,
    new_lines,
    routes,
):
    expert_lines = jnp.transpose(expert_weights, (0, 2, 1, 3))
    migration = Migration(expert_lines, old_lines, new_lines)
    for _ in range(len(migration.pieces) - 2):
        migration.send()
    attended = attend(queries, new_kv, prompt_kv, suffix_kv, lengths)
    projected = jnp.dot(attended, w_out, preferred_element_type=jnp.float32)
    h_mid = (hidden.astype(jnp.float32) + projected).astype(jnp.bfloat16)
    (h_mid,) = after([h_mid], migration.packed)
    mixed = experts_part(h_mid, moe_gain, w_router, expert_lines, routes, migration)
    migration.send([mixed])
    moved = migration.finish()
    return (h_mid.astype(jnp.float32) + mixed, jnp.transpose(moved, (0, 2, 1, 3)))


def solution(mesh):
    return jax.shard_map(
        local,
        mesh=mesh,
        in_specs=(
            P("row", "col"),
            P("row", None),
            P("row", None, None),
            P("row", None, "col", None),
            P("row", None, "col", None),
            P("row"),
            P(None, "col"),
            P("col"),
            P("col", None),
            P(None, "row", None, "col"),
            P(),
            P(),
            P(),
        ),
        out_specs=(P("row", "col"), P(None, "row", None, "col")),
        check_vma=False,
    )
```

```python
import functools

import jax
import jax.numpy as jnp
from jax import lax
from jax.experimental import pallas as pl
from jax.experimental.pallas import tpu as pltpu
from jax.sharding import PartitionSpec as P

KVH = 16
HD = 128
REP = 2
TILE = 16
LANES = 128

norm_eps = 1e-06
neg_big = -1e30
VMEM_LIMIT = 48 * 1024 * 1024


def up_to(value, unit):
    return -(-value // unit) * unit


def iota(shape, axis):
    return lax.broadcasted_iota(jnp.int32, shape, axis)


def ones_where(mask):
    return jnp.where(mask, 1.0, 0.0).astype(jnp.bfloat16)


def params():
    return pltpu.CompilerParams(vmem_limit_bytes=VMEM_LIMIT)


def counting(shape, axis):
    return iota(shape, axis).astype(jnp.float32).astype(jnp.bfloat16)


def as_bf16(values):
    return values.astype(jnp.float32).astype(jnp.bfloat16)


def equal_ones(left, right):
    one = jnp.ones((), jnp.bfloat16)
    return jnp.where(left == right, one, jnp.zeros((), jnp.bfloat16))


def within(place, block):
    place = place - 256 * block
    return as_bf16(jnp.where((place >= 0) & (place < 256), place, -1))


def look_up(table_row, id_row, numbers, values):
    full = table_row.shape[1]
    ids = id_row.shape[1]
    high_count = up_to(-(-full // 64), 16)
    table_high = equal_ones(numbers[:high_count], as_bf16(table_row >> 6))
    low = as_bf16(table_row & 63)
    zero = jnp.zeros((), jnp.bfloat16)
    table_low = jnp.concatenate(
        [jnp.where(numbers[:64] == low, part, zero) for part in values], axis=0
    )
    square = lax.dot_general(
        table_low, table_high, (((1,), (1,)), ((), ())), preferred_element_type=jnp.float32
    )
    id_high = equal_ones(numbers[:high_count, :ids], as_bf16(id_row >> 6))
    spread = jnp.dot(square.astype(jnp.bfloat16), id_high, preferred_element_type=jnp.float32)
    wanted = iota((64, ids), 0) == (id_row & 63)
    return [
        jnp.sum(jnp.where(wanted, spread[64 * n : 64 * n + 64], 0.0), axis=0, keepdims=True)
        for n in range(len(values))
    ]


def numbers_for(full):
    return counting((max(up_to(-(-full // 64), 16), 64), full), 0)


def segment_plan(counts, experts, rows):
    starts = []
    running = jnp.zeros((rows, LANES), jnp.float32)
    for e in range(experts):
        starts.append(running)
        running = running + counts[e * rows : (e + 1) * rows]
    start = jnp.concatenate(starts, axis=0)
    lead = jnp.floor(start * (1.0 / TILE))
    tail = jnp.floor((start + counts + (TILE - 1.0)) * (1.0 / TILE))
    tiles = jnp.where(counts > 0.0, tail - lead, 0.0)
    pairs = experts * rows
    line = iota((pairs, pairs), 0)
    column = iota((pairs, pairs), 1)
    earlier = ones_where((line // rows == column // rows) & (column < line))
    base = jnp.dot(earlier, tiles.astype(jnp.bfloat16), preferred_element_type=jnp.float32)
    return start, lead, tiles, base


def write_plan(plan_ref, start, lead, tiles, base):
    shared = start - lead * TILE
    for n, part in enumerate((lead, tiles, base, shared)):
        plan_ref[n] = part.astype(jnp.int32)


def outgoing_kernel(lines, rows, new_ref, held_ref, stack_ref, plan_ref):
    experts = new_ref.shape[0]
    width = held_ref.shape[1]
    real = iota((1, width), 1) < lines
    hits = []
    full = new_ref.shape[1]
    numbers = numbers_for(full)
    slot = iota((64, full), 1).astype(jnp.float32)
    values = (jnp.floor((slot + 0.5) * (1.0 / lines)).astype(jnp.bfloat16),)
    for e in range(experts):
        (peer,) = look_up(new_ref[e : e + 1, :], held_ref[e : e + 1, :], numbers, values)
        peer = peer.astype(jnp.int32)
        hits.append(jnp.where((iota((rows, width), 0) == peer) & real, 1.0, 0.0))
    hits = jnp.concatenate(hits, axis=0)
    until = ones_where(iota((width, width), 0) <= iota((width, width), 1))
    ranks = jnp.dot(hits.astype(jnp.bfloat16), until, preferred_element_type=jnp.float32)
    counts = jnp.broadcast_to(jnp.sum(hits, axis=1, keepdims=True), (experts * rows, LANES))
    start, lead, tiles, base = segment_plan(counts, experts, rows)
    write_plan(plan_ref, start, lead, tiles, base)
    offset = (base * TILE + start - lead * TILE - 1.0)[:, :1]
    placed = hits * (ranks + offset)
    for e in range(experts):
        row = jnp.sum(placed[e * rows : (e + 1) * rows], axis=0, keepdims=True)
        stack_ref[e] = jnp.where(real, row, -1.0).astype(jnp.int32)


def incoming_kernel(lines, rows, old_ref, wanted_ref, stack_ref, plan_ref):
    experts = old_ref.shape[0]
    width = wanted_ref.shape[1]
    real = iota((1, width), 1) < lines
    held_at = []
    hits = []
    full = old_ref.shape[1]
    numbers = numbers_for(full)
    slot = iota((64, full), 1)
    values = (as_bf16(slot >> 7), as_bf16(slot & 127))
    for e in range(experts):
        high, low = look_up(old_ref[e : e + 1, :], wanted_ref[e : e + 1, :], numbers, values)
        slots = high * 128.0 + low
        held_at.append(jnp.where(real, slots, 1e9))
        peer = jnp.floor((slots + 0.5) * (1.0 / lines)).astype(jnp.int32)
        hits.append(jnp.where((iota((rows, width), 0) == peer) & real, 1.0, 0.0))
    hits = jnp.concatenate(hits, axis=0)
    counts = jnp.broadcast_to(jnp.sum(hits, axis=1, keepdims=True), (experts * rows, LANES))
    start, lead, tiles, base = segment_plan(counts, experts, rows)
    write_plan(plan_ref, start, lead, tiles, base)
    blank = jnp.zeros((LANES - experts, width), jnp.float32)
    columns = jnp.transpose(jnp.concatenate(held_at + [blank], axis=0))
    rows_out = []
    for e in range(experts):
        mine = slice(e * rows, (e + 1) * rows)
        before = jnp.where(columns[:, e : e + 1] < held_at[e], 1.0, 0.0)
        rank = jnp.sum(before, axis=0, keepdims=True)
        ahead = jnp.zeros((1, LANES), jnp.float32)
        firsts = []
        for r in range(rows):
            firsts.append(ahead)
            ahead = ahead + counts[e * rows + r : e * rows + r + 1]
        first = jnp.concatenate(firsts, axis=0)
        offset = (base[mine] * TILE + start[mine] - lead[mine] * TILE - first)[:, :1]
        rows_out.append(jnp.sum(hits[mine] * (rank + offset), axis=0, keepdims=True))
    stack_ref[...] = jnp.transpose(jnp.concatenate(rows_out + [blank], axis=0))


STRAIGHT = 8


def tile_at(index):
    return pl.ds(pl.multiple_of(index * TILE, TILE), TILE)


def pack_kernel(rows, plan_ref, place_ref, lines_ref, out_ref, stage_ref, number_ref):
    e = pl.program_id(0)
    pairs = pl.num_programs(0) * rows
    deep, _ = stage_ref.shape
    lines = lines_ref.shape[2]

    @pl.when(e == 0)
    def _():
        number_ref[...] = counting(number_ref.shape, 0)

    place = place_ref[0][:, :lines]
    source_lines = lines_ref[0, 0]
    for first in range(0, deep, 256):
        count = min(256, deep - first)
        onehot = equal_ones(number_ref[:count], within(place, first // 256))
        stage_ref[first : first + count] = jnp.dot(
            onehot, source_lines, preferred_element_type=jnp.float32
        ).astype(jnp.bfloat16)

    def one_peer(d, carry):
        k = e * rows + d
        lead = plan_ref[k]
        tiles = plan_ref[pairs + k]
        base = plan_ref[2 * pairs + k]
        shared = plan_ref[3 * pairs + k] > 0

        @pl.when(tiles > 0)
        def _():
            earlier = out_ref[d, tile_at(lead), :]
            for t in range(1, STRAIGHT):
                n = jnp.minimum(t, tiles - 1)
                out_ref[d, tile_at(lead + n), :] = stage_ref[tile_at(base + n), :]
            earlier = jnp.where(shared, earlier, jnp.zeros_like(earlier))
            out_ref[d, tile_at(lead), :] = earlier + stage_ref[tile_at(base), :]

        def put(t, c):
            out_ref[d, tile_at(lead + t), :] = stage_ref[tile_at(base + t), :]
            return c

        return lax.fori_loop(STRAIGHT, tiles, put, carry)

    lax.fori_loop(0, rows, one_peer, 0, unroll=rows <= 8)


def unpack_kernel(rows, plan_ref, place_ref, block_ref, *rest):
    out_ref, stage_ref, number_ref = rest[-3:]
    e = pl.program_id(0)
    pairs = pl.num_programs(0) * rows
    deep, _ = stage_ref.shape
    lines = out_ref.shape[2]

    @pl.when(e == 0)
    def _():
        stage_ref[...] = jnp.zeros_like(stage_ref)
        number_ref[...] = counting(number_ref.shape, 1)

    def one_peer(s, carry):
        k = e * rows + s
        lead = plan_ref[k]
        tiles = plan_ref[pairs + k]
        base = plan_ref[2 * pairs + k]

        @pl.when(tiles > 0)
        def _():
            for t in range(STRAIGHT):
                n = jnp.minimum(t, tiles - 1)
                stage_ref[tile_at(base + n), :] = block_ref[s, tile_at(lead + n), :]

        def put(t, c):
            stage_ref[tile_at(base + t), :] = block_ref[s, tile_at(lead + t), :]
            return c

        return lax.fori_loop(STRAIGHT, tiles, put, carry)

    lax.fori_loop(0, rows, one_peer, 0, unroll=rows <= 8)
    place = jnp.where(iota((lines, LANES), 1) == e, place_ref[:lines, :], 0.0)
    place = jnp.sum(place, axis=1, keepdims=True).astype(jnp.int32)
    onehot = jnp.concatenate(
        [equal_ones(number_ref[...], within(place, block)) for block in range(deep // 256)], axis=1
    )
    out_ref[0, 0] = jnp.dot(
        onehot, stage_ref[...], preferred_element_type=jnp.float32
    ).astype(jnp.bfloat16)


def call_plan(kernel, name, table, ids, lines, rows, transposed):
    experts, width = ids.shape
    stack = (
        jax.ShapeDtypeStruct((width, LANES), jnp.float32)
        if transposed
        else jax.ShapeDtypeStruct((experts, 1, width), jnp.int32)
    )
    stack, plan = pl.pallas_call(
        functools.partial(kernel, lines, rows),
        out_shape=(stack, jax.ShapeDtypeStruct((4, experts * rows, LANES), jnp.int32)),
        compiler_params=params(),
        cost_estimate=pl.CostEstimate(
            flops=20 * experts * table.shape[1] * 256,
            bytes_accessed=8 * table.size,
            transcendentals=0,
        ),
        name=name,
    )(table, ids)
    return stack, plan[:, :, 0].reshape(-1)


def pack(expert_lines, place, plan, piece, rows, block_rows, deep):
    experts, _, lines, _ = expert_lines.shape
    part, column, width = piece
    return pl.pallas_call(
        functools.partial(pack_kernel, rows),
        grid_spec=pltpu.PrefetchScalarGridSpec(
            num_scalar_prefetch=1,
            grid=(experts,),
            in_specs=[
                pl.BlockSpec((1, 1, place.shape[2]), lambda e, plan: (e, 0, 0)),
                pl.BlockSpec((1, 1, lines, width), lambda e, plan: (e, part, 0, column)),
            ],
            out_specs=pl.BlockSpec((rows, block_rows, width), lambda e, plan: (0, 0, 0)),
            scratch_shapes=[
                pltpu.VMEM((deep, width), jnp.bfloat16),
                pltpu.VMEM((256, lines), jnp.bfloat16),
            ],
        ),
        out_shape=jax.ShapeDtypeStruct((rows, block_rows, width), jnp.bfloat16),
        compiler_params=params(),
        cost_estimate=pl.CostEstimate(
            flops=2 * experts * deep * lines * width,
            bytes_accessed=4 * experts * lines * width,
            transcendentals=0,
        ),
        name="pack_lines",
    )(plan, place, expert_lines)


def unpack(arrived, place, plan, piece, shape, deep, previous):
    experts, _, lines, _ = shape
    part, column, width = piece
    rows, block_rows, _ = arrived.shape
    in_specs = [
        pl.BlockSpec(place.shape, lambda e, plan: (0, 0)),
        pl.BlockSpec((rows, block_rows, width), lambda e, plan: (0, 0, 0)),
    ]
    operands = [plan, place, arrived]
    aliases = {}
    if previous is not None:
        in_specs.append(pl.BlockSpec(memory_space=pl.ANY))
        operands.append(previous)
        aliases = {3: 0}
    return pl.pallas_call(
        functools.partial(unpack_kernel, rows),
        grid_spec=pltpu.PrefetchScalarGridSpec(
            num_scalar_prefetch=1,
            grid=(experts,),
            in_specs=in_specs,
            out_specs=pl.BlockSpec((1, 1, lines, width), lambda e, plan: (e, part, 0, column)),
            scratch_shapes=[
                pltpu.VMEM((deep, width), jnp.bfloat16),
                pltpu.VMEM((lines, 256), jnp.bfloat16),
            ],
        ),
        out_shape=jax.ShapeDtypeStruct(shape, jnp.bfloat16),
        input_output_aliases=aliases,
        compiler_params=params(),
        cost_estimate=pl.CostEstimate(
            flops=2 * experts * deep * lines * width,
            bytes_accessed=4 * experts * lines * width,
            transcendentals=0,
        ),
        name="unpack_lines",
    )(*operands)


def after_kernel(*refs):
    del refs


def after(values, signals):
    anywhere = pl.BlockSpec(memory_space=pl.ANY)
    return pl.pallas_call(
        after_kernel,
        in_specs=[anywhere] * (len(values) + len(signals)),
        out_specs=[anywhere] * len(values),
        out_shape=[jax.ShapeDtypeStruct(v.shape, v.dtype) for v in values],
        input_output_aliases={n: n for n in range(len(values))},
        name="after",
    )(*values, *signals)


def own_ids(table, lines, width):
    mine = lax.dynamic_slice_in_dim(table, lax.axis_index("row") * lines, lines, 1)
    return jnp.pad(mine, ((0, 0), (0, width - lines)), constant_values=-1)


def from_peer(block, axis, offset):
    size = lax.axis_size(axis)
    return lax.ppermute(block, axis, [(i, i ^ offset) for i in range(size)])


def bulk_pieces(parts, width):
    return [(part, 0, width) for part in range(parts)]


class Migration:
    def __init__(self, expert_lines, old_lines, new_lines):
        rows = lax.axis_size("row")
        experts, parts, lines, width = expert_lines.shape
        padded = up_to(lines, LANES)
        block_rows = up_to(experts * lines // rows, TILE)
        self.deep = up_to(lines + 2 * (TILE - 1) * rows, TILE)
        self.shape = expert_lines.shape
        self.pieces = bulk_pieces(parts, width)
        out_place, out_plan = call_plan(
            outgoing_kernel, "outgoing_plan", new_lines, own_ids(old_lines, lines, padded),
            lines, rows, False,
        )
        self.in_place, self.in_plan = call_plan(
            incoming_kernel, "incoming_plan", old_lines, own_ids(new_lines, lines, padded),
            lines, rows, True,
        )
        self.packed = [
            pack(expert_lines, out_place, out_plan, piece, rows, block_rows, self.deep)
            for piece in self.pieces
        ]
        self.arrived = []
        self.moved = None

    def send(self, signals=()):
        block = self.packed[len(self.arrived)]
        if signals:
            (block,) = after([block], signals)
        self.arrived.append(
            lax.all_to_all(block, "row", split_axis=0, concat_axis=0, tiled=True)
        )

    def receive(self, piece):
        self.moved = unpack(
            self.arrived[piece], self.in_place, self.in_plan, self.pieces[piece], self.shape,
            up_to(self.deep, 256), self.moved,
        )


def attend(queries, new_kv, prompt_kv, suffix_kv, lengths):
    seq_count = queries.shape[0]
    prompt_rows = prompt_kv.shape[2]
    suffix_rows = suffix_kv.shape[2]
    col_index = lax.axis_index("col")
    query_heads = queries.reshape(seq_count, KVH, REP, HD)
    prompt_keys = prompt_kv[0, 0].reshape(prompt_rows, KVH, HD)
    prompt_values = prompt_kv[0, 1].reshape(prompt_rows, KVH, HD)
    suffix_keys = suffix_kv[:, 0].reshape(seq_count, suffix_rows, KVH, HD)
    suffix_values = suffix_kv[:, 1].reshape(seq_count, suffix_rows, KVH, HD)
    own_keys = new_kv[:, 0].reshape(seq_count, KVH, HD)
    own_values = new_kv[:, 1].reshape(seq_count, KVH, HD)
    score_scale = HD ** (-0.5)
    prompt_scores = (
        jnp.einsum("skgd,pkd->skgp", query_heads, prompt_keys, preferred_element_type=jnp.float32)
        * score_scale
    )
    suffix_scores = (
        jnp.einsum("skgd,spkd->skgp", query_heads, suffix_keys, preferred_element_type=jnp.float32)
        * score_scale
    )
    own_scores = (
        jnp.einsum("skgd,skd->skg", query_heads, own_keys, preferred_element_type=jnp.float32)
        * score_scale
    )
    positions = col_index * suffix_rows + jnp.arange(suffix_rows, dtype=jnp.int32)
    live_slots = (positions[None, :] < lengths[:, None])[:, None, None, :]
    holder = col_index == 0
    suffix_scores = jnp.where(live_slots, suffix_scores, neg_big)
    own_scores = jnp.where(holder, own_scores, neg_big)
    highest = jnp.maximum(
        jnp.maximum(jnp.max(prompt_scores, axis=-1), jnp.max(suffix_scores, axis=-1)), own_scores
    )
    prompt_weights = jnp.exp(prompt_scores - highest[..., None])
    suffix_weights = jnp.where(live_slots, jnp.exp(suffix_scores - highest[..., None]), 0.0)
    own_weights = jnp.where(holder, jnp.exp(own_scores - highest), 0.0)
    totals = jnp.sum(prompt_weights, axis=-1) + jnp.sum(suffix_weights, axis=-1) + own_weights
    mixture = jnp.einsum(
        "skgp,pkd->skgd",
        prompt_weights.astype(jnp.bfloat16),
        prompt_values,
        preferred_element_type=jnp.float32,
    )
    mixture = mixture + jnp.einsum(
        "skgp,spkd->skgd",
        suffix_weights.astype(jnp.bfloat16),
        suffix_values,
        preferred_element_type=jnp.float32,
    )
    own_rounded = lax.optimization_barrier(own_weights.astype(jnp.bfloat16)).astype(jnp.float32)
    mixture = mixture + own_rounded[..., None] * own_values.astype(jnp.float32)[:, :, None, :]
    heads = KVH * REP
    bundle = jnp.concatenate(
        [
            mixture.reshape(seq_count, heads * HD),
            highest.reshape(seq_count, heads),
            totals.reshape(seq_count, heads),
            jnp.zeros((seq_count, LANES - 2 * heads), jnp.float32),
        ],
        axis=1,
    )
    bundles = [bundle] + [from_peer(bundle, "col", o) for o in range(1, lax.axis_size("col"))]
    every = jnp.stack(bundles)
    mixtures = every[:, :, : heads * HD].reshape(-1, seq_count, heads, HD)
    peaks = every[:, :, heads * HD : heads * HD + heads]
    sums = every[:, :, heads * HD + heads : heads * HD + 2 * heads]
    factors = jnp.exp(peaks - jnp.max(peaks, axis=0))
    total = jnp.sum(sums * factors, axis=0)
    mixed = jnp.sum(mixtures * factors[..., None], axis=0)
    return (mixed / total[..., None]).astype(jnp.bfloat16).reshape(seq_count, heads * HD)


def gate_up_kernel(me_ref, h_ref, gain_ref, router_ref, routes_ref, gate_ref, up_ref, out_ref, acc_ref):
    e = pl.program_id(0)
    tokens = h_ref.shape[0]
    lines = gate_ref.shape[2]
    padded = out_ref.shape[3]
    h = h_ref[...].astype(jnp.float32)
    scaled = (h * gain_ref[...].astype(jnp.float32)).astype(jnp.bfloat16)

    @pl.when(e == 0)
    def _():
        acc_ref[...] = jnp.zeros_like(acc_ref)

    against = (((1,), (1,)), ((), ()))
    gate = lax.dot_general(scaled, gate_ref[0, 0], against, preferred_element_type=jnp.float32)
    up = lax.dot_general(scaled, up_ref[0, 0], against, preferred_element_type=jnp.float32)
    for k in range(routes_ref.shape[1]):
        chosen = routes_ref[:, k : k + 1] == e
        acc_ref[2 * k, :, :lines] += jnp.where(chosen, gate, 0.0)
        acc_ref[2 * k + 1, :, :lines] += jnp.where(chosen, up, 0.0)

    @pl.when(e == pl.num_programs(0) - 1)
    def _():
        last = padded - LANES
        shift = lines - last
        experts = pl.num_programs(0)
        extra = jnp.dot(scaled, router_ref[...], preferred_element_type=jnp.float32)
        lane = iota((tokens, LANES), 1)
        square = jnp.sum(h * h, axis=1, keepdims=True)
        extra = jnp.where(lane == shift + experts, square, extra)
        high = extra.astype(jnp.bfloat16).astype(jnp.float32)
        low = extra - high
        acc_ref[0, :, last:] += jnp.where(lane >= shift, high, 0.0)
        acc_ref[1, :, last:] += jnp.where(lane >= shift, low, 0.0)
        peers, _, share, _ = out_ref.shape
        me = me_ref[0]
        for o in range(peers):
            begin = pl.multiple_of((me ^ o) * share, share)
            out_ref[o] = acc_ref[:, pl.ds(begin, share), :].astype(jnp.bfloat16)


def activate_kernel(lines, experts, model_width, routes_ref, *refs):
    out_ref = refs[-1]
    summed = refs[0][...].astype(jnp.float32)
    for ref in refs[1:-1]:
        summed = summed + ref[...].astype(jnp.float32)
    _, share, padded = summed.shape
    last = padded - LANES
    shift = lines - last
    extra = summed[0, :, last:] + summed[1, :, last:]
    lane = iota((share, LANES), 1)
    square = jnp.sum(jnp.where(lane == shift + experts, extra, 0.0), axis=1, keepdims=True)
    inverse_rms = lax.rsqrt(square / model_width + norm_eps)
    logits = []
    for k in range(out_ref.shape[0]):
        wanted = lane == routes_ref[:, k : k + 1] + shift
        logits.append(jnp.sum(jnp.where(wanted, extra, 0.0), axis=1, keepdims=True) * inverse_rms)
    peak = functools.reduce(jnp.maximum, logits)
    shares = [jnp.exp(v - peak) for v in logits]
    total = functools.reduce(jnp.add, shares)
    inside = iota((share, padded), 1) < lines
    for k in range(out_ref.shape[0]):
        gate = summed[2 * k] * inverse_rms
        up = summed[2 * k + 1] * inverse_rms
        act = gate / (1.0 + jnp.exp(-gate)) * up
        out_ref[k] = jnp.where(inside, act * (shares[k] / total), 0.0).astype(jnp.bfloat16)


def down_kernel(me_ref, routes_ref, *refs):
    down_ref, out_ref, act_ref = refs[-3:]
    chunks = refs[:-3]
    e = pl.program_id(0)
    topk, share, _ = chunks[0].shape
    lines = down_ref.shape[2]

    @pl.when(e == 0)
    def _():
        me = me_ref[0]
        out_ref[...] = jnp.zeros_like(out_ref)
        for o, chunk in enumerate(chunks):
            begin = pl.multiple_of((me ^ o) * share, share)
            act_ref[:, pl.ds(begin, share), :] = chunk[...]

    mine = jnp.zeros((act_ref.shape[1], lines), jnp.float32)
    for k in range(topk):
        chosen = routes_ref[:, k : k + 1] == e
        mine = mine + jnp.where(chosen, act_ref[k, :, :lines].astype(jnp.float32), 0.0)
    out_ref[...] += jnp.dot(
        mine.astype(jnp.bfloat16), down_ref[0, 0], preferred_element_type=jnp.float32
    )


def experts_part(h_mid, moe_gain, w_router, expert_lines, routes, migration):
    rows = lax.axis_size("row")
    cols = lax.axis_size("col")
    row_index = lax.axis_index("row")
    col_index = lax.axis_index("col")
    experts, _, lines, width = expert_lines.shape
    own, _ = h_mid.shape
    tokens = own * rows
    topk = routes.shape[1]
    share = tokens // cols
    padded = up_to(lines + experts + 1, LANES)
    shift = lines - (padded - LANES)
    me = col_index.astype(jnp.int32).reshape(1)

    order = row_index ^ jnp.arange(rows, dtype=jnp.int32)
    routes = routes.reshape(rows, own, topk)[order].reshape(tokens, topk)
    my_routes = lax.dynamic_slice_in_dim(routes, col_index * share, share, 0)
    router = jnp.pad(w_router, ((0, 0), (shift, LANES - shift - experts)))
    every_h = jnp.concatenate(
        [h_mid] + [from_peer(h_mid, "row", o) for o in range(1, rows)], axis=0
    )
    migration.send([every_h])
    part_spec = lambda part: pl.BlockSpec((1, 1, lines, width), lambda e, me: (e, part, 0, 0))
    whole = lambda a: pl.BlockSpec(a.shape, lambda e, me: (0,) * a.ndim)
    gain = moe_gain.reshape(1, width)
    partial = pl.pallas_call(
        gate_up_kernel,
        grid_spec=pltpu.PrefetchScalarGridSpec(
            num_scalar_prefetch=1,
            grid=(experts,),
            in_specs=[whole(every_h), whole(gain), whole(router), whole(routes)]
            + [part_spec(0), part_spec(1)],
            out_specs=pl.BlockSpec((cols, 2 * topk, share, padded), lambda e, me: (0, 0, 0, 0)),
            scratch_shapes=[pltpu.VMEM((2 * topk, tokens, padded), jnp.float32)],
        ),
        out_shape=jax.ShapeDtypeStruct((cols, 2 * topk, share, padded), jnp.bfloat16),
        compiler_params=params(),
        cost_estimate=pl.CostEstimate(
            flops=4 * experts * tokens * lines * width,
            bytes_accessed=4 * experts * lines * width,
            transcendentals=0,
        ),
        name="gate_up",
    )(me, every_h, gain, router, routes, expert_lines, expert_lines)
    gathered = [partial[0]] + [from_peer(partial[o], "col", o) for o in range(1, cols)]
    activated = pl.pallas_call(
        functools.partial(activate_kernel, lines, experts, width * cols),
        out_shape=jax.ShapeDtypeStruct((topk, share, padded), jnp.bfloat16),
        compiler_params=params(),
        name="activate",
    )(my_routes, *gathered)
    chunks = [activated] + [from_peer(activated, "col", o) for o in range(1, cols)]
    produced = pl.pallas_call(
        down_kernel,
        grid_spec=pltpu.PrefetchScalarGridSpec(
            num_scalar_prefetch=1,
            grid=(experts,),
            in_specs=[whole(routes)] + [whole(c) for c in chunks] + [part_spec(2)],
            out_specs=pl.BlockSpec((tokens, width), lambda e, me: (0, 0)),
            scratch_shapes=[pltpu.VMEM((topk, tokens, padded), jnp.bfloat16)],
        ),
        out_shape=jax.ShapeDtypeStruct((tokens, width), jnp.float32),
        compiler_params=params(),
        cost_estimate=pl.CostEstimate(
            flops=2 * experts * tokens * lines * width,
            bytes_accessed=2 * experts * lines * width,
            transcendentals=0,
        ),
        name="down",
    )(me, routes, *chunks, expert_lines)
    migration.receive(0)
    (produced,) = after([produced], [migration.moved])
    blocks = produced.reshape(rows, own, width)
    mixed = blocks[0]
    for o in range(1, rows):
        mixed = mixed + from_peer(blocks[o], "row", o)
    return mixed


def local(
    hidden,
    queries,
    new_kv,
    prompt_kv,
    suffix_kv,
    lengths,
    w_out,
    moe_gain,
    w_router,
    expert_weights,
    old_lines,
    new_lines,
    routes,
):
    expert_lines = jnp.transpose(expert_weights, (0, 2, 1, 3))
    migration = Migration(expert_lines, old_lines, new_lines)
    for _ in range(len(migration.pieces) - 2):
        migration.send()
    attended = attend(queries, new_kv, prompt_kv, suffix_kv, lengths)
    projected = jnp.dot(attended, w_out, preferred_element_type=jnp.float32)
    h_mid = (hidden.astype(jnp.float32) + projected).astype(jnp.bfloat16)
    (h_mid,) = after([h_mid], migration.packed)
    mixed = experts_part(h_mid, moe_gain, w_router, expert_lines, routes, migration)
    migration.send([mixed])
    for piece in range(1, len(migration.pieces)):
        migration.receive(piece)
    return (h_mid.astype(jnp.float32) + mixed, jnp.transpose(migration.moved, (0, 2, 1, 3)))


def solution(mesh):
    return jax.shard_map(
        local,
        mesh=mesh,
        in_specs=(
            P("row", "col"),
            P("row", None),
            P("row", None, None),
            P("row", None, "col", None),
            P("row", None, "col", None),
            P("row"),
            P(None, "col"),
            P("col"),
            P("col", None),
            P(None, "row", None, "col"),
            P(),
            P(),
            P(),
        ),
        out_specs=(P("row", "col"), P(None, "row", None, "col")),
        check_vma=False,
    )
```

```python
import functools

import jax
import jax.numpy as jnp
from jax import lax
from jax.experimental import pallas as pl
from jax.experimental.pallas import tpu as pltpu
from jax.sharding import PartitionSpec as P

KVH = 16
HD = 128
REP = 2
TILE = 16
LANES = 128

norm_eps = 1e-06
neg_big = -1e30
VMEM_LIMIT = 48 * 1024 * 1024


def up_to(value, unit):
    return -(-value // unit) * unit


def iota(shape, axis):
    return lax.broadcasted_iota(jnp.int32, shape, axis)


def ones_where(mask):
    return jnp.where(mask, 1.0, 0.0).astype(jnp.bfloat16)


def params():
    return pltpu.CompilerParams(vmem_limit_bytes=VMEM_LIMIT)


def counting(shape, axis):
    return iota(shape, axis).astype(jnp.float32).astype(jnp.bfloat16)


def as_bf16(values):
    return values.astype(jnp.float32).astype(jnp.bfloat16)


def equal_ones(left, right):
    one = jnp.ones((), jnp.bfloat16)
    return jnp.maximum(one - jnp.abs(left - right), jnp.zeros((), jnp.bfloat16))


def within(place, block):
    place = place - 256 * block
    return as_bf16(jnp.where((place >= 0) & (place < 256), place, -1))


def look_up(table_row, id_row, numbers, values):
    full = table_row.shape[1]
    ids = id_row.shape[1]
    high_count = up_to(-(-full // 64), 16)
    table_high = equal_ones(numbers[:high_count], as_bf16(table_row >> 6))
    low = as_bf16(table_row & 63)
    zero = jnp.zeros((), jnp.bfloat16)
    table_low = jnp.concatenate(
        [jnp.where(numbers[:64] == low, part, zero) for part in values], axis=0
    )
    square = lax.dot_general(
        table_low, table_high, (((1,), (1,)), ((), ())), preferred_element_type=jnp.float32
    )
    id_high = equal_ones(numbers[:high_count, :ids], as_bf16(id_row >> 6))
    spread = jnp.dot(square.astype(jnp.bfloat16), id_high, preferred_element_type=jnp.float32)
    wanted = iota((64, ids), 0) == (id_row & 63)
    return [
        jnp.sum(jnp.where(wanted, spread[64 * n : 64 * n + 64], 0.0), axis=0, keepdims=True)
        for n in range(len(values))
    ]


def numbers_for(full):
    return counting((max(up_to(-(-full // 64), 16), 64), full), 0)


def segment_plan(counts, experts, rows):
    starts = []
    running = jnp.zeros((rows, LANES), jnp.float32)
    for e in range(experts):
        starts.append(running)
        running = running + counts[e * rows : (e + 1) * rows]
    start = jnp.concatenate(starts, axis=0)
    lead = jnp.where(counts > 0.0, jnp.floor(start * (1.0 / TILE)), 0.0)
    tail = jnp.floor((start + counts + (TILE - 1.0)) * (1.0 / TILE))
    tiles = jnp.where(counts > 0.0, tail - lead, 0.0)
    pairs = experts * rows
    line = iota((pairs, pairs), 0)
    column = iota((pairs, pairs), 1)
    earlier = ones_where((line // rows == column // rows) & (column < line))
    base = jnp.dot(earlier, tiles.astype(jnp.bfloat16), preferred_element_type=jnp.float32)
    return start, lead, tiles, base


def write_plan(plan_ref, start, lead, tiles, base):
    shared = start - lead * TILE
    for n, part in enumerate((lead, tiles, base, shared)):
        plan_ref[n] = part.astype(jnp.int32)


def outgoing_kernel(lines, rows, new_ref, held_ref, stack_ref, plan_ref):
    experts = new_ref.shape[0]
    width = held_ref.shape[1]
    real = iota((1, width), 1) < lines
    hits = []
    full = new_ref.shape[1]
    numbers = numbers_for(full)
    slot = iota((64, full), 1).astype(jnp.float32)
    values = (jnp.floor((slot + 0.5) * (1.0 / lines)).astype(jnp.bfloat16),)
    for e in range(experts):
        (peer,) = look_up(new_ref[e : e + 1, :], held_ref[e : e + 1, :], numbers, values)
        peer = peer.astype(jnp.int32)
        hits.append(jnp.where((iota((rows, width), 0) == peer) & real, 1.0, 0.0))
    hits = jnp.concatenate(hits, axis=0)
    until = ones_where(iota((width, width), 0) <= iota((width, width), 1))
    ranks = jnp.dot(hits.astype(jnp.bfloat16), until, preferred_element_type=jnp.float32)
    counts = jnp.broadcast_to(jnp.sum(hits, axis=1, keepdims=True), (experts * rows, LANES))
    start, lead, tiles, base = segment_plan(counts, experts, rows)
    write_plan(plan_ref, start, lead, tiles, base)
    offset = (base * TILE + start - lead * TILE - 1.0)[:, :1]
    placed = hits * (ranks + offset)
    for e in range(experts):
        row = jnp.sum(placed[e * rows : (e + 1) * rows], axis=0, keepdims=True)
        stack_ref[e] = jnp.where(real, row, -1.0).astype(jnp.int32)


def incoming_kernel(lines, rows, old_ref, wanted_ref, stack_ref, plan_ref):
    experts = old_ref.shape[0]
    width = wanted_ref.shape[1]
    real = iota((1, width), 1) < lines
    held_at = []
    hits = []
    full = old_ref.shape[1]
    numbers = numbers_for(full)
    slot = iota((64, full), 1)
    values = (as_bf16(slot >> 7), as_bf16(slot & 127))
    for e in range(experts):
        high, low = look_up(old_ref[e : e + 1, :], wanted_ref[e : e + 1, :], numbers, values)
        slots = high * 128.0 + low
        held_at.append(jnp.where(real, slots, 1e9))
        peer = jnp.floor((slots + 0.5) * (1.0 / lines)).astype(jnp.int32)
        hits.append(jnp.where((iota((rows, width), 0) == peer) & real, 1.0, 0.0))
    hits = jnp.concatenate(hits, axis=0)
    counts = jnp.broadcast_to(jnp.sum(hits, axis=1, keepdims=True), (experts * rows, LANES))
    start, lead, tiles, base = segment_plan(counts, experts, rows)
    write_plan(plan_ref, start, lead, tiles, base)
    blank = jnp.zeros((LANES - experts, width), jnp.float32)
    columns = jnp.transpose(jnp.concatenate(held_at + [blank], axis=0))
    rows_out = []
    for e in range(experts):
        mine = slice(e * rows, (e + 1) * rows)
        before = jnp.where(columns[:, e : e + 1] < held_at[e], 1.0, 0.0)
        rank = jnp.sum(before, axis=0, keepdims=True)
        ahead = jnp.zeros((1, LANES), jnp.float32)
        firsts = []
        for r in range(rows):
            firsts.append(ahead)
            ahead = ahead + counts[e * rows + r : e * rows + r + 1]
        first = jnp.concatenate(firsts, axis=0)
        offset = (base[mine] * TILE + start[mine] - lead[mine] * TILE - first)[:, :1]
        rows_out.append(jnp.sum(hits[mine] * (rank + offset), axis=0, keepdims=True))
    stack_ref[...] = jnp.transpose(jnp.concatenate(rows_out + [blank], axis=0))


STRAIGHT = 8


def tile_at(index):
    return pl.ds(pl.multiple_of(index * TILE, TILE), TILE)


def pack_kernel(rows, span, plan_ref, place_ref, lines_ref, out_ref, packed_ref, number_ref, sem, *stages):
    step = pl.program_id(0)
    pairs = pl.num_programs(0) * span * rows
    deep, _ = stages[0].shape
    lines = lines_ref.shape[2]

    @pl.when(step == 0)
    def _():
        number_ref[...] = counting(number_ref.shape, 0)

    def entry(n, j, d):
        return plan_ref[n * pairs + (step * span + j) * rows + d]

    for j, stage_ref in enumerate(stages):
        place = place_ref[j][:, :lines]
        source_lines = lines_ref[j, 0]
        for first in range(0, deep, 256):
            count = min(256, deep - first)
            onehot = equal_ones(number_ref[:count], within(place, first // 256))
            stage_ref[first : first + count] = jnp.dot(
                onehot, source_lines, preferred_element_type=jnp.float32
            ).astype(jnp.bfloat16)

        def one_peer(d, most, j=j, stage_ref=stage_ref):
            lead, tiles, base = entry(0, j, d), entry(1, j, d), entry(2, j, d)
            shared = entry(3, j, d) > 0
            earlier = packed_ref[d, tile_at(lead), :]
            for t in range(1, STRAIGHT):
                n = jnp.maximum(jnp.minimum(t, tiles - 1), 0)
                packed_ref[d, tile_at(lead + n), :] = stage_ref[tile_at(base + n), :]
            kept = jnp.where(shared | (tiles == 0), earlier, jnp.zeros_like(earlier))
            fresh = stage_ref[tile_at(base), :]
            fresh = jnp.where(tiles == 0, jnp.zeros_like(fresh), fresh)
            packed_ref[d, tile_at(lead), :] = kept + fresh
            return jnp.maximum(most, tiles)

        most = lax.fori_loop(0, rows, one_peer, 0, unroll=rows <= 8)

        @pl.when(most > STRAIGHT)
        def _(j=j, stage_ref=stage_ref):
            def long_peer(d, carry):
                lead, tiles, base = entry(0, j, d), entry(1, j, d), entry(2, j, d)

                def put(t, c):
                    packed_ref[d, tile_at(lead + t), :] = stage_ref[tile_at(base + t), :]
                    return c

                return lax.fori_loop(STRAIGHT, tiles, put, carry)

            lax.fori_loop(0, rows, long_peer, 0)

    @pl.when(step == pl.num_programs(0) - 1)
    def _():
        copy = pltpu.make_async_copy(packed_ref, out_ref, sem)
        copy.start()
        copy.wait()


def unpack_kernel(rows, span, stage_count, plan_ref, place_ref, block_ref, *rest):
    stages = rest[-stage_count:]
    out_ref, number_ref = rest[-stage_count - 2 : -stage_count]
    step = pl.program_id(0)
    pairs = pl.num_programs(0) * span * rows
    deep, _ = stages[0].shape
    lines = out_ref.shape[2]

    @pl.when(step == 0)
    def _():
        for stage_ref in stages:
            stage_ref[...] = jnp.zeros_like(stage_ref)
        number_ref[...] = counting(number_ref.shape, 1)

    def entry(n, j, d):
        return plan_ref[n * pairs + (step * span + j) * rows + d]

    for j, stage_ref in enumerate(stages):

        def one_peer(s, most, j=j, stage_ref=stage_ref):
            lead, tiles, base = entry(0, j, s), entry(1, j, s), entry(2, j, s)
            for t in range(STRAIGHT):
                n = jnp.maximum(jnp.minimum(t, tiles - 1), 0)
                stage_ref[tile_at(base + n), :] = block_ref[s, tile_at(lead + n), :]
            return jnp.maximum(most, tiles)

        most = lax.fori_loop(0, rows, one_peer, 0, unroll=rows <= 8)

        @pl.when(most > STRAIGHT)
        def _(j=j, stage_ref=stage_ref):
            def long_peer(s, carry):
                lead, tiles, base = entry(0, j, s), entry(1, j, s), entry(2, j, s)

                def put(t, c):
                    stage_ref[tile_at(base + t), :] = block_ref[s, tile_at(lead + t), :]
                    return c

                return lax.fori_loop(STRAIGHT, tiles, put, carry)

            lax.fori_loop(0, rows, long_peer, 0)

    for j, stage_ref in enumerate(stages):
        place = jnp.where(iota((lines, LANES), 1) == step * span + j, place_ref[:lines, :], 0.0)
        place = jnp.sum(place, axis=1, keepdims=True).astype(jnp.int32)
        onehot = jnp.concatenate(
            [equal_ones(number_ref[...], within(place, n)) for n in range(deep // 256)], axis=1
        )
        out_ref[j, 0] = jnp.dot(
            onehot, stage_ref[...], preferred_element_type=jnp.float32
        ).astype(jnp.bfloat16)


def call_plan(kernel, name, table, ids, lines, rows, transposed):
    experts, width = ids.shape
    stack = (
        jax.ShapeDtypeStruct((width, LANES), jnp.float32)
        if transposed
        else jax.ShapeDtypeStruct((experts, 1, width), jnp.int32)
    )
    stack, plan = pl.pallas_call(
        functools.partial(kernel, lines, rows),
        out_shape=(stack, jax.ShapeDtypeStruct((4, experts * rows, LANES), jnp.int32)),
        compiler_params=params(),
        cost_estimate=pl.CostEstimate(
            flops=20 * experts * table.shape[1] * 256,
            bytes_accessed=8 * table.size,
            transcendentals=0,
        ),
        name=name,
    )(table, ids)
    return stack, plan[:, :, 0].reshape(-1)


def pack(expert_lines, place, plan, piece, rows, block_rows, deep):
    experts, _, lines, _ = expert_lines.shape
    part, column, width = piece
    span = 2 - experts % 2
    return pl.pallas_call(
        functools.partial(pack_kernel, rows, span),
        grid_spec=pltpu.PrefetchScalarGridSpec(
            num_scalar_prefetch=1,
            grid=(experts // span,),
            in_specs=[
                pl.BlockSpec((span, 1, place.shape[2]), lambda e, plan: (e, 0, 0)),
                pl.BlockSpec((span, 1, lines, width), lambda e, plan: (e, part, 0, column)),
            ],
            out_specs=pl.BlockSpec(memory_space=pltpu.HBM),
            scratch_shapes=[
                pltpu.VMEM((rows, block_rows, width), jnp.bfloat16),
                pltpu.VMEM((256, lines), jnp.bfloat16),
                pltpu.SemaphoreType.DMA(()),
            ]
            + [pltpu.VMEM((deep, width), jnp.bfloat16)] * span,
        ),
        out_shape=jax.ShapeDtypeStruct((rows, block_rows, width), jnp.bfloat16),
        compiler_params=params(),
        cost_estimate=pl.CostEstimate(
            flops=2 * experts * deep * lines * width,
            bytes_accessed=4 * experts * lines * width,
            transcendentals=0,
        ),
        name="pack_lines",
    )(plan, place, expert_lines)


def unpack(arrived, place, plan, piece, shape, deep, previous):
    experts, _, lines, _ = shape
    part, column, width = piece
    rows, block_rows, _ = arrived.shape
    span = 2 - experts % 2
    in_specs = [
        pl.BlockSpec(place.shape, lambda e, plan: (0, 0)),
        pl.BlockSpec((rows, block_rows, width), lambda e, plan: (0, 0, 0)),
    ]
    operands = [plan, place, arrived]
    aliases = {}
    if previous is not None:
        in_specs.append(pl.BlockSpec(memory_space=pl.ANY))
        operands.append(previous)
        aliases = {3: 0}
    return pl.pallas_call(
        functools.partial(unpack_kernel, rows, span, span),
        grid_spec=pltpu.PrefetchScalarGridSpec(
            num_scalar_prefetch=1,
            grid=(experts // span,),
            in_specs=in_specs,
            out_specs=pl.BlockSpec((span, 1, lines, width), lambda e, plan: (e, part, 0, column)),
            scratch_shapes=[pltpu.VMEM((lines, 256), jnp.bfloat16)]
            + [pltpu.VMEM((deep, width), jnp.bfloat16)] * span,
        ),
        out_shape=jax.ShapeDtypeStruct(shape, jnp.bfloat16),
        input_output_aliases=aliases,
        compiler_params=params(),
        cost_estimate=pl.CostEstimate(
            flops=2 * experts * deep * lines * width,
            bytes_accessed=4 * experts * lines * width,
            transcendentals=0,
        ),
        name="unpack_lines",
    )(*operands)


def after_kernel(*refs):
    del refs


def after(values, signals):
    anywhere = pl.BlockSpec(memory_space=pl.ANY)
    return pl.pallas_call(
        after_kernel,
        in_specs=[anywhere] * (len(values) + len(signals)),
        out_specs=[anywhere] * len(values),
        out_shape=[jax.ShapeDtypeStruct(v.shape, v.dtype) for v in values],
        input_output_aliases={n: n for n in range(len(values))},
        name="after",
    )(*values, *signals)


def own_ids(table, lines, width):
    mine = lax.dynamic_slice_in_dim(table, lax.axis_index("row") * lines, lines, 1)
    return jnp.pad(mine, ((0, 0), (0, width - lines)), constant_values=-1)


def from_peer(block, axis, offset):
    size = lax.axis_size(axis)
    return lax.ppermute(block, axis, [(i, i ^ offset) for i in range(size)])


def bulk_pieces(parts, width):
    return [(part, 0, width) for part in range(parts)]


class Migration:
    def __init__(self, expert_lines, old_lines, new_lines):
        rows = lax.axis_size("row")
        experts, parts, lines, width = expert_lines.shape
        padded = up_to(lines, LANES)
        block_rows = up_to(experts * lines // rows, TILE)
        self.deep = up_to(lines + 2 * (TILE - 1) * rows, TILE) + TILE
        self.shape = expert_lines.shape
        self.pieces = bulk_pieces(parts, width)
        out_place, out_plan = call_plan(
            outgoing_kernel, "outgoing_plan", new_lines, own_ids(old_lines, lines, padded),
            lines, rows, False,
        )
        self.in_place, self.in_plan = call_plan(
            incoming_kernel, "incoming_plan", old_lines, own_ids(new_lines, lines, padded),
            lines, rows, True,
        )
        self.packed = [
            pack(expert_lines, out_place, out_plan, piece, rows, block_rows, self.deep)
            for piece in self.pieces
        ]
        self.arrived = []
        self.moved = None

    def send(self, signals=()):
        block = self.packed[len(self.arrived)]
        if signals:
            (block,) = after([block], signals)
        self.arrived.append(
            lax.all_to_all(block, "row", split_axis=0, concat_axis=0, tiled=True)
        )

    def receive(self, piece):
        self.moved = unpack(
            self.arrived[piece], self.in_place, self.in_plan, self.pieces[piece], self.shape,
            up_to(self.deep, 256), self.moved,
        )


def attend(queries, new_kv, prompt_kv, suffix_kv, lengths):
    seq_count = queries.shape[0]
    prompt_rows = prompt_kv.shape[2]
    suffix_rows = suffix_kv.shape[2]
    col_index = lax.axis_index("col")
    query_heads = queries.reshape(seq_count, KVH, REP, HD)
    prompt_keys = prompt_kv[0, 0].reshape(prompt_rows, KVH, HD)
    prompt_values = prompt_kv[0, 1].reshape(prompt_rows, KVH, HD)
    suffix_keys = suffix_kv[:, 0].reshape(seq_count, suffix_rows, KVH, HD)
    suffix_values = suffix_kv[:, 1].reshape(seq_count, suffix_rows, KVH, HD)
    own_keys = new_kv[:, 0].reshape(seq_count, KVH, HD)
    own_values = new_kv[:, 1].reshape(seq_count, KVH, HD)
    score_scale = HD ** (-0.5)
    prompt_scores = (
        jnp.einsum("skgd,pkd->skgp", query_heads, prompt_keys, preferred_element_type=jnp.float32)
        * score_scale
    )
    suffix_scores = (
        jnp.einsum("skgd,spkd->skgp", query_heads, suffix_keys, preferred_element_type=jnp.float32)
        * score_scale
    )
    own_scores = (
        jnp.einsum("skgd,skd->skg", query_heads, own_keys, preferred_element_type=jnp.float32)
        * score_scale
    )
    positions = col_index * suffix_rows + jnp.arange(suffix_rows, dtype=jnp.int32)
    live_slots = (positions[None, :] < lengths[:, None])[:, None, None, :]
    holder = col_index == 0
    suffix_scores = jnp.where(live_slots, suffix_scores, neg_big)
    own_scores = jnp.where(holder, own_scores, neg_big)
    highest = jnp.maximum(
        jnp.maximum(jnp.max(prompt_scores, axis=-1), jnp.max(suffix_scores, axis=-1)), own_scores
    )
    prompt_weights = jnp.exp(prompt_scores - highest[..., None])
    suffix_weights = jnp.where(live_slots, jnp.exp(suffix_scores - highest[..., None]), 0.0)
    own_weights = jnp.where(holder, jnp.exp(own_scores - highest), 0.0)
    totals = jnp.sum(prompt_weights, axis=-1) + jnp.sum(suffix_weights, axis=-1) + own_weights
    mixture = jnp.einsum(
        "skgp,pkd->skgd",
        prompt_weights.astype(jnp.bfloat16),
        prompt_values,
        preferred_element_type=jnp.float32,
    )
    mixture = mixture + jnp.einsum(
        "skgp,spkd->skgd",
        suffix_weights.astype(jnp.bfloat16),
        suffix_values,
        preferred_element_type=jnp.float32,
    )
    own_rounded = lax.optimization_barrier(own_weights.astype(jnp.bfloat16)).astype(jnp.float32)
    mixture = mixture + own_rounded[..., None] * own_values.astype(jnp.float32)[:, :, None, :]
    heads = KVH * REP
    bundle = jnp.concatenate(
        [
            mixture.reshape(seq_count, heads * HD),
            highest.reshape(seq_count, heads),
            totals.reshape(seq_count, heads),
            jnp.zeros((seq_count, LANES - 2 * heads), jnp.float32),
        ],
        axis=1,
    )
    bundles = [bundle] + [from_peer(bundle, "col", o) for o in range(1, lax.axis_size("col"))]
    every = jnp.stack(bundles)
    mixtures = every[:, :, : heads * HD].reshape(-1, seq_count, heads, HD)
    peaks = every[:, :, heads * HD : heads * HD + heads]
    sums = every[:, :, heads * HD + heads : heads * HD + 2 * heads]
    factors = jnp.exp(peaks - jnp.max(peaks, axis=0))
    total = jnp.sum(sums * factors, axis=0)
    mixed = jnp.sum(mixtures * factors[..., None], axis=0)
    return (mixed / total[..., None]).astype(jnp.bfloat16).reshape(seq_count, heads * HD)


def gate_up_kernel(me_ref, h_ref, gain_ref, router_ref, routes_ref, gate_ref, up_ref, out_ref, acc_ref):
    e = pl.program_id(0)
    tokens = h_ref.shape[0]
    lines = gate_ref.shape[2]
    padded = out_ref.shape[3]
    h = h_ref[...].astype(jnp.float32)
    scaled = (h * gain_ref[...].astype(jnp.float32)).astype(jnp.bfloat16)

    @pl.when(e == 0)
    def _():
        acc_ref[...] = jnp.zeros_like(acc_ref)

    against = (((1,), (1,)), ((), ()))
    gate = lax.dot_general(scaled, gate_ref[0, 0], against, preferred_element_type=jnp.float32)
    up = lax.dot_general(scaled, up_ref[0, 0], against, preferred_element_type=jnp.float32)
    for k in range(routes_ref.shape[1]):
        chosen = routes_ref[:, k : k + 1] == e
        acc_ref[2 * k, :, :lines] += jnp.where(chosen, gate, 0.0)
        acc_ref[2 * k + 1, :, :lines] += jnp.where(chosen, up, 0.0)

    @pl.when(e == pl.num_programs(0) - 1)
    def _():
        last = padded - LANES
        shift = lines - last
        experts = pl.num_programs(0)
        extra = jnp.dot(scaled, router_ref[...], preferred_element_type=jnp.float32)
        lane = iota((tokens, LANES), 1)
        square = jnp.sum(h * h, axis=1, keepdims=True)
        extra = jnp.where(lane == shift + experts, square, extra)
        high = extra.astype(jnp.bfloat16).astype(jnp.float32)
        low = extra - high
        acc_ref[0, :, last:] += jnp.where(lane >= shift, high, 0.0)
        acc_ref[1, :, last:] += jnp.where(lane >= shift, low, 0.0)
        peers, _, share, _ = out_ref.shape
        me = me_ref[0]
        for o in range(peers):
            begin = pl.multiple_of((me ^ o) * share, share)
            out_ref[o] = acc_ref[:, pl.ds(begin, share), :].astype(jnp.bfloat16)


def activate_kernel(lines, experts, model_width, routes_ref, *refs):
    out_ref = refs[-1]
    summed = refs[0][...].astype(jnp.float32)
    for ref in refs[1:-1]:
        summed = summed + ref[...].astype(jnp.float32)
    _, share, padded = summed.shape
    last = padded - LANES
    shift = lines - last
    extra = summed[0, :, last:] + summed[1, :, last:]
    lane = iota((share, LANES), 1)
    square = jnp.sum(jnp.where(lane == shift + experts, extra, 0.0), axis=1, keepdims=True)
    inverse_rms = lax.rsqrt(square / model_width + norm_eps)
    logits = []
    for k in range(out_ref.shape[0]):
        wanted = lane == routes_ref[:, k : k + 1] + shift
        logits.append(jnp.sum(jnp.where(wanted, extra, 0.0), axis=1, keepdims=True) * inverse_rms)
    peak = functools.reduce(jnp.maximum, logits)
    shares = [jnp.exp(v - peak) for v in logits]
    total = functools.reduce(jnp.add, shares)
    inside = iota((share, padded), 1) < lines
    for k in range(out_ref.shape[0]):
        gate = summed[2 * k] * inverse_rms
        up = summed[2 * k + 1] * inverse_rms
        act = gate / (1.0 + jnp.exp(-gate)) * up
        out_ref[k] = jnp.where(inside, act * (shares[k] / total), 0.0).astype(jnp.bfloat16)


def down_kernel(me_ref, routes_ref, *refs):
    down_ref, out_ref, act_ref = refs[-3:]
    chunks = refs[:-3]
    e = pl.program_id(0)
    topk, share, _ = chunks[0].shape
    lines = down_ref.shape[2]

    @pl.when(e == 0)
    def _():
        me = me_ref[0]
        out_ref[...] = jnp.zeros_like(out_ref)
        for o, chunk in enumerate(chunks):
            begin = pl.multiple_of((me ^ o) * share, share)
            act_ref[:, pl.ds(begin, share), :] = chunk[...]

    mine = jnp.zeros((act_ref.shape[1], lines), jnp.float32)
    for k in range(topk):
        chosen = routes_ref[:, k : k + 1] == e
        mine = mine + jnp.where(chosen, act_ref[k, :, :lines].astype(jnp.float32), 0.0)
    out_ref[...] += jnp.dot(
        mine.astype(jnp.bfloat16), down_ref[0, 0], preferred_element_type=jnp.float32
    )


def experts_part(h_mid, moe_gain, w_router, expert_lines, routes, migration):
    rows = lax.axis_size("row")
    cols = lax.axis_size("col")
    row_index = lax.axis_index("row")
    col_index = lax.axis_index("col")
    experts, _, lines, width = expert_lines.shape
    own, _ = h_mid.shape
    tokens = own * rows
    topk = routes.shape[1]
    share = tokens // cols
    padded = up_to(lines + experts + 1, LANES)
    shift = lines - (padded - LANES)
    me = col_index.astype(jnp.int32).reshape(1)

    order = row_index ^ jnp.array(sorted(range(rows), key=lambda o: (o % 2, o)), jnp.int32)
    routes = routes.reshape(rows, own, topk)[order].reshape(tokens, topk)
    my_routes = lax.dynamic_slice_in_dim(routes, col_index * share, share, 0)
    router = jnp.pad(w_router, ((0, 0), (shift, LANES - shift - experts)))
    same_core = jnp.concatenate(
        [h_mid] + [from_peer(h_mid, "row", o) for o in range(2, rows, 2)], axis=0
    )
    every_h = jnp.concatenate([same_core, from_peer(same_core, "row", 1)], axis=0)
    migration.send([every_h])
    part_spec = lambda part: pl.BlockSpec((1, 1, lines, width), lambda e, me: (e, part, 0, 0))
    whole = lambda a: pl.BlockSpec(a.shape, lambda e, me: (0,) * a.ndim)
    gain = moe_gain.reshape(1, width)
    partial = pl.pallas_call(
        gate_up_kernel,
        grid_spec=pltpu.PrefetchScalarGridSpec(
            num_scalar_prefetch=1,
            grid=(experts,),
            in_specs=[whole(every_h), whole(gain), whole(router), whole(routes)]
            + [part_spec(0), part_spec(1)],
            out_specs=pl.BlockSpec((cols, 2 * topk, share, padded), lambda e, me: (0, 0, 0, 0)),
            scratch_shapes=[pltpu.VMEM((2 * topk, tokens, padded), jnp.float32)],
        ),
        out_shape=jax.ShapeDtypeStruct((cols, 2 * topk, share, padded), jnp.bfloat16),
        compiler_params=params(),
        cost_estimate=pl.CostEstimate(
            flops=4 * experts * tokens * lines * width,
            bytes_accessed=4 * experts * lines * width,
            transcendentals=0,
        ),
        name="gate_up",
    )(me, every_h, gain, router, routes, expert_lines, expert_lines)
    gathered = [partial[0]] + [from_peer(partial[o], "col", o) for o in range(1, cols)]
    activated = pl.pallas_call(
        functools.partial(activate_kernel, lines, experts, width * cols),
        out_shape=jax.ShapeDtypeStruct((topk, share, padded), jnp.bfloat16),
        compiler_params=params(),
        name="activate",
    )(my_routes, *gathered)
    chunks = [activated] + [from_peer(activated, "col", o) for o in range(1, cols)]
    produced = pl.pallas_call(
        down_kernel,
        grid_spec=pltpu.PrefetchScalarGridSpec(
            num_scalar_prefetch=1,
            grid=(experts,),
            in_specs=[whole(routes)] + [whole(c) for c in chunks] + [part_spec(2)],
            out_specs=pl.BlockSpec((tokens, width), lambda e, me: (0, 0)),
            scratch_shapes=[pltpu.VMEM((topk, tokens, padded), jnp.bfloat16)],
        ),
        out_shape=jax.ShapeDtypeStruct((tokens, width), jnp.float32),
        compiler_params=params(),
        cost_estimate=pl.CostEstimate(
            flops=2 * experts * tokens * lines * width,
            bytes_accessed=2 * experts * lines * width,
            transcendentals=0,
        ),
        name="down",
    )(me, routes, *chunks, expert_lines)
    half = tokens // 2
    both_cores = produced[:half] + from_peer(produced[half:], "row", 1)
    blocks = both_cores.reshape(rows // 2, own, width)
    mixed = blocks[0]
    for n in range(1, rows // 2):
        mixed = mixed + from_peer(blocks[n], "row", 2 * n)
    return mixed


def local(
    hidden,
    queries,
    new_kv,
    prompt_kv,
    suffix_kv,
    lengths,
    w_out,
    moe_gain,
    w_router,
    expert_weights,
    old_lines,
    new_lines,
    routes,
):
    expert_lines = jnp.transpose(expert_weights, (0, 2, 1, 3))
    migration = Migration(expert_lines, old_lines, new_lines)
    for _ in range(len(migration.pieces) - 2):
        migration.send()
    attended = attend(queries, new_kv, prompt_kv, suffix_kv, lengths)
    projected = jnp.dot(attended, w_out, preferred_element_type=jnp.float32)
    h_mid = (hidden.astype(jnp.float32) + projected).astype(jnp.bfloat16)
    (h_mid,) = after([h_mid], migration.packed)
    mixed = experts_part(h_mid, moe_gain, w_router, expert_lines, routes, migration)
    migration.send([mixed])
    for piece in range(len(migration.pieces)):
        migration.receive(piece)
    return (h_mid.astype(jnp.float32) + mixed, jnp.transpose(migration.moved, (0, 2, 1, 3)))


def solution(mesh):
    return jax.shard_map(
        local,
        mesh=mesh,
        in_specs=(
            P("row", "col"),
            P("row", None),
            P("row", None, None),
            P("row", None, "col", None),
            P("row", None, "col", None),
            P("row"),
            P(None, "col"),
            P("col"),
            P("col", None),
            P(None, "row", None, "col"),
            P(),
            P(),
            P(),
        ),
        out_specs=(P("row", "col"), P(None, "row", None, "col")),
        check_vma=False,
    )
```

```python
import functools

import jax
import jax.numpy as jnp
from jax import lax
from jax.experimental import pallas as pl
from jax.experimental.pallas import tpu as pltpu
from jax.sharding import PartitionSpec as P

KVH = 16
HD = 128
REP = 2
TILE = 16
LANES = 128

norm_eps = 1e-06
neg_big = -1e30
VMEM_LIMIT = 48 * 1024 * 1024
PACK_LIMIT = 61 * 1024 * 1024


def up_to(value, unit):
    return -(-value // unit) * unit


def iota(shape, axis):
    return lax.broadcasted_iota(jnp.int32, shape, axis)


def ones_where(mask):
    return jnp.where(mask, 1.0, 0.0).astype(jnp.bfloat16)


def params():
    return pltpu.CompilerParams(vmem_limit_bytes=VMEM_LIMIT)


def counting(shape, axis):
    return iota(shape, axis).astype(jnp.float32).astype(jnp.bfloat16)


def as_bf16(values):
    return values.astype(jnp.float32).astype(jnp.bfloat16)


def equal_ones(left, right):
    one = jnp.ones((), jnp.bfloat16)
    return jnp.maximum(one - jnp.abs(left - right), jnp.zeros((), jnp.bfloat16))


def within(place, block):
    place = place - 256 * block
    return as_bf16(jnp.where((place >= 0) & (place < 256), place, -1))


def look_up(table_row, id_row, numbers, values):
    full = table_row.shape[1]
    ids = id_row.shape[1]
    high_count = up_to(-(-full // 64), 16)
    table_high = equal_ones(numbers[:high_count], as_bf16(table_row >> 6))
    low = as_bf16(table_row & 63)
    zero = jnp.zeros((), jnp.bfloat16)
    table_low = jnp.concatenate(
        [jnp.where(numbers[:64] == low, part, zero) for part in values], axis=0
    )
    square = lax.dot_general(
        table_low, table_high, (((1,), (1,)), ((), ())), preferred_element_type=jnp.float32
    )
    id_high = equal_ones(numbers[:high_count, :ids], as_bf16(id_row >> 6))
    spread = jnp.dot(square.astype(jnp.bfloat16), id_high, preferred_element_type=jnp.float32)
    wanted = iota((64, ids), 0) == (id_row & 63)
    return [
        jnp.sum(jnp.where(wanted, spread[64 * n : 64 * n + 64], 0.0), axis=0, keepdims=True)
        for n in range(len(values))
    ]


def numbers_for(full):
    return counting((max(up_to(-(-full // 64), 16), 64), full), 0)


def segment_plan(counts, experts, rows):
    starts = []
    running = jnp.zeros((rows, LANES), jnp.float32)
    for e in range(experts):
        starts.append(running)
        running = running + counts[e * rows : (e + 1) * rows]
    start = jnp.concatenate(starts, axis=0)
    lead = jnp.where(counts > 0.0, jnp.floor(start * (1.0 / TILE)), 0.0)
    tail = jnp.floor((start + counts + (TILE - 1.0)) * (1.0 / TILE))
    tiles = jnp.where(counts > 0.0, tail - lead, 0.0)
    pairs = experts * rows
    line = iota((pairs, pairs), 0)
    column = iota((pairs, pairs), 1)
    earlier = ones_where((line // rows == column // rows) & (column < line))
    base = jnp.dot(earlier, tiles.astype(jnp.bfloat16), preferred_element_type=jnp.float32)
    return start, lead, tiles, base


def outgoing_kernel(lines, rows, new_ref, held_ref, stack_ref, plan_ref):
    experts = new_ref.shape[0]
    width = held_ref.shape[1]
    real = iota((1, width), 1) < lines
    hits = []
    full = new_ref.shape[1]
    numbers = numbers_for(full)
    slot = iota((64, full), 1).astype(jnp.float32)
    values = (jnp.floor((slot + 0.5) * (1.0 / lines)).astype(jnp.bfloat16),)
    for e in range(experts):
        (peer,) = look_up(new_ref[e : e + 1, :], held_ref[e : e + 1, :], numbers, values)
        peer = peer.astype(jnp.int32)
        hits.append(jnp.where((iota((rows, width), 0) == peer) & real, 1.0, 0.0))
    hits = jnp.concatenate(hits, axis=0)
    until = ones_where(iota((width, width), 0) <= iota((width, width), 1))
    ranks = jnp.dot(hits.astype(jnp.bfloat16), until, preferred_element_type=jnp.float32)
    counts = jnp.broadcast_to(jnp.sum(hits, axis=1, keepdims=True), (experts * rows, LANES))
    start, lead, tiles, base = segment_plan(counts, experts, rows)
    for n, part in enumerate((lead, tiles, base, start - lead * TILE)):
        plan_ref[n] = part.astype(jnp.int32)
    offset = (base * TILE + start - lead * TILE - 1.0)[:, :1]
    placed = hits * (ranks + offset)
    for e in range(experts):
        row = jnp.sum(placed[e * rows : (e + 1) * rows], axis=0, keepdims=True)
        stack_ref[e] = jnp.where(real, row, -1.0).astype(jnp.int32)


def incoming_kernel(lines, rows, block_tiles, slot, old_ref, wanted_ref, stack_ref, plan_ref):
    experts = old_ref.shape[0]
    width = wanted_ref.shape[1]
    real = iota((1, width), 1) < lines
    held_at = []
    hits = []
    full = old_ref.shape[1]
    numbers = numbers_for(full)
    at = iota((64, full), 1)
    values = (as_bf16(at >> 7), as_bf16(at & 127))
    for e in range(experts):
        high, low = look_up(old_ref[e : e + 1, :], wanted_ref[e : e + 1, :], numbers, values)
        slots = high * 128.0 + low
        held_at.append(jnp.where(real, slots, 1e9))
        peer = jnp.floor((slots + 0.5) * (1.0 / lines)).astype(jnp.int32)
        hits.append(jnp.where((iota((rows, width), 0) == peer) & real, 1.0, 0.0))
    hits = jnp.concatenate(hits, axis=0)
    counts = jnp.broadcast_to(jnp.sum(hits, axis=1, keepdims=True), (experts * rows, LANES))
    start, lead, tiles, base = segment_plan(counts, experts, rows)
    line = iota((experts * rows, LANES), 0)
    peer = (line % rows).astype(jnp.float32)
    longest = [
        jnp.max(tiles[e * rows : (e + 1) * rows], axis=0, keepdims=True) for e in range(experts)
    ]
    longest = jnp.concatenate(
        [jnp.broadcast_to(most, (rows, LANES)) for most in longest], axis=0
    )
    slotted = longest <= slot
    lead = jnp.where(slotted, jnp.minimum(lead, float(block_tiles - slot)), lead)
    base = jnp.where(slotted, peer * slot, base)
    for n, part in enumerate((lead, tiles, base, jnp.where(slotted, 1.0, 0.0))):
        plan_ref[n] = part.astype(jnp.int32)
    blank = jnp.zeros((LANES - experts, width), jnp.float32)
    columns = jnp.transpose(jnp.concatenate(held_at + [blank], axis=0))
    rows_out = []
    for e in range(experts):
        mine = slice(e * rows, (e + 1) * rows)
        before = jnp.where(columns[:, e : e + 1] < held_at[e], 1.0, 0.0)
        rank = jnp.sum(before, axis=0, keepdims=True)
        ahead = jnp.zeros((1, LANES), jnp.float32)
        firsts = []
        for r in range(rows):
            firsts.append(ahead)
            ahead = ahead + counts[e * rows + r : e * rows + r + 1]
        first = jnp.concatenate(firsts, axis=0)
        offset = (base[mine] * TILE + start[mine] - lead[mine] * TILE - first)[:, :1]
        rows_out.append(jnp.sum(hits[mine] * (rank + offset), axis=0, keepdims=True))
    places = jnp.transpose(jnp.concatenate(rows_out + [blank], axis=0))
    for e in range(experts):
        place = jnp.broadcast_to(places[:lines, e : e + 1], (lines, LANES))
        block = jnp.floor(place * (1.0 / 256.0))
        stack_ref[e, 0] = (place - 256.0 * block).astype(jnp.bfloat16)
        stack_ref[e, 1] = block.astype(jnp.bfloat16)


STRAIGHT = 8


def tile_at(index):
    return pl.ds(pl.multiple_of(index * TILE, TILE), TILE)


def pack_kernel(rows, span, plan_ref, place_ref, lines_ref, out_ref, packed_ref, number_ref, sem, *stages):
    part = pl.program_id(0)
    step = pl.program_id(1)
    pairs = pl.num_programs(1) * span * rows
    deep, _ = stages[0].shape
    lines = lines_ref.shape[2]

    @pl.when((part == 0) & (step == 0))
    def _():
        number_ref[...] = counting(number_ref.shape, 0)

    def entry(n, j, d):
        return plan_ref[n * pairs + (step * span + j) * rows + d]

    for j, stage_ref in enumerate(stages):
        place = place_ref[j][:, :lines]
        source_lines = lines_ref[j, 0]
        for first in range(0, deep, 256):
            count = min(256, deep - first)
            onehot = equal_ones(number_ref[:count], within(place, first // 256))
            stage_ref[first : first + count] = jnp.dot(
                onehot, source_lines, preferred_element_type=jnp.float32
            ).astype(jnp.bfloat16)

        def one_peer(d, most, j=j, stage_ref=stage_ref):
            lead, tiles, base = entry(0, j, d), entry(1, j, d), entry(2, j, d)
            shared = entry(3, j, d) > 0
            earlier = packed_ref[d, tile_at(lead), :]
            for t in range(1, STRAIGHT):
                n = jnp.maximum(jnp.minimum(t, tiles - 1), 0)
                packed_ref[d, tile_at(lead + n), :] = stage_ref[tile_at(base + n), :]
            kept = jnp.where(shared | (tiles == 0), earlier, jnp.zeros_like(earlier))
            fresh = stage_ref[tile_at(base), :]
            fresh = jnp.where(tiles == 0, jnp.zeros_like(fresh), fresh)
            packed_ref[d, tile_at(lead), :] = kept + fresh
            return jnp.maximum(most, tiles)

        most = lax.fori_loop(0, rows, one_peer, 0, unroll=rows <= 8)

        @pl.when(most > STRAIGHT)
        def _(j=j, stage_ref=stage_ref):
            def long_peer(d, carry):
                lead, tiles, base = entry(0, j, d), entry(1, j, d), entry(2, j, d)

                def put(t, c):
                    packed_ref[d, tile_at(lead + t), :] = stage_ref[tile_at(base + t), :]
                    return c

                return lax.fori_loop(STRAIGHT, tiles, put, carry)

            lax.fori_loop(0, rows, long_peer, 0)

    @pl.when(step == pl.num_programs(1) - 1)
    def _():
        copy = pltpu.make_async_copy(packed_ref, out_ref.at[:, part], sem)
        copy.start()
        copy.wait()


def unpack_kernel(slot, plan_ref, place_ref, block_ref, *rest):
    out_ref, stage_ref, sems = rest[-3:]
    experts = pl.num_programs(1)
    rows = block_ref.shape[0]
    pairs = experts * rows
    _, deep, _ = stage_ref.shape
    lines = out_ref.shape[2]
    step = pl.program_id(0) * experts + pl.program_id(1)
    steps = pl.num_programs(0) * experts

    def entry(n, e, s):
        return plan_ref[n * pairs + e * rows + s]

    def slotted(e):
        return entry(3, e, 0) > 0

    def slot_copy(at, s):
        part, e, buffer = at // experts, at % experts, at % 2
        there = pl.ds(pl.multiple_of(entry(0, e, s) * TILE, TILE), slot * TILE)
        return pltpu.make_async_copy(
            block_ref.at[s, part, there],
            stage_ref.at[buffer, pl.ds(s * slot * TILE, slot * TILE)],
            sems.at[buffer, s],
        )

    def begin(at):
        @pl.when(slotted(at % experts))
        def _():
            for s in range(rows):
                slot_copy(at, s).start()

    @pl.when(step == 0)
    def _():
        stage_ref[...] = jnp.zeros_like(stage_ref)
        begin(step)

    @pl.when(step + 1 < steps)
    def _():
        begin(step + 1)

    part, e, buffer = pl.program_id(0), pl.program_id(1), step % 2

    @pl.when(slotted(e))
    def _():
        for s in range(rows):
            slot_copy(step, s).wait()

    @pl.when(jnp.logical_not(slotted(e)))
    def _():
        def one_peer(s, carry):
            def put(t, c):
                copy = pltpu.make_async_copy(
                    block_ref.at[s, part, tile_at(entry(0, e, s) + t)],
                    stage_ref.at[buffer, tile_at(entry(2, e, s) + t)],
                    sems.at[buffer, 0],
                )
                copy.start()
                copy.wait()
                return c

            return lax.fori_loop(0, entry(1, e, s), put, carry)

        lax.fori_loop(0, rows, one_peer, 0)

    within_block, block = place_ref[0, 0], place_ref[0, 1]
    lane = counting((lines, LANES), 1)
    pieces = []
    for first in range(0, deep, LANES):
        away = jnp.abs(block - jnp.asarray(first // 256, jnp.bfloat16))
        place = within_block + away * jnp.asarray(512, jnp.bfloat16)
        pieces.append(equal_ones(lane + jnp.asarray(first % 256, jnp.bfloat16), place))
    onehot = jnp.concatenate(pieces, axis=1)
    out_ref[0, 0] = jnp.dot(
        onehot, stage_ref[buffer], preferred_element_type=jnp.float32
    ).astype(jnp.bfloat16)


def call_plan(kernel, name, table, ids, pairs, place):
    return pl.pallas_call(
        kernel,
        out_shape=(place, jax.ShapeDtypeStruct((4, pairs, LANES), jnp.int32)),
        compiler_params=params(),
        cost_estimate=pl.CostEstimate(
            flops=20 * table.size * 256, bytes_accessed=8 * table.size, transcendentals=0
        ),
        name=name,
    )(table, ids)


def pack(expert_lines, place, plan, piece, rows, block_rows, deep):
    experts, _, lines, width = expert_lines.shape
    first, count = piece
    span = 2 - experts % 2
    return pl.pallas_call(
        functools.partial(pack_kernel, rows, span),
        grid_spec=pltpu.PrefetchScalarGridSpec(
            num_scalar_prefetch=1,
            grid=(count, experts // span),
            in_specs=[
                pl.BlockSpec((span, 1, place.shape[2]), lambda p, e, plan: (e, 0, 0)),
                pl.BlockSpec((span, 1, lines, width), lambda p, e, plan: (e, first + p, 0, 0)),
            ],
            out_specs=pl.BlockSpec(memory_space=pltpu.HBM),
            scratch_shapes=[
                pltpu.VMEM((rows, block_rows, width), jnp.bfloat16),
                pltpu.VMEM((256, lines), jnp.bfloat16),
                pltpu.SemaphoreType.DMA(()),
            ]
            + [pltpu.VMEM((deep, width), jnp.bfloat16)] * span,
        ),
        out_shape=jax.ShapeDtypeStruct((rows, count, block_rows, width), jnp.bfloat16),
        compiler_params=pltpu.CompilerParams(vmem_limit_bytes=PACK_LIMIT),
        cost_estimate=pl.CostEstimate(
            flops=2 * count * experts * deep * lines * width,
            bytes_accessed=4 * count * experts * lines * width,
            transcendentals=0,
        ),
        name="pack_lines",
    )(plan, place, expert_lines)


def unpack(arrived, place, plan, piece, shape, deep, slot, previous):
    experts, _, lines, width = shape
    first, count = piece
    rows = arrived.shape[0]
    in_specs = [
        pl.BlockSpec((1, 2, lines, LANES), lambda p, e, plan: (e, 0, 0, 0)),
        pl.BlockSpec(memory_space=pl.ANY),
    ]
    operands = [plan, place, arrived]
    aliases = {}
    if previous is not None:
        in_specs.append(pl.BlockSpec(memory_space=pl.ANY))
        operands.append(previous)
        aliases = {3: 0}
    return pl.pallas_call(
        functools.partial(unpack_kernel, slot),
        grid_spec=pltpu.PrefetchScalarGridSpec(
            num_scalar_prefetch=1,
            grid=(count, experts),
            in_specs=in_specs,
            out_specs=pl.BlockSpec((1, 1, lines, width), lambda p, e, plan: (e, first + p, 0, 0)),
            scratch_shapes=[
                pltpu.VMEM((2, deep, width), jnp.bfloat16),
                pltpu.SemaphoreType.DMA((2, rows)),
            ],
        ),
        out_shape=jax.ShapeDtypeStruct(shape, jnp.bfloat16),
        input_output_aliases=aliases,
        compiler_params=params(),
        cost_estimate=pl.CostEstimate(
            flops=2 * count * experts * deep * lines * width,
            bytes_accessed=4 * count * experts * lines * width,
            transcendentals=0,
        ),
        name="unpack_lines",
    )(*operands)


def after_kernel(*refs):
    del refs


def after(values, signals):
    anywhere = pl.BlockSpec(memory_space=pl.ANY)
    return pl.pallas_call(
        after_kernel,
        in_specs=[anywhere] * (len(values) + len(signals)),
        out_specs=[anywhere] * len(values),
        out_shape=[jax.ShapeDtypeStruct(v.shape, v.dtype) for v in values],
        input_output_aliases={n: n for n in range(len(values))},
        compiler_params=pltpu.CompilerParams(vmem_limit_bytes=PACK_LIMIT),
        name="after",
    )(*values, *signals)


def own_ids(table, lines, width):
    mine = lax.dynamic_slice_in_dim(table, lax.axis_index("row") * lines, lines, 1)
    return jnp.pad(mine, ((0, 0), (0, width - lines)), constant_values=-1)


def from_peer(block, axis, offset):
    size = lax.axis_size(axis)
    return lax.ppermute(block, axis, [(i, i ^ offset) for i in range(size)])


class Migration:
    def __init__(self, expert_lines, old_lines, new_lines):
        rows = lax.axis_size("row")
        experts, parts, lines, width = expert_lines.shape
        padded = up_to(lines, LANES)
        block_rows = up_to(experts * lines // rows, TILE)
        pairs = experts * rows
        compact = up_to(lines + 2 * (TILE - 1) * rows, TILE) + TILE
        self.slot = min(STRAIGHT, block_rows // TILE)
        self.deep = up_to(max(compact, rows * self.slot * TILE), 256)
        self.shape = expert_lines.shape
        self.pieces = [(0, 1), (1, parts - 1)]
        out_place, out_plan = call_plan(
            functools.partial(outgoing_kernel, lines, rows), "outgoing_plan",
            new_lines, own_ids(old_lines, lines, padded), pairs,
            jax.ShapeDtypeStruct((experts, 1, padded), jnp.int32),
        )
        self.in_place, in_plan = call_plan(
            functools.partial(incoming_kernel, lines, rows, block_rows // TILE, self.slot),
            "incoming_plan",
            old_lines, own_ids(new_lines, lines, padded), pairs,
            jax.ShapeDtypeStruct((experts, 2, lines, LANES), jnp.bfloat16),
        )
        out_plan = out_plan[:, :, 0].reshape(-1)
        self.in_plan = in_plan[:, :, 0].reshape(-1)
        self.packed = [
            pack(expert_lines, out_place, out_plan, piece, rows, block_rows, compact)
            for piece in self.pieces
        ]
        self.arrived = []
        self.moved = None

    def send(self, signals=()):
        block = self.packed[len(self.arrived)]
        if signals:
            (block,) = after([block], signals)
        self.arrived.append(
            lax.all_to_all(block, "row", split_axis=0, concat_axis=0, tiled=True)
        )

    def receive(self, piece):
        self.moved = unpack(
            self.arrived[piece], self.in_place, self.in_plan, self.pieces[piece], self.shape,
            self.deep, self.slot, self.moved,
        )


def attend(queries, new_kv, prompt_kv, suffix_kv, lengths):
    seq_count = queries.shape[0]
    prompt_rows = prompt_kv.shape[2]
    suffix_rows = suffix_kv.shape[2]
    col_index = lax.axis_index("col")
    query_heads = queries.reshape(seq_count, KVH, REP, HD)
    prompt_keys = prompt_kv[0, 0].reshape(prompt_rows, KVH, HD)
    prompt_values = prompt_kv[0, 1].reshape(prompt_rows, KVH, HD)
    suffix_keys = suffix_kv[:, 0].reshape(seq_count, suffix_rows, KVH, HD)
    suffix_values = suffix_kv[:, 1].reshape(seq_count, suffix_rows, KVH, HD)
    own_keys = new_kv[:, 0].reshape(seq_count, KVH, HD)
    own_values = new_kv[:, 1].reshape(seq_count, KVH, HD)
    score_scale = HD ** (-0.5)
    prompt_scores = (
        jnp.einsum("skgd,pkd->skgp", query_heads, prompt_keys, preferred_element_type=jnp.float32)
        * score_scale
    )
    suffix_scores = (
        jnp.einsum("skgd,spkd->skgp", query_heads, suffix_keys, preferred_element_type=jnp.float32)
        * score_scale
    )
    own_scores = (
        jnp.einsum("skgd,skd->skg", query_heads, own_keys, preferred_element_type=jnp.float32)
        * score_scale
    )
    positions = col_index * suffix_rows + jnp.arange(suffix_rows, dtype=jnp.int32)
    live_slots = (positions[None, :] < lengths[:, None])[:, None, None, :]
    holder = col_index == 0
    suffix_scores = jnp.where(live_slots, suffix_scores, neg_big)
    own_scores = jnp.where(holder, own_scores, neg_big)
    highest = jnp.maximum(
        jnp.maximum(jnp.max(prompt_scores, axis=-1), jnp.max(suffix_scores, axis=-1)), own_scores
    )
    prompt_weights = jnp.exp(prompt_scores - highest[..., None])
    suffix_weights = jnp.where(live_slots, jnp.exp(suffix_scores - highest[..., None]), 0.0)
    own_weights = jnp.where(holder, jnp.exp(own_scores - highest), 0.0)
    totals = jnp.sum(prompt_weights, axis=-1) + jnp.sum(suffix_weights, axis=-1) + own_weights
    mixture = jnp.einsum(
        "skgp,pkd->skgd",
        prompt_weights.astype(jnp.bfloat16),
        prompt_values,
        preferred_element_type=jnp.float32,
    )
    mixture = mixture + jnp.einsum(
        "skgp,spkd->skgd",
        suffix_weights.astype(jnp.bfloat16),
        suffix_values,
        preferred_element_type=jnp.float32,
    )
    own_rounded = lax.optimization_barrier(own_weights.astype(jnp.bfloat16)).astype(jnp.float32)
    mixture = mixture + own_rounded[..., None] * own_values.astype(jnp.float32)[:, :, None, :]
    heads = KVH * REP
    bundle = jnp.concatenate(
        [
            mixture.reshape(seq_count, heads * HD),
            highest.reshape(seq_count, heads),
            totals.reshape(seq_count, heads),
            jnp.zeros((seq_count, LANES - 2 * heads), jnp.float32),
        ],
        axis=1,
    )
    bundles = [bundle] + [from_peer(bundle, "col", o) for o in range(1, lax.axis_size("col"))]
    every = jnp.stack(bundles)
    mixtures = every[:, :, : heads * HD].reshape(-1, seq_count, heads, HD)
    peaks = every[:, :, heads * HD : heads * HD + heads]
    sums = every[:, :, heads * HD + heads : heads * HD + 2 * heads]
    factors = jnp.exp(peaks - jnp.max(peaks, axis=0))
    total = jnp.sum(sums * factors, axis=0)
    mixed = jnp.sum(mixtures * factors[..., None], axis=0)
    return (mixed / total[..., None]).astype(jnp.bfloat16).reshape(seq_count, heads * HD)


def gate_up_kernel(me_ref, h_ref, gain_ref, router_ref, routes_ref, gate_ref, up_ref, out_ref, acc_ref):
    e = pl.program_id(0)
    tokens = h_ref.shape[0]
    lines = gate_ref.shape[2]
    padded = out_ref.shape[3]
    h = h_ref[...].astype(jnp.float32)
    scaled = (h * gain_ref[...].astype(jnp.float32)).astype(jnp.bfloat16)

    @pl.when(e == 0)
    def _():
        acc_ref[...] = jnp.zeros_like(acc_ref)

    against = (((1,), (1,)), ((), ()))
    gate = lax.dot_general(scaled, gate_ref[0, 0], against, preferred_element_type=jnp.float32)
    up = lax.dot_general(scaled, up_ref[0, 0], against, preferred_element_type=jnp.float32)
    for k in range(routes_ref.shape[1]):
        chosen = routes_ref[:, k : k + 1] == e
        acc_ref[2 * k, :, :lines] += jnp.where(chosen, gate, 0.0)
        acc_ref[2 * k + 1, :, :lines] += jnp.where(chosen, up, 0.0)

    @pl.when(e == pl.num_programs(0) - 1)
    def _():
        last = padded - LANES
        shift = lines - last
        experts = pl.num_programs(0)
        extra = jnp.dot(scaled, router_ref[...], preferred_element_type=jnp.float32)
        lane = iota((tokens, LANES), 1)
        square = jnp.sum(h * h, axis=1, keepdims=True)
        extra = jnp.where(lane == shift + experts, square, extra)
        high = extra.astype(jnp.bfloat16).astype(jnp.float32)
        low = extra - high
        acc_ref[0, :, last:] += jnp.where(lane >= shift, high, 0.0)
        acc_ref[1, :, last:] += jnp.where(lane >= shift, low, 0.0)
        peers, _, share, _ = out_ref.shape
        me = me_ref[0]
        for o in range(peers):
            begin = pl.multiple_of((me ^ o) * share, share)
            out_ref[o] = acc_ref[:, pl.ds(begin, share), :].astype(jnp.bfloat16)


def activate_kernel(lines, experts, model_width, routes_ref, *refs):
    out_ref = refs[-1]
    summed = refs[0][...].astype(jnp.float32)
    for ref in refs[1:-1]:
        summed = summed + ref[...].astype(jnp.float32)
    _, share, padded = summed.shape
    last = padded - LANES
    shift = lines - last
    extra = summed[0, :, last:] + summed[1, :, last:]
    lane = iota((share, LANES), 1)
    square = jnp.sum(jnp.where(lane == shift + experts, extra, 0.0), axis=1, keepdims=True)
    inverse_rms = lax.rsqrt(square / model_width + norm_eps)
    logits = []
    for k in range(out_ref.shape[0]):
        wanted = lane == routes_ref[:, k : k + 1] + shift
        logits.append(jnp.sum(jnp.where(wanted, extra, 0.0), axis=1, keepdims=True) * inverse_rms)
    peak = functools.reduce(jnp.maximum, logits)
    shares = [jnp.exp(v - peak) for v in logits]
    total = functools.reduce(jnp.add, shares)
    inside = iota((share, padded), 1) < lines
    for k in range(out_ref.shape[0]):
        gate = summed[2 * k] * inverse_rms
        up = summed[2 * k + 1] * inverse_rms
        act = gate / (1.0 + jnp.exp(-gate)) * up
        out_ref[k] = jnp.where(inside, act * (shares[k] / total), 0.0).astype(jnp.bfloat16)


def down_kernel(me_ref, routes_ref, *refs):
    down_ref, out_ref, act_ref = refs[-3:]
    chunks = refs[:-3]
    e = pl.program_id(0)
    topk, share, _ = chunks[0].shape
    lines = down_ref.shape[2]

    @pl.when(e == 0)
    def _():
        me = me_ref[0]
        out_ref[...] = jnp.zeros_like(out_ref)
        for o, chunk in enumerate(chunks):
            begin = pl.multiple_of((me ^ o) * share, share)
            act_ref[:, pl.ds(begin, share), :] = chunk[...]

    mine = jnp.zeros((act_ref.shape[1], lines), jnp.float32)
    for k in range(topk):
        chosen = routes_ref[:, k : k + 1] == e
        mine = mine + jnp.where(chosen, act_ref[k, :, :lines].astype(jnp.float32), 0.0)
    out_ref[...] += jnp.dot(
        mine.astype(jnp.bfloat16), down_ref[0, 0], preferred_element_type=jnp.float32
    )


def experts_part(h_mid, moe_gain, w_router, expert_lines, routes, migration):
    rows = lax.axis_size("row")
    cols = lax.axis_size("col")
    row_index = lax.axis_index("row")
    col_index = lax.axis_index("col")
    experts, _, lines, width = expert_lines.shape
    own, _ = h_mid.shape
    tokens = own * rows
    topk = routes.shape[1]
    share = tokens // cols
    padded = up_to(lines + experts + 1, LANES)
    shift = lines - (padded - LANES)
    me = col_index.astype(jnp.int32).reshape(1)

    order = row_index ^ jnp.array(sorted(range(rows), key=lambda o: (o % 2, o)), jnp.int32)
    routes = routes.reshape(rows, own, topk)[order].reshape(tokens, topk)
    my_routes = lax.dynamic_slice_in_dim(routes, col_index * share, share, 0)
    router = jnp.pad(w_router, ((0, 0), (shift, LANES - shift - experts)))
    same_core = jnp.concatenate(
        [h_mid] + [from_peer(h_mid, "row", o) for o in range(2, rows, 2)], axis=0
    )
    every_h = jnp.concatenate([same_core, from_peer(same_core, "row", 1)], axis=0)
    migration.send([every_h])
    part_spec = lambda part: pl.BlockSpec((1, 1, lines, width), lambda e, me: (e, part, 0, 0))
    whole = lambda a: pl.BlockSpec(a.shape, lambda e, me: (0,) * a.ndim)
    gain = moe_gain.reshape(1, width)
    partial = pl.pallas_call(
        gate_up_kernel,
        grid_spec=pltpu.PrefetchScalarGridSpec(
            num_scalar_prefetch=1,
            grid=(experts,),
            in_specs=[whole(every_h), whole(gain), whole(router), whole(routes)]
            + [part_spec(0), part_spec(1)],
            out_specs=pl.BlockSpec((cols, 2 * topk, share, padded), lambda e, me: (0, 0, 0, 0)),
            scratch_shapes=[pltpu.VMEM((2 * topk, tokens, padded), jnp.float32)],
        ),
        out_shape=jax.ShapeDtypeStruct((cols, 2 * topk, share, padded), jnp.bfloat16),
        compiler_params=params(),
        cost_estimate=pl.CostEstimate(
            flops=4 * experts * tokens * lines * width,
            bytes_accessed=4 * experts * lines * width,
            transcendentals=0,
        ),
        name="gate_up",
    )(me, every_h, gain, router, routes, expert_lines, expert_lines)
    gathered = [partial[0]] + [from_peer(partial[o], "col", o) for o in range(1, cols)]
    activated = pl.pallas_call(
        functools.partial(activate_kernel, lines, experts, width * cols),
        out_shape=jax.ShapeDtypeStruct((topk, share, padded), jnp.bfloat16),
        compiler_params=params(),
        name="activate",
    )(my_routes, *gathered)
    chunks = [activated] + [from_peer(activated, "col", o) for o in range(1, cols)]
    produced = pl.pallas_call(
        down_kernel,
        grid_spec=pltpu.PrefetchScalarGridSpec(
            num_scalar_prefetch=1,
            grid=(experts,),
            in_specs=[whole(routes)] + [whole(c) for c in chunks] + [part_spec(2)],
            out_specs=pl.BlockSpec((tokens, width), lambda e, me: (0, 0)),
            scratch_shapes=[pltpu.VMEM((topk, tokens, padded), jnp.bfloat16)],
        ),
        out_shape=jax.ShapeDtypeStruct((tokens, width), jnp.float32),
        compiler_params=params(),
        cost_estimate=pl.CostEstimate(
            flops=2 * experts * tokens * lines * width,
            bytes_accessed=2 * experts * lines * width,
            transcendentals=0,
        ),
        name="down",
    )(me, routes, *chunks, expert_lines)
    migration.receive(0)
    (produced,) = after([produced], [migration.moved])
    half = tokens // 2
    both_cores = produced[:half] + from_peer(produced[half:], "row", 1)
    blocks = both_cores.reshape(rows // 2, own, width)
    mixed = blocks[0]
    for n in range(1, rows // 2):
        mixed = mixed + from_peer(blocks[n], "row", 2 * n)
    return mixed


def local(
    hidden,
    queries,
    new_kv,
    prompt_kv,
    suffix_kv,
    lengths,
    w_out,
    moe_gain,
    w_router,
    expert_weights,
    old_lines,
    new_lines,
    routes,
):
    expert_lines = jnp.transpose(expert_weights, (0, 2, 1, 3))
    migration = Migration(expert_lines, old_lines, new_lines)
    migration.send()
    attended = attend(queries, new_kv, prompt_kv, suffix_kv, lengths)
    projected = jnp.dot(attended, w_out, preferred_element_type=jnp.float32)
    h_mid = (hidden.astype(jnp.float32) + projected).astype(jnp.bfloat16)
    (h_mid,) = after([h_mid], migration.packed)
    mixed = experts_part(h_mid, moe_gain, w_router, expert_lines, routes, migration)
    migration.receive(1)
    return (h_mid.astype(jnp.float32) + mixed, jnp.transpose(migration.moved, (0, 2, 1, 3)))


def solution(mesh):
    return jax.shard_map(
        local,
        mesh=mesh,
        in_specs=(
            P("row", "col"),
            P("row", None),
            P("row", None, None),
            P("row", None, "col", None),
            P("row", None, "col", None),
            P("row"),
            P(None, "col"),
            P("col"),
            P("col", None),
            P(None, "row", None, "col"),
            P(),
            P(),
            P(),
        ),
        out_specs=(P("row", "col"), P(None, "row", None, "col")),
        check_vma=False,
    )
```

```python
import functools

import jax
import jax.numpy as jnp
from jax import lax
from jax.experimental import pallas as pl
from jax.experimental.pallas import tpu as pltpu
from jax.sharding import PartitionSpec as P

KVH = 16
HD = 128
REP = 2
TILE = 16
LANES = 128

norm_eps = 1e-06
neg_big = -1e30
VMEM_LIMIT = 48 * 1024 * 1024
PACK_LIMIT = 61 * 1024 * 1024


def up_to(value, unit):
    return -(-value // unit) * unit


def iota(shape, axis):
    return lax.broadcasted_iota(jnp.int32, shape, axis)


def ones_where(mask):
    return jnp.where(mask, 1.0, 0.0).astype(jnp.bfloat16)


def params():
    return pltpu.CompilerParams(vmem_limit_bytes=VMEM_LIMIT)


def counting(shape, axis):
    return iota(shape, axis).astype(jnp.float32).astype(jnp.bfloat16)


def as_bf16(values):
    return values.astype(jnp.float32).astype(jnp.bfloat16)


def equal_ones(left, right):
    one = jnp.ones((), jnp.bfloat16)
    return jnp.maximum(one - jnp.abs(left - right), jnp.zeros((), jnp.bfloat16))


def within(place, block):
    place = place - 256 * block
    return as_bf16(jnp.where((place >= 0) & (place < 256), place, -1))


def look_up(table_row, id_row, numbers, values):
    full = table_row.shape[1]
    ids = id_row.shape[1]
    high_count = up_to(-(-full // 64), 16)
    table_high = equal_ones(numbers[:high_count], as_bf16(table_row >> 6))
    low = as_bf16(table_row & 63)
    zero = jnp.zeros((), jnp.bfloat16)
    table_low = jnp.concatenate(
        [jnp.where(numbers[:64] == low, part, zero) for part in values], axis=0
    )
    square = lax.dot_general(
        table_low, table_high, (((1,), (1,)), ((), ())), preferred_element_type=jnp.float32
    )
    id_high = equal_ones(numbers[:high_count, :ids], as_bf16(id_row >> 6))
    spread = jnp.dot(square.astype(jnp.bfloat16), id_high, preferred_element_type=jnp.float32)
    wanted = iota((64, ids), 0) == (id_row & 63)
    return [
        jnp.sum(jnp.where(wanted, spread[64 * n : 64 * n + 64], 0.0), axis=0, keepdims=True)
        for n in range(len(values))
    ]


def numbers_for(full):
    return counting((max(up_to(-(-full // 64), 16), 64), full), 0)


def segment_plan(counts, experts, rows):
    starts = []
    running = jnp.zeros((rows, LANES), jnp.float32)
    for e in range(experts):
        starts.append(running)
        running = running + counts[e * rows : (e + 1) * rows]
    start = jnp.concatenate(starts, axis=0)
    lead = jnp.where(counts > 0.0, jnp.floor(start * (1.0 / TILE)), 0.0)
    tail = jnp.floor((start + counts + (TILE - 1.0)) * (1.0 / TILE))
    tiles = jnp.where(counts > 0.0, tail - lead, 0.0)
    pairs = experts * rows
    line = iota((pairs, pairs), 0)
    column = iota((pairs, pairs), 1)
    earlier = ones_where((line // rows == column // rows) & (column < line))
    base = jnp.dot(earlier, tiles.astype(jnp.bfloat16), preferred_element_type=jnp.float32)
    return start, lead, tiles, base


def outgoing_kernel(lines, rows, new_ref, held_ref, stack_ref, plan_ref):
    experts = new_ref.shape[0]
    width = held_ref.shape[1]
    real = iota((1, width), 1) < lines
    hits = []
    full = new_ref.shape[1]
    numbers = numbers_for(full)
    slot = iota((64, full), 1).astype(jnp.float32)
    values = (jnp.floor((slot + 0.5) * (1.0 / lines)).astype(jnp.bfloat16),)
    for e in range(experts):
        (peer,) = look_up(new_ref[e : e + 1, :], held_ref[e : e + 1, :], numbers, values)
        peer = peer.astype(jnp.int32)
        hits.append(jnp.where((iota((rows, width), 0) == peer) & real, 1.0, 0.0))
    hits = jnp.concatenate(hits, axis=0)
    until = ones_where(iota((width, width), 0) <= iota((width, width), 1))
    ranks = jnp.dot(hits.astype(jnp.bfloat16), until, preferred_element_type=jnp.float32)
    counts = jnp.broadcast_to(jnp.sum(hits, axis=1, keepdims=True), (experts * rows, LANES))
    start, lead, tiles, base = segment_plan(counts, experts, rows)
    for n, part in enumerate((lead, tiles, base, start - lead * TILE)):
        plan_ref[n] = part.astype(jnp.int32)
    offset = (base * TILE + start - lead * TILE - 1.0)[:, :1]
    placed = hits * (ranks + offset)
    for e in range(experts):
        row = jnp.sum(placed[e * rows : (e + 1) * rows], axis=0, keepdims=True)
        stack_ref[e] = jnp.where(real, row, -1.0).astype(jnp.int32)


def incoming_kernel(lines, rows, block_tiles, slot, old_ref, wanted_ref, stack_ref, plan_ref):
    experts = old_ref.shape[0]
    width = wanted_ref.shape[1]
    real = iota((1, width), 1) < lines
    held_at = []
    hits = []
    full = old_ref.shape[1]
    numbers = numbers_for(full)
    at = iota((64, full), 1)
    values = (as_bf16(at >> 7), as_bf16(at & 127))
    for e in range(experts):
        high, low = look_up(old_ref[e : e + 1, :], wanted_ref[e : e + 1, :], numbers, values)
        slots = high * 128.0 + low
        held_at.append(jnp.where(real, slots, 1e9))
        peer = jnp.floor((slots + 0.5) * (1.0 / lines)).astype(jnp.int32)
        hits.append(jnp.where((iota((rows, width), 0) == peer) & real, 1.0, 0.0))
    hits = jnp.concatenate(hits, axis=0)
    counts = jnp.broadcast_to(jnp.sum(hits, axis=1, keepdims=True), (experts * rows, LANES))
    start, lead, tiles, base = segment_plan(counts, experts, rows)
    line = iota((experts * rows, LANES), 0)
    peer = (line % rows).astype(jnp.float32)
    longest = [
        jnp.max(tiles[e * rows : (e + 1) * rows], axis=0, keepdims=True) for e in range(experts)
    ]
    longest = jnp.concatenate(
        [jnp.broadcast_to(most, (rows, LANES)) for most in longest], axis=0
    )
    slotted = longest <= slot
    lead = jnp.where(slotted, jnp.minimum(lead, float(block_tiles - slot)), lead)
    base = jnp.where(slotted, peer * slot, base)
    for n, part in enumerate((lead, tiles, base, jnp.where(slotted, 1.0, 0.0))):
        plan_ref[n] = part.astype(jnp.int32)
    blank = jnp.zeros((LANES - experts, width), jnp.float32)
    columns = jnp.transpose(jnp.concatenate(held_at + [blank], axis=0))
    rows_out = []
    for e in range(experts):
        mine = slice(e * rows, (e + 1) * rows)
        before = jnp.where(columns[:, e : e + 1] < held_at[e], 1.0, 0.0)
        rank = jnp.sum(before, axis=0, keepdims=True)
        ahead = jnp.zeros((1, LANES), jnp.float32)
        firsts = []
        for r in range(rows):
            firsts.append(ahead)
            ahead = ahead + counts[e * rows + r : e * rows + r + 1]
        first = jnp.concatenate(firsts, axis=0)
        offset = (base[mine] * TILE + start[mine] - lead[mine] * TILE - first)[:, :1]
        rows_out.append(jnp.sum(hits[mine] * (rank + offset), axis=0, keepdims=True))
    places = jnp.transpose(jnp.concatenate(rows_out + [blank], axis=0))
    for e in range(experts):
        place = jnp.broadcast_to(places[:lines, e : e + 1], (lines, LANES))
        block = jnp.floor(place * (1.0 / 256.0))
        stack_ref[e, 0] = (place - 256.0 * block).astype(jnp.bfloat16)
        stack_ref[e, 1] = block.astype(jnp.bfloat16)


STRAIGHT = 8


def tile_at(index):
    return pl.ds(pl.multiple_of(index * TILE, TILE), TILE)


def pack_kernel(rows, span, plan_ref, place_ref, lines_ref, out_ref, packed_ref, number_ref, sem, *stages):
    part = pl.program_id(0)
    step = pl.program_id(1)
    pairs = pl.num_programs(1) * span * rows
    deep, _ = stages[0].shape
    lines = lines_ref.shape[2]

    @pl.when((part == 0) & (step == 0))
    def _():
        number_ref[...] = counting(number_ref.shape, 0)

    def entry(n, j, d):
        return plan_ref[n * pairs + (step * span + j) * rows + d]

    usual = min(deep, up_to(lines + rows * TILE, TILE))

    def move(j, begin, end):
        place = place_ref[j][:, :lines]
        onehot = [
            equal_ones(number_ref[: min(256, end - row)], within(place - begin, (row - begin) // 256))
            for row in range(begin, end, 256)
        ]
        stages[j][begin:end] = jnp.dot(
            jnp.concatenate(onehot, axis=0), lines_ref[j, 0], preferred_element_type=jnp.float32
        ).astype(jnp.bfloat16)

    for j in range(span):
        move(j, 0, usual)
    if usual < deep:
        for j in range(span):
            used = entry(1, j, rows - 1) + entry(2, j, rows - 1)

            @pl.when(used * TILE > usual)
            def _(j=j):
                move(j, usual, deep)

    for j, stage_ref in enumerate(stages):

        def one_peer(d, most, j=j, stage_ref=stage_ref):
            lead, tiles, base = entry(0, j, d), entry(1, j, d), entry(2, j, d)
            shared = entry(3, j, d) > 0
            earlier = packed_ref[d, tile_at(lead), :]
            for t in range(1, STRAIGHT):
                n = jnp.maximum(jnp.minimum(t, tiles - 1), 0)
                packed_ref[d, tile_at(lead + n), :] = stage_ref[tile_at(base + n), :]
            kept = jnp.where(shared | (tiles == 0), earlier, jnp.zeros_like(earlier))
            fresh = stage_ref[tile_at(base), :]
            fresh = jnp.where(tiles == 0, jnp.zeros_like(fresh), fresh)
            packed_ref[d, tile_at(lead), :] = kept + fresh
            return jnp.maximum(most, tiles)

        most = lax.fori_loop(0, rows, one_peer, 0, unroll=rows <= 8)

        @pl.when(most > STRAIGHT)
        def _(j=j, stage_ref=stage_ref):
            def long_peer(d, carry):
                lead, tiles, base = entry(0, j, d), entry(1, j, d), entry(2, j, d)

                def put(t, c):
                    packed_ref[d, tile_at(lead + t), :] = stage_ref[tile_at(base + t), :]
                    return c

                return lax.fori_loop(STRAIGHT, tiles, put, carry)

            lax.fori_loop(0, rows, long_peer, 0)

    @pl.when(step == pl.num_programs(1) - 1)
    def _():
        copy = pltpu.make_async_copy(packed_ref, out_ref.at[:, part], sem)
        copy.start()
        copy.wait()


def unpack_kernel(slot, plan_ref, place_ref, block_ref, *rest):
    out_ref, stage_ref, sems = rest[-3:]
    experts = pl.num_programs(0)
    rows, count, _, width = block_ref.shape
    pairs = experts * rows
    _, deep, _ = stage_ref.shape
    lines = out_ref.shape[2]
    e = pl.program_id(0)
    buffer = e % 2

    def entry(n, e, s):
        return plan_ref[n * pairs + e * rows + s]

    def slotted(e):
        return entry(3, e, 0) > 0

    def columns(part):
        return pl.ds(part * width, width)

    def slot_copies(e):
        for s in range(rows):
            there = pl.ds(pl.multiple_of(entry(0, e, s) * TILE, TILE), slot * TILE)
            here = pl.ds(s * slot * TILE, slot * TILE)
            for part in range(count):
                yield pltpu.make_async_copy(
                    block_ref.at[s, part, there],
                    stage_ref.at[e % 2, here, columns(part)],
                    sems.at[e % 2, s * count + part],
                )

    def begin(e):
        @pl.when(slotted(e))
        def _():
            for copy in slot_copies(e):
                copy.start()

    @pl.when(e == 0)
    def _():
        stage_ref[...] = jnp.zeros_like(stage_ref)
        begin(e)

    @pl.when(e + 1 < experts)
    def _():
        begin(e + 1)

    @pl.when(slotted(e))
    def _():
        for copy in slot_copies(e):
            copy.wait()

    @pl.when(jnp.logical_not(slotted(e)))
    def _():
        def one_peer(s, carry):
            def put(t, c):
                for part in range(count):
                    copy = pltpu.make_async_copy(
                        block_ref.at[s, part, tile_at(entry(0, e, s) + t)],
                        stage_ref.at[buffer, tile_at(entry(2, e, s) + t), columns(part)],
                        sems.at[buffer, part],
                    )
                    copy.start()
                    copy.wait()
                return c

            return lax.fori_loop(0, entry(1, e, s), put, carry)

        lax.fori_loop(0, rows, one_peer, 0)

    within_block, block = place_ref[0, 0], place_ref[0, 1]
    lane = counting((lines, LANES), 1)
    pieces = []
    for first in range(0, deep, LANES):
        away = jnp.abs(block - jnp.asarray(first // 256, jnp.bfloat16))
        place = within_block + away * jnp.asarray(512, jnp.bfloat16)
        pieces.append(equal_ones(lane + jnp.asarray(first % 256, jnp.bfloat16), place))
    onehot = jnp.concatenate(pieces, axis=1)
    moved = jnp.dot(
        onehot, stage_ref[buffer], preferred_element_type=jnp.float32
    ).astype(jnp.bfloat16)
    for part in range(count):
        out_ref[0, part] = moved[:, part * width : (part + 1) * width]


def call_plan(kernel, name, table, ids, pairs, place):
    return pl.pallas_call(
        kernel,
        out_shape=(place, jax.ShapeDtypeStruct((4, pairs, LANES), jnp.int32)),
        compiler_params=params(),
        cost_estimate=pl.CostEstimate(
            flops=20 * table.size * 256, bytes_accessed=8 * table.size, transcendentals=0
        ),
        name=name,
    )(table, ids)


def pack(expert_lines, place, plan, piece, rows, block_rows, deep):
    experts, _, lines, width = expert_lines.shape
    first, count = piece
    span = 2 - experts % 2
    return pl.pallas_call(
        functools.partial(pack_kernel, rows, span),
        grid_spec=pltpu.PrefetchScalarGridSpec(
            num_scalar_prefetch=1,
            grid=(count, experts // span),
            in_specs=[
                pl.BlockSpec((span, 1, place.shape[2]), lambda p, e, plan: (e, 0, 0)),
                pl.BlockSpec((span, 1, lines, width), lambda p, e, plan: (e, first + p, 0, 0)),
            ],
            out_specs=pl.BlockSpec(memory_space=pltpu.HBM),
            scratch_shapes=[
                pltpu.VMEM((rows, block_rows, width), jnp.bfloat16),
                pltpu.VMEM((256, lines), jnp.bfloat16),
                pltpu.SemaphoreType.DMA(()),
            ]
            + [pltpu.VMEM((deep, width), jnp.bfloat16)] * span,
        ),
        out_shape=jax.ShapeDtypeStruct((rows, count, block_rows, width), jnp.bfloat16),
        compiler_params=pltpu.CompilerParams(vmem_limit_bytes=PACK_LIMIT),
        cost_estimate=pl.CostEstimate(
            flops=2 * count * experts * deep * lines * width,
            bytes_accessed=4 * count * experts * lines * width,
            transcendentals=0,
        ),
        name="pack_lines",
    )(plan, place, expert_lines)


def unpack(arrived, place, plan, piece, shape, deep, slot, previous):
    experts, _, lines, width = shape
    first, count = piece
    rows = arrived.shape[0]
    in_specs = [
        pl.BlockSpec((1, 2, lines, LANES), lambda e, plan: (e, 0, 0, 0)),
        pl.BlockSpec(memory_space=pl.ANY),
    ]
    operands = [plan, place, arrived]
    aliases = {}
    if previous is not None:
        in_specs.append(pl.BlockSpec(memory_space=pl.ANY))
        operands.append(previous)
        aliases = {3: 0}
    return pl.pallas_call(
        functools.partial(unpack_kernel, slot),
        grid_spec=pltpu.PrefetchScalarGridSpec(
            num_scalar_prefetch=1,
            grid=(experts,),
            in_specs=in_specs,
            out_specs=pl.BlockSpec((1, count, lines, width), lambda e, plan: (e, first // count, 0, 0)),
            scratch_shapes=[
                pltpu.VMEM((2, deep, count * width), jnp.bfloat16),
                pltpu.SemaphoreType.DMA((2, rows * count)),
            ],
        ),
        out_shape=jax.ShapeDtypeStruct(shape, jnp.bfloat16),
        input_output_aliases=aliases,
        compiler_params=params(),
        cost_estimate=pl.CostEstimate(
            flops=2 * count * experts * deep * lines * width,
            bytes_accessed=4 * count * experts * lines * width,
            transcendentals=0,
        ),
        name="unpack_lines",
    )(*operands)


def after_kernel(*refs):
    del refs


def after(values, signals):
    anywhere = pl.BlockSpec(memory_space=pl.ANY)
    return pl.pallas_call(
        after_kernel,
        in_specs=[anywhere] * (len(values) + len(signals)),
        out_specs=[anywhere] * len(values),
        out_shape=[jax.ShapeDtypeStruct(v.shape, v.dtype) for v in values],
        input_output_aliases={n: n for n in range(len(values))},
        compiler_params=pltpu.CompilerParams(vmem_limit_bytes=PACK_LIMIT),
        name="after",
    )(*values, *signals)


def own_ids(table, lines, width):
    mine = lax.dynamic_slice_in_dim(table, lax.axis_index("row") * lines, lines, 1)
    return jnp.pad(mine, ((0, 0), (0, width - lines)), constant_values=-1)


def from_peer(block, axis, offset):
    size = lax.axis_size(axis)
    return lax.ppermute(block, axis, [(i, i ^ offset) for i in range(size)])


class Migration:
    def __init__(self, expert_lines, old_lines, new_lines):
        rows = lax.axis_size("row")
        experts, parts, lines, width = expert_lines.shape
        padded = up_to(lines, LANES)
        block_rows = up_to(experts * lines // rows, TILE)
        pairs = experts * rows
        compact = up_to(lines + 2 * (TILE - 1) * rows, TILE) + TILE
        self.slot = min(STRAIGHT, block_rows // TILE)
        self.deep = up_to(max(compact, rows * self.slot * TILE), 256)
        self.shape = expert_lines.shape
        self.pieces = [(parts - 1, 1), (0, parts - 1)]
        out_place, out_plan = call_plan(
            functools.partial(outgoing_kernel, lines, rows), "outgoing_plan",
            new_lines, own_ids(old_lines, lines, padded), pairs,
            jax.ShapeDtypeStruct((experts, 1, padded), jnp.int32),
        )
        self.in_place, in_plan = call_plan(
            functools.partial(incoming_kernel, lines, rows, block_rows // TILE, self.slot),
            "incoming_plan",
            old_lines, own_ids(new_lines, lines, padded), pairs,
            jax.ShapeDtypeStruct((experts, 2, lines, LANES), jnp.bfloat16),
        )
        out_plan = out_plan[:, :, 0].reshape(-1)
        self.in_plan = in_plan[:, :, 0].reshape(-1)
        self.packed = [
            pack(expert_lines, out_place, out_plan, piece, rows, block_rows, compact)
            for piece in self.pieces
        ]
        self.arrived = []
        self.moved = None

    def send(self, signals=()):
        block = self.packed[len(self.arrived)]
        if signals:
            (block,) = after([block], signals)
        self.arrived.append(
            lax.all_to_all(block, "row", split_axis=0, concat_axis=0, tiled=True)
        )

    def receive(self, piece):
        self.moved = unpack(
            self.arrived[piece], self.in_place, self.in_plan, self.pieces[piece], self.shape,
            self.deep, self.slot, self.moved,
        )


def attend(queries, new_kv, prompt_kv, suffix_kv, lengths):
    seq_count = queries.shape[0]
    prompt_rows = prompt_kv.shape[2]
    suffix_rows = suffix_kv.shape[2]
    col_index = lax.axis_index("col")
    query_heads = queries.reshape(seq_count, KVH, REP, HD)
    prompt_keys = prompt_kv[0, 0].reshape(prompt_rows, KVH, HD)
    prompt_values = prompt_kv[0, 1].reshape(prompt_rows, KVH, HD)
    suffix_keys = suffix_kv[:, 0].reshape(seq_count, suffix_rows, KVH, HD)
    suffix_values = suffix_kv[:, 1].reshape(seq_count, suffix_rows, KVH, HD)
    own_keys = new_kv[:, 0].reshape(seq_count, KVH, HD)
    own_values = new_kv[:, 1].reshape(seq_count, KVH, HD)
    score_scale = HD ** (-0.5)
    prompt_scores = (
        jnp.einsum("skgd,pkd->skgp", query_heads, prompt_keys, preferred_element_type=jnp.float32)
        * score_scale
    )
    suffix_scores = (
        jnp.einsum("skgd,spkd->skgp", query_heads, suffix_keys, preferred_element_type=jnp.float32)
        * score_scale
    )
    own_scores = (
        jnp.einsum("skgd,skd->skg", query_heads, own_keys, preferred_element_type=jnp.float32)
        * score_scale
    )
    positions = col_index * suffix_rows + jnp.arange(suffix_rows, dtype=jnp.int32)
    live_slots = (positions[None, :] < lengths[:, None])[:, None, None, :]
    holder = col_index == 0
    suffix_scores = jnp.where(live_slots, suffix_scores, neg_big)
    own_scores = jnp.where(holder, own_scores, neg_big)
    highest = jnp.maximum(
        jnp.maximum(jnp.max(prompt_scores, axis=-1), jnp.max(suffix_scores, axis=-1)), own_scores
    )
    prompt_weights = jnp.exp(prompt_scores - highest[..., None])
    suffix_weights = jnp.where(live_slots, jnp.exp(suffix_scores - highest[..., None]), 0.0)
    own_weights = jnp.where(holder, jnp.exp(own_scores - highest), 0.0)
    totals = jnp.sum(prompt_weights, axis=-1) + jnp.sum(suffix_weights, axis=-1) + own_weights
    mixture = jnp.einsum(
        "skgp,pkd->skgd",
        prompt_weights.astype(jnp.bfloat16),
        prompt_values,
        preferred_element_type=jnp.float32,
    )
    mixture = mixture + jnp.einsum(
        "skgp,spkd->skgd",
        suffix_weights.astype(jnp.bfloat16),
        suffix_values,
        preferred_element_type=jnp.float32,
    )
    own_rounded = lax.optimization_barrier(own_weights.astype(jnp.bfloat16)).astype(jnp.float32)
    mixture = mixture + own_rounded[..., None] * own_values.astype(jnp.float32)[:, :, None, :]
    heads = KVH * REP
    bundle = jnp.concatenate(
        [
            mixture.reshape(seq_count, heads * HD),
            highest.reshape(seq_count, heads),
            totals.reshape(seq_count, heads),
            jnp.zeros((seq_count, LANES - 2 * heads), jnp.float32),
        ],
        axis=1,
    )
    bundles = [bundle] + [from_peer(bundle, "col", o) for o in range(1, lax.axis_size("col"))]
    every = jnp.stack(bundles)
    mixtures = every[:, :, : heads * HD].reshape(-1, seq_count, heads, HD)
    peaks = every[:, :, heads * HD : heads * HD + heads]
    sums = every[:, :, heads * HD + heads : heads * HD + 2 * heads]
    factors = jnp.exp(peaks - jnp.max(peaks, axis=0))
    total = jnp.sum(sums * factors, axis=0)
    mixed = jnp.sum(mixtures * factors[..., None], axis=0)
    return (mixed / total[..., None]).astype(jnp.bfloat16).reshape(seq_count, heads * HD)


def gate_up_kernel(me_ref, h_ref, gain_ref, router_ref, routes_ref, gate_ref, up_ref, out_ref, acc_ref):
    e = pl.program_id(0)
    tokens = h_ref.shape[0]
    lines = gate_ref.shape[2]
    padded = out_ref.shape[3]
    h = h_ref[...].astype(jnp.float32)
    scaled = (h * gain_ref[...].astype(jnp.float32)).astype(jnp.bfloat16)

    @pl.when(e == 0)
    def _():
        acc_ref[...] = jnp.zeros_like(acc_ref)

    against = (((1,), (1,)), ((), ()))
    gate = lax.dot_general(scaled, gate_ref[0, 0], against, preferred_element_type=jnp.float32)
    up = lax.dot_general(scaled, up_ref[0, 0], against, preferred_element_type=jnp.float32)
    for k in range(routes_ref.shape[1]):
        chosen = routes_ref[:, k : k + 1] == e
        acc_ref[2 * k, :, :lines] += jnp.where(chosen, gate, 0.0)
        acc_ref[2 * k + 1, :, :lines] += jnp.where(chosen, up, 0.0)

    @pl.when(e == pl.num_programs(0) - 1)
    def _():
        last = padded - LANES
        shift = lines - last
        experts = pl.num_programs(0)
        extra = jnp.dot(scaled, router_ref[...], preferred_element_type=jnp.float32)
        lane = iota((tokens, LANES), 1)
        square = jnp.sum(h * h, axis=1, keepdims=True)
        extra = jnp.where(lane == shift + experts, square, extra)
        high = extra.astype(jnp.bfloat16).astype(jnp.float32)
        low = extra - high
        acc_ref[0, :, last:] += jnp.where(lane >= shift, high, 0.0)
        acc_ref[1, :, last:] += jnp.where(lane >= shift, low, 0.0)
        peers, _, share, _ = out_ref.shape
        me = me_ref[0]
        for o in range(peers):
            begin = pl.multiple_of((me ^ o) * share, share)
            out_ref[o] = acc_ref[:, pl.ds(begin, share), :].astype(jnp.bfloat16)


def activate_kernel(lines, experts, model_width, routes_ref, *refs):
    out_ref = refs[-1]
    summed = refs[0][...].astype(jnp.float32)
    for ref in refs[1:-1]:
        summed = summed + ref[...].astype(jnp.float32)
    _, share, padded = summed.shape
    last = padded - LANES
    shift = lines - last
    extra = summed[0, :, last:] + summed[1, :, last:]
    lane = iota((share, LANES), 1)
    square = jnp.sum(jnp.where(lane == shift + experts, extra, 0.0), axis=1, keepdims=True)
    inverse_rms = lax.rsqrt(square / model_width + norm_eps)
    logits = []
    for k in range(out_ref.shape[0]):
        wanted = lane == routes_ref[:, k : k + 1] + shift
        logits.append(jnp.sum(jnp.where(wanted, extra, 0.0), axis=1, keepdims=True) * inverse_rms)
    peak = functools.reduce(jnp.maximum, logits)
    shares = [jnp.exp(v - peak) for v in logits]
    total = functools.reduce(jnp.add, shares)
    inside = iota((share, padded), 1) < lines
    for k in range(out_ref.shape[0]):
        gate = summed[2 * k] * inverse_rms
        up = summed[2 * k + 1] * inverse_rms
        act = gate / (1.0 + jnp.exp(-gate)) * up
        out_ref[k] = jnp.where(inside, act * (shares[k] / total), 0.0).astype(jnp.bfloat16)


def down_kernel(me_ref, routes_ref, *refs):
    down_ref, out_ref, act_ref = refs[-3:]
    chunks = refs[:-3]
    e = pl.program_id(0)
    topk, share, _ = chunks[0].shape
    lines = down_ref.shape[2]

    @pl.when(e == 0)
    def _():
        me = me_ref[0]
        out_ref[...] = jnp.zeros_like(out_ref)
        for o, chunk in enumerate(chunks):
            begin = pl.multiple_of((me ^ o) * share, share)
            act_ref[:, pl.ds(begin, share), :] = chunk[...]

    mine = jnp.zeros((act_ref.shape[1], lines), jnp.float32)
    for k in range(topk):
        chosen = routes_ref[:, k : k + 1] == e
        mine = mine + jnp.where(chosen, act_ref[k, :, :lines].astype(jnp.float32), 0.0)
    out_ref[...] += jnp.dot(
        mine.astype(jnp.bfloat16), down_ref[0, 0], preferred_element_type=jnp.float32
    )


def experts_part(h_mid, moe_gain, w_router, expert_lines, routes, migration):
    rows = lax.axis_size("row")
    cols = lax.axis_size("col")
    row_index = lax.axis_index("row")
    col_index = lax.axis_index("col")
    experts, _, lines, width = expert_lines.shape
    own, _ = h_mid.shape
    tokens = own * rows
    topk = routes.shape[1]
    share = tokens // cols
    padded = up_to(lines + experts + 1, LANES)
    shift = lines - (padded - LANES)
    me = col_index.astype(jnp.int32).reshape(1)

    order = row_index ^ jnp.array(sorted(range(rows), key=lambda o: (o % 2, o)), jnp.int32)
    routes = routes.reshape(rows, own, topk)[order].reshape(tokens, topk)
    my_routes = lax.dynamic_slice_in_dim(routes, col_index * share, share, 0)
    router = jnp.pad(w_router, ((0, 0), (shift, LANES - shift - experts)))
    same_core = jnp.concatenate(
        [h_mid] + [from_peer(h_mid, "row", o) for o in range(2, rows, 2)], axis=0
    )
    every_h = jnp.concatenate([same_core, from_peer(same_core, "row", 1)], axis=0)
    migration.send([every_h])
    part_spec = lambda part: pl.BlockSpec((1, 1, lines, width), lambda e, me: (e, part, 0, 0))
    whole = lambda a: pl.BlockSpec(a.shape, lambda e, me: (0,) * a.ndim)
    gain = moe_gain.reshape(1, width)
    partial = pl.pallas_call(
        gate_up_kernel,
        grid_spec=pltpu.PrefetchScalarGridSpec(
            num_scalar_prefetch=1,
            grid=(experts,),
            in_specs=[whole(every_h), whole(gain), whole(router), whole(routes)]
            + [part_spec(0), part_spec(1)],
            out_specs=pl.BlockSpec((cols, 2 * topk, share, padded), lambda e, me: (0, 0, 0, 0)),
            scratch_shapes=[pltpu.VMEM((2 * topk, tokens, padded), jnp.float32)],
        ),
        out_shape=jax.ShapeDtypeStruct((cols, 2 * topk, share, padded), jnp.bfloat16),
        compiler_params=params(),
        cost_estimate=pl.CostEstimate(
            flops=4 * experts * tokens * lines * width,
            bytes_accessed=4 * experts * lines * width,
            transcendentals=0,
        ),
        name="gate_up",
    )(me, every_h, gain, router, routes, expert_lines, expert_lines)
    gathered = [partial[0]] + [from_peer(partial[o], "col", o) for o in range(1, cols)]
    activated = pl.pallas_call(
        functools.partial(activate_kernel, lines, experts, width * cols),
        out_shape=jax.ShapeDtypeStruct((topk, share, padded), jnp.bfloat16),
        compiler_params=params(),
        name="activate",
    )(my_routes, *gathered)
    chunks = [activated] + [from_peer(activated, "col", o) for o in range(1, cols)]
    produced = pl.pallas_call(
        down_kernel,
        grid_spec=pltpu.PrefetchScalarGridSpec(
            num_scalar_prefetch=1,
            grid=(experts,),
            in_specs=[whole(routes)] + [whole(c) for c in chunks] + [part_spec(2)],
            out_specs=pl.BlockSpec((tokens, width), lambda e, me: (0, 0)),
            scratch_shapes=[pltpu.VMEM((topk, tokens, padded), jnp.bfloat16)],
        ),
        out_shape=jax.ShapeDtypeStruct((tokens, width), jnp.float32),
        compiler_params=params(),
        cost_estimate=pl.CostEstimate(
            flops=2 * experts * tokens * lines * width,
            bytes_accessed=2 * experts * lines * width,
            transcendentals=0,
        ),
        name="down",
    )(me, routes, *chunks, expert_lines)
    migration.receive(0)
    (produced,) = after([produced], [migration.moved])
    half = tokens // 2
    both_cores = produced[:half] + from_peer(produced[half:], "row", 1)
    blocks = both_cores.reshape(rows // 2, own, width)
    mixed = blocks[0]
    for n in range(1, rows // 2):
        mixed = mixed + from_peer(blocks[n], "row", 2 * n)
    return mixed


def local(
    hidden,
    queries,
    new_kv,
    prompt_kv,
    suffix_kv,
    lengths,
    w_out,
    moe_gain,
    w_router,
    expert_weights,
    old_lines,
    new_lines,
    routes,
):
    expert_lines = jnp.transpose(expert_weights, (0, 2, 1, 3))
    migration = Migration(expert_lines, old_lines, new_lines)
    migration.send()
    attended = attend(queries, new_kv, prompt_kv, suffix_kv, lengths)
    projected = jnp.dot(attended, w_out, preferred_element_type=jnp.float32)
    h_mid = (hidden.astype(jnp.float32) + projected).astype(jnp.bfloat16)
    (h_mid,) = after([h_mid], migration.packed)
    mixed = experts_part(h_mid, moe_gain, w_router, expert_lines, routes, migration)
    migration.receive(1)
    return (h_mid.astype(jnp.float32) + mixed, jnp.transpose(migration.moved, (0, 2, 1, 3)))


def solution(mesh):
    return jax.shard_map(
        local,
        mesh=mesh,
        in_specs=(
            P("row", "col"),
            P("row", None),
            P("row", None, None),
            P("row", None, "col", None),
            P("row", None, "col", None),
            P("row"),
            P(None, "col"),
            P("col"),
            P("col", None),
            P(None, "row", None, "col"),
            P(),
            P(),
            P(),
        ),
        out_specs=(P("row", "col"), P(None, "row", None, "col")),
        check_vma=False,
    )
```

```python
import functools

import jax
import jax.numpy as jnp
from jax import lax
from jax.experimental import pallas as pl
from jax.experimental.pallas import tpu as pltpu
from jax.sharding import PartitionSpec as P

KVH = 16
HD = 128
REP = 2
TILE = 16
LANES = 128

norm_eps = 1e-06
neg_big = -1e30
VMEM_LIMIT = 48 * 1024 * 1024
PACK_LIMIT = 61 * 1024 * 1024


def up_to(value, unit):
    return -(-value // unit) * unit


def iota(shape, axis):
    return lax.broadcasted_iota(jnp.int32, shape, axis)


def ones_where(mask):
    return jnp.where(mask, 1.0, 0.0).astype(jnp.bfloat16)


def params():
    return pltpu.CompilerParams(vmem_limit_bytes=VMEM_LIMIT)


def counting(shape, axis):
    return iota(shape, axis).astype(jnp.float32).astype(jnp.bfloat16)


def as_bf16(values):
    return values.astype(jnp.float32).astype(jnp.bfloat16)


def equal_ones(left, right):
    one = jnp.ones((), jnp.bfloat16)
    return jnp.maximum(one - jnp.abs(left - right), jnp.zeros((), jnp.bfloat16))


def within(place, block):
    place = place - 256 * block
    return as_bf16(jnp.where((place >= 0) & (place < 256), place, -1))


def look_up(table_row, id_row, numbers, values):
    full = table_row.shape[1]
    ids = id_row.shape[1]
    high_count = up_to(-(-full // 64), 16)
    table_high = equal_ones(numbers[:high_count], as_bf16(table_row >> 6))
    low = as_bf16(table_row & 63)
    zero = jnp.zeros((), jnp.bfloat16)
    table_low = jnp.concatenate(
        [jnp.where(numbers[:64] == low, part, zero) for part in values], axis=0
    )
    square = lax.dot_general(
        table_low, table_high, (((1,), (1,)), ((), ())), preferred_element_type=jnp.float32
    )
    id_high = equal_ones(numbers[:high_count, :ids], as_bf16(id_row >> 6))
    spread = jnp.dot(square.astype(jnp.bfloat16), id_high, preferred_element_type=jnp.float32)
    wanted = iota((64, ids), 0) == (id_row & 63)
    return [
        jnp.sum(jnp.where(wanted, spread[64 * n : 64 * n + 64], 0.0), axis=0, keepdims=True)
        for n in range(len(values))
    ]


def numbers_for(full):
    return counting((max(up_to(-(-full // 64), 16), 64), full), 0)


def segment_plan(counts, experts, rows):
    starts = []
    running = jnp.zeros((rows, LANES), jnp.float32)
    for e in range(experts):
        starts.append(running)
        running = running + counts[e * rows : (e + 1) * rows]
    start = jnp.concatenate(starts, axis=0)
    lead = jnp.floor(start * (1.0 / TILE))
    tail = jnp.floor((start + counts + (TILE - 1.0)) * (1.0 / TILE))
    tiles = jnp.where(counts > 0.0, tail - lead, 0.0)
    pairs = experts * rows
    line = iota((pairs, pairs), 0)
    column = iota((pairs, pairs), 1)
    earlier = ones_where((line // rows == column // rows) & (column < line))
    base = jnp.dot(earlier, tiles.astype(jnp.bfloat16), preferred_element_type=jnp.float32)
    return start, lead, tiles, base


def write_plan(plan_ref, parts):
    for n, part in enumerate(parts):
        short = -part.shape[0] % LANES
        if short:
            part = jnp.concatenate([part, jnp.zeros((short, LANES), jnp.float32)], axis=0)
        plan_ref[n : n + 1, :] = jnp.transpose(part)[:1].astype(jnp.int32)


def outgoing_kernel(lines, rows, new_ref, held_ref, stack_ref, plan_ref):
    experts = new_ref.shape[0]
    width = held_ref.shape[1]
    real = iota((1, width), 1) < lines
    hits = []
    full = new_ref.shape[1]
    numbers = numbers_for(full)
    slot = iota((64, full), 1).astype(jnp.float32)
    values = (jnp.floor((slot + 0.5) * (1.0 / lines)).astype(jnp.bfloat16),)
    for e in range(experts):
        (peer,) = look_up(new_ref[e : e + 1, :], held_ref[e : e + 1, :], numbers, values)
        peer = peer.astype(jnp.int32)
        hits.append(jnp.where((iota((rows, width), 0) == peer) & real, 1.0, 0.0))
    hits = jnp.concatenate(hits, axis=0)
    until = ones_where(iota((width, width), 0) <= iota((width, width), 1))
    ranks = jnp.dot(hits.astype(jnp.bfloat16), until, preferred_element_type=jnp.float32)
    counts = jnp.broadcast_to(jnp.sum(hits, axis=1, keepdims=True), (experts * rows, LANES))
    start, lead, tiles, base = segment_plan(counts, experts, rows)
    write_plan(plan_ref, (lead, tiles, base, start - lead * TILE))
    offset = (base * TILE + start - lead * TILE - 1.0)[:, :1]
    placed = hits * (ranks + offset)
    for e in range(experts):
        row = jnp.sum(placed[e * rows : (e + 1) * rows], axis=0, keepdims=True)
        stack_ref[e] = jnp.where(real, row, -1.0).astype(jnp.int32)


def incoming_kernel(lines, rows, block_tiles, slot, old_ref, wanted_ref, stack_ref, plan_ref):
    experts = old_ref.shape[0]
    width = wanted_ref.shape[1]
    real = iota((1, width), 1) < lines
    held_at = []
    hits = []
    full = old_ref.shape[1]
    numbers = numbers_for(full)
    at = iota((64, full), 1)
    values = (as_bf16(at >> 7), as_bf16(at & 127))
    for e in range(experts):
        high, low = look_up(old_ref[e : e + 1, :], wanted_ref[e : e + 1, :], numbers, values)
        slots = high * 128.0 + low
        held_at.append(jnp.where(real, slots, 1e9))
        peer = jnp.floor((slots + 0.5) * (1.0 / lines)).astype(jnp.int32)
        hits.append(jnp.where((iota((rows, width), 0) == peer) & real, 1.0, 0.0))
    hits = jnp.concatenate(hits, axis=0)
    counts = jnp.broadcast_to(jnp.sum(hits, axis=1, keepdims=True), (experts * rows, LANES))
    start, lead, tiles, base = segment_plan(counts, experts, rows)
    line = iota((experts * rows, LANES), 0)
    peer = (line % rows).astype(jnp.float32)
    longest = [
        jnp.max(tiles[e * rows : (e + 1) * rows], axis=0, keepdims=True) for e in range(experts)
    ]
    longest = jnp.concatenate(
        [jnp.broadcast_to(most, (rows, LANES)) for most in longest], axis=0
    )
    slotted = longest <= slot
    lead = jnp.where(slotted, jnp.minimum(lead, float(block_tiles - slot)), lead)
    base = jnp.where(slotted, peer * slot, base)
    write_plan(plan_ref, (lead, tiles, base, jnp.where(slotted, 1.0, 0.0)))
    blank = jnp.zeros((LANES - experts, width), jnp.float32)
    columns = jnp.transpose(jnp.concatenate(held_at + [blank], axis=0))
    rows_out = []
    for e in range(experts):
        mine = slice(e * rows, (e + 1) * rows)
        before = jnp.where(columns[:, e : e + 1] < held_at[e], 1.0, 0.0)
        rank = jnp.sum(before, axis=0, keepdims=True)
        ahead = jnp.zeros((1, LANES), jnp.float32)
        firsts = []
        for r in range(rows):
            firsts.append(ahead)
            ahead = ahead + counts[e * rows + r : e * rows + r + 1]
        first = jnp.concatenate(firsts, axis=0)
        offset = (base[mine] * TILE + start[mine] - lead[mine] * TILE - first)[:, :1]
        rows_out.append(jnp.sum(hits[mine] * (rank + offset), axis=0, keepdims=True))
    places = jnp.transpose(jnp.concatenate(rows_out + [blank], axis=0))
    for e in range(experts):
        place = jnp.broadcast_to(places[:lines, e : e + 1], (lines, LANES))
        block = jnp.floor(place * (1.0 / 256.0))
        stack_ref[e, 0] = (place - 256.0 * block).astype(jnp.bfloat16)
        stack_ref[e, 1] = block.astype(jnp.bfloat16)


STRAIGHT = 8


def tile_at(index):
    return pl.ds(pl.multiple_of(index * TILE, TILE), TILE)


def pack_kernel(rows, span, plan_ref, place_ref, lines_ref, out_ref, packed_ref, number_ref, sem, *stages):
    part = pl.program_id(0)
    step = pl.program_id(1)
    deep = stages[0].shape[0] - STRAIGHT * TILE
    lines = lines_ref.shape[2]

    @pl.when((part == 0) & (step == 0))
    def _():
        number_ref[...] = counting(number_ref.shape, 0)

    def entry(n, j, d):
        return plan_ref[n, (step * span + j) * rows + d]

    usual = min(deep, up_to(lines + rows * TILE, TILE))

    def move(j, begin, end):
        place = place_ref[j][:, :lines]
        onehot = [
            equal_ones(number_ref[: min(256, end - row)], within(place - begin, (row - begin) // 256))
            for row in range(begin, end, 256)
        ]
        stages[j][begin:end] = jnp.dot(
            jnp.concatenate(onehot, axis=0), lines_ref[j, 0], preferred_element_type=jnp.float32
        ).astype(jnp.bfloat16)

    for j in range(span):
        move(j, 0, usual)
    if usual < deep:
        for j in range(span):
            used = entry(1, j, rows - 1) + entry(2, j, rows - 1)

            @pl.when(used * TILE > usual)
            def _(j=j):
                move(j, usual, deep)

    for j, stage_ref in enumerate(stages):

        def one_peer(d, most, j=j, stage_ref=stage_ref):
            lead, tiles, base = entry(0, j, d), entry(1, j, d), entry(2, j, d)
            there = pl.multiple_of(lead * TILE, TILE)
            here = pl.multiple_of(base * TILE, TILE)
            earlier = packed_ref[d, pl.ds(there, TILE), :]
            fresh = stage_ref[pl.ds(here, STRAIGHT * TILE), :]
            packed_ref[d, pl.ds(there + TILE, (STRAIGHT - 1) * TILE), :] = fresh[TILE:]
            kept = jnp.where(entry(3, j, d) > 0, earlier, jnp.zeros_like(earlier))
            added = jnp.where(tiles > 0, fresh[:TILE], jnp.zeros_like(earlier))
            packed_ref[d, pl.ds(there, TILE), :] = kept + added
            return jnp.maximum(most, tiles)

        most = lax.fori_loop(0, rows, one_peer, 0, unroll=rows <= 8)

        @pl.when(most > STRAIGHT)
        def _(j=j, stage_ref=stage_ref):
            def long_peer(d, carry):
                lead, tiles, base = entry(0, j, d), entry(1, j, d), entry(2, j, d)

                def put(t, c):
                    packed_ref[d, tile_at(lead + t), :] = stage_ref[tile_at(base + t), :]
                    return c

                return lax.fori_loop(STRAIGHT, tiles, put, carry)

            lax.fori_loop(0, rows, long_peer, 0)

    @pl.when(step == pl.num_programs(1) - 1)
    def _():
        full = packed_ref.at[:, pl.ds(0, out_ref.shape[2])]
        copy = pltpu.make_async_copy(full, out_ref.at[:, part], sem)
        copy.start()
        copy.wait()


def unpack_kernel(slot, makes, plan_ref, place_ref, block_ref, *rest):
    stage_ref, sems = rest[-2:]
    out_ref = rest[-4] if makes else rest[-3]
    experts = pl.num_programs(0)
    rows, count, _, width = block_ref.shape
    _, deep, _ = stage_ref.shape
    lines = out_ref.shape[2]
    e = pl.program_id(0)
    buffer = e % 2

    def entry(n, e, s):
        return plan_ref[n, e * rows + s]

    def slotted(e):
        return entry(3, e, 0) > 0

    def columns(part):
        return pl.ds(part * width, width)

    def slot_copies(e):
        for s in range(rows):
            there = pl.ds(pl.multiple_of(entry(0, e, s) * TILE, TILE), slot * TILE)
            here = pl.ds(s * slot * TILE, slot * TILE)
            for part in range(count):
                yield pltpu.make_async_copy(
                    block_ref.at[s, part, there],
                    stage_ref.at[e % 2, here, columns(part)],
                    sems.at[e % 2, s * count + part],
                )

    def begin(e):
        @pl.when(slotted(e))
        def _():
            for copy in slot_copies(e):
                copy.start()

    @pl.when(e == 0)
    def _():
        stage_ref[...] = jnp.zeros_like(stage_ref)
        begin(e)

    @pl.when(e + 1 < experts)
    def _():
        begin(e + 1)

    @pl.when(slotted(e))
    def _():
        for copy in slot_copies(e):
            copy.wait()

    @pl.when(jnp.logical_not(slotted(e)))
    def _():
        def one_peer(s, carry):
            def put(t, c):
                for part in range(count):
                    copy = pltpu.make_async_copy(
                        block_ref.at[s, part, tile_at(entry(0, e, s) + t)],
                        stage_ref.at[buffer, tile_at(entry(2, e, s) + t), columns(part)],
                        sems.at[buffer, part],
                    )
                    copy.start()
                    copy.wait()
                return c

            return lax.fori_loop(0, entry(1, e, s), put, carry)

        lax.fori_loop(0, rows, one_peer, 0)

    if makes:
        onehot_ref = rest[-3]
        within_block, block = place_ref[0, 0], place_ref[0, 1]
        lane = counting((lines, LANES), 1)
        for first in range(0, deep, LANES):
            away = jnp.abs(block - jnp.asarray(first // 256, jnp.bfloat16))
            place = within_block + away * jnp.asarray(512, jnp.bfloat16)
            onehot_ref[0, :, first : first + LANES] = equal_ones(
                lane + jnp.asarray(first % 256, jnp.bfloat16), place
            )
    else:
        onehot_ref = place_ref
    moved = jnp.dot(
        onehot_ref[0], stage_ref[buffer], preferred_element_type=jnp.float32
    ).astype(jnp.bfloat16)
    for part in range(count):
        out_ref[0, part] = moved[:, part * width : (part + 1) * width]


def call_plan(kernel, name, table, ids, pairs, place):
    return pl.pallas_call(
        kernel,
        out_shape=(place, jax.ShapeDtypeStruct((4, up_to(pairs, LANES)), jnp.int32)),
        compiler_params=params(),
        cost_estimate=pl.CostEstimate(
            flops=20 * table.size * 256, bytes_accessed=8 * table.size, transcendentals=0
        ),
        name=name,
    )(table, ids)


def pack(expert_lines, place, plan, piece, rows, block_rows, deep):
    experts, _, lines, width = expert_lines.shape
    first, count = piece
    span = 2 - experts % 2
    return pl.pallas_call(
        functools.partial(pack_kernel, rows, span),
        grid_spec=pltpu.PrefetchScalarGridSpec(
            num_scalar_prefetch=1,
            grid=(count, experts // span),
            in_specs=[
                pl.BlockSpec((span, 1, place.shape[2]), lambda p, e, plan: (e, 0, 0)),
                pl.BlockSpec((span, 1, lines, width), lambda p, e, plan: (e, first + p, 0, 0)),
            ],
            out_specs=pl.BlockSpec(memory_space=pltpu.HBM),
            scratch_shapes=[
                pltpu.VMEM((rows, block_rows + STRAIGHT * TILE, width), jnp.bfloat16),
                pltpu.VMEM((256, lines), jnp.bfloat16),
                pltpu.SemaphoreType.DMA(()),
            ]
            + [pltpu.VMEM((deep + STRAIGHT * TILE, width), jnp.bfloat16)] * span,
        ),
        out_shape=jax.ShapeDtypeStruct((rows, count, block_rows, width), jnp.bfloat16),
        compiler_params=pltpu.CompilerParams(vmem_limit_bytes=PACK_LIMIT),
        cost_estimate=pl.CostEstimate(
            flops=2 * count * experts * deep * lines * width,
            bytes_accessed=4 * count * experts * lines * width,
            transcendentals=0,
        ),
        name="pack_lines",
    )(plan, place, expert_lines)


def unpack(arrived, place, plan, piece, shape, deep, slot, previous):
    experts, _, lines, width = shape
    first, count = piece
    rows = arrived.shape[0]
    makes = previous is None
    onehot_spec = pl.BlockSpec((1, lines, deep), lambda e, plan: (e, 0, 0))
    place_spec = pl.BlockSpec((1, 2, lines, LANES), lambda e, plan: (e, 0, 0, 0))
    in_specs = [
        place_spec if makes else onehot_spec,
        pl.BlockSpec(memory_space=pl.ANY),
    ]
    operands = [plan, place, arrived]
    aliases = {}
    if previous is not None:
        in_specs.append(pl.BlockSpec(memory_space=pl.ANY))
        operands.append(previous)
        aliases = {3: 0}
    return pl.pallas_call(
        functools.partial(unpack_kernel, slot, makes),
        grid_spec=pltpu.PrefetchScalarGridSpec(
            num_scalar_prefetch=1,
            grid=(experts,),
            in_specs=in_specs,
            out_specs=[
                pl.BlockSpec((1, count, lines, width), lambda e, plan: (e, first // count, 0, 0))
            ]
            + [onehot_spec] * makes,
            scratch_shapes=[
                pltpu.VMEM((2, deep, count * width), jnp.bfloat16),
                pltpu.SemaphoreType.DMA((2, rows * count)),
            ],
        ),
        out_shape=[jax.ShapeDtypeStruct(shape, jnp.bfloat16)]
        + [jax.ShapeDtypeStruct((experts, lines, deep), jnp.bfloat16)] * makes,
        input_output_aliases=aliases,
        compiler_params=params(),
        cost_estimate=pl.CostEstimate(
            flops=2 * count * experts * deep * lines * width,
            bytes_accessed=4 * count * experts * lines * width,
            transcendentals=0,
        ),
        name="unpack_lines",
    )(*operands)


def after_kernel(*refs):
    del refs


def after(values, signals):
    anywhere = pl.BlockSpec(memory_space=pl.ANY)
    return pl.pallas_call(
        after_kernel,
        in_specs=[anywhere] * (len(values) + len(signals)),
        out_specs=[anywhere] * len(values),
        out_shape=[jax.ShapeDtypeStruct(v.shape, v.dtype) for v in values],
        input_output_aliases={n: n for n in range(len(values))},
        compiler_params=pltpu.CompilerParams(vmem_limit_bytes=PACK_LIMIT),
        name="after",
    )(*values, *signals)


def own_ids(table, lines, width):
    mine = lax.dynamic_slice_in_dim(table, lax.axis_index("row") * lines, lines, 1)
    return jnp.pad(mine, ((0, 0), (0, width - lines)), constant_values=-1)


def from_peer(block, axis, offset):
    size = lax.axis_size(axis)
    return lax.ppermute(block, axis, [(i, i ^ offset) for i in range(size)])


class Migration:
    def __init__(self, expert_lines, old_lines, new_lines):
        rows = lax.axis_size("row")
        experts, parts, lines, width = expert_lines.shape
        padded = up_to(lines, LANES)
        block_rows = up_to(experts * lines // rows, TILE)
        pairs = experts * rows
        compact = up_to(lines + 2 * (TILE - 1) * rows, TILE)
        self.slot = min(STRAIGHT, block_rows // TILE)
        self.deep = up_to(max(compact, rows * self.slot * TILE), 256)
        self.shape = expert_lines.shape
        self.pieces = [(parts - 1, 1), (0, parts - 1)]
        out_place, out_plan = call_plan(
            functools.partial(outgoing_kernel, lines, rows), "outgoing_plan",
            new_lines, own_ids(old_lines, lines, padded), pairs,
            jax.ShapeDtypeStruct((experts, 1, padded), jnp.int32),
        )
        self.in_place, self.in_plan = call_plan(
            functools.partial(incoming_kernel, lines, rows, block_rows // TILE, self.slot),
            "incoming_plan",
            old_lines, own_ids(new_lines, lines, padded), pairs,
            jax.ShapeDtypeStruct((experts, 2, lines, LANES), jnp.bfloat16),
        )
        self.packed = [
            pack(expert_lines, out_place, out_plan, piece, rows, block_rows, compact)
            for piece in self.pieces
        ]
        self.arrived = []
        self.moved = None

    def send(self, signals=()):
        block = self.packed[len(self.arrived)]
        if signals:
            (block,) = after([block], signals)
        self.arrived.append(
            lax.all_to_all(block, "row", split_axis=0, concat_axis=0, tiled=True)
        )

    def receive(self, piece):
        self.moved, *onehots = unpack(
            self.arrived[piece], self.in_place, self.in_plan, self.pieces[piece], self.shape,
            self.deep, self.slot, self.moved,
        )
        if onehots:
            (self.in_place,) = onehots


def attend(queries, new_kv, prompt_kv, suffix_kv, lengths):
    seq_count = queries.shape[0]
    prompt_rows = prompt_kv.shape[2]
    suffix_rows = suffix_kv.shape[2]
    col_index = lax.axis_index("col")
    query_heads = queries.reshape(seq_count, KVH, REP, HD)
    prompt_keys = prompt_kv[0, 0].reshape(prompt_rows, KVH, HD)
    prompt_values = prompt_kv[0, 1].reshape(prompt_rows, KVH, HD)
    suffix_keys = suffix_kv[:, 0].reshape(seq_count, suffix_rows, KVH, HD)
    suffix_values = suffix_kv[:, 1].reshape(seq_count, suffix_rows, KVH, HD)
    own_keys = new_kv[:, 0].reshape(seq_count, KVH, HD)
    own_values = new_kv[:, 1].reshape(seq_count, KVH, HD)
    score_scale = HD ** (-0.5)
    prompt_scores = (
        jnp.einsum("skgd,pkd->skgp", query_heads, prompt_keys, preferred_element_type=jnp.float32)
        * score_scale
    )
    suffix_scores = (
        jnp.einsum("skgd,spkd->skgp", query_heads, suffix_keys, preferred_element_type=jnp.float32)
        * score_scale
    )
    own_scores = (
        jnp.einsum("skgd,skd->skg", query_heads, own_keys, preferred_element_type=jnp.float32)
        * score_scale
    )
    positions = col_index * suffix_rows + jnp.arange(suffix_rows, dtype=jnp.int32)
    live_slots = (positions[None, :] < lengths[:, None])[:, None, None, :]
    holder = col_index == 0
    suffix_scores = jnp.where(live_slots, suffix_scores, neg_big)
    own_scores = jnp.where(holder, own_scores, neg_big)
    highest = jnp.maximum(
        jnp.maximum(jnp.max(prompt_scores, axis=-1), jnp.max(suffix_scores, axis=-1)), own_scores
    )
    prompt_weights = jnp.exp(prompt_scores - highest[..., None])
    suffix_weights = jnp.where(live_slots, jnp.exp(suffix_scores - highest[..., None]), 0.0)
    own_weights = jnp.where(holder, jnp.exp(own_scores - highest), 0.0)
    totals = jnp.sum(prompt_weights, axis=-1) + jnp.sum(suffix_weights, axis=-1) + own_weights
    mixture = jnp.einsum(
        "skgp,pkd->skgd",
        prompt_weights.astype(jnp.bfloat16),
        prompt_values,
        preferred_element_type=jnp.float32,
    )
    mixture = mixture + jnp.einsum(
        "skgp,spkd->skgd",
        suffix_weights.astype(jnp.bfloat16),
        suffix_values,
        preferred_element_type=jnp.float32,
    )
    own_rounded = lax.optimization_barrier(own_weights.astype(jnp.bfloat16)).astype(jnp.float32)
    mixture = mixture + own_rounded[..., None] * own_values.astype(jnp.float32)[:, :, None, :]
    heads = KVH * REP
    bundle = jnp.concatenate(
        [
            mixture.reshape(seq_count, heads * HD),
            highest.reshape(seq_count, heads),
            totals.reshape(seq_count, heads),
            jnp.zeros((seq_count, LANES - 2 * heads), jnp.float32),
        ],
        axis=1,
    )
    bundles = [bundle] + [from_peer(bundle, "col", o) for o in range(1, lax.axis_size("col"))]
    every = jnp.stack(bundles)
    mixtures = every[:, :, : heads * HD].reshape(-1, seq_count, heads, HD)
    peaks = every[:, :, heads * HD : heads * HD + heads]
    sums = every[:, :, heads * HD + heads : heads * HD + 2 * heads]
    factors = jnp.exp(peaks - jnp.max(peaks, axis=0))
    total = jnp.sum(sums * factors, axis=0)
    mixed = jnp.sum(mixtures * factors[..., None], axis=0)
    return (mixed / total[..., None]).astype(jnp.bfloat16).reshape(seq_count, heads * HD)


def gate_up_kernel(me_ref, h_ref, gain_ref, router_ref, routes_ref, gate_ref, up_ref, out_ref, acc_ref):
    e = pl.program_id(0)
    tokens = h_ref.shape[0]
    lines = gate_ref.shape[2]
    padded = out_ref.shape[3]
    h = h_ref[...].astype(jnp.float32)
    scaled = (h * gain_ref[...].astype(jnp.float32)).astype(jnp.bfloat16)

    @pl.when(e == 0)
    def _():
        acc_ref[...] = jnp.zeros_like(acc_ref)

    against = (((1,), (1,)), ((), ()))
    gate = lax.dot_general(scaled, gate_ref[0, 0], against, preferred_element_type=jnp.float32)
    up = lax.dot_general(scaled, up_ref[0, 0], against, preferred_element_type=jnp.float32)
    for k in range(routes_ref.shape[1]):
        chosen = routes_ref[:, k : k + 1] == e
        acc_ref[2 * k, :, :lines] += jnp.where(chosen, gate, 0.0)
        acc_ref[2 * k + 1, :, :lines] += jnp.where(chosen, up, 0.0)

    @pl.when(e == pl.num_programs(0) - 1)
    def _():
        last = padded - LANES
        shift = lines - last
        experts = pl.num_programs(0)
        extra = jnp.dot(scaled, router_ref[...], preferred_element_type=jnp.float32)
        lane = iota((tokens, LANES), 1)
        square = jnp.sum(h * h, axis=1, keepdims=True)
        extra = jnp.where(lane == shift + experts, square, extra)
        high = extra.astype(jnp.bfloat16).astype(jnp.float32)
        low = extra - high
        acc_ref[0, :, last:] += jnp.where(lane >= shift, high, 0.0)
        acc_ref[1, :, last:] += jnp.where(lane >= shift, low, 0.0)
        peers, _, share, _ = out_ref.shape
        me = me_ref[0]
        for o in range(peers):
            begin = pl.multiple_of((me ^ o) * share, share)
            out_ref[o] = acc_ref[:, pl.ds(begin, share), :].astype(jnp.bfloat16)


def activate_kernel(lines, experts, model_width, routes_ref, *refs):
    out_ref = refs[-1]
    summed = refs[0][...].astype(jnp.float32)
    for ref in refs[1:-1]:
        summed = summed + ref[...].astype(jnp.float32)
    _, share, padded = summed.shape
    last = padded - LANES
    shift = lines - last
    extra = summed[0, :, last:] + summed[1, :, last:]
    lane = iota((share, LANES), 1)
    square = jnp.sum(jnp.where(lane == shift + experts, extra, 0.0), axis=1, keepdims=True)
    inverse_rms = lax.rsqrt(square / model_width + norm_eps)
    logits = []
    for k in range(out_ref.shape[0]):
        wanted = lane == routes_ref[:, k : k + 1] + shift
        logits.append(jnp.sum(jnp.where(wanted, extra, 0.0), axis=1, keepdims=True) * inverse_rms)
    peak = functools.reduce(jnp.maximum, logits)
    shares = [jnp.exp(v - peak) for v in logits]
    total = functools.reduce(jnp.add, shares)
    inside = iota((share, padded), 1) < lines
    for k in range(out_ref.shape[0]):
        gate = summed[2 * k] * inverse_rms
        up = summed[2 * k + 1] * inverse_rms
        act = gate / (1.0 + jnp.exp(-gate)) * up
        out_ref[k] = jnp.where(inside, act * (shares[k] / total), 0.0).astype(jnp.bfloat16)


def down_kernel(me_ref, routes_ref, *refs):
    down_ref, out_ref, act_ref = refs[-3:]
    chunks = refs[:-3]
    e = pl.program_id(0)
    topk, share, _ = chunks[0].shape
    lines = down_ref.shape[2]

    @pl.when(e == 0)
    def _():
        me = me_ref[0]
        out_ref[...] = jnp.zeros_like(out_ref)
        for o, chunk in enumerate(chunks):
            begin = pl.multiple_of((me ^ o) * share, share)
            act_ref[:, pl.ds(begin, share), :] = chunk[...]

    mine = jnp.zeros((act_ref.shape[1], lines), jnp.float32)
    for k in range(topk):
        chosen = routes_ref[:, k : k + 1] == e
        mine = mine + jnp.where(chosen, act_ref[k, :, :lines].astype(jnp.float32), 0.0)
    out_ref[...] += jnp.dot(
        mine.astype(jnp.bfloat16), down_ref[0, 0], preferred_element_type=jnp.float32
    )


def experts_part(h_mid, moe_gain, w_router, expert_lines, routes, migration):
    rows = lax.axis_size("row")
    cols = lax.axis_size("col")
    row_index = lax.axis_index("row")
    col_index = lax.axis_index("col")
    experts, _, lines, width = expert_lines.shape
    own, _ = h_mid.shape
    tokens = own * rows
    topk = routes.shape[1]
    share = tokens // cols
    padded = up_to(lines + experts + 1, LANES)
    shift = lines - (padded - LANES)
    me = col_index.astype(jnp.int32).reshape(1)

    order = row_index ^ jnp.array(sorted(range(rows), key=lambda o: (o % 2, o)), jnp.int32)
    routes = routes.reshape(rows, own, topk)[order].reshape(tokens, topk)
    my_routes = lax.dynamic_slice_in_dim(routes, col_index * share, share, 0)
    router = jnp.pad(w_router, ((0, 0), (shift, LANES - shift - experts)))
    same_core = jnp.concatenate(
        [h_mid] + [from_peer(h_mid, "row", o) for o in range(2, rows, 2)], axis=0
    )
    every_h = jnp.concatenate([same_core, from_peer(same_core, "row", 1)], axis=0)
    migration.send([every_h])
    part_spec = lambda part: pl.BlockSpec((1, 1, lines, width), lambda e, me: (e, part, 0, 0))
    whole = lambda a: pl.BlockSpec(a.shape, lambda e, me: (0,) * a.ndim)
    gain = moe_gain.reshape(1, width)
    partial = pl.pallas_call(
        gate_up_kernel,
        grid_spec=pltpu.PrefetchScalarGridSpec(
            num_scalar_prefetch=1,
            grid=(experts,),
            in_specs=[whole(every_h), whole(gain), whole(router), whole(routes)]
            + [part_spec(0), part_spec(1)],
            out_specs=pl.BlockSpec((cols, 2 * topk, share, padded), lambda e, me: (0, 0, 0, 0)),
            scratch_shapes=[pltpu.VMEM((2 * topk, tokens, padded), jnp.float32)],
        ),
        out_shape=jax.ShapeDtypeStruct((cols, 2 * topk, share, padded), jnp.bfloat16),
        compiler_params=params(),
        cost_estimate=pl.CostEstimate(
            flops=4 * experts * tokens * lines * width,
            bytes_accessed=4 * experts * lines * width,
            transcendentals=0,
        ),
        name="gate_up",
    )(me, every_h, gain, router, routes, expert_lines, expert_lines)
    gathered = [partial[0]] + [from_peer(partial[o], "col", o) for o in range(1, cols)]
    activated = pl.pallas_call(
        functools.partial(activate_kernel, lines, experts, width * cols),
        out_shape=jax.ShapeDtypeStruct((topk, share, padded), jnp.bfloat16),
        compiler_params=params(),
        name="activate",
    )(my_routes, *gathered)
    chunks = [activated] + [from_peer(activated, "col", o) for o in range(1, cols)]
    produced = pl.pallas_call(
        down_kernel,
        grid_spec=pltpu.PrefetchScalarGridSpec(
            num_scalar_prefetch=1,
            grid=(experts,),
            in_specs=[whole(routes)] + [whole(c) for c in chunks] + [part_spec(2)],
            out_specs=pl.BlockSpec((tokens, width), lambda e, me: (0, 0)),
            scratch_shapes=[pltpu.VMEM((topk, tokens, padded), jnp.bfloat16)],
        ),
        out_shape=jax.ShapeDtypeStruct((tokens, width), jnp.float32),
        compiler_params=params(),
        cost_estimate=pl.CostEstimate(
            flops=2 * experts * tokens * lines * width,
            bytes_accessed=2 * experts * lines * width,
            transcendentals=0,
        ),
        name="down",
    )(me, routes, *chunks, expert_lines)
    migration.receive(0)
    (produced,) = after([produced], [migration.moved])
    half = tokens // 2
    both_cores = produced[:half] + from_peer(produced[half:], "row", 1)
    blocks = both_cores.reshape(rows // 2, own, width)
    mixed = blocks[0]
    for n in range(1, rows // 2):
        mixed = mixed + from_peer(blocks[n], "row", 2 * n)
    return mixed


def local(
    hidden,
    queries,
    new_kv,
    prompt_kv,
    suffix_kv,
    lengths,
    w_out,
    moe_gain,
    w_router,
    expert_weights,
    old_lines,
    new_lines,
    routes,
):
    expert_lines = jnp.transpose(expert_weights, (0, 2, 1, 3))
    migration = Migration(expert_lines, old_lines, new_lines)
    migration.send()
    attended = attend(queries, new_kv, prompt_kv, suffix_kv, lengths)
    projected = jnp.dot(attended, w_out, preferred_element_type=jnp.float32)
    h_mid = (hidden.astype(jnp.float32) + projected).astype(jnp.bfloat16)
    (h_mid,) = after([h_mid], migration.packed)
    mixed = experts_part(h_mid, moe_gain, w_router, expert_lines, routes, migration)
    migration.receive(1)
    return (h_mid.astype(jnp.float32) + mixed, jnp.transpose(migration.moved, (0, 2, 1, 3)))


def solution(mesh):
    return jax.shard_map(
        local,
        mesh=mesh,
        in_specs=(
            P("row", "col"),
            P("row", None),
            P("row", None, None),
            P("row", None, "col", None),
            P("row", None, "col", None),
            P("row"),
            P(None, "col"),
            P("col"),
            P("col", None),
            P(None, "row", None, "col"),
            P(),
            P(),
            P(),
        ),
        out_specs=(P("row", "col"), P(None, "row", None, "col")),
        check_vma=False,
    )
```

```python
import functools

import jax
import jax.numpy as jnp
from jax import lax
from jax.experimental import pallas as pl
from jax.experimental.pallas import tpu as pltpu
from jax.sharding import PartitionSpec as P

KVH = 16
HD = 128
REP = 2
TILE = 16
LANES = 128

norm_eps = 1e-06
neg_big = -1e30
VMEM_LIMIT = 48 * 1024 * 1024
PACK_LIMIT = 61 * 1024 * 1024
UNPACK_LIMIT = 24 * 1024 * 1024


def up_to(value, unit):
    return -(-value // unit) * unit


def iota(shape, axis):
    return lax.broadcasted_iota(jnp.int32, shape, axis)


def ones_where(mask):
    return jnp.where(mask, 1.0, 0.0).astype(jnp.bfloat16)


def params():
    return pltpu.CompilerParams(vmem_limit_bytes=VMEM_LIMIT)


def counting(shape, axis):
    return iota(shape, axis).astype(jnp.float32).astype(jnp.bfloat16)


def as_bf16(values):
    return values.astype(jnp.float32).astype(jnp.bfloat16)


def equal_ones(left, right):
    one = jnp.ones((), jnp.bfloat16)
    return jnp.maximum(one - jnp.abs(left - right), jnp.zeros((), jnp.bfloat16))


def within(place, block):
    place = place - 256 * block
    return as_bf16(jnp.where((place >= 0) & (place < 256), place, -1))


def look_up(table_rows, id_rows, numbers, values):
    full = table_rows[0].shape[1]
    ids = id_rows[0].shape[1]
    high_count = up_to(-(-full // 64), 16)
    zero = jnp.zeros((), jnp.bfloat16)
    highs = [equal_ones(numbers[:high_count], as_bf16(row >> 6)) for row in table_rows]
    lows = []
    for row in table_rows:
        hit = numbers[:64] == as_bf16(row & 63)
        lows += [jnp.where(hit, part, zero) for part in values]
    square = lax.dot_general(
        jnp.concatenate(highs, axis=0),
        jnp.concatenate(lows, axis=0),
        (((1,), (1,)), ((), ())),
        preferred_element_type=jnp.float32,
    )
    wide = 64 * len(values)
    found = []
    for n, row in enumerate(id_rows):
        block = square[n * high_count : (n + 1) * high_count, n * wide : (n + 1) * wide]
        id_high = equal_ones(numbers[:high_count, :ids], as_bf16(row >> 6))
        spread = lax.dot_general(
            block.astype(jnp.bfloat16), id_high, (((0,), (0,)), ((), ())),
            preferred_element_type=jnp.float32,
        )
        wanted = iota((64, ids), 0) == (row & 63)
        found.append(
            [
                jnp.sum(jnp.where(wanted, spread[64 * m : 64 * m + 64], 0.0), axis=0, keepdims=True)
                for m in range(len(values))
            ]
        )
    return found


def look_up_all(table_ref, id_ref, numbers, values):
    experts = table_ref.shape[0]
    group = 4 // len(values)
    found = []
    for first in range(0, experts, group):
        members = range(first, min(first + group, experts))
        found += look_up(
            [table_ref[e : e + 1, :] for e in members],
            [id_ref[e : e + 1, :] for e in members],
            numbers,
            values,
        )
    return found


def numbers_for(full):
    return counting((max(up_to(-(-full // 64), 16), 64), full), 0)


def segment_plan(counts, experts, rows):
    starts = []
    running = jnp.zeros((rows, LANES), jnp.float32)
    for e in range(experts):
        starts.append(running)
        running = running + counts[e * rows : (e + 1) * rows]
    start = jnp.concatenate(starts, axis=0)
    lead = jnp.floor(start * (1.0 / TILE))
    tail = jnp.floor((start + counts + (TILE - 1.0)) * (1.0 / TILE))
    tiles = jnp.where(counts > 0.0, tail - lead, 0.0)
    pairs = experts * rows
    line = iota((pairs, pairs), 0)
    column = iota((pairs, pairs), 1)
    earlier = ones_where((line // rows == column // rows) & (column < line))
    base = jnp.dot(earlier, tiles.astype(jnp.bfloat16), preferred_element_type=jnp.float32)
    return start, lead, tiles, base


def write_plan(plan_ref, parts):
    for n, part in enumerate(parts):
        short = -part.shape[0] % LANES
        if short:
            part = jnp.concatenate([part, jnp.zeros((short, LANES), jnp.float32)], axis=0)
        plan_ref[n : n + 1, :] = jnp.transpose(part)[:1].astype(jnp.int32)


def outgoing_kernel(lines, rows, new_ref, held_ref, stack_ref, plan_ref):
    experts = new_ref.shape[0]
    width = held_ref.shape[1]
    real = iota((1, width), 1) < lines
    hits = []
    full = new_ref.shape[1]
    numbers = numbers_for(full)
    slot = iota((64, full), 1).astype(jnp.float32)
    values = (jnp.floor((slot + 0.5) * (1.0 / lines)).astype(jnp.bfloat16),)
    for (peer,) in look_up_all(new_ref, held_ref, numbers, values):
        peer = peer.astype(jnp.int32)
        hits.append(jnp.where((iota((rows, width), 0) == peer) & real, 1.0, 0.0))
    hits = jnp.concatenate(hits, axis=0)
    until = ones_where(iota((width, width), 0) <= iota((width, width), 1))
    ranks = jnp.dot(hits.astype(jnp.bfloat16), until, preferred_element_type=jnp.float32)
    counts = jnp.broadcast_to(jnp.sum(hits, axis=1, keepdims=True), (experts * rows, LANES))
    start, lead, tiles, base = segment_plan(counts, experts, rows)
    write_plan(plan_ref, (lead, tiles, base, start - lead * TILE))
    offset = (base * TILE + start - lead * TILE - 1.0)[:, :1]
    placed = hits * (ranks + offset)
    for e in range(experts):
        row = jnp.sum(placed[e * rows : (e + 1) * rows], axis=0, keepdims=True)
        stack_ref[e] = jnp.where(real, row, -1.0).astype(jnp.int32)


def incoming_kernel(lines, rows, block_tiles, slot, old_ref, wanted_ref, stack_ref, plan_ref):
    experts = old_ref.shape[0]
    width = wanted_ref.shape[1]
    real = iota((1, width), 1) < lines
    held_at = []
    hits = []
    full = old_ref.shape[1]
    numbers = numbers_for(full)
    at = iota((64, full), 1)
    values = (as_bf16(at >> 7), as_bf16(at & 127))
    for high, low in look_up_all(old_ref, wanted_ref, numbers, values):
        slots = high * 128.0 + low
        held_at.append(jnp.where(real, slots, 1e9))
        peer = jnp.floor((slots + 0.5) * (1.0 / lines)).astype(jnp.int32)
        hits.append(jnp.where((iota((rows, width), 0) == peer) & real, 1.0, 0.0))
    hits = jnp.concatenate(hits, axis=0)
    counts = jnp.broadcast_to(jnp.sum(hits, axis=1, keepdims=True), (experts * rows, LANES))
    start, lead, tiles, base = segment_plan(counts, experts, rows)
    line = iota((experts * rows, LANES), 0)
    peer = (line % rows).astype(jnp.float32)
    longest = [
        jnp.max(tiles[e * rows : (e + 1) * rows], axis=0, keepdims=True) for e in range(experts)
    ]
    longest = jnp.concatenate(
        [jnp.broadcast_to(most, (rows, LANES)) for most in longest], axis=0
    )
    slotted = longest <= slot
    lead = jnp.where(slotted, jnp.minimum(lead, float(block_tiles - slot)), lead)
    base = jnp.where(slotted, peer * slot, base)
    write_plan(plan_ref, (lead, tiles, base, jnp.where(slotted, 1.0, 0.0)))
    blank = jnp.zeros((LANES - experts, width), jnp.float32)
    columns = jnp.transpose(jnp.concatenate(held_at + [blank], axis=0))
    rows_out = []
    for e in range(experts):
        mine = slice(e * rows, (e + 1) * rows)
        before = jnp.where(columns[:, e : e + 1] < held_at[e], 1.0, 0.0)
        rank = jnp.sum(before, axis=0, keepdims=True)
        ahead = jnp.zeros((1, LANES), jnp.float32)
        firsts = []
        for r in range(rows):
            firsts.append(ahead)
            ahead = ahead + counts[e * rows + r : e * rows + r + 1]
        first = jnp.concatenate(firsts, axis=0)
        offset = (base[mine] * TILE + start[mine] - lead[mine] * TILE - first)[:, :1]
        rows_out.append(jnp.sum(hits[mine] * (rank + offset), axis=0, keepdims=True))
    places = jnp.transpose(jnp.concatenate(rows_out + [blank], axis=0))
    for e in range(experts):
        place = jnp.broadcast_to(places[:lines, e : e + 1], (lines, LANES))
        block = jnp.floor(place * (1.0 / 256.0))
        stack_ref[e, 0] = (place - 256.0 * block).astype(jnp.bfloat16)
        stack_ref[e, 1] = block.astype(jnp.bfloat16)


STRAIGHT = 8
SLOT = 7


def tile_at(index):
    return pl.ds(pl.multiple_of(index * TILE, TILE), TILE)


def pack_kernel(rows, span, plan_ref, place_ref, lines_ref, out_ref, packed_ref, number_ref, sems, *stages):
    part = pl.program_id(0)
    step = pl.program_id(1)
    deep = stages[0].shape[0] - STRAIGHT * TILE
    lines = lines_ref.shape[2]

    @pl.when((part == 0) & (step == 0))
    def _():
        number_ref[...] = counting(number_ref.shape, 0)

    def entry(n, j, d):
        return plan_ref[n, (step * span + j) * rows + d]

    usual = min(deep, up_to(lines + rows * TILE, TILE))

    def move(j, begin, end):
        place = place_ref[j][:, :lines]
        onehot = [
            equal_ones(number_ref[: min(256, end - row)], within(place - begin, (row - begin) // 256))
            for row in range(begin, end, 256)
        ]
        stages[j][begin:end] = jnp.dot(
            jnp.concatenate(onehot, axis=0), lines_ref[j, 0], preferred_element_type=jnp.float32
        ).astype(jnp.bfloat16)

    for j in range(span):
        move(j, 0, usual)
    if usual < deep:
        for j in range(span):
            used = entry(1, j, rows - 1) + entry(2, j, rows - 1)

            @pl.when(used * TILE > usual)
            def _(j=j):
                move(j, usual, deep)

    for j, stage_ref in enumerate(stages):

        def one_peer(d, most, j=j, stage_ref=stage_ref):
            lead, tiles, base = entry(0, j, d), entry(1, j, d), entry(2, j, d)
            there = pl.multiple_of(lead * TILE, TILE)
            here = pl.multiple_of(base * TILE, TILE)
            earlier = packed_ref[d, pl.ds(there, TILE), :]
            fresh = stage_ref[pl.ds(here, STRAIGHT * TILE), :]
            packed_ref[d, pl.ds(there + TILE, (STRAIGHT - 1) * TILE), :] = fresh[TILE:]
            kept = jnp.where(entry(3, j, d) > 0, earlier, jnp.zeros_like(earlier))
            added = jnp.where(tiles > 0, fresh[:TILE], jnp.zeros_like(earlier))
            packed_ref[d, pl.ds(there, TILE), :] = kept + added
            return jnp.maximum(most, tiles)

        most = lax.fori_loop(0, rows, one_peer, 0, unroll=rows <= 8)

        @pl.when(most > STRAIGHT)
        def _(j=j, stage_ref=stage_ref):
            def long_peer(d, carry):
                lead, tiles, base = entry(0, j, d), entry(1, j, d), entry(2, j, d)

                def put(t, c):
                    packed_ref[d, tile_at(lead + t), :] = stage_ref[tile_at(base + t), :]
                    return c

                return lax.fori_loop(STRAIGHT, tiles, put, carry)

            lax.fori_loop(0, rows, long_peer, 0)

    @pl.when(step == pl.num_programs(1) - 1)
    def _():
        copies = [
            pltpu.make_async_copy(
                packed_ref.at[d, pl.ds(0, out_ref.shape[2])], out_ref.at[d, part], sems.at[d]
            )
            for d in range(rows)
        ]
        for copy in copies:
            copy.start()
        for copy in copies:
            copy.wait()


def unpack_kernel(slot, makes, plan_ref, place_ref, block_ref, *rest):
    stage_ref, sems = rest[-2:]
    out_ref = rest[-4] if makes else rest[-3]
    experts = pl.num_programs(0)
    rows, count, _, width = block_ref.shape
    _, deep, _ = stage_ref.shape
    lines = out_ref.shape[2]
    e = pl.program_id(0)
    buffer = e % 2

    def entry(n, e, s):
        return plan_ref[n, e * rows + s]

    def slotted(e):
        return entry(3, e, 0) > 0

    def columns(part):
        return pl.ds(part * width, width)

    def slot_copies(e):
        for s in range(rows):
            there = pl.ds(pl.multiple_of(entry(0, e, s) * TILE, TILE), slot * TILE)
            here = pl.ds(s * slot * TILE, slot * TILE)
            for part in range(count):
                yield pltpu.make_async_copy(
                    block_ref.at[s, part, there],
                    stage_ref.at[e % 2, here, columns(part)],
                    sems.at[e % 2, s * count + part],
                )

    def begin(e):
        @pl.when(slotted(e))
        def _():
            for copy in slot_copies(e):
                copy.start()

    @pl.when(e == 0)
    def _():
        stage_ref[...] = jnp.zeros_like(stage_ref)
        begin(e)

    @pl.when(e + 1 < experts)
    def _():
        begin(e + 1)

    @pl.when(slotted(e))
    def _():
        for copy in slot_copies(e):
            copy.wait()

    @pl.when(jnp.logical_not(slotted(e)))
    def _():
        def one_peer(s, carry):
            def put(t, c):
                for part in range(count):
                    copy = pltpu.make_async_copy(
                        block_ref.at[s, part, tile_at(entry(0, e, s) + t)],
                        stage_ref.at[buffer, tile_at(entry(2, e, s) + t), columns(part)],
                        sems.at[buffer, part],
                    )
                    copy.start()
                    copy.wait()
                return c

            return lax.fori_loop(0, entry(1, e, s), put, carry)

        lax.fori_loop(0, rows, one_peer, 0)

    if makes:
        onehot_ref = rest[-3]
        within_block, block = place_ref[0, 0], place_ref[0, 1]
        lane = counting((lines, LANES), 1)
        for first in range(0, deep, LANES):
            away = jnp.abs(block - jnp.asarray(first // 256, jnp.bfloat16))
            place = within_block + away * jnp.asarray(512, jnp.bfloat16)
            onehot_ref[0, :, first : first + LANES] = equal_ones(
                lane + jnp.asarray(first % 256, jnp.bfloat16), place
            )
    else:
        onehot_ref = place_ref
    moved = jnp.dot(
        onehot_ref[0], stage_ref[buffer], preferred_element_type=jnp.float32
    ).astype(jnp.bfloat16)
    for part in range(count):
        out_ref[0, part] = moved[:, part * width : (part + 1) * width]


def call_plan(kernel, name, table, ids, pairs, place):
    return pl.pallas_call(
        kernel,
        out_shape=(place, jax.ShapeDtypeStruct((4, up_to(pairs, LANES)), jnp.int32)),
        compiler_params=params(),
        cost_estimate=pl.CostEstimate(
            flops=20 * table.size * 256, bytes_accessed=8 * table.size, transcendentals=0
        ),
        name=name,
    )(table, ids)


def pack(expert_lines, place, plan, piece, rows, block_rows, deep):
    experts, _, lines, width = expert_lines.shape
    first, count = piece
    span = 2 - experts % 2
    return pl.pallas_call(
        functools.partial(pack_kernel, rows, span),
        grid_spec=pltpu.PrefetchScalarGridSpec(
            num_scalar_prefetch=1,
            grid=(count, experts // span),
            in_specs=[
                pl.BlockSpec((span, 1, place.shape[2]), lambda p, e, plan: (e, 0, 0)),
                pl.BlockSpec((span, 1, lines, width), lambda p, e, plan: (e, first + p, 0, 0)),
            ],
            out_specs=pl.BlockSpec(memory_space=pltpu.HBM),
            scratch_shapes=[
                pltpu.VMEM((rows, block_rows + STRAIGHT * TILE, width), jnp.bfloat16),
                pltpu.VMEM((256, lines), jnp.bfloat16),
                pltpu.SemaphoreType.DMA((rows,)),
            ]
            + [pltpu.VMEM((deep + STRAIGHT * TILE, width), jnp.bfloat16)] * span,
        ),
        out_shape=jax.ShapeDtypeStruct((rows, count, block_rows, width), jnp.bfloat16),
        compiler_params=pltpu.CompilerParams(vmem_limit_bytes=PACK_LIMIT),
        cost_estimate=pl.CostEstimate(
            flops=2 * count * experts * deep * lines * width,
            bytes_accessed=4 * count * experts * lines * width,
            transcendentals=0,
        ),
        name="pack_lines",
    )(plan, place, expert_lines)


def unpack(arrived, place, plan, piece, shape, deep, slot, previous):
    experts, _, lines, width = shape
    first, count = piece
    rows = arrived.shape[0]
    makes = previous is None
    onehot_spec = pl.BlockSpec((1, lines, deep), lambda e, plan: (e, 0, 0))
    place_spec = pl.BlockSpec((1, 2, lines, LANES), lambda e, plan: (e, 0, 0, 0))
    in_specs = [
        place_spec if makes else onehot_spec,
        pl.BlockSpec(memory_space=pl.ANY),
    ]
    operands = [plan, place, arrived]
    aliases = {}
    if previous is not None:
        in_specs.append(pl.BlockSpec(memory_space=pl.ANY))
        operands.append(previous)
        aliases = {3: 0}
    return pl.pallas_call(
        functools.partial(unpack_kernel, slot, makes),
        grid_spec=pltpu.PrefetchScalarGridSpec(
            num_scalar_prefetch=1,
            grid=(experts,),
            in_specs=in_specs,
            out_specs=[
                pl.BlockSpec((1, count, lines, width), lambda e, plan: (e, first // count, 0, 0))
            ]
            + [onehot_spec] * makes,
            scratch_shapes=[
                pltpu.VMEM((2, deep, count * width), jnp.bfloat16),
                pltpu.SemaphoreType.DMA((2, rows * count)),
            ],
        ),
        out_shape=[jax.ShapeDtypeStruct(shape, jnp.bfloat16)]
        + [jax.ShapeDtypeStruct((experts, lines, deep), jnp.bfloat16)] * makes,
        input_output_aliases=aliases,
        compiler_params=pltpu.CompilerParams(vmem_limit_bytes=UNPACK_LIMIT),
        cost_estimate=pl.CostEstimate(
            flops=2 * count * experts * deep * lines * width,
            bytes_accessed=4 * count * experts * lines * width,
            transcendentals=0,
        ),
        name="unpack_lines",
    )(*operands)


def after_kernel(*refs):
    del refs


def after(values, signals):
    anywhere = pl.BlockSpec(memory_space=pl.ANY)
    return pl.pallas_call(
        after_kernel,
        in_specs=[anywhere] * (len(values) + len(signals)),
        out_specs=[anywhere] * len(values),
        out_shape=[jax.ShapeDtypeStruct(v.shape, v.dtype) for v in values],
        input_output_aliases={n: n for n in range(len(values))},
        compiler_params=pltpu.CompilerParams(vmem_limit_bytes=PACK_LIMIT),
        name="after",
    )(*values, *signals)


def own_ids(table, lines, width):
    mine = lax.dynamic_slice_in_dim(table, lax.axis_index("row") * lines, lines, 1)
    return jnp.pad(mine, ((0, 0), (0, width - lines)), constant_values=-1)


def from_peer(block, axis, offset):
    size = lax.axis_size(axis)
    return lax.ppermute(block, axis, [(i, i ^ offset) for i in range(size)])


class Migration:
    def __init__(self, expert_lines, old_lines, new_lines):
        rows = lax.axis_size("row")
        experts, parts, lines, width = expert_lines.shape
        padded = up_to(lines, LANES)
        block_rows = up_to(experts * lines // rows, TILE)
        pairs = experts * rows
        compact = up_to(lines + 2 * (TILE - 1) * rows, TILE)
        self.slot = min(SLOT, block_rows // TILE)
        self.deep = up_to(max(compact, rows * self.slot * TILE), 256)
        self.shape = expert_lines.shape
        self.pieces = [(parts - 1, 1), (0, parts - 1)]
        out_place, out_plan = call_plan(
            functools.partial(outgoing_kernel, lines, rows), "outgoing_plan",
            new_lines, own_ids(old_lines, lines, padded), pairs,
            jax.ShapeDtypeStruct((experts, 1, padded), jnp.int32),
        )
        self.in_place, self.in_plan = call_plan(
            functools.partial(incoming_kernel, lines, rows, block_rows // TILE, self.slot),
            "incoming_plan",
            old_lines, own_ids(new_lines, lines, padded), pairs,
            jax.ShapeDtypeStruct((experts, 2, lines, LANES), jnp.bfloat16),
        )
        self.packed = [
            pack(expert_lines, out_place, out_plan, piece, rows, block_rows, compact)
            for piece in self.pieces
        ]
        self.arrived = []
        self.moved = None

    def send(self, signals=()):
        block = self.packed[len(self.arrived)]
        if signals:
            (block,) = after([block], signals)
        self.arrived.append(
            lax.all_to_all(block, "row", split_axis=0, concat_axis=0, tiled=True)
        )

    def receive(self, piece):
        self.moved, *onehots = unpack(
            self.arrived[piece], self.in_place, self.in_plan, self.pieces[piece], self.shape,
            self.deep, self.slot, self.moved,
        )
        if onehots:
            (self.in_place,) = onehots


def attend(queries, new_kv, prompt_kv, suffix_kv, lengths):
    seq_count = queries.shape[0]
    prompt_rows = prompt_kv.shape[2]
    suffix_rows = suffix_kv.shape[2]
    col_index = lax.axis_index("col")
    query_heads = queries.reshape(seq_count, KVH, REP, HD)
    prompt_keys = prompt_kv[0, 0].reshape(prompt_rows, KVH, HD)
    prompt_values = prompt_kv[0, 1].reshape(prompt_rows, KVH, HD)
    suffix_keys = suffix_kv[:, 0].reshape(seq_count, suffix_rows, KVH, HD)
    suffix_values = suffix_kv[:, 1].reshape(seq_count, suffix_rows, KVH, HD)
    own_keys = new_kv[:, 0].reshape(seq_count, KVH, HD)
    own_values = new_kv[:, 1].reshape(seq_count, KVH, HD)
    score_scale = HD ** (-0.5)
    prompt_scores = (
        jnp.einsum("skgd,pkd->skgp", query_heads, prompt_keys, preferred_element_type=jnp.float32)
        * score_scale
    )
    suffix_scores = (
        jnp.einsum("skgd,spkd->skgp", query_heads, suffix_keys, preferred_element_type=jnp.float32)
        * score_scale
    )
    own_scores = (
        jnp.einsum("skgd,skd->skg", query_heads, own_keys, preferred_element_type=jnp.float32)
        * score_scale
    )
    positions = col_index * suffix_rows + jnp.arange(suffix_rows, dtype=jnp.int32)
    live_slots = (positions[None, :] < lengths[:, None])[:, None, None, :]
    holder = col_index == 0
    suffix_scores = jnp.where(live_slots, suffix_scores, neg_big)
    own_scores = jnp.where(holder, own_scores, neg_big)
    highest = jnp.maximum(
        jnp.maximum(jnp.max(prompt_scores, axis=-1), jnp.max(suffix_scores, axis=-1)), own_scores
    )
    prompt_weights = jnp.exp(prompt_scores - highest[..., None])
    suffix_weights = jnp.where(live_slots, jnp.exp(suffix_scores - highest[..., None]), 0.0)
    own_weights = jnp.where(holder, jnp.exp(own_scores - highest), 0.0)
    totals = jnp.sum(prompt_weights, axis=-1) + jnp.sum(suffix_weights, axis=-1) + own_weights
    mixture = jnp.einsum(
        "skgp,pkd->skgd",
        prompt_weights.astype(jnp.bfloat16),
        prompt_values,
        preferred_element_type=jnp.float32,
    )
    mixture = mixture + jnp.einsum(
        "skgp,spkd->skgd",
        suffix_weights.astype(jnp.bfloat16),
        suffix_values,
        preferred_element_type=jnp.float32,
    )
    own_rounded = lax.optimization_barrier(own_weights.astype(jnp.bfloat16)).astype(jnp.float32)
    mixture = mixture + own_rounded[..., None] * own_values.astype(jnp.float32)[:, :, None, :]
    heads = KVH * REP
    bundle = jnp.concatenate(
        [
            mixture.reshape(seq_count, heads * HD),
            highest.reshape(seq_count, heads),
            totals.reshape(seq_count, heads),
            jnp.zeros((seq_count, LANES - 2 * heads), jnp.float32),
        ],
        axis=1,
    )
    bundles = [bundle] + [from_peer(bundle, "col", o) for o in range(1, lax.axis_size("col"))]
    every = jnp.stack(bundles)
    mixtures = every[:, :, : heads * HD].reshape(-1, seq_count, heads, HD)
    peaks = every[:, :, heads * HD : heads * HD + heads]
    sums = every[:, :, heads * HD + heads : heads * HD + 2 * heads]
    factors = jnp.exp(peaks - jnp.max(peaks, axis=0))
    total = jnp.sum(sums * factors, axis=0)
    mixed = jnp.sum(mixtures * factors[..., None], axis=0)
    return (mixed / total[..., None]).astype(jnp.bfloat16).reshape(seq_count, heads * HD)


def gate_up_kernel(me_ref, h_ref, gain_ref, router_ref, routes_ref, gate_ref, up_ref, out_ref, acc_ref):
    e = pl.program_id(0)
    tokens = h_ref.shape[0]
    lines = gate_ref.shape[2]
    padded = out_ref.shape[3]
    h = h_ref[...].astype(jnp.float32)
    scaled = (h * gain_ref[...].astype(jnp.float32)).astype(jnp.bfloat16)

    @pl.when(e == 0)
    def _():
        acc_ref[...] = jnp.zeros_like(acc_ref)

    against = (((1,), (1,)), ((), ()))
    gate = lax.dot_general(scaled, gate_ref[0, 0], against, preferred_element_type=jnp.float32)
    up = lax.dot_general(scaled, up_ref[0, 0], against, preferred_element_type=jnp.float32)
    for k in range(routes_ref.shape[1]):
        chosen = routes_ref[:, k : k + 1] == e
        acc_ref[2 * k, :, :lines] += jnp.where(chosen, gate, 0.0)
        acc_ref[2 * k + 1, :, :lines] += jnp.where(chosen, up, 0.0)

    @pl.when(e == pl.num_programs(0) - 1)
    def _():
        last = padded - LANES
        shift = lines - last
        experts = pl.num_programs(0)
        extra = jnp.dot(scaled, router_ref[...], preferred_element_type=jnp.float32)
        lane = iota((tokens, LANES), 1)
        square = jnp.sum(h * h, axis=1, keepdims=True)
        extra = jnp.where(lane == shift + experts, square, extra)
        high = extra.astype(jnp.bfloat16).astype(jnp.float32)
        low = extra - high
        acc_ref[0, :, last:] += jnp.where(lane >= shift, high, 0.0)
        acc_ref[1, :, last:] += jnp.where(lane >= shift, low, 0.0)
        peers, _, share, _ = out_ref.shape
        me = me_ref[0]
        for o in range(peers):
            begin = pl.multiple_of((me ^ o) * share, share)
            out_ref[o] = acc_ref[:, pl.ds(begin, share), :].astype(jnp.bfloat16)


def activate_kernel(lines, experts, model_width, routes_ref, *refs):
    out_ref = refs[-1]
    summed = refs[0][...].astype(jnp.float32)
    for ref in refs[1:-1]:
        summed = summed + ref[...].astype(jnp.float32)
    _, share, padded = summed.shape
    last = padded - LANES
    shift = lines - last
    extra = summed[0, :, last:] + summed[1, :, last:]
    lane = iota((share, LANES), 1)
    square = jnp.sum(jnp.where(lane == shift + experts, extra, 0.0), axis=1, keepdims=True)
    inverse_rms = lax.rsqrt(square / model_width + norm_eps)
    logits = []
    for k in range(out_ref.shape[0]):
        wanted = lane == routes_ref[:, k : k + 1] + shift
        logits.append(jnp.sum(jnp.where(wanted, extra, 0.0), axis=1, keepdims=True) * inverse_rms)
    peak = functools.reduce(jnp.maximum, logits)
    shares = [jnp.exp(v - peak) for v in logits]
    total = functools.reduce(jnp.add, shares)
    inside = iota((share, padded), 1) < lines
    for k in range(out_ref.shape[0]):
        gate = summed[2 * k] * inverse_rms
        up = summed[2 * k + 1] * inverse_rms
        act = gate / (1.0 + jnp.exp(-gate)) * up
        out_ref[k] = jnp.where(inside, act * (shares[k] / total), 0.0).astype(jnp.bfloat16)


def down_kernel(me_ref, routes_ref, *refs):
    down_ref, out_ref, act_ref = refs[-3:]
    chunks = refs[:-3]
    e = pl.program_id(0)
    topk, share, _ = chunks[0].shape
    lines = down_ref.shape[2]

    @pl.when(e == 0)
    def _():
        me = me_ref[0]
        out_ref[...] = jnp.zeros_like(out_ref)
        for o, chunk in enumerate(chunks):
            begin = pl.multiple_of((me ^ o) * share, share)
            act_ref[:, pl.ds(begin, share), :] = chunk[...]

    mine = jnp.zeros((act_ref.shape[1], lines), jnp.float32)
    for k in range(topk):
        chosen = routes_ref[:, k : k + 1] == e
        mine = mine + jnp.where(chosen, act_ref[k, :, :lines].astype(jnp.float32), 0.0)
    out_ref[...] += jnp.dot(
        mine.astype(jnp.bfloat16), down_ref[0, 0], preferred_element_type=jnp.float32
    )


def experts_part(h_mid, moe_gain, w_router, expert_lines, routes, migration):
    rows = lax.axis_size("row")
    cols = lax.axis_size("col")
    row_index = lax.axis_index("row")
    col_index = lax.axis_index("col")
    experts, _, lines, width = expert_lines.shape
    own, _ = h_mid.shape
    tokens = own * rows
    topk = routes.shape[1]
    share = tokens // cols
    padded = up_to(lines + experts + 1, LANES)
    shift = lines - (padded - LANES)
    me = col_index.astype(jnp.int32).reshape(1)

    order = row_index ^ jnp.array(sorted(range(rows), key=lambda o: (o % 2, o)), jnp.int32)
    routes = routes.reshape(rows, own, topk)[order].reshape(tokens, topk)
    my_routes = lax.dynamic_slice_in_dim(routes, col_index * share, share, 0)
    router = jnp.pad(w_router, ((0, 0), (shift, LANES - shift - experts)))
    same_core = jnp.concatenate(
        [h_mid] + [from_peer(h_mid, "row", o) for o in range(2, rows, 2)], axis=0
    )
    every_h = jnp.concatenate([same_core, from_peer(same_core, "row", 1)], axis=0)
    migration.send([every_h])
    part_spec = lambda part: pl.BlockSpec((1, 1, lines, width), lambda e, me: (e, part, 0, 0))
    whole = lambda a: pl.BlockSpec(a.shape, lambda e, me: (0,) * a.ndim)
    gain = moe_gain.reshape(1, width)
    partial = pl.pallas_call(
        gate_up_kernel,
        grid_spec=pltpu.PrefetchScalarGridSpec(
            num_scalar_prefetch=1,
            grid=(experts,),
            in_specs=[whole(every_h), whole(gain), whole(router), whole(routes)]
            + [part_spec(0), part_spec(1)],
            out_specs=pl.BlockSpec((cols, 2 * topk, share, padded), lambda e, me: (0, 0, 0, 0)),
            scratch_shapes=[pltpu.VMEM((2 * topk, tokens, padded), jnp.float32)],
        ),
        out_shape=jax.ShapeDtypeStruct((cols, 2 * topk, share, padded), jnp.bfloat16),
        compiler_params=params(),
        cost_estimate=pl.CostEstimate(
            flops=4 * experts * tokens * lines * width,
            bytes_accessed=4 * experts * lines * width,
            transcendentals=0,
        ),
        name="gate_up",
    )(me, every_h, gain, router, routes, expert_lines, expert_lines)
    gathered = [partial[0]] + [from_peer(partial[o], "col", o) for o in range(1, cols)]
    activated = pl.pallas_call(
        functools.partial(activate_kernel, lines, experts, width * cols),
        out_shape=jax.ShapeDtypeStruct((topk, share, padded), jnp.bfloat16),
        compiler_params=params(),
        name="activate",
    )(my_routes, *gathered)
    chunks = [activated] + [from_peer(activated, "col", o) for o in range(1, cols)]
    produced = pl.pallas_call(
        down_kernel,
        grid_spec=pltpu.PrefetchScalarGridSpec(
            num_scalar_prefetch=1,
            grid=(experts,),
            in_specs=[whole(routes)] + [whole(c) for c in chunks] + [part_spec(2)],
            out_specs=pl.BlockSpec((tokens, width), lambda e, me: (0, 0)),
            scratch_shapes=[pltpu.VMEM((topk, tokens, padded), jnp.bfloat16)],
        ),
        out_shape=jax.ShapeDtypeStruct((tokens, width), jnp.float32),
        compiler_params=params(),
        cost_estimate=pl.CostEstimate(
            flops=2 * experts * tokens * lines * width,
            bytes_accessed=2 * experts * lines * width,
            transcendentals=0,
        ),
        name="down",
    )(me, routes, *chunks, expert_lines)
    migration.receive(0)
    (produced,) = after([produced], [migration.moved])
    half = tokens // 2
    both_cores = produced[:half] + from_peer(produced[half:], "row", 1)
    blocks = both_cores.reshape(rows // 2, own, width)
    mixed = blocks[0]
    for n in range(1, rows // 2):
        mixed = mixed + from_peer(blocks[n], "row", 2 * n)
    return mixed


def local(
    hidden,
    queries,
    new_kv,
    prompt_kv,
    suffix_kv,
    lengths,
    w_out,
    moe_gain,
    w_router,
    expert_weights,
    old_lines,
    new_lines,
    routes,
):
    expert_lines = jnp.transpose(expert_weights, (0, 2, 1, 3))
    migration = Migration(expert_lines, old_lines, new_lines)
    migration.send()
    attended = attend(queries, new_kv, prompt_kv, suffix_kv, lengths)
    projected = jnp.dot(attended, w_out, preferred_element_type=jnp.float32)
    h_mid = (hidden.astype(jnp.float32) + projected).astype(jnp.bfloat16)
    (h_mid,) = after([h_mid], migration.packed)
    mixed = experts_part(h_mid, moe_gain, w_router, expert_lines, routes, migration)
    migration.receive(1)
    return (h_mid.astype(jnp.float32) + mixed, jnp.transpose(migration.moved, (0, 2, 1, 3)))


def solution(mesh):
    return jax.shard_map(
        local,
        mesh=mesh,
        in_specs=(
            P("row", "col"),
            P("row", None),
            P("row", None, None),
            P("row", None, "col", None),
            P("row", None, "col", None),
            P("row"),
            P(None, "col"),
            P("col"),
            P("col", None),
            P(None, "row", None, "col"),
            P(),
            P(),
            P(),
        ),
        out_specs=(P("row", "col"), P(None, "row", None, "col")),
        check_vma=False,
    )
```

```python
import functools

import jax
import jax.numpy as jnp
from jax import lax
from jax.experimental import pallas as pl
from jax.experimental.pallas import tpu as pltpu
from jax.sharding import PartitionSpec as P

KVH = 16
HD = 128
REP = 2
TILE = 16
LANES = 128

norm_eps = 1e-06
neg_big = -1e30
VMEM_LIMIT = 48 * 1024 * 1024
PACK_LIMIT = 61 * 1024 * 1024


def up_to(value, unit):
    return -(-value // unit) * unit


def iota(shape, axis):
    return lax.broadcasted_iota(jnp.int32, shape, axis)


def ones_where(mask):
    return jnp.where(mask, 1.0, 0.0).astype(jnp.bfloat16)


def params():
    return pltpu.CompilerParams(vmem_limit_bytes=VMEM_LIMIT)


def counting(shape, axis):
    return iota(shape, axis).astype(jnp.float32).astype(jnp.bfloat16)


def as_bf16(values):
    return values.astype(jnp.float32).astype(jnp.bfloat16)


def equal_ones(left, right):
    one = jnp.ones((), jnp.bfloat16)
    return jnp.maximum(one - jnp.abs(left - right), jnp.zeros((), jnp.bfloat16))


def within(place, block):
    place = place - 256 * block
    return as_bf16(jnp.where((place >= 0) & (place < 256), place, -1))


def look_up(table_rows, id_rows, numbers, values):
    full = table_rows[0].shape[1]
    ids = id_rows[0].shape[1]
    high_count = up_to(-(-full // 64), 16)
    zero = jnp.zeros((), jnp.bfloat16)
    highs = [equal_ones(numbers[:high_count], as_bf16(row >> 6)) for row in table_rows]
    lows = []
    for row in table_rows:
        hit = numbers[:64] == as_bf16(row & 63)
        lows += [jnp.where(hit, part, zero) for part in values]
    square = lax.dot_general(
        jnp.concatenate(highs, axis=0),
        jnp.concatenate(lows, axis=0),
        (((1,), (1,)), ((), ())),
        preferred_element_type=jnp.float32,
    )
    wide = 64 * len(values)
    found = []
    for n, row in enumerate(id_rows):
        block = square[n * high_count : (n + 1) * high_count, n * wide : (n + 1) * wide]
        id_high = equal_ones(numbers[:high_count, :ids], as_bf16(row >> 6))
        spread = lax.dot_general(
            block.astype(jnp.bfloat16), id_high, (((0,), (0,)), ((), ())),
            preferred_element_type=jnp.float32,
        )
        wanted = iota((64, ids), 0) == (row & 63)
        found.append(
            [
                jnp.sum(jnp.where(wanted, spread[64 * m : 64 * m + 64], 0.0), axis=0, keepdims=True)
                for m in range(len(values))
            ]
        )
    return found


def look_up_all(table_ref, id_ref, numbers, values):
    experts = table_ref.shape[0]
    group = 4 // len(values)
    found = []
    for first in range(0, experts, group):
        members = range(first, min(first + group, experts))
        found += look_up(
            [table_ref[e : e + 1, :] for e in members],
            [id_ref[e : e + 1, :] for e in members],
            numbers,
            values,
        )
    return found


def numbers_for(full):
    return counting((max(up_to(-(-full // 64), 16), 64), full), 0)


def segment_plan(counts, experts, rows):
    starts = []
    running = jnp.zeros((rows, LANES), jnp.float32)
    for e in range(experts):
        starts.append(running)
        running = running + counts[e * rows : (e + 1) * rows]
    start = jnp.concatenate(starts, axis=0)
    lead = jnp.floor(start * (1.0 / TILE))
    tail = jnp.floor((start + counts + (TILE - 1.0)) * (1.0 / TILE))
    tiles = jnp.where(counts > 0.0, tail - lead, 0.0)
    pairs = experts * rows
    line = iota((pairs, pairs), 0)
    column = iota((pairs, pairs), 1)
    earlier = ones_where((line // rows == column // rows) & (column < line))
    base = jnp.dot(earlier, tiles.astype(jnp.bfloat16), preferred_element_type=jnp.float32)
    return start, lead, tiles, base


def write_plan(plan_ref, parts):
    for n, part in enumerate(parts):
        short = -part.shape[0] % LANES
        if short:
            part = jnp.concatenate([part, jnp.zeros((short, LANES), jnp.float32)], axis=0)
        plan_ref[n : n + 1, :] = jnp.transpose(part)[:1].astype(jnp.int32)


def outgoing_kernel(lines, rows, new_ref, held_ref, stack_ref, plan_ref):
    experts = new_ref.shape[0]
    width = held_ref.shape[1]
    real = iota((1, width), 1) < lines
    hits = []
    full = new_ref.shape[1]
    numbers = numbers_for(full)
    slot = iota((64, full), 1).astype(jnp.float32)
    values = (jnp.floor((slot + 0.5) * (1.0 / lines)).astype(jnp.bfloat16),)
    for (peer,) in look_up_all(new_ref, held_ref, numbers, values):
        peer = peer.astype(jnp.int32)
        hits.append(jnp.where((iota((rows, width), 0) == peer) & real, 1.0, 0.0))
    hits = jnp.concatenate(hits, axis=0)
    until = ones_where(iota((width, width), 0) <= iota((width, width), 1))
    ranks = jnp.dot(hits.astype(jnp.bfloat16), until, preferred_element_type=jnp.float32)
    counts = jnp.broadcast_to(jnp.sum(hits, axis=1, keepdims=True), (experts * rows, LANES))
    start, lead, tiles, base = segment_plan(counts, experts, rows)
    write_plan(plan_ref, (lead, tiles, base, start - lead * TILE))
    offset = (base * TILE + start - lead * TILE - 1.0)[:, :1]
    placed = hits * (ranks + offset)
    for e in range(experts):
        row = jnp.sum(placed[e * rows : (e + 1) * rows], axis=0, keepdims=True)
        stack_ref[e] = jnp.where(real, row, -1.0).astype(jnp.int32)


def incoming_kernel(lines, rows, block_tiles, slot, old_ref, wanted_ref, stack_ref, plan_ref):
    experts = old_ref.shape[0]
    width = wanted_ref.shape[1]
    real = iota((1, width), 1) < lines
    held_at = []
    hits = []
    full = old_ref.shape[1]
    numbers = numbers_for(full)
    at = iota((64, full), 1)
    values = (as_bf16(at >> 7), as_bf16(at & 127))
    for high, low in look_up_all(old_ref, wanted_ref, numbers, values):
        slots = high * 128.0 + low
        held_at.append(jnp.where(real, slots, 1e9))
        peer = jnp.floor((slots + 0.5) * (1.0 / lines)).astype(jnp.int32)
        hits.append(jnp.where((iota((rows, width), 0) == peer) & real, 1.0, 0.0))
    hits = jnp.concatenate(hits, axis=0)
    counts = jnp.broadcast_to(jnp.sum(hits, axis=1, keepdims=True), (experts * rows, LANES))
    start, lead, tiles, base = segment_plan(counts, experts, rows)
    line = iota((experts * rows, LANES), 0)
    peer = (line % rows).astype(jnp.float32)
    longest = [
        jnp.max(tiles[e * rows : (e + 1) * rows], axis=0, keepdims=True) for e in range(experts)
    ]
    longest = jnp.concatenate(
        [jnp.broadcast_to(most, (rows, LANES)) for most in longest], axis=0
    )
    slotted = longest <= slot
    lead = jnp.where(slotted, jnp.minimum(lead, float(block_tiles - slot)), lead)
    base = jnp.where(slotted, peer * slot, base)
    write_plan(plan_ref, (lead, tiles, base, jnp.where(slotted, 1.0, 0.0)))
    blank = jnp.zeros((LANES - experts, width), jnp.float32)
    columns = jnp.transpose(jnp.concatenate(held_at + [blank], axis=0))
    rows_out = []
    for e in range(experts):
        mine = slice(e * rows, (e + 1) * rows)
        before = jnp.where(columns[:, e : e + 1] < held_at[e], 1.0, 0.0)
        rank = jnp.sum(before, axis=0, keepdims=True)
        ahead = jnp.zeros((1, LANES), jnp.float32)
        firsts = []
        for r in range(rows):
            firsts.append(ahead)
            ahead = ahead + counts[e * rows + r : e * rows + r + 1]
        first = jnp.concatenate(firsts, axis=0)
        offset = (base[mine] * TILE + start[mine] - lead[mine] * TILE - first)[:, :1]
        rows_out.append(jnp.sum(hits[mine] * (rank + offset), axis=0, keepdims=True))
    places = jnp.transpose(jnp.concatenate(rows_out + [blank], axis=0))
    for e in range(experts):
        place = jnp.broadcast_to(places[:lines, e : e + 1], (lines, LANES))
        block = jnp.floor(place * (1.0 / 256.0))
        stack_ref[e, 0] = (place - 256.0 * block).astype(jnp.bfloat16)
        stack_ref[e, 1] = block.astype(jnp.bfloat16)


STRAIGHT = 8
SLOT = 7


def tile_at(index):
    return pl.ds(pl.multiple_of(index * TILE, TILE), TILE)


def pack_kernel(rows, span, plan_ref, place_ref, lines_ref, out_ref, packed_ref, number_ref, sems, *stages):
    part = pl.program_id(0)
    step = pl.program_id(1)
    deep = stages[0].shape[0] - STRAIGHT * TILE
    lines = lines_ref.shape[2]

    @pl.when((part == 0) & (step == 0))
    def _():
        number_ref[...] = counting(number_ref.shape, 0)

    def entry(n, j, d):
        return plan_ref[n, (step * span + j) * rows + d]

    usual = min(deep, up_to(lines + rows * TILE, TILE))

    def move(j, begin, end):
        place = place_ref[j][:, :lines]
        onehot = [
            equal_ones(number_ref[: min(256, end - row)], within(place - begin, (row - begin) // 256))
            for row in range(begin, end, 256)
        ]
        stages[j][begin:end] = jnp.dot(
            jnp.concatenate(onehot, axis=0), lines_ref[j, 0], preferred_element_type=jnp.float32
        ).astype(jnp.bfloat16)

    for j in range(span):
        move(j, 0, usual)
    if usual < deep:
        for j in range(span):
            used = entry(1, j, rows - 1) + entry(2, j, rows - 1)

            @pl.when(used * TILE > usual)
            def _(j=j):
                move(j, usual, deep)

    for j, stage_ref in enumerate(stages):

        def one_peer(d, most, j=j, stage_ref=stage_ref):
            lead, tiles, base = entry(0, j, d), entry(1, j, d), entry(2, j, d)
            there = pl.multiple_of(lead * TILE, TILE)
            here = pl.multiple_of(base * TILE, TILE)
            earlier = packed_ref[d, pl.ds(there, TILE), :]
            fresh = stage_ref[pl.ds(here, STRAIGHT * TILE), :]
            packed_ref[d, pl.ds(there + TILE, (STRAIGHT - 1) * TILE), :] = fresh[TILE:]
            kept = jnp.where(entry(3, j, d) > 0, earlier, jnp.zeros_like(earlier))
            added = jnp.where(tiles > 0, fresh[:TILE], jnp.zeros_like(earlier))
            packed_ref[d, pl.ds(there, TILE), :] = kept + added
            return jnp.maximum(most, tiles)

        most = lax.fori_loop(0, rows, one_peer, 0, unroll=rows <= 8)

        @pl.when(most > STRAIGHT)
        def _(j=j, stage_ref=stage_ref):
            def long_peer(d, carry):
                lead, tiles, base = entry(0, j, d), entry(1, j, d), entry(2, j, d)

                def put(t, c):
                    packed_ref[d, tile_at(lead + t), :] = stage_ref[tile_at(base + t), :]
                    return c

                return lax.fori_loop(STRAIGHT, tiles, put, carry)

            lax.fori_loop(0, rows, long_peer, 0)

    @pl.when(step == pl.num_programs(1) - 1)
    def _():
        copies = [
            pltpu.make_async_copy(
                packed_ref.at[d, pl.ds(0, out_ref.shape[2])], out_ref.at[d, part], sems.at[d]
            )
            for d in range(rows)
        ]
        for copy in copies:
            copy.start()
        for copy in copies:
            copy.wait()


def unpack_kernel(slot, span, plan_ref, place_ref, block_ref, *rest):
    out_ref, stage_ref, sems = rest[-3:]
    step = pl.program_id(0)
    steps = pl.num_programs(0)
    rows, count, _, width = block_ref.shape
    deep = stage_ref.shape[3]
    lines = out_ref.shape[2]
    buffer = step % 2

    def entry(n, e, s):
        return plan_ref[n, e * rows + s]

    def slotted(e):
        return entry(3, e, 0) > 0

    def begin(step):
        for j in range(span):
            e = step * span + j

            @pl.when(slotted(e))
            def _(e=e, j=j):
                for s in range(rows):
                    there = pl.ds(pl.multiple_of(entry(0, e, s) * TILE, TILE), slot * TILE)
                    here = pl.ds(s * slot * TILE, slot * TILE)
                    pltpu.make_async_copy(
                        block_ref.at[s, :, there],
                        stage_ref.at[step % 2, j, :, here],
                        sems.at[step % 2, j],
                    ).start()

    @pl.when(step == 0)
    def _():
        stage_ref[...] = jnp.zeros_like(stage_ref)
        begin(step)

    @pl.when(step + 1 < steps)
    def _():
        begin(step + 1)

    for j in range(span):
        e = step * span + j

        @pl.when(slotted(e))
        def _(j=j):
            all_slots = stage_ref.at[buffer, j, :, pl.ds(0, rows * slot * TILE)]
            pltpu.make_async_copy(all_slots, all_slots, sems.at[buffer, j]).wait()

        @pl.when(jnp.logical_not(slotted(e)))
        def _(e=e, j=j):
            def one_peer(s, carry):
                def put(t, c):
                    copy = pltpu.make_async_copy(
                        block_ref.at[s, :, tile_at(entry(0, e, s) + t)],
                        stage_ref.at[buffer, j, :, tile_at(entry(2, e, s) + t)],
                        sems.at[buffer, j],
                    )
                    copy.start()
                    copy.wait()
                    return c

                return lax.fori_loop(0, entry(1, e, s), put, carry)

            lax.fori_loop(0, rows, one_peer, 0)

    lane = counting((lines, LANES), 1)
    for j in range(span):
        within_block, block = place_ref[j, 0], place_ref[j, 1]
        pieces = []
        for first in range(0, deep, LANES):
            away = jnp.abs(block - jnp.asarray(first // 256, jnp.bfloat16))
            place = within_block + away * jnp.asarray(512, jnp.bfloat16)
            pieces.append(equal_ones(lane + jnp.asarray(first % 256, jnp.bfloat16), place))
        onehot = jnp.concatenate(pieces, axis=1)
        for part in range(count):
            out_ref[j, part] = jnp.dot(
                onehot, stage_ref[buffer, j, part], preferred_element_type=jnp.float32
            ).astype(jnp.bfloat16)


def call_plan(kernel, name, table, ids, pairs, place):
    return pl.pallas_call(
        kernel,
        out_shape=(place, jax.ShapeDtypeStruct((4, up_to(pairs, LANES)), jnp.int32)),
        compiler_params=params(),
        cost_estimate=pl.CostEstimate(
            flops=20 * table.size * 256, bytes_accessed=8 * table.size, transcendentals=0
        ),
        name=name,
    )(table, ids)


def pack(expert_lines, place, plan, piece, rows, block_rows, deep):
    experts, _, lines, width = expert_lines.shape
    first, count = piece
    span = 2 - experts % 2
    return pl.pallas_call(
        functools.partial(pack_kernel, rows, span),
        grid_spec=pltpu.PrefetchScalarGridSpec(
            num_scalar_prefetch=1,
            grid=(count, experts // span),
            in_specs=[
                pl.BlockSpec((span, 1, place.shape[2]), lambda p, e, plan: (e, 0, 0)),
                pl.BlockSpec((span, 1, lines, width), lambda p, e, plan: (e, first + p, 0, 0)),
            ],
            out_specs=pl.BlockSpec(memory_space=pltpu.HBM),
            scratch_shapes=[
                pltpu.VMEM((rows, block_rows + STRAIGHT * TILE, width), jnp.bfloat16),
                pltpu.VMEM((256, lines), jnp.bfloat16),
                pltpu.SemaphoreType.DMA((rows,)),
            ]
            + [pltpu.VMEM((deep + STRAIGHT * TILE, width), jnp.bfloat16)] * span,
        ),
        out_shape=jax.ShapeDtypeStruct((rows, count, block_rows, width), jnp.bfloat16),
        compiler_params=pltpu.CompilerParams(vmem_limit_bytes=PACK_LIMIT),
        cost_estimate=pl.CostEstimate(
            flops=2 * count * experts * deep * lines * width,
            bytes_accessed=4 * count * experts * lines * width,
            transcendentals=0,
        ),
        name="pack_lines",
    )(plan, place, expert_lines)


def unpack(arrived, place, plan, piece, shape, deep, slot, previous):
    experts, _, lines, width = shape
    first, count = piece
    span = 2 - experts % 2
    in_specs = [
        pl.BlockSpec((span, 2, lines, LANES), lambda e, plan: (e, 0, 0, 0)),
        pl.BlockSpec(memory_space=pl.ANY),
    ]
    operands = [plan, place, arrived]
    aliases = {}
    if previous is not None:
        in_specs.append(pl.BlockSpec(memory_space=pl.ANY))
        operands.append(previous)
        aliases = {3: 0}
    return pl.pallas_call(
        functools.partial(unpack_kernel, slot, span),
        grid_spec=pltpu.PrefetchScalarGridSpec(
            num_scalar_prefetch=1,
            grid=(experts // span,),
            in_specs=in_specs,
            out_specs=pl.BlockSpec(
                (span, count, lines, width), lambda e, plan: (e, first // count, 0, 0)
            ),
            scratch_shapes=[
                pltpu.VMEM((2, span, count, deep, width), jnp.bfloat16),
                pltpu.SemaphoreType.DMA((2, span)),
            ],
        ),
        out_shape=jax.ShapeDtypeStruct(shape, jnp.bfloat16),
        input_output_aliases=aliases,
        compiler_params=params(),
        cost_estimate=pl.CostEstimate(
            flops=2 * count * experts * deep * lines * width,
            bytes_accessed=4 * count * experts * lines * width,
            transcendentals=0,
        ),
        name="unpack_lines",
    )(*operands)


def after_kernel(*refs):
    del refs


def after(values, signals):
    anywhere = pl.BlockSpec(memory_space=pl.ANY)
    return pl.pallas_call(
        after_kernel,
        in_specs=[anywhere] * (len(values) + len(signals)),
        out_specs=[anywhere] * len(values),
        out_shape=[jax.ShapeDtypeStruct(v.shape, v.dtype) for v in values],
        input_output_aliases={n: n for n in range(len(values))},
        compiler_params=pltpu.CompilerParams(vmem_limit_bytes=PACK_LIMIT),
        name="after",
    )(*values, *signals)


def own_ids(table, lines, width):
    mine = lax.dynamic_slice_in_dim(table, lax.axis_index("row") * lines, lines, 1)
    return jnp.pad(mine, ((0, 0), (0, width - lines)), constant_values=-1)


def from_peer(block, axis, offset):
    size = lax.axis_size(axis)
    return lax.ppermute(block, axis, [(i, i ^ offset) for i in range(size)])


class Migration:
    def __init__(self, expert_lines, old_lines, new_lines):
        rows = lax.axis_size("row")
        experts, parts, lines, width = expert_lines.shape
        padded = up_to(lines, LANES)
        block_rows = up_to(experts * lines // rows, TILE)
        pairs = experts * rows
        compact = up_to(lines + 2 * (TILE - 1) * rows, TILE)
        self.slot = min(SLOT, block_rows // TILE)
        self.deep = up_to(max(compact, rows * self.slot * TILE), 256)
        self.shape = expert_lines.shape
        self.pieces = [(parts - 1, 1), (0, parts - 1)]
        out_place, out_plan = call_plan(
            functools.partial(outgoing_kernel, lines, rows), "outgoing_plan",
            new_lines, own_ids(old_lines, lines, padded), pairs,
            jax.ShapeDtypeStruct((experts, 1, padded), jnp.int32),
        )
        self.in_place, self.in_plan = call_plan(
            functools.partial(incoming_kernel, lines, rows, block_rows // TILE, self.slot),
            "incoming_plan",
            old_lines, own_ids(new_lines, lines, padded), pairs,
            jax.ShapeDtypeStruct((experts, 2, lines, LANES), jnp.bfloat16),
        )
        self.packed = [
            pack(expert_lines, out_place, out_plan, piece, rows, block_rows, compact)
            for piece in self.pieces
        ]
        self.arrived = []
        self.moved = None

    def send(self, signals=()):
        block = self.packed[len(self.arrived)]
        if signals:
            (block,) = after([block], signals)
        self.arrived.append(
            lax.all_to_all(block, "row", split_axis=0, concat_axis=0, tiled=True)
        )

    def receive(self, piece):
        self.moved = unpack(
            self.arrived[piece], self.in_place, self.in_plan, self.pieces[piece], self.shape,
            self.deep, self.slot, self.moved,
        )


def attend(queries, new_kv, prompt_kv, suffix_kv, lengths):
    seq_count = queries.shape[0]
    prompt_rows = prompt_kv.shape[2]
    suffix_rows = suffix_kv.shape[2]
    col_index = lax.axis_index("col")
    query_heads = queries.reshape(seq_count, KVH, REP, HD)
    prompt_keys = prompt_kv[0, 0].reshape(prompt_rows, KVH, HD)
    prompt_values = prompt_kv[0, 1].reshape(prompt_rows, KVH, HD)
    suffix_keys = suffix_kv[:, 0].reshape(seq_count, suffix_rows, KVH, HD)
    suffix_values = suffix_kv[:, 1].reshape(seq_count, suffix_rows, KVH, HD)
    own_keys = new_kv[:, 0].reshape(seq_count, KVH, HD)
    own_values = new_kv[:, 1].reshape(seq_count, KVH, HD)
    score_scale = HD ** (-0.5)
    prompt_scores = (
        jnp.einsum("skgd,pkd->skgp", query_heads, prompt_keys, preferred_element_type=jnp.float32)
        * score_scale
    )
    suffix_scores = (
        jnp.einsum("skgd,spkd->skgp", query_heads, suffix_keys, preferred_element_type=jnp.float32)
        * score_scale
    )
    own_scores = (
        jnp.einsum("skgd,skd->skg", query_heads, own_keys, preferred_element_type=jnp.float32)
        * score_scale
    )
    positions = col_index * suffix_rows + jnp.arange(suffix_rows, dtype=jnp.int32)
    live_slots = (positions[None, :] < lengths[:, None])[:, None, None, :]
    holder = col_index == 0
    suffix_scores = jnp.where(live_slots, suffix_scores, neg_big)
    own_scores = jnp.where(holder, own_scores, neg_big)
    highest = jnp.maximum(
        jnp.maximum(jnp.max(prompt_scores, axis=-1), jnp.max(suffix_scores, axis=-1)), own_scores
    )
    prompt_weights = jnp.exp(prompt_scores - highest[..., None])
    suffix_weights = jnp.where(live_slots, jnp.exp(suffix_scores - highest[..., None]), 0.0)
    own_weights = jnp.where(holder, jnp.exp(own_scores - highest), 0.0)
    totals = jnp.sum(prompt_weights, axis=-1) + jnp.sum(suffix_weights, axis=-1) + own_weights
    mixture = jnp.einsum(
        "skgp,pkd->skgd",
        prompt_weights.astype(jnp.bfloat16),
        prompt_values,
        preferred_element_type=jnp.float32,
    )
    mixture = mixture + jnp.einsum(
        "skgp,spkd->skgd",
        suffix_weights.astype(jnp.bfloat16),
        suffix_values,
        preferred_element_type=jnp.float32,
    )
    own_rounded = lax.optimization_barrier(own_weights.astype(jnp.bfloat16)).astype(jnp.float32)
    mixture = mixture + own_rounded[..., None] * own_values.astype(jnp.float32)[:, :, None, :]
    heads = KVH * REP
    bundle = jnp.concatenate(
        [
            mixture.reshape(seq_count, heads * HD),
            highest.reshape(seq_count, heads),
            totals.reshape(seq_count, heads),
            jnp.zeros((seq_count, LANES - 2 * heads), jnp.float32),
        ],
        axis=1,
    )
    bundles = [bundle] + [from_peer(bundle, "col", o) for o in range(1, lax.axis_size("col"))]
    every = jnp.stack(bundles)
    mixtures = every[:, :, : heads * HD].reshape(-1, seq_count, heads, HD)
    peaks = every[:, :, heads * HD : heads * HD + heads]
    sums = every[:, :, heads * HD + heads : heads * HD + 2 * heads]
    factors = jnp.exp(peaks - jnp.max(peaks, axis=0))
    total = jnp.sum(sums * factors, axis=0)
    mixed = jnp.sum(mixtures * factors[..., None], axis=0)
    return (mixed / total[..., None]).astype(jnp.bfloat16).reshape(seq_count, heads * HD)


def gate_up_kernel(me_ref, h_ref, gain_ref, router_ref, routes_ref, gate_ref, up_ref, out_ref, acc_ref):
    e = pl.program_id(0)
    tokens = h_ref.shape[0]
    lines = gate_ref.shape[2]
    padded = out_ref.shape[3]
    h = h_ref[...].astype(jnp.float32)
    scaled = (h * gain_ref[...].astype(jnp.float32)).astype(jnp.bfloat16)

    @pl.when(e == 0)
    def _():
        acc_ref[...] = jnp.zeros_like(acc_ref)

    against = (((1,), (1,)), ((), ()))
    gate = lax.dot_general(scaled, gate_ref[0, 0], against, preferred_element_type=jnp.float32)
    up = lax.dot_general(scaled, up_ref[0, 0], against, preferred_element_type=jnp.float32)
    for k in range(routes_ref.shape[1]):
        chosen = routes_ref[:, k : k + 1] == e
        acc_ref[2 * k, :, :lines] += jnp.where(chosen, gate, 0.0)
        acc_ref[2 * k + 1, :, :lines] += jnp.where(chosen, up, 0.0)

    @pl.when(e == pl.num_programs(0) - 1)
    def _():
        last = padded - LANES
        shift = lines - last
        experts = pl.num_programs(0)
        extra = jnp.dot(scaled, router_ref[...], preferred_element_type=jnp.float32)
        lane = iota((tokens, LANES), 1)
        square = jnp.sum(h * h, axis=1, keepdims=True)
        extra = jnp.where(lane == shift + experts, square, extra)
        high = extra.astype(jnp.bfloat16).astype(jnp.float32)
        low = extra - high
        acc_ref[0, :, last:] += jnp.where(lane >= shift, high, 0.0)
        acc_ref[1, :, last:] += jnp.where(lane >= shift, low, 0.0)
        peers, _, share, _ = out_ref.shape
        me = me_ref[0]
        for o in range(peers):
            begin = pl.multiple_of((me ^ o) * share, share)
            out_ref[o] = acc_ref[:, pl.ds(begin, share), :].astype(jnp.bfloat16)


def activate_kernel(lines, experts, model_width, routes_ref, *refs):
    out_ref = refs[-1]
    summed = refs[0][...].astype(jnp.float32)
    for ref in refs[1:-1]:
        summed = summed + ref[...].astype(jnp.float32)
    _, share, padded = summed.shape
    last = padded - LANES
    shift = lines - last
    extra = summed[0, :, last:] + summed[1, :, last:]
    lane = iota((share, LANES), 1)
    square = jnp.sum(jnp.where(lane == shift + experts, extra, 0.0), axis=1, keepdims=True)
    inverse_rms = lax.rsqrt(square / model_width + norm_eps)
    logits = []
    for k in range(out_ref.shape[0]):
        wanted = lane == routes_ref[:, k : k + 1] + shift
        logits.append(jnp.sum(jnp.where(wanted, extra, 0.0), axis=1, keepdims=True) * inverse_rms)
    peak = functools.reduce(jnp.maximum, logits)
    shares = [jnp.exp(v - peak) for v in logits]
    total = functools.reduce(jnp.add, shares)
    inside = iota((share, padded), 1) < lines
    for k in range(out_ref.shape[0]):
        gate = summed[2 * k] * inverse_rms
        up = summed[2 * k + 1] * inverse_rms
        act = gate / (1.0 + jnp.exp(-gate)) * up
        out_ref[k] = jnp.where(inside, act * (shares[k] / total), 0.0).astype(jnp.bfloat16)


def down_kernel(me_ref, routes_ref, *refs):
    down_ref, out_ref, act_ref = refs[-3:]
    chunks = refs[:-3]
    e = pl.program_id(0)
    topk, share, _ = chunks[0].shape
    lines = down_ref.shape[2]

    @pl.when(e == 0)
    def _():
        me = me_ref[0]
        out_ref[...] = jnp.zeros_like(out_ref)
        for o, chunk in enumerate(chunks):
            begin = pl.multiple_of((me ^ o) * share, share)
            act_ref[:, pl.ds(begin, share), :] = chunk[...]

    mine = jnp.zeros((act_ref.shape[1], lines), jnp.float32)
    for k in range(topk):
        chosen = routes_ref[:, k : k + 1] == e
        mine = mine + jnp.where(chosen, act_ref[k, :, :lines].astype(jnp.float32), 0.0)
    out_ref[...] += jnp.dot(
        mine.astype(jnp.bfloat16), down_ref[0, 0], preferred_element_type=jnp.float32
    )


def experts_part(h_mid, moe_gain, w_router, expert_lines, routes, migration):
    rows = lax.axis_size("row")
    cols = lax.axis_size("col")
    row_index = lax.axis_index("row")
    col_index = lax.axis_index("col")
    experts, _, lines, width = expert_lines.shape
    own, _ = h_mid.shape
    tokens = own * rows
    topk = routes.shape[1]
    share = tokens // cols
    padded = up_to(lines + experts + 1, LANES)
    shift = lines - (padded - LANES)
    me = col_index.astype(jnp.int32).reshape(1)

    order = row_index ^ jnp.array(sorted(range(rows), key=lambda o: (o % 2, o)), jnp.int32)
    routes = routes.reshape(rows, own, topk)[order].reshape(tokens, topk)
    my_routes = lax.dynamic_slice_in_dim(routes, col_index * share, share, 0)
    router = jnp.pad(w_router, ((0, 0), (shift, LANES - shift - experts)))
    same_core = jnp.concatenate(
        [h_mid] + [from_peer(h_mid, "row", o) for o in range(2, rows, 2)], axis=0
    )
    every_h = jnp.concatenate([same_core, from_peer(same_core, "row", 1)], axis=0)
    migration.send([same_core])
    part_spec = lambda part: pl.BlockSpec((1, 1, lines, width), lambda e, me: (e, part, 0, 0))
    whole = lambda a: pl.BlockSpec(a.shape, lambda e, me: (0,) * a.ndim)
    gain = moe_gain.reshape(1, width)
    partial = pl.pallas_call(
        gate_up_kernel,
        grid_spec=pltpu.PrefetchScalarGridSpec(
            num_scalar_prefetch=1,
            grid=(experts,),
            in_specs=[whole(every_h), whole(gain), whole(router), whole(routes)]
            + [part_spec(0), part_spec(1)],
            out_specs=pl.BlockSpec((cols, 2 * topk, share, padded), lambda e, me: (0, 0, 0, 0)),
            scratch_shapes=[pltpu.VMEM((2 * topk, tokens, padded), jnp.float32)],
        ),
        out_shape=jax.ShapeDtypeStruct((cols, 2 * topk, share, padded), jnp.bfloat16),
        compiler_params=params(),
        cost_estimate=pl.CostEstimate(
            flops=4 * experts * tokens * lines * width,
            bytes_accessed=4 * experts * lines * width,
            transcendentals=0,
        ),
        name="gate_up",
    )(me, every_h, gain, router, routes, expert_lines, expert_lines)
    gathered = [partial[0]] + [from_peer(partial[o], "col", o) for o in range(1, cols)]
    activated = pl.pallas_call(
        functools.partial(activate_kernel, lines, experts, width * cols),
        out_shape=jax.ShapeDtypeStruct((topk, share, padded), jnp.bfloat16),
        compiler_params=params(),
        name="activate",
    )(my_routes, *gathered)
    chunks = [activated] + [from_peer(activated, "col", o) for o in range(1, cols)]
    produced = pl.pallas_call(
        down_kernel,
        grid_spec=pltpu.PrefetchScalarGridSpec(
            num_scalar_prefetch=1,
            grid=(experts,),
            in_specs=[whole(routes)] + [whole(c) for c in chunks] + [part_spec(2)],
            out_specs=pl.BlockSpec((tokens, width), lambda e, me: (0, 0)),
            scratch_shapes=[pltpu.VMEM((topk, tokens, padded), jnp.bfloat16)],
        ),
        out_shape=jax.ShapeDtypeStruct((tokens, width), jnp.float32),
        compiler_params=params(),
        cost_estimate=pl.CostEstimate(
            flops=2 * experts * tokens * lines * width,
            bytes_accessed=2 * experts * lines * width,
            transcendentals=0,
        ),
        name="down",
    )(me, routes, *chunks, expert_lines)
    migration.receive(0)
    (produced,) = after([produced], [migration.moved])
    half = tokens // 2
    both_cores = produced[:half] + from_peer(produced[half:], "row", 1)
    blocks = both_cores.reshape(rows // 2, own, width)
    mixed = blocks[0]
    for n in range(1, rows // 2):
        mixed = mixed + from_peer(blocks[n], "row", 2 * n)
    return mixed


def local(
    hidden,
    queries,
    new_kv,
    prompt_kv,
    suffix_kv,
    lengths,
    w_out,
    moe_gain,
    w_router,
    expert_weights,
    old_lines,
    new_lines,
    routes,
):
    expert_lines = jnp.transpose(expert_weights, (0, 2, 1, 3))
    migration = Migration(expert_lines, old_lines, new_lines)
    migration.send()
    attended = attend(queries, new_kv, prompt_kv, suffix_kv, lengths)
    projected = jnp.dot(attended, w_out, preferred_element_type=jnp.float32)
    h_mid = (hidden.astype(jnp.float32) + projected).astype(jnp.bfloat16)
    (h_mid,) = after([h_mid], migration.packed)
    mixed = experts_part(h_mid, moe_gain, w_router, expert_lines, routes, migration)
    migration.receive(1)
    return (h_mid.astype(jnp.float32) + mixed, jnp.transpose(migration.moved, (0, 2, 1, 3)))


def solution(mesh):
    return jax.shard_map(
        local,
        mesh=mesh,
        in_specs=(
            P("row", "col"),
            P("row", None),
            P("row", None, None),
            P("row", None, "col", None),
            P("row", None, "col", None),
            P("row"),
            P(None, "col"),
            P("col"),
            P("col", None),
            P(None, "row", None, "col"),
            P(),
            P(),
            P(),
        ),
        out_specs=(P("row", "col"), P(None, "row", None, "col")),
        check_vma=False,
    )
```

```python
import functools

import jax
import jax.numpy as jnp
from jax import lax
from jax.experimental import pallas as pl
from jax.experimental.pallas import tpu as pltpu
from jax.sharding import PartitionSpec as P

KVH = 16
HD = 128
REP = 2
TILE = 16
LANES = 128

norm_eps = 1e-06
neg_big = -1e30
VMEM_LIMIT = 48 * 1024 * 1024
PACK_LIMIT = 61 * 1024 * 1024


def up_to(value, unit):
    return -(-value // unit) * unit


def iota(shape, axis):
    return lax.broadcasted_iota(jnp.int32, shape, axis)


def ones_where(mask):
    return jnp.where(mask, 1.0, 0.0).astype(jnp.bfloat16)


def params():
    return pltpu.CompilerParams(vmem_limit_bytes=VMEM_LIMIT)


def counting(shape, axis):
    return iota(shape, axis).astype(jnp.float32).astype(jnp.bfloat16)


def as_bf16(values):
    return values.astype(jnp.float32).astype(jnp.bfloat16)


def equal_ones(left, right):
    one = jnp.ones((), jnp.bfloat16)
    return jnp.maximum(one - jnp.abs(left - right), jnp.zeros((), jnp.bfloat16))


def within(place, block):
    place = place - 256 * block
    return as_bf16(jnp.where((place >= 0) & (place < 256), place, -1))


def look_up(table_rows, id_rows, numbers, values):
    full = table_rows[0].shape[1]
    ids = id_rows[0].shape[1]
    high_count = up_to(-(-full // 64), 16)
    zero = jnp.zeros((), jnp.bfloat16)
    highs = [equal_ones(numbers[:high_count], as_bf16(row >> 6)) for row in table_rows]
    lows = []
    for row in table_rows:
        hit = numbers[:64] == as_bf16(row & 63)
        lows += [jnp.where(hit, part, zero) for part in values]
    square = lax.dot_general(
        jnp.concatenate(highs, axis=0),
        jnp.concatenate(lows, axis=0),
        (((1,), (1,)), ((), ())),
        preferred_element_type=jnp.float32,
    )
    wide = 64 * len(values)
    found = []
    for n, row in enumerate(id_rows):
        block = square[n * high_count : (n + 1) * high_count, n * wide : (n + 1) * wide]
        id_high = equal_ones(numbers[:high_count, :ids], as_bf16(row >> 6))
        spread = lax.dot_general(
            block.astype(jnp.bfloat16), id_high, (((0,), (0,)), ((), ())),
            preferred_element_type=jnp.float32,
        )
        wanted = iota((64, ids), 0) == (row & 63)
        found.append(
            [
                jnp.sum(jnp.where(wanted, spread[64 * m : 64 * m + 64], 0.0), axis=0, keepdims=True)
                for m in range(len(values))
            ]
        )
    return found


def look_up_all(table_ref, id_ref, numbers, values):
    experts = table_ref.shape[0]
    group = 4 // len(values)
    found = []
    for first in range(0, experts, group):
        members = range(first, min(first + group, experts))
        found += look_up(
            [table_ref[e : e + 1, :] for e in members],
            [id_ref[e : e + 1, :] for e in members],
            numbers,
            values,
        )
    return found


def numbers_for(full):
    return counting((max(up_to(-(-full // 64), 16), 64), full), 0)


def segment_plan(counts, experts, rows):
    starts = []
    running = jnp.zeros((rows, LANES), jnp.float32)
    for e in range(experts):
        starts.append(running)
        running = running + counts[e * rows : (e + 1) * rows]
    start = jnp.concatenate(starts, axis=0)
    lead = jnp.floor(start * (1.0 / TILE))
    tail = jnp.floor((start + counts + (TILE - 1.0)) * (1.0 / TILE))
    tiles = jnp.where(counts > 0.0, tail - lead, 0.0)
    pairs = experts * rows
    line = iota((pairs, pairs), 0)
    column = iota((pairs, pairs), 1)
    earlier = ones_where((line // rows == column // rows) & (column < line))
    base = jnp.dot(earlier, tiles.astype(jnp.bfloat16), preferred_element_type=jnp.float32)
    return start, lead, tiles, base


def write_plan(plan_ref, parts):
    for n, part in enumerate(parts):
        short = -part.shape[0] % LANES
        if short:
            part = jnp.concatenate([part, jnp.zeros((short, LANES), jnp.float32)], axis=0)
        plan_ref[n : n + 1, :] = jnp.transpose(part)[:1].astype(jnp.int32)


def outgoing_kernel(lines, rows, new_ref, held_ref, stack_ref, plan_ref):
    experts = new_ref.shape[0]
    width = held_ref.shape[1]
    real = iota((1, width), 1) < lines
    hits = []
    full = new_ref.shape[1]
    numbers = numbers_for(full)
    slot = iota((64, full), 1).astype(jnp.float32)
    values = (jnp.floor((slot + 0.5) * (1.0 / lines)).astype(jnp.bfloat16),)
    for (peer,) in look_up_all(new_ref, held_ref, numbers, values):
        peer = peer.astype(jnp.int32)
        hits.append(jnp.where((iota((rows, width), 0) == peer) & real, 1.0, 0.0))
    hits = jnp.concatenate(hits, axis=0)
    until = ones_where(iota((width, width), 0) <= iota((width, width), 1))
    ranks = jnp.dot(hits.astype(jnp.bfloat16), until, preferred_element_type=jnp.float32)
    counts = jnp.broadcast_to(jnp.sum(hits, axis=1, keepdims=True), (experts * rows, LANES))
    start, lead, tiles, base = segment_plan(counts, experts, rows)
    write_plan(plan_ref, (lead, tiles, base, start - lead * TILE))
    offset = (base * TILE + start - lead * TILE - 1.0)[:, :1]
    placed = hits * (ranks + offset)
    for e in range(experts):
        row = jnp.sum(placed[e * rows : (e + 1) * rows], axis=0, keepdims=True)
        stack_ref[e] = jnp.where(real, row, -1.0).astype(jnp.int32)


def incoming_kernel(lines, rows, block_tiles, slot, old_ref, wanted_ref, stack_ref, plan_ref):
    experts = old_ref.shape[0]
    width = wanted_ref.shape[1]
    real = iota((1, width), 1) < lines
    held_at = []
    hits = []
    full = old_ref.shape[1]
    numbers = numbers_for(full)
    at = iota((64, full), 1)
    values = (as_bf16(at >> 7), as_bf16(at & 127))
    for high, low in look_up_all(old_ref, wanted_ref, numbers, values):
        slots = high * 128.0 + low
        held_at.append(jnp.where(real, slots, 1e9))
        peer = jnp.floor((slots + 0.5) * (1.0 / lines)).astype(jnp.int32)
        hits.append(jnp.where((iota((rows, width), 0) == peer) & real, 1.0, 0.0))
    hits = jnp.concatenate(hits, axis=0)
    counts = jnp.broadcast_to(jnp.sum(hits, axis=1, keepdims=True), (experts * rows, LANES))
    start, lead, tiles, base = segment_plan(counts, experts, rows)
    line = iota((experts * rows, LANES), 0)
    peer = (line % rows).astype(jnp.float32)
    longest = [
        jnp.max(tiles[e * rows : (e + 1) * rows], axis=0, keepdims=True) for e in range(experts)
    ]
    longest = jnp.concatenate(
        [jnp.broadcast_to(most, (rows, LANES)) for most in longest], axis=0
    )
    slotted = longest <= slot
    lead = jnp.where(slotted, jnp.minimum(lead, float(block_tiles - slot)), lead)
    base = jnp.where(slotted, peer * slot, base)
    write_plan(plan_ref, (lead, tiles, base, jnp.where(slotted, 1.0, 0.0)))
    blank = jnp.zeros((LANES - experts, width), jnp.float32)
    columns = jnp.transpose(jnp.concatenate(held_at + [blank], axis=0))
    rows_out = []
    for e in range(experts):
        mine = slice(e * rows, (e + 1) * rows)
        before = jnp.where(columns[:, e : e + 1] < held_at[e], 1.0, 0.0)
        rank = jnp.sum(before, axis=0, keepdims=True)
        ahead = jnp.zeros((1, LANES), jnp.float32)
        firsts = []
        for r in range(rows):
            firsts.append(ahead)
            ahead = ahead + counts[e * rows + r : e * rows + r + 1]
        first = jnp.concatenate(firsts, axis=0)
        offset = (base[mine] * TILE + start[mine] - lead[mine] * TILE - first)[:, :1]
        rows_out.append(jnp.sum(hits[mine] * (rank + offset), axis=0, keepdims=True))
    places = jnp.transpose(jnp.concatenate(rows_out + [blank], axis=0))
    for e in range(experts):
        place = jnp.broadcast_to(places[:lines, e : e + 1], (lines, LANES))
        block = jnp.floor(place * (1.0 / 256.0))
        stack_ref[e, 0] = (place - 256.0 * block).astype(jnp.bfloat16)
        stack_ref[e, 1] = block.astype(jnp.bfloat16)


STRAIGHT = 8
SLOT = 7


def tile_at(index):
    return pl.ds(pl.multiple_of(index * TILE, TILE), TILE)


def pack_kernel(rows, span, steps, plan_ref, place_ref, lines_ref, out_ref, packed_ref, number_ref, sems, *stages):
    part = pl.program_id(0)
    step = pl.program_id(1)
    deep = stages[0].shape[0] - STRAIGHT * TILE
    lines = lines_ref.shape[2]

    @pl.when((part == 0) & (step == 0))
    def _():
        number_ref[...] = counting(number_ref.shape, 0)

    def entry(n, j, d):
        return plan_ref[n, (step * span + j) * rows + d]

    usual = min(deep, up_to(lines + rows * TILE, TILE))

    def move(j, begin, end):
        place = place_ref[j][:, :lines]
        onehot = [
            equal_ones(number_ref[: min(256, end - row)], within(place - begin, (row - begin) // 256))
            for row in range(begin, end, 256)
        ]
        stages[j][begin:end] = jnp.dot(
            jnp.concatenate(onehot, axis=0), lines_ref[j, 0], preferred_element_type=jnp.float32
        ).astype(jnp.bfloat16)

    for j in range(span):
        move(j, 0, usual)
    if usual < deep:
        for j in range(span):
            used = entry(1, j, rows - 1) + entry(2, j, rows - 1)

            @pl.when(used * TILE > usual)
            def _(j=j):
                move(j, usual, deep)

    for j, stage_ref in enumerate(stages):

        def one_peer(d, most, j=j, stage_ref=stage_ref):
            lead, tiles, base = entry(0, j, d), entry(1, j, d), entry(2, j, d)
            there = pl.multiple_of(lead * TILE, TILE)
            here = pl.multiple_of(base * TILE, TILE)
            earlier = packed_ref[d, pl.ds(there, TILE), :]
            fresh = stage_ref[pl.ds(here, STRAIGHT * TILE), :]
            packed_ref[d, pl.ds(there + TILE, (STRAIGHT - 1) * TILE), :] = fresh[TILE:]
            kept = jnp.where(entry(3, j, d) > 0, earlier, jnp.zeros_like(earlier))
            added = jnp.where(tiles > 0, fresh[:TILE], jnp.zeros_like(earlier))
            packed_ref[d, pl.ds(there, TILE), :] = kept + added
            return jnp.maximum(most, tiles)

        most = lax.fori_loop(0, rows, one_peer, 0, unroll=rows <= 8)

        @pl.when(most > STRAIGHT)
        def _(j=j, stage_ref=stage_ref):
            def long_peer(d, carry):
                lead, tiles, base = entry(0, j, d), entry(1, j, d), entry(2, j, d)

                def put(t, c):
                    packed_ref[d, tile_at(lead + t), :] = stage_ref[tile_at(base + t), :]
                    return c

                return lax.fori_loop(STRAIGHT, tiles, put, carry)

            lax.fori_loop(0, rows, long_peer, 0)

    block_rows = out_ref.shape[2]
    chunks = []
    begin = 0
    for after_step in range(steps):
        end = block_rows
        if after_step < steps - 1:
            end = max(begin, block_rows * (after_step + 1) // steps // TILE * TILE - 2 * TILE)
        if end > begin:
            chunks.append((after_step, begin, end))
        begin = end

    def chunk_copy(n):
        _, begin, end = chunks[n]
        here = pl.ds(begin, end - begin)
        return pltpu.make_async_copy(
            packed_ref.at[:, here], out_ref.at[:, part, here], sems.at[n]
        )

    def final_by(n):
        after_step, _, end = chunks[n]
        first = (after_step + 1) * span * rows
        least = functools.reduce(jnp.minimum, [plan_ref[0, first + d] for d in range(rows)])
        return least * TILE >= end

    for n in range(len(chunks) - 1):

        @pl.when((step == chunks[n][0]) & final_by(n))
        def _(n=n):
            chunk_copy(n).start()

    @pl.when(step == steps - 1)
    def _():
        for n in range(len(chunks) - 1):

            @pl.when(jnp.logical_not(final_by(n)))
            def _(n=n):
                chunk_copy(n).start()

        chunk_copy(len(chunks) - 1).start()
        for n in range(len(chunks)):
            chunk_copy(n).wait()


def unpack_kernel(slot, span, plan_ref, place_ref, block_ref, *rest):
    out_ref, stage_ref, sems = rest[-3:]
    step = pl.program_id(0)
    steps = pl.num_programs(0)
    rows, count, _, width = block_ref.shape
    deep = stage_ref.shape[3]
    lines = out_ref.shape[2]
    buffer = step % 2

    def entry(n, e, s):
        return plan_ref[n, e * rows + s]

    def slotted(e):
        return entry(3, e, 0) > 0

    def begin(step):
        for j in range(span):
            e = step * span + j

            @pl.when(slotted(e))
            def _(e=e, j=j):
                for s in range(rows):
                    there = pl.ds(pl.multiple_of(entry(0, e, s) * TILE, TILE), slot * TILE)
                    here = pl.ds(s * slot * TILE, slot * TILE)
                    pltpu.make_async_copy(
                        block_ref.at[s, :, there],
                        stage_ref.at[step % 2, j, :, here],
                        sems.at[step % 2, j],
                    ).start()

    @pl.when(step == 0)
    def _():
        begin(step)

    @pl.when(step + 1 < steps)
    def _():
        begin(step + 1)

    lane = counting((lines, LANES), 1)

    def multiply(j, depth):
        within_block, block = place_ref[j, 0], place_ref[j, 1]
        pieces = []
        for first in range(0, depth, LANES):
            away = jnp.abs(block - jnp.asarray(first // 256, jnp.bfloat16))
            place = within_block + away * jnp.asarray(512, jnp.bfloat16)
            pieces.append(equal_ones(lane + jnp.asarray(first % 256, jnp.bfloat16), place))
        onehot = jnp.concatenate(pieces, axis=1)
        for part in range(count):
            out_ref[j, part] = jnp.dot(
                onehot, stage_ref[buffer, j, part, :depth], preferred_element_type=jnp.float32
            ).astype(jnp.bfloat16)

    for j in range(span):
        e = step * span + j
        staged = rows * slot * TILE

        @pl.when(slotted(e))
        def _(j=j):
            all_slots = stage_ref.at[buffer, j, :, pl.ds(0, staged)]
            pltpu.make_async_copy(all_slots, all_slots, sems.at[buffer, j]).wait()
            if staged % LANES:
                stage_ref[buffer, j, :, staged:] = jnp.zeros(
                    (count, deep - staged, width), jnp.bfloat16
                )
                multiply(j, deep)
            else:
                multiply(j, staged)

        @pl.when(jnp.logical_not(slotted(e)))
        def _(e=e, j=j):
            stage_ref[buffer, j] = jnp.zeros((count, deep, width), jnp.bfloat16)

            def one_peer(s, carry):
                def put(t, c):
                    copy = pltpu.make_async_copy(
                        block_ref.at[s, :, tile_at(entry(0, e, s) + t)],
                        stage_ref.at[buffer, j, :, tile_at(entry(2, e, s) + t)],
                        sems.at[buffer, j],
                    )
                    copy.start()
                    copy.wait()
                    return c

                return lax.fori_loop(0, entry(1, e, s), put, carry)

            lax.fori_loop(0, rows, one_peer, 0)
            multiply(j, deep)


def call_plan(kernel, name, table, ids, pairs, place):
    return pl.pallas_call(
        kernel,
        out_shape=(place, jax.ShapeDtypeStruct((4, up_to(pairs, LANES)), jnp.int32)),
        compiler_params=params(),
        cost_estimate=pl.CostEstimate(
            flops=20 * table.size * 256, bytes_accessed=8 * table.size, transcendentals=0
        ),
        name=name,
    )(table, ids)


def pack(expert_lines, place, plan, piece, rows, block_rows, deep):
    experts, _, lines, width = expert_lines.shape
    first, count = piece
    span = 2 - experts % 2
    return pl.pallas_call(
        functools.partial(pack_kernel, rows, span, experts // span),
        grid_spec=pltpu.PrefetchScalarGridSpec(
            num_scalar_prefetch=1,
            grid=(count, experts // span),
            in_specs=[
                pl.BlockSpec((span, 1, place.shape[2]), lambda p, e, plan: (e, 0, 0)),
                pl.BlockSpec((span, 1, lines, width), lambda p, e, plan: (e, first + p, 0, 0)),
            ],
            out_specs=pl.BlockSpec(memory_space=pltpu.HBM),
            scratch_shapes=[
                pltpu.VMEM((rows, block_rows + STRAIGHT * TILE, width), jnp.bfloat16),
                pltpu.VMEM((256, lines), jnp.bfloat16),
                pltpu.SemaphoreType.DMA((experts // span,)),
            ]
            + [pltpu.VMEM((deep + STRAIGHT * TILE, width), jnp.bfloat16)] * span,
        ),
        out_shape=jax.ShapeDtypeStruct((rows, count, block_rows, width), jnp.bfloat16),
        compiler_params=pltpu.CompilerParams(vmem_limit_bytes=PACK_LIMIT),
        cost_estimate=pl.CostEstimate(
            flops=2 * count * experts * deep * lines * width,
            bytes_accessed=4 * count * experts * lines * width,
            transcendentals=0,
        ),
        name="pack_lines",
    )(plan, place, expert_lines)


def unpack(arrived, place, plan, piece, shape, deep, slot, previous):
    experts, _, lines, width = shape
    first, count = piece
    span = 2 - experts % 2
    in_specs = [
        pl.BlockSpec((span, 2, lines, LANES), lambda e, plan: (e, 0, 0, 0)),
        pl.BlockSpec(memory_space=pl.ANY),
    ]
    operands = [plan, place, arrived]
    aliases = {}
    if previous is not None:
        in_specs.append(pl.BlockSpec(memory_space=pl.ANY))
        operands.append(previous)
        aliases = {3: 0}
    return pl.pallas_call(
        functools.partial(unpack_kernel, slot, span),
        grid_spec=pltpu.PrefetchScalarGridSpec(
            num_scalar_prefetch=1,
            grid=(experts // span,),
            in_specs=in_specs,
            out_specs=pl.BlockSpec(
                (span, count, lines, width), lambda e, plan: (e, first // count, 0, 0)
            ),
            scratch_shapes=[
                pltpu.VMEM((2, span, count, deep, width), jnp.bfloat16),
                pltpu.SemaphoreType.DMA((2, span)),
            ],
        ),
        out_shape=jax.ShapeDtypeStruct(shape, jnp.bfloat16),
        input_output_aliases=aliases,
        compiler_params=params(),
        cost_estimate=pl.CostEstimate(
            flops=2 * count * experts * deep * lines * width,
            bytes_accessed=4 * count * experts * lines * width,
            transcendentals=0,
        ),
        name="unpack_lines",
    )(*operands)


def after_kernel(*refs):
    del refs


def after(values, signals):
    anywhere = pl.BlockSpec(memory_space=pl.ANY)
    return pl.pallas_call(
        after_kernel,
        in_specs=[anywhere] * (len(values) + len(signals)),
        out_specs=[anywhere] * len(values),
        out_shape=[jax.ShapeDtypeStruct(v.shape, v.dtype) for v in values],
        input_output_aliases={n: n for n in range(len(values))},
        compiler_params=pltpu.CompilerParams(vmem_limit_bytes=PACK_LIMIT),
        name="after",
    )(*values, *signals)


def own_ids(table, lines, width):
    mine = lax.dynamic_slice_in_dim(table, lax.axis_index("row") * lines, lines, 1)
    return jnp.pad(mine, ((0, 0), (0, width - lines)), constant_values=-1)


def from_peer(block, axis, offset):
    size = lax.axis_size(axis)
    return lax.ppermute(block, axis, [(i, i ^ offset) for i in range(size)])


class Migration:
    def __init__(self, expert_lines, old_lines, new_lines):
        rows = lax.axis_size("row")
        experts, parts, lines, width = expert_lines.shape
        padded = up_to(lines, LANES)
        block_rows = up_to(experts * lines // rows, TILE)
        pairs = experts * rows
        compact = up_to(lines + 2 * (TILE - 1) * rows, TILE)
        self.slot = min(SLOT, block_rows // TILE)
        self.deep = up_to(max(compact, rows * self.slot * TILE), 256)
        self.shape = expert_lines.shape
        self.pieces = [(parts - 1, 1), (0, parts - 1)]
        out_place, out_plan = call_plan(
            functools.partial(outgoing_kernel, lines, rows), "outgoing_plan",
            new_lines, own_ids(old_lines, lines, padded), pairs,
            jax.ShapeDtypeStruct((experts, 1, padded), jnp.int32),
        )
        self.in_place, self.in_plan = call_plan(
            functools.partial(incoming_kernel, lines, rows, block_rows // TILE, self.slot),
            "incoming_plan",
            old_lines, own_ids(new_lines, lines, padded), pairs,
            jax.ShapeDtypeStruct((experts, 2, lines, LANES), jnp.bfloat16),
        )
        self.packed = [
            pack(expert_lines, out_place, out_plan, piece, rows, block_rows, compact)
            for piece in self.pieces
        ]
        self.arrived = []
        self.moved = None

    def send(self, signals=()):
        block = self.packed[len(self.arrived)]
        if signals:
            (block,) = after([block], signals)
        self.arrived.append(
            lax.all_to_all(block, "row", split_axis=0, concat_axis=0, tiled=True)
        )

    def receive(self, piece):
        self.moved = unpack(
            self.arrived[piece], self.in_place, self.in_plan, self.pieces[piece], self.shape,
            self.deep, self.slot, self.moved,
        )


def attend(queries, new_kv, prompt_kv, suffix_kv, lengths):
    seq_count = queries.shape[0]
    prompt_rows = prompt_kv.shape[2]
    suffix_rows = suffix_kv.shape[2]
    col_index = lax.axis_index("col")
    query_heads = queries.reshape(seq_count, KVH, REP, HD)
    prompt_keys = prompt_kv[0, 0].reshape(prompt_rows, KVH, HD)
    prompt_values = prompt_kv[0, 1].reshape(prompt_rows, KVH, HD)
    suffix_keys = suffix_kv[:, 0].reshape(seq_count, suffix_rows, KVH, HD)
    suffix_values = suffix_kv[:, 1].reshape(seq_count, suffix_rows, KVH, HD)
    own_keys = new_kv[:, 0].reshape(seq_count, KVH, HD)
    own_values = new_kv[:, 1].reshape(seq_count, KVH, HD)
    score_scale = HD ** (-0.5)
    prompt_scores = (
        jnp.einsum("skgd,pkd->skgp", query_heads, prompt_keys, preferred_element_type=jnp.float32)
        * score_scale
    )
    suffix_scores = (
        jnp.einsum("skgd,spkd->skgp", query_heads, suffix_keys, preferred_element_type=jnp.float32)
        * score_scale
    )
    own_scores = (
        jnp.einsum("skgd,skd->skg", query_heads, own_keys, preferred_element_type=jnp.float32)
        * score_scale
    )
    positions = col_index * suffix_rows + jnp.arange(suffix_rows, dtype=jnp.int32)
    live_slots = (positions[None, :] < lengths[:, None])[:, None, None, :]
    holder = col_index == 0
    suffix_scores = jnp.where(live_slots, suffix_scores, neg_big)
    own_scores = jnp.where(holder, own_scores, neg_big)
    highest = jnp.maximum(
        jnp.maximum(jnp.max(prompt_scores, axis=-1), jnp.max(suffix_scores, axis=-1)), own_scores
    )
    prompt_weights = jnp.exp(prompt_scores - highest[..., None])
    suffix_weights = jnp.where(live_slots, jnp.exp(suffix_scores - highest[..., None]), 0.0)
    own_weights = jnp.where(holder, jnp.exp(own_scores - highest), 0.0)
    totals = jnp.sum(prompt_weights, axis=-1) + jnp.sum(suffix_weights, axis=-1) + own_weights
    mixture = jnp.einsum(
        "skgp,pkd->skgd",
        prompt_weights.astype(jnp.bfloat16),
        prompt_values,
        preferred_element_type=jnp.float32,
    )
    mixture = mixture + jnp.einsum(
        "skgp,spkd->skgd",
        suffix_weights.astype(jnp.bfloat16),
        suffix_values,
        preferred_element_type=jnp.float32,
    )
    own_rounded = lax.optimization_barrier(own_weights.astype(jnp.bfloat16)).astype(jnp.float32)
    mixture = mixture + own_rounded[..., None] * own_values.astype(jnp.float32)[:, :, None, :]
    heads = KVH * REP
    bundle = jnp.concatenate(
        [
            mixture.reshape(seq_count, heads * HD),
            highest.reshape(seq_count, heads),
            totals.reshape(seq_count, heads),
            jnp.zeros((seq_count, LANES - 2 * heads), jnp.float32),
        ],
        axis=1,
    )
    bundles = [bundle] + [from_peer(bundle, "col", o) for o in range(1, lax.axis_size("col"))]
    every = jnp.stack(bundles)
    mixtures = every[:, :, : heads * HD].reshape(-1, seq_count, heads, HD)
    peaks = every[:, :, heads * HD : heads * HD + heads]
    sums = every[:, :, heads * HD + heads : heads * HD + 2 * heads]
    factors = jnp.exp(peaks - jnp.max(peaks, axis=0))
    total = jnp.sum(sums * factors, axis=0)
    mixed = jnp.sum(mixtures * factors[..., None], axis=0)
    return (mixed / total[..., None]).astype(jnp.bfloat16).reshape(seq_count, heads * HD)


def gate_up_kernel(me_ref, h_ref, gain_ref, router_ref, routes_ref, gate_ref, up_ref, out_ref, acc_ref):
    e = pl.program_id(0)
    tokens = h_ref.shape[0]
    lines = gate_ref.shape[2]
    padded = out_ref.shape[3]
    h = h_ref[...].astype(jnp.float32)
    scaled = (h * gain_ref[...].astype(jnp.float32)).astype(jnp.bfloat16)

    @pl.when(e == 0)
    def _():
        acc_ref[...] = jnp.zeros_like(acc_ref)

    against = (((1,), (1,)), ((), ()))
    gate = lax.dot_general(scaled, gate_ref[0, 0], against, preferred_element_type=jnp.float32)
    up = lax.dot_general(scaled, up_ref[0, 0], against, preferred_element_type=jnp.float32)
    for k in range(routes_ref.shape[1]):
        chosen = routes_ref[:, k : k + 1] == e
        acc_ref[2 * k, :, :lines] += jnp.where(chosen, gate, 0.0)
        acc_ref[2 * k + 1, :, :lines] += jnp.where(chosen, up, 0.0)

    @pl.when(e == pl.num_programs(0) - 1)
    def _():
        last = padded - LANES
        shift = lines - last
        experts = pl.num_programs(0)
        extra = jnp.dot(scaled, router_ref[...], preferred_element_type=jnp.float32)
        lane = iota((tokens, LANES), 1)
        square = jnp.sum(h * h, axis=1, keepdims=True)
        extra = jnp.where(lane == shift + experts, square, extra)
        high = extra.astype(jnp.bfloat16).astype(jnp.float32)
        low = extra - high
        acc_ref[0, :, last:] += jnp.where(lane >= shift, high, 0.0)
        acc_ref[1, :, last:] += jnp.where(lane >= shift, low, 0.0)
        peers, _, share, _ = out_ref.shape
        me = me_ref[0]
        for o in range(peers):
            begin = pl.multiple_of((me ^ o) * share, share)
            out_ref[o] = acc_ref[:, pl.ds(begin, share), :].astype(jnp.bfloat16)


def activate_kernel(lines, experts, model_width, routes_ref, *refs):
    out_ref = refs[-1]
    summed = refs[0][...].astype(jnp.float32)
    for ref in refs[1:-1]:
        summed = summed + ref[...].astype(jnp.float32)
    _, share, padded = summed.shape
    last = padded - LANES
    shift = lines - last
    extra = summed[0, :, last:] + summed[1, :, last:]
    lane = iota((share, LANES), 1)
    square = jnp.sum(jnp.where(lane == shift + experts, extra, 0.0), axis=1, keepdims=True)
    inverse_rms = lax.rsqrt(square / model_width + norm_eps)
    logits = []
    for k in range(out_ref.shape[0]):
        wanted = lane == routes_ref[:, k : k + 1] + shift
        logits.append(jnp.sum(jnp.where(wanted, extra, 0.0), axis=1, keepdims=True) * inverse_rms)
    peak = functools.reduce(jnp.maximum, logits)
    shares = [jnp.exp(v - peak) for v in logits]
    total = functools.reduce(jnp.add, shares)
    inside = iota((share, padded), 1) < lines
    for k in range(out_ref.shape[0]):
        gate = summed[2 * k] * inverse_rms
        up = summed[2 * k + 1] * inverse_rms
        act = gate / (1.0 + jnp.exp(-gate)) * up
        out_ref[k] = jnp.where(inside, act * (shares[k] / total), 0.0).astype(jnp.bfloat16)


def down_kernel(me_ref, routes_ref, *refs):
    down_ref, out_ref, act_ref = refs[-3:]
    chunks = refs[:-3]
    e = pl.program_id(0)
    topk, share, _ = chunks[0].shape
    lines = down_ref.shape[2]

    @pl.when(e == 0)
    def _():
        me = me_ref[0]
        out_ref[...] = jnp.zeros_like(out_ref)
        for o, chunk in enumerate(chunks):
            begin = pl.multiple_of((me ^ o) * share, share)
            act_ref[:, pl.ds(begin, share), :] = chunk[...]

    mine = jnp.zeros((act_ref.shape[1], lines), jnp.float32)
    for k in range(topk):
        chosen = routes_ref[:, k : k + 1] == e
        mine = mine + jnp.where(chosen, act_ref[k, :, :lines].astype(jnp.float32), 0.0)
    out_ref[...] += jnp.dot(
        mine.astype(jnp.bfloat16), down_ref[0, 0], preferred_element_type=jnp.float32
    )


def experts_part(h_mid, moe_gain, w_router, expert_lines, routes, migration):
    rows = lax.axis_size("row")
    cols = lax.axis_size("col")
    row_index = lax.axis_index("row")
    col_index = lax.axis_index("col")
    experts, _, lines, width = expert_lines.shape
    own, _ = h_mid.shape
    tokens = own * rows
    topk = routes.shape[1]
    share = tokens // cols
    padded = up_to(lines + experts + 1, LANES)
    shift = lines - (padded - LANES)
    me = col_index.astype(jnp.int32).reshape(1)

    order = row_index ^ jnp.array(sorted(range(rows), key=lambda o: (o % 2, o)), jnp.int32)
    routes = routes.reshape(rows, own, topk)[order].reshape(tokens, topk)
    my_routes = lax.dynamic_slice_in_dim(routes, col_index * share, share, 0)
    router = jnp.pad(w_router, ((0, 0), (shift, LANES - shift - experts)))
    same_core = jnp.concatenate(
        [h_mid] + [from_peer(h_mid, "row", o) for o in range(2, rows, 2)], axis=0
    )
    every_h = jnp.concatenate([same_core, from_peer(same_core, "row", 1)], axis=0)
    migration.send([same_core])
    part_spec = lambda part: pl.BlockSpec((1, 1, lines, width), lambda e, me: (e, part, 0, 0))
    whole = lambda a: pl.BlockSpec(a.shape, lambda e, me: (0,) * a.ndim)
    gain = moe_gain.reshape(1, width)
    partial = pl.pallas_call(
        gate_up_kernel,
        grid_spec=pltpu.PrefetchScalarGridSpec(
            num_scalar_prefetch=1,
            grid=(experts,),
            in_specs=[whole(every_h), whole(gain), whole(router), whole(routes)]
            + [part_spec(0), part_spec(1)],
            out_specs=pl.BlockSpec((cols, 2 * topk, share, padded), lambda e, me: (0, 0, 0, 0)),
            scratch_shapes=[pltpu.VMEM((2 * topk, tokens, padded), jnp.float32)],
        ),
        out_shape=jax.ShapeDtypeStruct((cols, 2 * topk, share, padded), jnp.bfloat16),
        compiler_params=params(),
        cost_estimate=pl.CostEstimate(
            flops=4 * experts * tokens * lines * width,
            bytes_accessed=4 * experts * lines * width,
            transcendentals=0,
        ),
        name="gate_up",
    )(me, every_h, gain, router, routes, expert_lines, expert_lines)
    gathered = [partial[0]] + [from_peer(partial[o], "col", o) for o in range(1, cols)]
    activated = pl.pallas_call(
        functools.partial(activate_kernel, lines, experts, width * cols),
        out_shape=jax.ShapeDtypeStruct((topk, share, padded), jnp.bfloat16),
        compiler_params=params(),
        name="activate",
    )(my_routes, *gathered)
    chunks = [activated] + [from_peer(activated, "col", o) for o in range(1, cols)]
    produced = pl.pallas_call(
        down_kernel,
        grid_spec=pltpu.PrefetchScalarGridSpec(
            num_scalar_prefetch=1,
            grid=(experts,),
            in_specs=[whole(routes)] + [whole(c) for c in chunks] + [part_spec(2)],
            out_specs=pl.BlockSpec((tokens, width), lambda e, me: (0, 0)),
            scratch_shapes=[pltpu.VMEM((topk, tokens, padded), jnp.bfloat16)],
        ),
        out_shape=jax.ShapeDtypeStruct((tokens, width), jnp.float32),
        compiler_params=params(),
        cost_estimate=pl.CostEstimate(
            flops=2 * experts * tokens * lines * width,
            bytes_accessed=2 * experts * lines * width,
            transcendentals=0,
        ),
        name="down",
    )(me, routes, *chunks, expert_lines)
    migration.receive(0)
    (produced,) = after([produced], [migration.moved])
    half = tokens // 2
    both_cores = produced[:half] + from_peer(produced[half:], "row", 1)
    blocks = both_cores.reshape(rows // 2, own, width)
    mixed = blocks[0]
    for n in range(1, rows // 2):
        mixed = mixed + from_peer(blocks[n], "row", 2 * n)
    return mixed


def local(
    hidden,
    queries,
    new_kv,
    prompt_kv,
    suffix_kv,
    lengths,
    w_out,
    moe_gain,
    w_router,
    expert_weights,
    old_lines,
    new_lines,
    routes,
):
    expert_lines = jnp.transpose(expert_weights, (0, 2, 1, 3))
    migration = Migration(expert_lines, old_lines, new_lines)
    migration.send()
    attended = attend(queries, new_kv, prompt_kv, suffix_kv, lengths)
    projected = jnp.dot(attended, w_out, preferred_element_type=jnp.float32)
    h_mid = (hidden.astype(jnp.float32) + projected).astype(jnp.bfloat16)
    (h_mid,) = after([h_mid], migration.packed)
    mixed = experts_part(h_mid, moe_gain, w_router, expert_lines, routes, migration)
    migration.receive(1)
    return (h_mid.astype(jnp.float32) + mixed, jnp.transpose(migration.moved, (0, 2, 1, 3)))


def solution(mesh):
    return jax.shard_map(
        local,
        mesh=mesh,
        in_specs=(
            P("row", "col"),
            P("row", None),
            P("row", None, None),
            P("row", None, "col", None),
            P("row", None, "col", None),
            P("row"),
            P(None, "col"),
            P("col"),
            P("col", None),
            P(None, "row", None, "col"),
            P(),
            P(),
            P(),
        ),
        out_specs=(P("row", "col"), P(None, "row", None, "col")),
        check_vma=False,
    )
```

```python
import functools

import jax
import jax.numpy as jnp
from jax import lax
from jax.experimental import pallas as pl
from jax.experimental.pallas import tpu as pltpu
from jax.sharding import PartitionSpec as P

KVH = 16
HD = 128
REP = 2
TILE = 16
LANES = 128

norm_eps = 1e-06
neg_big = -1e30
VMEM_LIMIT = 48 * 1024 * 1024
PACK_LIMIT = 59 * 1024 * 1024


def up_to(value, unit):
    return -(-value // unit) * unit


def iota(shape, axis):
    return lax.broadcasted_iota(jnp.int32, shape, axis)


def ones_where(mask):
    return jnp.where(mask, 1.0, 0.0).astype(jnp.bfloat16)


def params():
    return pltpu.CompilerParams(vmem_limit_bytes=VMEM_LIMIT)


def counting(shape, axis):
    return iota(shape, axis).astype(jnp.float32).astype(jnp.bfloat16)


def as_bf16(values):
    return values.astype(jnp.float32).astype(jnp.bfloat16)


def equal_ones(left, right):
    one = jnp.ones((), jnp.bfloat16)
    return jnp.maximum(one - jnp.abs(left - right), jnp.zeros((), jnp.bfloat16))


def within(place, block):
    place = place - 256 * block
    return as_bf16(jnp.where((place >= 0) & (place < 256), place, -1))


def look_up(table_rows, id_rows, numbers, values):
    full = table_rows[0].shape[1]
    ids = id_rows[0].shape[1]
    high_count = up_to(-(-full // 64), 16)
    zero = jnp.zeros((), jnp.bfloat16)
    highs = [equal_ones(numbers[:high_count], as_bf16(row >> 6)) for row in table_rows]
    lows = []
    for row in table_rows:
        hit = numbers[:64] == as_bf16(row & 63)
        lows += [jnp.where(hit, part, zero) for part in values]
    square = lax.dot_general(
        jnp.concatenate(highs, axis=0),
        jnp.concatenate(lows, axis=0),
        (((1,), (1,)), ((), ())),
        preferred_element_type=jnp.float32,
    )
    wide = 64 * len(values)
    found = []
    for n, row in enumerate(id_rows):
        block = square[n * high_count : (n + 1) * high_count, n * wide : (n + 1) * wide]
        id_high = equal_ones(numbers[:high_count, :ids], as_bf16(row >> 6))
        spread = lax.dot_general(
            block.astype(jnp.bfloat16), id_high, (((0,), (0,)), ((), ())),
            preferred_element_type=jnp.float32,
        )
        wanted = iota((64, ids), 0) == (row & 63)
        found.append(
            [
                jnp.sum(jnp.where(wanted, spread[64 * m : 64 * m + 64], 0.0), axis=0, keepdims=True)
                for m in range(len(values))
            ]
        )
    return found


def look_up_all(table_ref, id_ref, numbers, values):
    experts = table_ref.shape[0]
    group = 4 // len(values)
    found = []
    for first in range(0, experts, group):
        members = range(first, min(first + group, experts))
        found += look_up(
            [table_ref[e : e + 1, :] for e in members],
            [id_ref[e : e + 1, :] for e in members],
            numbers,
            values,
        )
    return found


def numbers_for(full):
    return counting((max(up_to(-(-full // 64), 16), 64), full), 0)


def segment_plan(counts, experts, rows):
    starts = []
    running = jnp.zeros((rows, LANES), jnp.float32)
    for e in range(experts):
        starts.append(running)
        running = running + counts[e * rows : (e + 1) * rows]
    start = jnp.concatenate(starts, axis=0)
    lead = jnp.floor(start * (1.0 / TILE))
    tail = jnp.floor((start + counts + (TILE - 1.0)) * (1.0 / TILE))
    tiles = jnp.where(counts > 0.0, tail - lead, 0.0)
    pairs = experts * rows
    line = iota((pairs, pairs), 0)
    column = iota((pairs, pairs), 1)
    earlier = ones_where((line // rows == column // rows) & (column < line))
    base = jnp.dot(earlier, tiles.astype(jnp.bfloat16), preferred_element_type=jnp.float32)
    return start, lead, tiles, base


def write_plan(plan_ref, parts):
    for n, part in enumerate(parts):
        short = -part.shape[0] % LANES
        if short:
            part = jnp.concatenate([part, jnp.zeros((short, LANES), jnp.float32)], axis=0)
        plan_ref[n : n + 1, :] = jnp.transpose(part)[:1].astype(jnp.int32)


def outgoing_kernel(lines, rows, new_ref, held_ref, stack_ref, plan_ref):
    experts = new_ref.shape[0]
    width = held_ref.shape[1]
    real = iota((1, width), 1) < lines
    hits = []
    full = new_ref.shape[1]
    numbers = numbers_for(full)
    slot = iota((64, full), 1).astype(jnp.float32)
    values = (jnp.floor((slot + 0.5) * (1.0 / lines)).astype(jnp.bfloat16),)
    for (peer,) in look_up_all(new_ref, held_ref, numbers, values):
        peer = peer.astype(jnp.int32)
        hits.append(jnp.where((iota((rows, width), 0) == peer) & real, 1.0, 0.0))
    hits = jnp.concatenate(hits, axis=0)
    until = ones_where(iota((width, width), 0) <= iota((width, width), 1))
    ranks = jnp.dot(hits.astype(jnp.bfloat16), until, preferred_element_type=jnp.float32)
    counts = jnp.broadcast_to(jnp.sum(hits, axis=1, keepdims=True), (experts * rows, LANES))
    start, lead, tiles, base = segment_plan(counts, experts, rows)
    write_plan(plan_ref, (lead, tiles, base, start - lead * TILE))
    offset = (base * TILE + start - lead * TILE - 1.0)[:, :1]
    placed = hits * (ranks + offset)
    for e in range(experts):
        row = jnp.sum(placed[e * rows : (e + 1) * rows], axis=0, keepdims=True)
        stack_ref[e] = jnp.where(real, row, -1.0).astype(jnp.int32)


def incoming_kernel(lines, rows, block_tiles, slot, old_ref, wanted_ref, stack_ref, plan_ref):
    experts = old_ref.shape[0]
    width = wanted_ref.shape[1]
    real = iota((1, width), 1) < lines
    held_at = []
    hits = []
    full = old_ref.shape[1]
    numbers = numbers_for(full)
    at = iota((64, full), 1)
    values = (as_bf16(at >> 7), as_bf16(at & 127))
    for high, low in look_up_all(old_ref, wanted_ref, numbers, values):
        slots = high * 128.0 + low
        held_at.append(jnp.where(real, slots, 1e9))
        peer = jnp.floor((slots + 0.5) * (1.0 / lines)).astype(jnp.int32)
        hits.append(jnp.where((iota((rows, width), 0) == peer) & real, 1.0, 0.0))
    hits = jnp.concatenate(hits, axis=0)
    counts = jnp.broadcast_to(jnp.sum(hits, axis=1, keepdims=True), (experts * rows, LANES))
    start, lead, tiles, base = segment_plan(counts, experts, rows)
    line = iota((experts * rows, LANES), 0)
    peer = (line % rows).astype(jnp.float32)
    longest = [
        jnp.max(tiles[e * rows : (e + 1) * rows], axis=0, keepdims=True) for e in range(experts)
    ]
    longest = jnp.concatenate(
        [jnp.broadcast_to(most, (rows, LANES)) for most in longest], axis=0
    )
    slotted = longest <= slot
    lead = jnp.where(slotted, jnp.minimum(lead, float(block_tiles - slot)), lead)
    base = jnp.where(slotted, peer * slot, base)
    write_plan(plan_ref, (lead, tiles, base, jnp.where(slotted, 1.0, 0.0)))
    blank = jnp.zeros((LANES - experts, width), jnp.float32)
    columns = jnp.transpose(jnp.concatenate(held_at + [blank], axis=0))
    rows_out = []
    for e in range(experts):
        mine = slice(e * rows, (e + 1) * rows)
        before = jnp.where(columns[:, e : e + 1] < held_at[e], 1.0, 0.0)
        rank = jnp.sum(before, axis=0, keepdims=True)
        ahead = jnp.zeros((1, LANES), jnp.float32)
        firsts = []
        for r in range(rows):
            firsts.append(ahead)
            ahead = ahead + counts[e * rows + r : e * rows + r + 1]
        first = jnp.concatenate(firsts, axis=0)
        offset = (base[mine] * TILE + start[mine] - lead[mine] * TILE - first)[:, :1]
        rows_out.append(jnp.sum(hits[mine] * (rank + offset), axis=0, keepdims=True))
    places = jnp.transpose(jnp.concatenate(rows_out + [blank], axis=0))
    for e in range(experts):
        place = jnp.broadcast_to(places[:lines, e : e + 1], (lines, LANES))
        block = jnp.floor(place * (1.0 / 256.0))
        stack_ref[e, 0] = (place - 256.0 * block).astype(jnp.bfloat16)
        stack_ref[e, 1] = block.astype(jnp.bfloat16)


STRAIGHT = 8
SLOT = 7


def tile_at(index):
    return pl.ds(pl.multiple_of(index * TILE, TILE), TILE)


def pack_kernel(rows, span, steps, plan_ref, place_ref, lines_ref, out_ref, packed_ref, number_ref, sems, *stages):
    part = pl.program_id(0)
    step = pl.program_id(1)
    deep = stages[0].shape[0] - STRAIGHT * TILE
    lines = lines_ref.shape[2]

    @pl.when((part == 0) & (step == 0))
    def _():
        number_ref[...] = counting(number_ref.shape, 0)

    def entry(n, j, d):
        return plan_ref[n, (step * span + j) * rows + d]

    usual = min(deep, up_to(lines + rows * TILE, TILE))

    def move(j, begin, end):
        place = place_ref[j][:, :lines]
        onehot = [
            equal_ones(number_ref[: min(256, end - row)], within(place - begin, (row - begin) // 256))
            for row in range(begin, end, 256)
        ]
        stages[j][begin:end] = jnp.dot(
            jnp.concatenate(onehot, axis=0), lines_ref[j, 0], preferred_element_type=jnp.float32
        ).astype(jnp.bfloat16)

    for j in range(span):
        move(j, 0, usual)
    if usual < deep:
        for j in range(span):
            used = entry(1, j, rows - 1) + entry(2, j, rows - 1)

            @pl.when(used * TILE > usual)
            def _(j=j):
                move(j, usual, deep)

    for j, stage_ref in enumerate(stages):

        def one_peer(d, most, j=j, stage_ref=stage_ref):
            lead, tiles, base = entry(0, j, d), entry(1, j, d), entry(2, j, d)
            there = pl.multiple_of(lead * TILE, TILE)
            here = pl.multiple_of(base * TILE, TILE)
            earlier = packed_ref[d, pl.ds(there, TILE), :]
            fresh = stage_ref[pl.ds(here, STRAIGHT * TILE), :]
            packed_ref[d, pl.ds(there + TILE, (STRAIGHT - 1) * TILE), :] = fresh[TILE:]
            kept = jnp.where(entry(3, j, d) > 0, earlier, jnp.zeros_like(earlier))
            added = jnp.where(tiles > 0, fresh[:TILE], jnp.zeros_like(earlier))
            packed_ref[d, pl.ds(there, TILE), :] = kept + added
            return jnp.maximum(most, tiles)

        most = lax.fori_loop(0, rows, one_peer, 0, unroll=rows <= 8)

        @pl.when(most > STRAIGHT)
        def _(j=j, stage_ref=stage_ref):
            def long_peer(d, carry):
                lead, tiles, base = entry(0, j, d), entry(1, j, d), entry(2, j, d)

                def put(t, c):
                    packed_ref[d, tile_at(lead + t), :] = stage_ref[tile_at(base + t), :]
                    return c

                return lax.fori_loop(STRAIGHT, tiles, put, carry)

            lax.fori_loop(0, rows, long_peer, 0)

    block_rows = out_ref.shape[2]
    chunks = []
    begin = 0
    for after_step in range(steps):
        end = block_rows
        if after_step < steps - 1:
            end = max(begin, block_rows * (after_step + 1) // steps // TILE * TILE - 2 * TILE)
        if end > begin:
            chunks.append((after_step, begin, end))
        begin = end

    def chunk_copy(n):
        _, begin, end = chunks[n]
        here = pl.ds(begin, end - begin)
        return pltpu.make_async_copy(
            packed_ref.at[:, here], out_ref.at[:, part, here], sems.at[n]
        )

    def final_by(n):
        after_step, _, end = chunks[n]
        first = (after_step + 1) * span * rows
        least = functools.reduce(jnp.minimum, [plan_ref[0, first + d] for d in range(rows)])
        return least * TILE >= end

    for n in range(len(chunks) - 1):

        @pl.when((step == chunks[n][0]) & final_by(n))
        def _(n=n):
            chunk_copy(n).start()

    @pl.when(step == steps - 1)
    def _():
        for n in range(len(chunks) - 1):

            @pl.when(jnp.logical_not(final_by(n)))
            def _(n=n):
                chunk_copy(n).start()

        chunk_copy(len(chunks) - 1).start()
        for n in range(len(chunks)):
            chunk_copy(n).wait()


def unpack_kernel(slot, span, plan_ref, place_ref, block_ref, *rest):
    out_ref, stage_ref, sems = rest[-3:]
    step = pl.program_id(0)
    steps = pl.num_programs(0)
    rows, count, _, width = block_ref.shape
    deep = stage_ref.shape[3]
    lines = out_ref.shape[2]
    buffer = step % 2

    def entry(n, e, s):
        return plan_ref[n, e * rows + s]

    def slotted(e):
        return entry(3, e, 0) > 0

    def begin(step, j):
        e = step * span + j

        @pl.when(slotted(e))
        def _():
            for s in range(rows):
                there = pl.ds(pl.multiple_of(entry(0, e, s) * TILE, TILE), slot * TILE)
                here = pl.ds(s * slot * TILE, slot * TILE)
                pltpu.make_async_copy(
                    block_ref.at[s, :, there],
                    stage_ref.at[step % 2, j, :, here],
                    sems.at[step % 2, j],
                ).start()

    @pl.when(step == 0)
    def _():
        for j in range(span):
            begin(step, j)

    lane = counting((lines, LANES), 1)

    def multiply(j, depth):
        within_block, block = place_ref[j, 0], place_ref[j, 1]
        pieces = []
        for first in range(0, depth, LANES):
            away = jnp.abs(block - jnp.asarray(first // 256, jnp.bfloat16))
            place = within_block + away * jnp.asarray(512, jnp.bfloat16)
            pieces.append(equal_ones(lane + jnp.asarray(first % 256, jnp.bfloat16), place))
        onehot = jnp.concatenate(pieces, axis=1)
        for part in range(count):
            out_ref[j, part] = jnp.dot(
                onehot, stage_ref[buffer, j, part, :depth], preferred_element_type=jnp.float32
            ).astype(jnp.bfloat16)

    for j in range(span):
        e = step * span + j
        staged = rows * slot * TILE

        @pl.when(slotted(e))
        def _(j=j):
            all_slots = stage_ref.at[buffer, j, :, pl.ds(0, staged)]
            pltpu.make_async_copy(all_slots, all_slots, sems.at[buffer, j]).wait()

        @pl.when(step + 1 < steps)
        def _(j=j):
            begin(step + 1, j)

        @pl.when(slotted(e))
        def _(j=j):
            if staged % LANES:
                stage_ref[buffer, j, :, staged:] = jnp.zeros(
                    (count, deep - staged, width), jnp.bfloat16
                )
                multiply(j, deep)
            else:
                multiply(j, staged)

        @pl.when(jnp.logical_not(slotted(e)))
        def _(e=e, j=j):
            stage_ref[buffer, j] = jnp.zeros((count, deep, width), jnp.bfloat16)

            def one_peer(s, carry):
                def put(t, c):
                    copy = pltpu.make_async_copy(
                        block_ref.at[s, :, tile_at(entry(0, e, s) + t)],
                        stage_ref.at[buffer, j, :, tile_at(entry(2, e, s) + t)],
                        sems.at[buffer, j],
                    )
                    copy.start()
                    copy.wait()
                    return c

                return lax.fori_loop(0, entry(1, e, s), put, carry)

            lax.fori_loop(0, rows, one_peer, 0)
            multiply(j, deep)


def call_plan(kernel, name, table, ids, pairs, place):
    return pl.pallas_call(
        kernel,
        out_shape=(place, jax.ShapeDtypeStruct((4, up_to(pairs, LANES)), jnp.int32)),
        compiler_params=params(),
        cost_estimate=pl.CostEstimate(
            flops=20 * table.size * 256, bytes_accessed=8 * table.size, transcendentals=0
        ),
        name=name,
    )(table, ids)


def pack(expert_lines, place, plan, piece, rows, block_rows, deep):
    experts, _, lines, width = expert_lines.shape
    first, count = piece
    span = 2 - experts % 2
    return pl.pallas_call(
        functools.partial(pack_kernel, rows, span, experts // span),
        grid_spec=pltpu.PrefetchScalarGridSpec(
            num_scalar_prefetch=1,
            grid=(count, experts // span),
            in_specs=[
                pl.BlockSpec((span, 1, place.shape[2]), lambda p, e, plan: (e, 0, 0)),
                pl.BlockSpec((span, 1, lines, width), lambda p, e, plan: (e, first + p, 0, 0)),
            ],
            out_specs=pl.BlockSpec(memory_space=pltpu.HBM),
            scratch_shapes=[
                pltpu.VMEM((rows, block_rows + STRAIGHT * TILE, width), jnp.bfloat16),
                pltpu.VMEM((256, lines), jnp.bfloat16),
                pltpu.SemaphoreType.DMA((experts // span,)),
            ]
            + [pltpu.VMEM((deep + STRAIGHT * TILE, width), jnp.bfloat16)] * span,
        ),
        out_shape=jax.ShapeDtypeStruct((rows, count, block_rows, width), jnp.bfloat16),
        compiler_params=pltpu.CompilerParams(vmem_limit_bytes=PACK_LIMIT),
        cost_estimate=pl.CostEstimate(
            flops=2 * count * experts * deep * lines * width,
            bytes_accessed=4 * count * experts * lines * width,
            transcendentals=0,
        ),
        name="pack_lines",
    )(plan, place, expert_lines)


def unpack(arrived, place, plan, piece, shape, deep, slot, previous):
    experts, _, lines, width = shape
    first, count = piece
    span = 2 - experts % 2
    in_specs = [
        pl.BlockSpec((span, 2, lines, LANES), lambda e, plan: (e, 0, 0, 0)),
        pl.BlockSpec(memory_space=pl.ANY),
    ]
    operands = [plan, place, arrived]
    aliases = {}
    if previous is not None:
        in_specs.append(pl.BlockSpec(memory_space=pl.ANY))
        operands.append(previous)
        aliases = {3: 0}
    return pl.pallas_call(
        functools.partial(unpack_kernel, slot, span),
        grid_spec=pltpu.PrefetchScalarGridSpec(
            num_scalar_prefetch=1,
            grid=(experts // span,),
            in_specs=in_specs,
            out_specs=pl.BlockSpec(
                (span, count, lines, width), lambda e, plan: (e, first // count, 0, 0)
            ),
            scratch_shapes=[
                pltpu.VMEM((2, span, count, deep, width), jnp.bfloat16),
                pltpu.SemaphoreType.DMA((2, span)),
            ],
        ),
        out_shape=jax.ShapeDtypeStruct(shape, jnp.bfloat16),
        input_output_aliases=aliases,
        compiler_params=params(),
        cost_estimate=pl.CostEstimate(
            flops=2 * count * experts * deep * lines * width,
            bytes_accessed=4 * count * experts * lines * width,
            transcendentals=0,
        ),
        name="unpack_lines",
    )(*operands)


def after_kernel(*refs):
    del refs


def after(values, signals):
    anywhere = pl.BlockSpec(memory_space=pl.ANY)
    return pl.pallas_call(
        after_kernel,
        in_specs=[anywhere] * (len(values) + len(signals)),
        out_specs=[anywhere] * len(values),
        out_shape=[jax.ShapeDtypeStruct(v.shape, v.dtype) for v in values],
        input_output_aliases={n: n for n in range(len(values))},
        compiler_params=pltpu.CompilerParams(vmem_limit_bytes=PACK_LIMIT),
        name="after",
    )(*values, *signals)


def own_ids(table, lines, width):
    mine = lax.dynamic_slice_in_dim(table, lax.axis_index("row") * lines, lines, 1)
    return jnp.pad(mine, ((0, 0), (0, width - lines)), constant_values=-1)


def from_peer(block, axis, offset):
    size = lax.axis_size(axis)
    return lax.ppermute(block, axis, [(i, i ^ offset) for i in range(size)])


class Migration:
    def __init__(self, expert_lines, old_lines, new_lines):
        rows = lax.axis_size("row")
        experts, parts, lines, width = expert_lines.shape
        padded = up_to(lines, LANES)
        block_rows = up_to(experts * lines // rows, TILE)
        pairs = experts * rows
        compact = up_to(lines + 2 * (TILE - 1) * rows, TILE)
        self.slot = min(SLOT, block_rows // TILE)
        self.deep = up_to(max(compact, rows * self.slot * TILE), 256)
        self.shape = expert_lines.shape
        self.pieces = [(parts - 1, 1), (0, parts - 1)]
        out_place, out_plan = call_plan(
            functools.partial(outgoing_kernel, lines, rows), "outgoing_plan",
            new_lines, own_ids(old_lines, lines, padded), pairs,
            jax.ShapeDtypeStruct((experts, 1, padded), jnp.int32),
        )
        self.in_place, self.in_plan = call_plan(
            functools.partial(incoming_kernel, lines, rows, block_rows // TILE, self.slot),
            "incoming_plan",
            old_lines, own_ids(new_lines, lines, padded), pairs,
            jax.ShapeDtypeStruct((experts, 2, lines, LANES), jnp.bfloat16),
        )
        self.packed = [
            pack(expert_lines, out_place, out_plan, piece, rows, block_rows, compact)
            for piece in self.pieces
        ]
        self.arrived = []
        self.moved = None

    def send(self, signals=()):
        block = self.packed[len(self.arrived)]
        if signals:
            (block,) = after([block], signals)
        self.arrived.append(
            lax.all_to_all(block, "row", split_axis=0, concat_axis=0, tiled=True)
        )

    def receive(self, piece):
        self.moved = unpack(
            self.arrived[piece], self.in_place, self.in_plan, self.pieces[piece], self.shape,
            self.deep, self.slot, self.moved,
        )


def attend(queries, new_kv, prompt_kv, suffix_kv, lengths):
    seq_count = queries.shape[0]
    prompt_rows = prompt_kv.shape[2]
    suffix_rows = suffix_kv.shape[2]
    col_index = lax.axis_index("col")
    query_heads = queries.reshape(seq_count, KVH, REP, HD)
    prompt_keys = prompt_kv[0, 0].reshape(prompt_rows, KVH, HD)
    prompt_values = prompt_kv[0, 1].reshape(prompt_rows, KVH, HD)
    suffix_keys = suffix_kv[:, 0].reshape(seq_count, suffix_rows, KVH, HD)
    suffix_values = suffix_kv[:, 1].reshape(seq_count, suffix_rows, KVH, HD)
    own_keys = new_kv[:, 0].reshape(seq_count, KVH, HD)
    own_values = new_kv[:, 1].reshape(seq_count, KVH, HD)
    score_scale = HD ** (-0.5)
    prompt_scores = (
        jnp.einsum("skgd,pkd->skgp", query_heads, prompt_keys, preferred_element_type=jnp.float32)
        * score_scale
    )
    suffix_scores = (
        jnp.einsum("skgd,spkd->skgp", query_heads, suffix_keys, preferred_element_type=jnp.float32)
        * score_scale
    )
    own_scores = (
        jnp.einsum("skgd,skd->skg", query_heads, own_keys, preferred_element_type=jnp.float32)
        * score_scale
    )
    positions = col_index * suffix_rows + jnp.arange(suffix_rows, dtype=jnp.int32)
    live_slots = (positions[None, :] < lengths[:, None])[:, None, None, :]
    holder = col_index == 0
    suffix_scores = jnp.where(live_slots, suffix_scores, neg_big)
    own_scores = jnp.where(holder, own_scores, neg_big)
    highest = jnp.maximum(
        jnp.maximum(jnp.max(prompt_scores, axis=-1), jnp.max(suffix_scores, axis=-1)), own_scores
    )
    prompt_weights = jnp.exp(prompt_scores - highest[..., None])
    suffix_weights = jnp.where(live_slots, jnp.exp(suffix_scores - highest[..., None]), 0.0)
    own_weights = jnp.where(holder, jnp.exp(own_scores - highest), 0.0)
    totals = jnp.sum(prompt_weights, axis=-1) + jnp.sum(suffix_weights, axis=-1) + own_weights
    mixture = jnp.einsum(
        "skgp,pkd->skgd",
        prompt_weights.astype(jnp.bfloat16),
        prompt_values,
        preferred_element_type=jnp.float32,
    )
    mixture = mixture + jnp.einsum(
        "skgp,spkd->skgd",
        suffix_weights.astype(jnp.bfloat16),
        suffix_values,
        preferred_element_type=jnp.float32,
    )
    own_rounded = lax.optimization_barrier(own_weights.astype(jnp.bfloat16)).astype(jnp.float32)
    mixture = mixture + own_rounded[..., None] * own_values.astype(jnp.float32)[:, :, None, :]
    heads = KVH * REP
    bundle = jnp.concatenate(
        [
            mixture.reshape(seq_count, heads * HD),
            highest.reshape(seq_count, heads),
            totals.reshape(seq_count, heads),
            jnp.zeros((seq_count, LANES - 2 * heads), jnp.float32),
        ],
        axis=1,
    )
    bundles = [bundle] + [from_peer(bundle, "col", o) for o in range(1, lax.axis_size("col"))]
    every = jnp.stack(bundles)
    mixtures = every[:, :, : heads * HD].reshape(-1, seq_count, heads, HD)
    peaks = every[:, :, heads * HD : heads * HD + heads]
    sums = every[:, :, heads * HD + heads : heads * HD + 2 * heads]
    factors = jnp.exp(peaks - jnp.max(peaks, axis=0))
    total = jnp.sum(sums * factors, axis=0)
    mixed = jnp.sum(mixtures * factors[..., None], axis=0)
    return (mixed / total[..., None]).astype(jnp.bfloat16).reshape(seq_count, heads * HD)


def gate_up_kernel(me_ref, h_ref, gain_ref, router_ref, routes_ref, gate_ref, up_ref, out_ref, acc_ref):
    e = pl.program_id(0)
    tokens = h_ref.shape[0]
    lines = gate_ref.shape[2]
    padded = out_ref.shape[3]
    h = h_ref[...].astype(jnp.float32)
    scaled = (h * gain_ref[...].astype(jnp.float32)).astype(jnp.bfloat16)

    @pl.when(e == 0)
    def _():
        acc_ref[...] = jnp.zeros_like(acc_ref)

    against = (((1,), (1,)), ((), ()))
    gate = lax.dot_general(scaled, gate_ref[0, 0], against, preferred_element_type=jnp.float32)
    up = lax.dot_general(scaled, up_ref[0, 0], against, preferred_element_type=jnp.float32)
    for k in range(routes_ref.shape[1]):
        chosen = routes_ref[:, k : k + 1] == e
        acc_ref[2 * k, :, :lines] += jnp.where(chosen, gate, 0.0)
        acc_ref[2 * k + 1, :, :lines] += jnp.where(chosen, up, 0.0)

    @pl.when(e == pl.num_programs(0) - 1)
    def _():
        last = padded - LANES
        shift = lines - last
        experts = pl.num_programs(0)
        extra = jnp.dot(scaled, router_ref[...], preferred_element_type=jnp.float32)
        lane = iota((tokens, LANES), 1)
        square = jnp.sum(h * h, axis=1, keepdims=True)
        extra = jnp.where(lane == shift + experts, square, extra)
        high = extra.astype(jnp.bfloat16).astype(jnp.float32)
        low = extra - high
        acc_ref[0, :, last:] += jnp.where(lane >= shift, high, 0.0)
        acc_ref[1, :, last:] += jnp.where(lane >= shift, low, 0.0)
        peers, _, share, _ = out_ref.shape
        me = me_ref[0]
        for o in range(peers):
            begin = pl.multiple_of((me ^ o) * share, share)
            out_ref[o] = acc_ref[:, pl.ds(begin, share), :].astype(jnp.bfloat16)


def activate_kernel(lines, experts, model_width, routes_ref, *refs):
    out_ref = refs[-1]
    summed = refs[0][...].astype(jnp.float32)
    for ref in refs[1:-1]:
        summed = summed + ref[...].astype(jnp.float32)
    _, share, padded = summed.shape
    last = padded - LANES
    shift = lines - last
    extra = summed[0, :, last:] + summed[1, :, last:]
    lane = iota((share, LANES), 1)
    square = jnp.sum(jnp.where(lane == shift + experts, extra, 0.0), axis=1, keepdims=True)
    inverse_rms = lax.rsqrt(square / model_width + norm_eps)
    logits = []
    for k in range(out_ref.shape[0]):
        wanted = lane == routes_ref[:, k : k + 1] + shift
        logits.append(jnp.sum(jnp.where(wanted, extra, 0.0), axis=1, keepdims=True) * inverse_rms)
    peak = functools.reduce(jnp.maximum, logits)
    shares = [jnp.exp(v - peak) for v in logits]
    total = functools.reduce(jnp.add, shares)
    inside = iota((share, padded), 1) < lines
    for k in range(out_ref.shape[0]):
        gate = summed[2 * k] * inverse_rms
        up = summed[2 * k + 1] * inverse_rms
        act = gate / (1.0 + jnp.exp(-gate)) * up
        out_ref[k] = jnp.where(inside, act * (shares[k] / total), 0.0).astype(jnp.bfloat16)


def down_kernel(me_ref, routes_ref, *refs):
    down_ref, out_ref, act_ref = refs[-3:]
    chunks = refs[:-3]
    e = pl.program_id(0)
    topk, share, _ = chunks[0].shape
    lines = down_ref.shape[2]

    @pl.when(e == 0)
    def _():
        me = me_ref[0]
        out_ref[...] = jnp.zeros_like(out_ref)
        for o, chunk in enumerate(chunks):
            begin = pl.multiple_of((me ^ o) * share, share)
            act_ref[:, pl.ds(begin, share), :] = chunk[...]

    mine = jnp.zeros((act_ref.shape[1], lines), jnp.float32)
    for k in range(topk):
        chosen = routes_ref[:, k : k + 1] == e
        mine = mine + jnp.where(chosen, act_ref[k, :, :lines].astype(jnp.float32), 0.0)
    out_ref[...] += jnp.dot(
        mine.astype(jnp.bfloat16), down_ref[0, 0], preferred_element_type=jnp.float32
    )


def experts_part(h_mid, moe_gain, w_router, expert_lines, routes, migration):
    rows = lax.axis_size("row")
    cols = lax.axis_size("col")
    row_index = lax.axis_index("row")
    col_index = lax.axis_index("col")
    experts, _, lines, width = expert_lines.shape
    own, _ = h_mid.shape
    tokens = own * rows
    topk = routes.shape[1]
    share = tokens // cols
    padded = up_to(lines + experts + 1, LANES)
    shift = lines - (padded - LANES)
    me = col_index.astype(jnp.int32).reshape(1)

    order = row_index ^ jnp.array(sorted(range(rows), key=lambda o: (o % 2, o)), jnp.int32)
    routes = routes.reshape(rows, own, topk)[order].reshape(tokens, topk)
    my_routes = lax.dynamic_slice_in_dim(routes, col_index * share, share, 0)
    router = jnp.pad(w_router, ((0, 0), (shift, LANES - shift - experts)))
    across = [from_peer(h_mid, "row", o) for o in range(2, rows, 2)]
    same_core = jnp.concatenate([h_mid] + across, axis=0)
    every_h = jnp.concatenate([same_core, from_peer(same_core, "row", 1)], axis=0)
    migration.send(across)
    part_spec = lambda part: pl.BlockSpec((1, 1, lines, width), lambda e, me: (e, part, 0, 0))
    whole = lambda a: pl.BlockSpec(a.shape, lambda e, me: (0,) * a.ndim)
    gain = moe_gain.reshape(1, width)
    partial = pl.pallas_call(
        gate_up_kernel,
        grid_spec=pltpu.PrefetchScalarGridSpec(
            num_scalar_prefetch=1,
            grid=(experts,),
            in_specs=[whole(every_h), whole(gain), whole(router), whole(routes)]
            + [part_spec(0), part_spec(1)],
            out_specs=pl.BlockSpec((cols, 2 * topk, share, padded), lambda e, me: (0, 0, 0, 0)),
            scratch_shapes=[pltpu.VMEM((2 * topk, tokens, padded), jnp.float32)],
        ),
        out_shape=jax.ShapeDtypeStruct((cols, 2 * topk, share, padded), jnp.bfloat16),
        compiler_params=params(),
        cost_estimate=pl.CostEstimate(
            flops=4 * experts * tokens * lines * width,
            bytes_accessed=4 * experts * lines * width,
            transcendentals=0,
        ),
        name="gate_up",
    )(me, every_h, gain, router, routes, expert_lines, expert_lines)
    gathered = [partial[0]] + [from_peer(partial[o], "col", o) for o in range(1, cols)]
    activated = pl.pallas_call(
        functools.partial(activate_kernel, lines, experts, width * cols),
        out_shape=jax.ShapeDtypeStruct((topk, share, padded), jnp.bfloat16),
        compiler_params=params(),
        name="activate",
    )(my_routes, *gathered)
    chunks = [activated] + [from_peer(activated, "col", o) for o in range(1, cols)]
    produced = pl.pallas_call(
        down_kernel,
        grid_spec=pltpu.PrefetchScalarGridSpec(
            num_scalar_prefetch=1,
            grid=(experts,),
            in_specs=[whole(routes)] + [whole(c) for c in chunks] + [part_spec(2)],
            out_specs=pl.BlockSpec((tokens, width), lambda e, me: (0, 0)),
            scratch_shapes=[pltpu.VMEM((topk, tokens, padded), jnp.bfloat16)],
        ),
        out_shape=jax.ShapeDtypeStruct((tokens, width), jnp.float32),
        compiler_params=params(),
        cost_estimate=pl.CostEstimate(
            flops=2 * experts * tokens * lines * width,
            bytes_accessed=2 * experts * lines * width,
            transcendentals=0,
        ),
        name="down",
    )(me, routes, *chunks, expert_lines)
    migration.receive(0)
    (produced,) = after([produced], [migration.moved])
    half = tokens // 2
    both_cores = produced[:half] + from_peer(produced[half:], "row", 1)
    blocks = both_cores.reshape(rows // 2, own, width)
    mixed = blocks[0]
    for n in range(1, rows // 2):
        mixed = mixed + from_peer(blocks[n], "row", 2 * n)
    return mixed


def local(
    hidden,
    queries,
    new_kv,
    prompt_kv,
    suffix_kv,
    lengths,
    w_out,
    moe_gain,
    w_router,
    expert_weights,
    old_lines,
    new_lines,
    routes,
):
    expert_lines = jnp.transpose(expert_weights, (0, 2, 1, 3))
    migration = Migration(expert_lines, old_lines, new_lines)
    migration.send()
    attended = attend(queries, new_kv, prompt_kv, suffix_kv, lengths)
    projected = jnp.dot(attended, w_out, preferred_element_type=jnp.float32)
    h_mid = (hidden.astype(jnp.float32) + projected).astype(jnp.bfloat16)
    (h_mid,) = after([h_mid], migration.packed)
    mixed = experts_part(h_mid, moe_gain, w_router, expert_lines, routes, migration)
    migration.receive(1)
    return (h_mid.astype(jnp.float32) + mixed, jnp.transpose(migration.moved, (0, 2, 1, 3)))


def solution(mesh):
    return jax.shard_map(
        local,
        mesh=mesh,
        in_specs=(
            P("row", "col"),
            P("row", None),
            P("row", None, None),
            P("row", None, "col", None),
            P("row", None, "col", None),
            P("row"),
            P(None, "col"),
            P("col"),
            P("col", None),
            P(None, "row", None, "col"),
            P(),
            P(),
            P(),
        ),
        out_specs=(P("row", "col"), P(None, "row", None, "col")),
        check_vma=False,
    )
```

```python
import functools

import jax
import jax.numpy as jnp
from jax import lax
from jax.experimental import pallas as pl
from jax.experimental.pallas import tpu as pltpu
from jax.sharding import PartitionSpec as P

KVH = 16
HD = 128
REP = 2
TILE = 16
LANES = 128

norm_eps = 1e-06
neg_big = -1e30
VMEM_LIMIT = 48 * 1024 * 1024
PACK_LIMIT = 59 * 1024 * 1024


def up_to(value, unit):
    return -(-value // unit) * unit


def iota(shape, axis):
    return lax.broadcasted_iota(jnp.int32, shape, axis)


def ones_where(mask):
    return jnp.where(mask, 1.0, 0.0).astype(jnp.bfloat16)


def params():
    return pltpu.CompilerParams(vmem_limit_bytes=VMEM_LIMIT)


def counting(shape, axis):
    return iota(shape, axis).astype(jnp.float32).astype(jnp.bfloat16)


def as_bf16(values):
    return values.astype(jnp.float32).astype(jnp.bfloat16)


def equal_ones(left, right):
    one = jnp.ones((), jnp.bfloat16)
    return jnp.maximum(one - jnp.abs(left - right), jnp.zeros((), jnp.bfloat16))


def within(place, block):
    place = place - 256 * block
    return as_bf16(jnp.where((place >= 0) & (place < 256), place, -1))


def look_up(table_rows, id_rows, numbers, values):
    full = table_rows[0].shape[1]
    ids = id_rows[0].shape[1]
    high_count = up_to(-(-full // 64), 16)
    zero = jnp.zeros((), jnp.bfloat16)
    highs = [equal_ones(numbers[:high_count], as_bf16(row >> 6)) for row in table_rows]
    lows = []
    for row in table_rows:
        hit = numbers[:64] == as_bf16(row & 63)
        lows += [jnp.where(hit, part, zero) for part in values]
    square = lax.dot_general(
        jnp.concatenate(highs, axis=0),
        jnp.concatenate(lows, axis=0),
        (((1,), (1,)), ((), ())),
        preferred_element_type=jnp.float32,
    )
    wide = 64 * len(values)
    found = []
    for n, row in enumerate(id_rows):
        block = square[n * high_count : (n + 1) * high_count, n * wide : (n + 1) * wide]
        id_high = equal_ones(numbers[:high_count, :ids], as_bf16(row >> 6))
        spread = lax.dot_general(
            block.astype(jnp.bfloat16), id_high, (((0,), (0,)), ((), ())),
            preferred_element_type=jnp.float32,
        )
        wanted = iota((64, ids), 0) == (row & 63)
        found.append(
            [
                jnp.sum(jnp.where(wanted, spread[64 * m : 64 * m + 64], 0.0), axis=0, keepdims=True)
                for m in range(len(values))
            ]
        )
    return found


def look_up_all(table_ref, id_ref, numbers, values):
    experts = table_ref.shape[0]
    group = 4 // len(values)
    found = []
    for first in range(0, experts, group):
        members = range(first, min(first + group, experts))
        found += look_up(
            [table_ref[e : e + 1, :] for e in members],
            [id_ref[e : e + 1, :] for e in members],
            numbers,
            values,
        )
    return found


def numbers_for(full):
    return counting((max(up_to(-(-full // 64), 16), 64), full), 0)


def segment_plan(counts, experts, rows):
    starts = []
    running = jnp.zeros((rows, LANES), jnp.float32)
    for e in range(experts):
        starts.append(running)
        running = running + counts[e * rows : (e + 1) * rows]
    start = jnp.concatenate(starts, axis=0)
    lead = jnp.floor(start * (1.0 / TILE))
    tail = jnp.floor((start + counts + (TILE - 1.0)) * (1.0 / TILE))
    tiles = jnp.where(counts > 0.0, tail - lead, 0.0)
    pairs = experts * rows
    line = iota((pairs, pairs), 0)
    column = iota((pairs, pairs), 1)
    earlier = ones_where((line // rows == column // rows) & (column < line))
    base = jnp.dot(earlier, tiles.astype(jnp.bfloat16), preferred_element_type=jnp.float32)
    return start, lead, tiles, base


def write_plan(plan_ref, parts):
    for n, part in enumerate(parts):
        short = -part.shape[0] % LANES
        if short:
            part = jnp.concatenate([part, jnp.zeros((short, LANES), jnp.float32)], axis=0)
        plan_ref[n : n + 1, :] = jnp.transpose(part)[:1].astype(jnp.int32)


def outgoing_kernel(lines, rows, new_ref, held_ref, stack_ref, plan_ref):
    experts = new_ref.shape[0]
    width = held_ref.shape[1]
    real = iota((1, width), 1) < lines
    hits = []
    full = new_ref.shape[1]
    numbers = numbers_for(full)
    slot = iota((64, full), 1).astype(jnp.float32)
    values = (jnp.floor((slot + 0.5) * (1.0 / lines)).astype(jnp.bfloat16),)
    for (peer,) in look_up_all(new_ref, held_ref, numbers, values):
        peer = peer.astype(jnp.int32)
        hits.append(jnp.where((iota((rows, width), 0) == peer) & real, 1.0, 0.0))
    hits = jnp.concatenate(hits, axis=0)
    until = ones_where(iota((width, width), 0) <= iota((width, width), 1))
    ranks = jnp.dot(hits.astype(jnp.bfloat16), until, preferred_element_type=jnp.float32)
    counts = jnp.broadcast_to(jnp.sum(hits, axis=1, keepdims=True), (experts * rows, LANES))
    start, lead, tiles, base = segment_plan(counts, experts, rows)
    write_plan(plan_ref, (lead, tiles, base, start - lead * TILE))
    offset = (base * TILE + start - lead * TILE - 1.0)[:, :1]
    placed = hits * (ranks + offset)
    for e in range(experts):
        row = jnp.sum(placed[e * rows : (e + 1) * rows], axis=0, keepdims=True)
        stack_ref[e] = jnp.where(real, row, -1.0).astype(jnp.int32)


def incoming_kernel(lines, rows, block_tiles, slot, old_ref, wanted_ref, stack_ref, plan_ref):
    experts = old_ref.shape[0]
    width = wanted_ref.shape[1]
    real = iota((1, width), 1) < lines
    held_at = []
    hits = []
    full = old_ref.shape[1]
    numbers = numbers_for(full)
    at = iota((64, full), 1)
    values = (as_bf16(at >> 7), as_bf16(at & 127))
    for high, low in look_up_all(old_ref, wanted_ref, numbers, values):
        slots = high * 128.0 + low
        held_at.append(jnp.where(real, slots, 1e9))
        peer = jnp.floor((slots + 0.5) * (1.0 / lines)).astype(jnp.int32)
        hits.append(jnp.where((iota((rows, width), 0) == peer) & real, 1.0, 0.0))
    hits = jnp.concatenate(hits, axis=0)
    counts = jnp.broadcast_to(jnp.sum(hits, axis=1, keepdims=True), (experts * rows, LANES))
    start, lead, tiles, base = segment_plan(counts, experts, rows)
    line = iota((experts * rows, LANES), 0)
    peer = (line % rows).astype(jnp.float32)
    longest = [
        jnp.max(tiles[e * rows : (e + 1) * rows], axis=0, keepdims=True) for e in range(experts)
    ]
    longest = jnp.concatenate(
        [jnp.broadcast_to(most, (rows, LANES)) for most in longest], axis=0
    )
    slotted = longest <= slot
    lead = jnp.where(slotted, jnp.minimum(lead, float(block_tiles - slot)), lead)
    base = jnp.where(slotted, peer * slot, base)
    write_plan(plan_ref, (lead, tiles, base, jnp.where(slotted, 1.0, 0.0)))
    blank = jnp.zeros((LANES - experts, width), jnp.float32)
    columns = jnp.transpose(jnp.concatenate(held_at + [blank], axis=0))
    rows_out = []
    for e in range(experts):
        mine = slice(e * rows, (e + 1) * rows)
        before = jnp.where(columns[:, e : e + 1] < held_at[e], 1.0, 0.0)
        rank = jnp.sum(before, axis=0, keepdims=True)
        ahead = jnp.zeros((1, LANES), jnp.float32)
        firsts = []
        for r in range(rows):
            firsts.append(ahead)
            ahead = ahead + counts[e * rows + r : e * rows + r + 1]
        first = jnp.concatenate(firsts, axis=0)
        offset = (base[mine] * TILE + start[mine] - lead[mine] * TILE - first)[:, :1]
        rows_out.append(jnp.sum(hits[mine] * (rank + offset), axis=0, keepdims=True))
    places = jnp.transpose(jnp.concatenate(rows_out + [blank], axis=0))
    for e in range(experts):
        place = jnp.broadcast_to(places[:lines, e : e + 1], (lines, LANES))
        block = jnp.floor(place * (1.0 / 256.0))
        stack_ref[e, 0] = (place - 256.0 * block).astype(jnp.bfloat16)
        stack_ref[e, 1] = block.astype(jnp.bfloat16)


STRAIGHT = 8
SLOT = 7


def tile_at(index):
    return pl.ds(pl.multiple_of(index * TILE, TILE), TILE)


def pack_kernel(rows, span, steps, plan_ref, place_ref, lines_ref, out_ref, packed_ref, number_ref, sems, *stages):
    part = pl.program_id(0)
    step = pl.program_id(1)
    deep = stages[0].shape[0] - STRAIGHT * TILE
    lines = lines_ref.shape[2]

    @pl.when((part == 0) & (step == 0))
    def _():
        number_ref[...] = counting(number_ref.shape, 0)

    def entry(n, j, d):
        return plan_ref[n, (step * span + j) * rows + d]

    usual = min(deep, up_to(lines + rows * TILE, TILE))

    def move(j, begin, end):
        place = place_ref[j][:, :lines]
        onehot = [
            equal_ones(number_ref[: min(256, end - row)], within(place - begin, (row - begin) // 256))
            for row in range(begin, end, 256)
        ]
        stages[j][begin:end] = jnp.dot(
            jnp.concatenate(onehot, axis=0), lines_ref[j, 0], preferred_element_type=jnp.float32
        ).astype(jnp.bfloat16)

    for j in range(span):
        move(j, 0, usual)
    if usual < deep:
        for j in range(span):
            used = entry(1, j, rows - 1) + entry(2, j, rows - 1)

            @pl.when(used * TILE > usual)
            def _(j=j):
                move(j, usual, deep)

    for j, stage_ref in enumerate(stages):

        def one_peer(d, most, j=j, stage_ref=stage_ref):
            lead, tiles, base = entry(0, j, d), entry(1, j, d), entry(2, j, d)
            there = pl.multiple_of(lead * TILE, TILE)
            here = pl.multiple_of(base * TILE, TILE)
            earlier = packed_ref[d, pl.ds(there, TILE), :]
            fresh = stage_ref[pl.ds(here, STRAIGHT * TILE), :]
            packed_ref[d, pl.ds(there + TILE, (STRAIGHT - 1) * TILE), :] = fresh[TILE:]
            kept = jnp.where(entry(3, j, d) > 0, earlier, jnp.zeros_like(earlier))
            added = jnp.where(tiles > 0, fresh[:TILE], jnp.zeros_like(earlier))
            packed_ref[d, pl.ds(there, TILE), :] = kept + added
            return jnp.maximum(most, tiles)

        most = lax.fori_loop(0, rows, one_peer, 0, unroll=rows <= 8)

        @pl.when(most > STRAIGHT)
        def _(j=j, stage_ref=stage_ref):
            def long_peer(d, carry):
                lead, tiles, base = entry(0, j, d), entry(1, j, d), entry(2, j, d)

                def put(t, c):
                    packed_ref[d, tile_at(lead + t), :] = stage_ref[tile_at(base + t), :]
                    return c

                return lax.fori_loop(STRAIGHT, tiles, put, carry)

            lax.fori_loop(0, rows, long_peer, 0)

    block_rows = out_ref.shape[2]
    chunks = []
    begin = 0
    for after_step in range(steps):
        end = block_rows
        if after_step < steps - 1:
            end = max(begin, block_rows * (after_step + 1) // steps // TILE * TILE - 2 * TILE)
        if end > begin:
            chunks.append((after_step, begin, end))
        begin = end

    def chunk_copy(n):
        _, begin, end = chunks[n]
        here = pl.ds(begin, end - begin)
        return pltpu.make_async_copy(
            packed_ref.at[:, here], out_ref.at[:, part, here], sems.at[n]
        )

    def final_by(n):
        after_step, _, end = chunks[n]
        first = (after_step + 1) * span * rows
        least = functools.reduce(jnp.minimum, [plan_ref[0, first + d] for d in range(rows)])
        return least * TILE >= end

    for n in range(len(chunks) - 1):

        @pl.when((step == chunks[n][0]) & final_by(n))
        def _(n=n):
            chunk_copy(n).start()

    @pl.when(step == steps - 1)
    def _():
        for n in range(len(chunks) - 1):

            @pl.when(jnp.logical_not(final_by(n)))
            def _(n=n):
                chunk_copy(n).start()

        chunk_copy(len(chunks) - 1).start()
        for n in range(len(chunks)):
            chunk_copy(n).wait()


def unpack_kernel(slot, span, plan_ref, place_ref, block_ref, *rest):
    out_ref, stage_ref, sems = rest[-3:]
    step = pl.program_id(0)
    steps = pl.num_programs(0)
    rows, count, _, width = block_ref.shape
    deep = stage_ref.shape[3]
    lines = out_ref.shape[2]
    buffer = step % 2

    def entry(n, e, s):
        return plan_ref[n, e * rows + s]

    def slotted(e):
        return entry(3, e, 0) > 0

    def begin(step, j):
        e = step * span + j

        @pl.when(slotted(e))
        def _():
            for s in range(rows):
                there = pl.ds(pl.multiple_of(entry(0, e, s) * TILE, TILE), slot * TILE)
                here = pl.ds(s * slot * TILE, slot * TILE)
                pltpu.make_async_copy(
                    block_ref.at[s, :, there],
                    stage_ref.at[step % 2, j, :, here],
                    sems.at[step % 2, j],
                ).start()

    @pl.when(step == 0)
    def _():
        for j in range(span):
            begin(step, j)

    lane = counting((lines, LANES), 1)

    def multiply(j, depth):
        within_block, block = place_ref[j, 0], place_ref[j, 1]
        pieces = []
        for first in range(0, depth, LANES):
            away = jnp.abs(block - jnp.asarray(first // 256, jnp.bfloat16))
            place = within_block + away * jnp.asarray(512, jnp.bfloat16)
            pieces.append(equal_ones(lane + jnp.asarray(first % 256, jnp.bfloat16), place))
        onehot = jnp.concatenate(pieces, axis=1)
        for part in range(count):
            out_ref[j, part] = jnp.dot(
                onehot, stage_ref[buffer, j, part, :depth], preferred_element_type=jnp.float32
            ).astype(jnp.bfloat16)

    for j in range(span):
        e = step * span + j
        staged = rows * slot * TILE

        @pl.when(slotted(e))
        def _(j=j):
            all_slots = stage_ref.at[buffer, j, :, pl.ds(0, staged)]
            pltpu.make_async_copy(all_slots, all_slots, sems.at[buffer, j]).wait()

        @pl.when(step + 1 < steps)
        def _(j=j):
            begin(step + 1, j)

        @pl.when(slotted(e))
        def _(j=j):
            if staged % LANES:
                stage_ref[buffer, j, :, staged:] = jnp.zeros(
                    (count, deep - staged, width), jnp.bfloat16
                )
                multiply(j, deep)
            else:
                multiply(j, staged)

        @pl.when(jnp.logical_not(slotted(e)))
        def _(e=e, j=j):
            stage_ref[buffer, j] = jnp.zeros((count, deep, width), jnp.bfloat16)

            def one_peer(s, carry):
                def put(t, c):
                    copy = pltpu.make_async_copy(
                        block_ref.at[s, :, tile_at(entry(0, e, s) + t)],
                        stage_ref.at[buffer, j, :, tile_at(entry(2, e, s) + t)],
                        sems.at[buffer, j],
                    )
                    copy.start()
                    copy.wait()
                    return c

                return lax.fori_loop(0, entry(1, e, s), put, carry)

            lax.fori_loop(0, rows, one_peer, 0)
            multiply(j, deep)


def call_plan(kernel, name, table, ids, pairs, place):
    return pl.pallas_call(
        kernel,
        out_shape=(place, jax.ShapeDtypeStruct((4, up_to(pairs, LANES)), jnp.int32)),
        compiler_params=params(),
        cost_estimate=pl.CostEstimate(
            flops=20 * table.size * 256, bytes_accessed=8 * table.size, transcendentals=0
        ),
        name=name,
    )(table, ids)


def pack(expert_lines, place, plan, piece, rows, block_rows, deep):
    experts, _, lines, _ = expert_lines.shape
    first, count, column, width = piece
    span = 2 - experts % 2
    return pl.pallas_call(
        functools.partial(pack_kernel, rows, span, experts // span),
        grid_spec=pltpu.PrefetchScalarGridSpec(
            num_scalar_prefetch=1,
            grid=(count, experts // span),
            in_specs=[
                pl.BlockSpec((span, 1, place.shape[2]), lambda p, e, plan: (e, 0, 0)),
                pl.BlockSpec((span, 1, lines, width), lambda p, e, plan: (e, first + p, 0, column)),
            ],
            out_specs=pl.BlockSpec(memory_space=pltpu.HBM),
            scratch_shapes=[
                pltpu.VMEM((rows, block_rows + STRAIGHT * TILE, width), jnp.bfloat16),
                pltpu.VMEM((256, lines), jnp.bfloat16),
                pltpu.SemaphoreType.DMA((experts // span,)),
            ]
            + [pltpu.VMEM((deep + STRAIGHT * TILE, width), jnp.bfloat16)] * span,
        ),
        out_shape=jax.ShapeDtypeStruct((rows, count, block_rows, width), jnp.bfloat16),
        compiler_params=pltpu.CompilerParams(vmem_limit_bytes=PACK_LIMIT),
        cost_estimate=pl.CostEstimate(
            flops=2 * count * experts * deep * lines * width,
            bytes_accessed=4 * count * experts * lines * width,
            transcendentals=0,
        ),
        name="pack_lines",
    )(plan, place, expert_lines)


def unpack(arrived, place, plan, piece, shape, deep, slot, previous):
    experts, _, lines, _ = shape
    first, count, column, width = piece
    span = 2 - experts % 2
    in_specs = [
        pl.BlockSpec((span, 2, lines, LANES), lambda e, plan: (e, 0, 0, 0)),
        pl.BlockSpec(memory_space=pl.ANY),
    ]
    operands = [plan, place, arrived]
    aliases = {}
    if previous is not None:
        in_specs.append(pl.BlockSpec(memory_space=pl.ANY))
        operands.append(previous)
        aliases = {3: 0}
    return pl.pallas_call(
        functools.partial(unpack_kernel, slot, span),
        grid_spec=pltpu.PrefetchScalarGridSpec(
            num_scalar_prefetch=1,
            grid=(experts // span,),
            in_specs=in_specs,
            out_specs=pl.BlockSpec(
                (span, count, lines, width), lambda e, plan: (e, first // count, 0, column)
            ),
            scratch_shapes=[
                pltpu.VMEM((2, span, count, deep, width), jnp.bfloat16),
                pltpu.SemaphoreType.DMA((2, span)),
            ],
        ),
        out_shape=jax.ShapeDtypeStruct(shape, jnp.bfloat16),
        input_output_aliases=aliases,
        compiler_params=params(),
        cost_estimate=pl.CostEstimate(
            flops=2 * count * experts * deep * lines * width,
            bytes_accessed=4 * count * experts * lines * width,
            transcendentals=0,
        ),
        name="unpack_lines",
    )(*operands)


def after_kernel(*refs):
    del refs


def after(values, signals):
    anywhere = pl.BlockSpec(memory_space=pl.ANY)
    return pl.pallas_call(
        after_kernel,
        in_specs=[anywhere] * (len(values) + len(signals)),
        out_specs=[anywhere] * len(values),
        out_shape=[jax.ShapeDtypeStruct(v.shape, v.dtype) for v in values],
        input_output_aliases={n: n for n in range(len(values))},
        compiler_params=pltpu.CompilerParams(vmem_limit_bytes=PACK_LIMIT),
        name="after",
    )(*values, *signals)


def own_ids(table, lines, width):
    mine = lax.dynamic_slice_in_dim(table, lax.axis_index("row") * lines, lines, 1)
    return jnp.pad(mine, ((0, 0), (0, width - lines)), constant_values=-1)


def from_peer(block, axis, offset):
    size = lax.axis_size(axis)
    return lax.ppermute(block, axis, [(i, i ^ offset) for i in range(size)])


class Migration:
    def __init__(self, expert_lines, old_lines, new_lines):
        rows = lax.axis_size("row")
        experts, parts, lines, width = expert_lines.shape
        padded = up_to(lines, LANES)
        block_rows = up_to(experts * lines // rows, TILE)
        pairs = experts * rows
        compact = up_to(lines + 2 * (TILE - 1) * rows, TILE)
        self.slot = min(SLOT, block_rows // TILE)
        self.deep = up_to(max(compact, rows * self.slot * TILE), 256)
        self.shape = expert_lines.shape
        quarter = width // 4
        if quarter % LANES:
            self.pieces = [(parts - 1, 1, 0, width), (0, parts - 1, 0, width)]
        else:
            self.pieces = [
                (parts - 1, 1, 0, 3 * quarter),
                (0, parts - 1, 0, width),
                (parts - 1, 1, 3, quarter),
            ]
        out_place, out_plan = call_plan(
            functools.partial(outgoing_kernel, lines, rows), "outgoing_plan",
            new_lines, own_ids(old_lines, lines, padded), pairs,
            jax.ShapeDtypeStruct((experts, 1, padded), jnp.int32),
        )
        self.in_place, self.in_plan = call_plan(
            functools.partial(incoming_kernel, lines, rows, block_rows // TILE, self.slot),
            "incoming_plan",
            old_lines, own_ids(new_lines, lines, padded), pairs,
            jax.ShapeDtypeStruct((experts, 2, lines, LANES), jnp.bfloat16),
        )
        self.packed = [
            pack(expert_lines, out_place, out_plan, piece, rows, block_rows, compact)
            for piece in self.pieces
        ]
        self.arrived = []
        self.moved = None

    def send(self, signals=()):
        block = self.packed[len(self.arrived)]
        if signals:
            (block,) = after([block], signals)
        self.arrived.append(
            lax.all_to_all(block, "row", split_axis=0, concat_axis=0, tiled=True)
        )

    def receive(self, piece):
        self.moved = unpack(
            self.arrived[piece], self.in_place, self.in_plan, self.pieces[piece], self.shape,
            self.deep, self.slot, self.moved,
        )


def attend(queries, new_kv, prompt_kv, suffix_kv, lengths):
    seq_count = queries.shape[0]
    prompt_rows = prompt_kv.shape[2]
    suffix_rows = suffix_kv.shape[2]
    col_index = lax.axis_index("col")
    query_heads = queries.reshape(seq_count, KVH, REP, HD)
    prompt_keys = prompt_kv[0, 0].reshape(prompt_rows, KVH, HD)
    prompt_values = prompt_kv[0, 1].reshape(prompt_rows, KVH, HD)
    suffix_keys = suffix_kv[:, 0].reshape(seq_count, suffix_rows, KVH, HD)
    suffix_values = suffix_kv[:, 1].reshape(seq_count, suffix_rows, KVH, HD)
    own_keys = new_kv[:, 0].reshape(seq_count, KVH, HD)
    own_values = new_kv[:, 1].reshape(seq_count, KVH, HD)
    score_scale = HD ** (-0.5)
    prompt_scores = (
        jnp.einsum("skgd,pkd->skgp", query_heads, prompt_keys, preferred_element_type=jnp.float32)
        * score_scale
    )
    suffix_scores = (
        jnp.einsum("skgd,spkd->skgp", query_heads, suffix_keys, preferred_element_type=jnp.float32)
        * score_scale
    )
    own_scores = (
        jnp.einsum("skgd,skd->skg", query_heads, own_keys, preferred_element_type=jnp.float32)
        * score_scale
    )
    positions = col_index * suffix_rows + jnp.arange(suffix_rows, dtype=jnp.int32)
    live_slots = (positions[None, :] < lengths[:, None])[:, None, None, :]
    holder = col_index == 0
    suffix_scores = jnp.where(live_slots, suffix_scores, neg_big)
    own_scores = jnp.where(holder, own_scores, neg_big)
    highest = jnp.maximum(
        jnp.maximum(jnp.max(prompt_scores, axis=-1), jnp.max(suffix_scores, axis=-1)), own_scores
    )
    prompt_weights = jnp.exp(prompt_scores - highest[..., None])
    suffix_weights = jnp.where(live_slots, jnp.exp(suffix_scores - highest[..., None]), 0.0)
    own_weights = jnp.where(holder, jnp.exp(own_scores - highest), 0.0)
    totals = jnp.sum(prompt_weights, axis=-1) + jnp.sum(suffix_weights, axis=-1) + own_weights
    mixture = jnp.einsum(
        "skgp,pkd->skgd",
        prompt_weights.astype(jnp.bfloat16),
        prompt_values,
        preferred_element_type=jnp.float32,
    )
    mixture = mixture + jnp.einsum(
        "skgp,spkd->skgd",
        suffix_weights.astype(jnp.bfloat16),
        suffix_values,
        preferred_element_type=jnp.float32,
    )
    own_rounded = lax.optimization_barrier(own_weights.astype(jnp.bfloat16)).astype(jnp.float32)
    mixture = mixture + own_rounded[..., None] * own_values.astype(jnp.float32)[:, :, None, :]
    heads = KVH * REP
    bundle = jnp.concatenate(
        [
            mixture.reshape(seq_count, heads * HD),
            highest.reshape(seq_count, heads),
            totals.reshape(seq_count, heads),
            jnp.zeros((seq_count, LANES - 2 * heads), jnp.float32),
        ],
        axis=1,
    )
    bundles = [bundle] + [from_peer(bundle, "col", o) for o in range(1, lax.axis_size("col"))]
    every = jnp.stack(bundles)
    mixtures = every[:, :, : heads * HD].reshape(-1, seq_count, heads, HD)
    peaks = every[:, :, heads * HD : heads * HD + heads]
    sums = every[:, :, heads * HD + heads : heads * HD + 2 * heads]
    factors = jnp.exp(peaks - jnp.max(peaks, axis=0))
    total = jnp.sum(sums * factors, axis=0)
    mixed = jnp.sum(mixtures * factors[..., None], axis=0)
    return (mixed / total[..., None]).astype(jnp.bfloat16).reshape(seq_count, heads * HD)


def gate_up_kernel(me_ref, h_ref, gain_ref, router_ref, routes_ref, gate_ref, up_ref, out_ref, acc_ref):
    e = pl.program_id(0)
    tokens = h_ref.shape[0]
    lines = gate_ref.shape[2]
    padded = out_ref.shape[3]
    h = h_ref[...].astype(jnp.float32)
    scaled = (h * gain_ref[...].astype(jnp.float32)).astype(jnp.bfloat16)

    @pl.when(e == 0)
    def _():
        acc_ref[...] = jnp.zeros_like(acc_ref)

    against = (((1,), (1,)), ((), ()))
    gate = lax.dot_general(scaled, gate_ref[0, 0], against, preferred_element_type=jnp.float32)
    up = lax.dot_general(scaled, up_ref[0, 0], against, preferred_element_type=jnp.float32)
    for k in range(routes_ref.shape[1]):
        chosen = routes_ref[:, k : k + 1] == e
        acc_ref[2 * k, :, :lines] += jnp.where(chosen, gate, 0.0)
        acc_ref[2 * k + 1, :, :lines] += jnp.where(chosen, up, 0.0)

    @pl.when(e == pl.num_programs(0) - 1)
    def _():
        last = padded - LANES
        shift = lines - last
        experts = pl.num_programs(0)
        extra = jnp.dot(scaled, router_ref[...], preferred_element_type=jnp.float32)
        lane = iota((tokens, LANES), 1)
        square = jnp.sum(h * h, axis=1, keepdims=True)
        extra = jnp.where(lane == shift + experts, square, extra)
        high = extra.astype(jnp.bfloat16).astype(jnp.float32)
        low = extra - high
        acc_ref[0, :, last:] += jnp.where(lane >= shift, high, 0.0)
        acc_ref[1, :, last:] += jnp.where(lane >= shift, low, 0.0)
        peers, _, share, _ = out_ref.shape
        me = me_ref[0]
        for o in range(peers):
            begin = pl.multiple_of((me ^ o) * share, share)
            out_ref[o] = acc_ref[:, pl.ds(begin, share), :].astype(jnp.bfloat16)


def activate_kernel(lines, experts, model_width, routes_ref, *refs):
    out_ref = refs[-1]
    summed = refs[0][...].astype(jnp.float32)
    for ref in refs[1:-1]:
        summed = summed + ref[...].astype(jnp.float32)
    _, share, padded = summed.shape
    last = padded - LANES
    shift = lines - last
    extra = summed[0, :, last:] + summed[1, :, last:]
    lane = iota((share, LANES), 1)
    square = jnp.sum(jnp.where(lane == shift + experts, extra, 0.0), axis=1, keepdims=True)
    inverse_rms = lax.rsqrt(square / model_width + norm_eps)
    logits = []
    for k in range(out_ref.shape[0]):
        wanted = lane == routes_ref[:, k : k + 1] + shift
        logits.append(jnp.sum(jnp.where(wanted, extra, 0.0), axis=1, keepdims=True) * inverse_rms)
    peak = functools.reduce(jnp.maximum, logits)
    shares = [jnp.exp(v - peak) for v in logits]
    total = functools.reduce(jnp.add, shares)
    inside = iota((share, padded), 1) < lines
    for k in range(out_ref.shape[0]):
        gate = summed[2 * k] * inverse_rms
        up = summed[2 * k + 1] * inverse_rms
        act = gate / (1.0 + jnp.exp(-gate)) * up
        out_ref[k] = jnp.where(inside, act * (shares[k] / total), 0.0).astype(jnp.bfloat16)


def down_kernel(me_ref, routes_ref, *refs):
    down_ref, out_ref, act_ref = refs[-3:]
    chunks = refs[:-3]
    e = pl.program_id(0)
    topk, share, _ = chunks[0].shape
    lines = down_ref.shape[2]

    @pl.when(e == 0)
    def _():
        me = me_ref[0]
        out_ref[...] = jnp.zeros_like(out_ref)
        for o, chunk in enumerate(chunks):
            begin = pl.multiple_of((me ^ o) * share, share)
            act_ref[:, pl.ds(begin, share), :] = chunk[...]

    mine = jnp.zeros((act_ref.shape[1], lines), jnp.float32)
    for k in range(topk):
        chosen = routes_ref[:, k : k + 1] == e
        mine = mine + jnp.where(chosen, act_ref[k, :, :lines].astype(jnp.float32), 0.0)
    out_ref[...] += jnp.dot(
        mine.astype(jnp.bfloat16), down_ref[0, 0], preferred_element_type=jnp.float32
    )


def experts_part(h_mid, moe_gain, w_router, expert_lines, routes, migration):
    rows = lax.axis_size("row")
    cols = lax.axis_size("col")
    row_index = lax.axis_index("row")
    col_index = lax.axis_index("col")
    experts, _, lines, width = expert_lines.shape
    own, _ = h_mid.shape
    tokens = own * rows
    topk = routes.shape[1]
    share = tokens // cols
    padded = up_to(lines + experts + 1, LANES)
    shift = lines - (padded - LANES)
    me = col_index.astype(jnp.int32).reshape(1)

    order = row_index ^ jnp.array(sorted(range(rows), key=lambda o: (o % 2, o)), jnp.int32)
    routes = routes.reshape(rows, own, topk)[order].reshape(tokens, topk)
    my_routes = lax.dynamic_slice_in_dim(routes, col_index * share, share, 0)
    router = jnp.pad(w_router, ((0, 0), (shift, LANES - shift - experts)))
    across = [from_peer(h_mid, "row", o) for o in range(2, rows, 2)]
    same_core = jnp.concatenate([h_mid] + across, axis=0)
    every_h = jnp.concatenate([same_core, from_peer(same_core, "row", 1)], axis=0)
    migration.send(across)
    part_spec = lambda part: pl.BlockSpec((1, 1, lines, width), lambda e, me: (e, part, 0, 0))
    whole = lambda a: pl.BlockSpec(a.shape, lambda e, me: (0,) * a.ndim)
    gain = moe_gain.reshape(1, width)
    partial = pl.pallas_call(
        gate_up_kernel,
        grid_spec=pltpu.PrefetchScalarGridSpec(
            num_scalar_prefetch=1,
            grid=(experts,),
            in_specs=[whole(every_h), whole(gain), whole(router), whole(routes)]
            + [part_spec(0), part_spec(1)],
            out_specs=pl.BlockSpec((cols, 2 * topk, share, padded), lambda e, me: (0, 0, 0, 0)),
            scratch_shapes=[pltpu.VMEM((2 * topk, tokens, padded), jnp.float32)],
        ),
        out_shape=jax.ShapeDtypeStruct((cols, 2 * topk, share, padded), jnp.bfloat16),
        compiler_params=params(),
        cost_estimate=pl.CostEstimate(
            flops=4 * experts * tokens * lines * width,
            bytes_accessed=4 * experts * lines * width,
            transcendentals=0,
        ),
        name="gate_up",
    )(me, every_h, gain, router, routes, expert_lines, expert_lines)
    gathered = [partial[0]] + [from_peer(partial[o], "col", o) for o in range(1, cols)]
    activated = pl.pallas_call(
        functools.partial(activate_kernel, lines, experts, width * cols),
        out_shape=jax.ShapeDtypeStruct((topk, share, padded), jnp.bfloat16),
        compiler_params=params(),
        name="activate",
    )(my_routes, *gathered)
    chunks = [activated] + [from_peer(activated, "col", o) for o in range(1, cols)]
    produced = pl.pallas_call(
        down_kernel,
        grid_spec=pltpu.PrefetchScalarGridSpec(
            num_scalar_prefetch=1,
            grid=(experts,),
            in_specs=[whole(routes)] + [whole(c) for c in chunks] + [part_spec(2)],
            out_specs=pl.BlockSpec((tokens, width), lambda e, me: (0, 0)),
            scratch_shapes=[pltpu.VMEM((topk, tokens, padded), jnp.bfloat16)],
        ),
        out_shape=jax.ShapeDtypeStruct((tokens, width), jnp.float32),
        compiler_params=params(),
        cost_estimate=pl.CostEstimate(
            flops=2 * experts * tokens * lines * width,
            bytes_accessed=2 * experts * lines * width,
            transcendentals=0,
        ),
        name="down",
    )(me, routes, *chunks, expert_lines)
    migration.receive(0)
    (produced,) = after([produced], [migration.moved] + migration.packed[2:])
    half = tokens // 2
    both_cores = produced[:half] + from_peer(produced[half:], "row", 1)
    blocks = both_cores.reshape(rows // 2, own, width)
    arrived = [from_peer(blocks[n], "row", 2 * n) for n in range(1, rows // 2)]
    for _ in migration.packed[2:]:
        migration.send(arrived)
    mixed = functools.reduce(jnp.add, arrived, blocks[0])
    return mixed


def local(
    hidden,
    queries,
    new_kv,
    prompt_kv,
    suffix_kv,
    lengths,
    w_out,
    moe_gain,
    w_router,
    expert_weights,
    old_lines,
    new_lines,
    routes,
):
    expert_lines = jnp.transpose(expert_weights, (0, 2, 1, 3))
    migration = Migration(expert_lines, old_lines, new_lines)
    migration.send()
    attended = attend(queries, new_kv, prompt_kv, suffix_kv, lengths)
    projected = jnp.dot(attended, w_out, preferred_element_type=jnp.float32)
    h_mid = (hidden.astype(jnp.float32) + projected).astype(jnp.bfloat16)
    (h_mid,) = after([h_mid], migration.packed[:2])
    mixed = experts_part(h_mid, moe_gain, w_router, expert_lines, routes, migration)
    for piece in range(1, len(migration.pieces)):
        migration.receive(piece)
    return (h_mid.astype(jnp.float32) + mixed, jnp.transpose(migration.moved, (0, 2, 1, 3)))


def solution(mesh):
    return jax.shard_map(
        local,
        mesh=mesh,
        in_specs=(
            P("row", "col"),
            P("row", None),
            P("row", None, None),
            P("row", None, "col", None),
            P("row", None, "col", None),
            P("row"),
            P(None, "col"),
            P("col"),
            P("col", None),
            P(None, "row", None, "col"),
            P(),
            P(),
            P(),
        ),
        out_specs=(P("row", "col"), P(None, "row", None, "col")),
        check_vma=False,
    )
```

```python
import functools

import jax
import jax.numpy as jnp
from jax import lax
from jax.experimental import pallas as pl
from jax.experimental.pallas import tpu as pltpu
from jax.sharding import PartitionSpec as P

KVH = 16
HD = 128
REP = 2
TILE = 16
LANES = 128

norm_eps = 1e-06
neg_big = -1e30
VMEM_LIMIT = 48 * 1024 * 1024
PACK_LIMIT = 59 * 1024 * 1024


def up_to(value, unit):
    return -(-value // unit) * unit


def iota(shape, axis):
    return lax.broadcasted_iota(jnp.int32, shape, axis)


def ones_where(mask):
    return jnp.where(mask, 1.0, 0.0).astype(jnp.bfloat16)


def params():
    return pltpu.CompilerParams(vmem_limit_bytes=VMEM_LIMIT)


def counting(shape, axis):
    return iota(shape, axis).astype(jnp.float32).astype(jnp.bfloat16)


def as_bf16(values):
    return values.astype(jnp.float32).astype(jnp.bfloat16)


def equal_ones(left, right):
    one = jnp.ones((), jnp.bfloat16)
    return jnp.maximum(one - jnp.abs(left - right), jnp.zeros((), jnp.bfloat16))


def within(place, block):
    place = place - 256 * block
    return as_bf16(jnp.where((place >= 0) & (place < 256), place, -1))


def look_up(table_rows, id_rows, numbers, values):
    full = table_rows[0].shape[1]
    ids = id_rows[0].shape[1]
    high_count = up_to(-(-full // 64), 16)
    zero = jnp.zeros((), jnp.bfloat16)
    highs = [equal_ones(numbers[:high_count], as_bf16(row >> 6)) for row in table_rows]
    lows = []
    for row in table_rows:
        hit = numbers[:64] == as_bf16(row & 63)
        lows += [jnp.where(hit, part, zero) for part in values]
    square = lax.dot_general(
        jnp.concatenate(highs, axis=0),
        jnp.concatenate(lows, axis=0),
        (((1,), (1,)), ((), ())),
        preferred_element_type=jnp.float32,
    )
    wide = 64 * len(values)
    found = []
    for n, row in enumerate(id_rows):
        block = square[n * high_count : (n + 1) * high_count, n * wide : (n + 1) * wide]
        id_high = equal_ones(numbers[:high_count, :ids], as_bf16(row >> 6))
        spread = lax.dot_general(
            block.astype(jnp.bfloat16), id_high, (((0,), (0,)), ((), ())),
            preferred_element_type=jnp.float32,
        )
        wanted = iota((64, ids), 0) == (row & 63)
        found.append(
            [
                jnp.sum(jnp.where(wanted, spread[64 * m : 64 * m + 64], 0.0), axis=0, keepdims=True)
                for m in range(len(values))
            ]
        )
    return found


def look_up_all(table_ref, id_ref, numbers, values):
    experts = table_ref.shape[0]
    group = 4 // len(values)
    found = []
    for first in range(0, experts, group):
        members = range(first, min(first + group, experts))
        found += look_up(
            [table_ref[e : e + 1, :] for e in members],
            [id_ref[e : e + 1, :] for e in members],
            numbers,
            values,
        )
    return found


def numbers_for(full):
    return counting((max(up_to(-(-full // 64), 16), 64), full), 0)


def segment_plan(counts, experts, rows):
    starts = []
    running = jnp.zeros((rows, LANES), jnp.float32)
    for e in range(experts):
        starts.append(running)
        running = running + counts[e * rows : (e + 1) * rows]
    start = jnp.concatenate(starts, axis=0)
    lead = jnp.floor(start * (1.0 / TILE))
    tail = jnp.floor((start + counts + (TILE - 1.0)) * (1.0 / TILE))
    tiles = jnp.where(counts > 0.0, tail - lead, 0.0)
    pairs = experts * rows
    line = iota((pairs, pairs), 0)
    column = iota((pairs, pairs), 1)
    earlier = ones_where((line // rows == column // rows) & (column < line))
    base = jnp.dot(earlier, tiles.astype(jnp.bfloat16), preferred_element_type=jnp.float32)
    return start, lead, tiles, base


def write_plan(plan_ref, parts):
    for n, part in enumerate(parts):
        short = -part.shape[0] % LANES
        if short:
            part = jnp.concatenate([part, jnp.zeros((short, LANES), jnp.float32)], axis=0)
        plan_ref[n : n + 1, :] = jnp.transpose(part)[:1].astype(jnp.int32)


def outgoing_kernel(lines, rows, new_ref, held_ref, stack_ref, plan_ref):
    width = held_ref.shape[1]
    full = new_ref.shape[1]
    numbers = numbers_for(full)
    slot = iota((64, full), 1).astype(jnp.float32)
    values = (jnp.floor((slot + 0.5) * (1.0 / lines)).astype(jnp.bfloat16),)
    hits = []
    reals = []
    for (peer,) in look_up_all(new_ref, held_ref, numbers, values):
        peer = peer.astype(jnp.int32)
        for first in range(0, width, BLOCK):
            real = iota((1, BLOCK), 1) < lines - first
            here = peer[:, first : first + BLOCK]
            hits.append(jnp.where((iota((rows, BLOCK), 0) == here) & real, 1.0, 0.0))
            reals.append(real)
    blocks = len(hits)
    hits = jnp.concatenate(hits, axis=0)
    until = ones_where(iota((BLOCK, BLOCK), 0) <= iota((BLOCK, BLOCK), 1))
    ranks = jnp.dot(hits.astype(jnp.bfloat16), until, preferred_element_type=jnp.float32)
    counts = jnp.broadcast_to(jnp.sum(hits, axis=1, keepdims=True), (blocks * rows, LANES))
    start, lead, tiles, base = segment_plan(counts, blocks, rows)
    write_plan(plan_ref, (lead, tiles, base, start - lead * TILE))
    offset = (base * TILE + start - lead * TILE - 1.0)[:, :1]
    placed = hits * (ranks + offset)
    for n, real in enumerate(reals):
        row = jnp.sum(placed[n * rows : (n + 1) * rows], axis=0, keepdims=True)
        stack_ref[n] = jnp.where(real, row, -1.0).astype(jnp.int32)


def incoming_kernel(lines, rows, block_tiles, slot, old_ref, wanted_ref, stack_ref, plan_ref):
    experts = old_ref.shape[0]
    width = wanted_ref.shape[1]
    real = iota((1, width), 1) < lines
    held_at = []
    hits = []
    full = old_ref.shape[1]
    numbers = numbers_for(full)
    at = iota((64, full), 1)
    values = (as_bf16(at >> 7), as_bf16(at & 127))
    for high, low in look_up_all(old_ref, wanted_ref, numbers, values):
        slots = high * 128.0 + low
        held_at.append(jnp.where(real, slots, 1e9))
        peer = jnp.floor((slots + 0.5) * (1.0 / lines)).astype(jnp.int32)
        hits.append(jnp.where((iota((rows, width), 0) == peer) & real, 1.0, 0.0))
    hits = jnp.concatenate(hits, axis=0)
    counts = jnp.broadcast_to(jnp.sum(hits, axis=1, keepdims=True), (experts * rows, LANES))
    start, lead, tiles, base = segment_plan(counts, experts, rows)
    line = iota((experts * rows, LANES), 0)
    peer = (line % rows).astype(jnp.float32)
    longest = [
        jnp.max(tiles[e * rows : (e + 1) * rows], axis=0, keepdims=True) for e in range(experts)
    ]
    longest = jnp.concatenate(
        [jnp.broadcast_to(most, (rows, LANES)) for most in longest], axis=0
    )
    slotted = longest <= slot
    lead = jnp.where(slotted, jnp.minimum(lead, float(block_tiles - slot)), lead)
    base = jnp.where(slotted, peer * slot, base)
    write_plan(plan_ref, (lead, tiles, base, jnp.where(slotted, 1.0, 0.0)))
    blank = jnp.zeros((LANES - experts, width), jnp.float32)
    columns = jnp.transpose(jnp.concatenate(held_at + [blank], axis=0))
    rows_out = []
    for e in range(experts):
        mine = slice(e * rows, (e + 1) * rows)
        before = jnp.where(columns[:, e : e + 1] < held_at[e], 1.0, 0.0)
        rank = jnp.sum(before, axis=0, keepdims=True)
        ahead = jnp.zeros((1, LANES), jnp.float32)
        firsts = []
        for r in range(rows):
            firsts.append(ahead)
            ahead = ahead + counts[e * rows + r : e * rows + r + 1]
        first = jnp.concatenate(firsts, axis=0)
        offset = (base[mine] * TILE + start[mine] - lead[mine] * TILE - first)[:, :1]
        rows_out.append(jnp.sum(hits[mine] * (rank + offset), axis=0, keepdims=True))
    places = jnp.transpose(jnp.concatenate(rows_out + [blank], axis=0))
    for e in range(experts):
        place = jnp.broadcast_to(places[:lines, e : e + 1], (lines, LANES))
        block = jnp.floor(place * (1.0 / 256.0))
        stack_ref[e, 0] = (place - 256.0 * block).astype(jnp.bfloat16)
        stack_ref[e, 1] = block.astype(jnp.bfloat16)


BLOCK = 256
STRAIGHT = 4
SLOT = 7


def tile_at(index):
    return pl.ds(pl.multiple_of(index * TILE, TILE), TILE)


def pack_kernel(rows, span, steps, plan_ref, place_ref, lines_ref, out_ref, packed_ref, number_ref, sems, *stages):
    part = pl.program_id(0)
    step = pl.program_id(1)
    deep = stages[0].shape[0] - STRAIGHT * TILE
    lines = lines_ref.shape[2]

    @pl.when((part == 0) & (step == 0))
    def _():
        number_ref[...] = counting(number_ref.shape, 0)

    blocks = len(stages) // span

    def entry(n, j, d):
        return plan_ref[n, (step * len(stages) + j) * rows + d]

    usual = min(deep, up_to(min(lines, BLOCK) + rows * TILE, TILE))

    def move(j, begin, end):
        first = j % blocks * BLOCK
        last = min(first + BLOCK, lines)
        place = place_ref[j][:, : last - first]
        onehot = [
            equal_ones(
                number_ref[: min(256, end - row), : last - first],
                within(place - begin, (row - begin) // 256),
            )
            for row in range(begin, end, 256)
        ]
        stages[j][begin:end] = jnp.dot(
            jnp.concatenate(onehot, axis=0),
            lines_ref[j // blocks, 0, first:last],
            preferred_element_type=jnp.float32,
        ).astype(jnp.bfloat16)

    for j in range(len(stages)):
        move(j, 0, usual)
    if usual < deep:
        for j in range(len(stages)):
            used = entry(1, j, rows - 1) + entry(2, j, rows - 1)

            @pl.when(used * TILE > usual)
            def _(j=j):
                move(j, usual, deep)

    for j, stage_ref in enumerate(stages):

        def one_peer(d, most, j=j, stage_ref=stage_ref):
            lead, tiles, base = entry(0, j, d), entry(1, j, d), entry(2, j, d)
            there = pl.multiple_of(lead * TILE, TILE)
            here = pl.multiple_of(base * TILE, TILE)
            earlier = packed_ref[d, pl.ds(there, TILE), :]
            fresh = stage_ref[pl.ds(here, STRAIGHT * TILE), :]
            packed_ref[d, pl.ds(there + TILE, (STRAIGHT - 1) * TILE), :] = fresh[TILE:]
            kept = jnp.where(entry(3, j, d) > 0, earlier, jnp.zeros_like(earlier))
            added = jnp.where(tiles > 0, fresh[:TILE], jnp.zeros_like(earlier))
            packed_ref[d, pl.ds(there, TILE), :] = kept + added
            return jnp.maximum(most, tiles)

        most = lax.fori_loop(0, rows, one_peer, 0, unroll=rows <= 8)

        @pl.when(most > STRAIGHT)
        def _(j=j, stage_ref=stage_ref):
            def long_peer(d, carry):
                lead, tiles, base = entry(0, j, d), entry(1, j, d), entry(2, j, d)

                def put(t, c):
                    packed_ref[d, tile_at(lead + t), :] = stage_ref[tile_at(base + t), :]
                    return c

                return lax.fori_loop(STRAIGHT, tiles, put, carry)

            lax.fori_loop(0, rows, long_peer, 0)

    block_rows = out_ref.shape[2]
    chunks = []
    begin = 0
    for after_step in range(steps):
        end = block_rows
        if after_step < steps - 1:
            end = max(begin, block_rows * (after_step + 1) // steps // TILE * TILE - 2 * TILE)
        if end > begin:
            chunks.append((after_step, begin, end))
        begin = end

    def chunk_copy(n):
        _, begin, end = chunks[n]
        here = pl.ds(begin, end - begin)
        return pltpu.make_async_copy(
            packed_ref.at[:, here], out_ref.at[:, part, here], sems.at[n]
        )

    def final_by(n):
        after_step, _, end = chunks[n]
        first = (after_step + 1) * len(stages) * rows
        least = functools.reduce(jnp.minimum, [plan_ref[0, first + d] for d in range(rows)])
        return least * TILE >= end

    for n in range(len(chunks) - 1):

        @pl.when((step == chunks[n][0]) & final_by(n))
        def _(n=n):
            chunk_copy(n).start()

    @pl.when(step == steps - 1)
    def _():
        for n in range(len(chunks) - 1):

            @pl.when(jnp.logical_not(final_by(n)))
            def _(n=n):
                chunk_copy(n).start()

        chunk_copy(len(chunks) - 1).start()
        for n in range(len(chunks)):
            chunk_copy(n).wait()


def unpack_kernel(slot, span, plan_ref, place_ref, block_ref, *rest):
    out_ref, stage_ref, sems = rest[-3:]
    step = pl.program_id(0)
    steps = pl.num_programs(0)
    rows, count, _, width = block_ref.shape
    deep = stage_ref.shape[3]
    lines = out_ref.shape[2]
    buffer = step % 2

    def entry(n, e, s):
        return plan_ref[n, e * rows + s]

    def slotted(e):
        return entry(3, e, 0) > 0

    def begin(step, j):
        e = step * span + j

        @pl.when(slotted(e))
        def _():
            for s in range(rows):
                there = pl.ds(pl.multiple_of(entry(0, e, s) * TILE, TILE), slot * TILE)
                here = pl.ds(s * slot * TILE, slot * TILE)
                pltpu.make_async_copy(
                    block_ref.at[s, :, there],
                    stage_ref.at[step % 2, j, :, here],
                    sems.at[step % 2, j],
                ).start()

    @pl.when(step == 0)
    def _():
        for j in range(span):
            begin(step, j)

    lane = counting((lines, LANES), 1)

    def multiply(j, depth):
        within_block, block = place_ref[j, 0], place_ref[j, 1]
        pieces = []
        for first in range(0, depth, LANES):
            away = jnp.abs(block - jnp.asarray(first // 256, jnp.bfloat16))
            place = within_block + away * jnp.asarray(512, jnp.bfloat16)
            pieces.append(equal_ones(lane + jnp.asarray(first % 256, jnp.bfloat16), place))
        onehot = jnp.concatenate(pieces, axis=1)
        for part in range(count):
            out_ref[j, part] = jnp.dot(
                onehot, stage_ref[buffer, j, part, :depth], preferred_element_type=jnp.float32
            ).astype(jnp.bfloat16)

    for j in range(span):
        e = step * span + j
        staged = rows * slot * TILE

        @pl.when(slotted(e))
        def _(j=j):
            all_slots = stage_ref.at[buffer, j, :, pl.ds(0, staged)]
            pltpu.make_async_copy(all_slots, all_slots, sems.at[buffer, j]).wait()

        @pl.when(step + 1 < steps)
        def _(j=j):
            begin(step + 1, j)

        @pl.when(slotted(e))
        def _(j=j):
            if staged % LANES:
                stage_ref[buffer, j, :, staged:] = jnp.zeros(
                    (count, deep - staged, width), jnp.bfloat16
                )
                multiply(j, deep)
            else:
                multiply(j, staged)

        @pl.when(jnp.logical_not(slotted(e)))
        def _(e=e, j=j):
            stage_ref[buffer, j] = jnp.zeros((count, deep, width), jnp.bfloat16)

            def one_peer(s, carry):
                def put(t, c):
                    copy = pltpu.make_async_copy(
                        block_ref.at[s, :, tile_at(entry(0, e, s) + t)],
                        stage_ref.at[buffer, j, :, tile_at(entry(2, e, s) + t)],
                        sems.at[buffer, j],
                    )
                    copy.start()
                    copy.wait()
                    return c

                return lax.fori_loop(0, entry(1, e, s), put, carry)

            lax.fori_loop(0, rows, one_peer, 0)
            multiply(j, deep)


def call_plan(kernel, name, table, ids, pairs, place):
    return pl.pallas_call(
        kernel,
        out_shape=(place, jax.ShapeDtypeStruct((4, up_to(pairs, LANES)), jnp.int32)),
        compiler_params=params(),
        cost_estimate=pl.CostEstimate(
            flops=20 * table.size * 256, bytes_accessed=8 * table.size, transcendentals=0
        ),
        name=name,
    )(table, ids)


def pack(expert_lines, place, plan, piece, rows, block_rows, deep):
    experts, _, lines, width = expert_lines.shape
    first, count = piece
    span = 2 - experts % 2
    stages = span * place.shape[0] // experts
    return pl.pallas_call(
        functools.partial(pack_kernel, rows, span, experts // span),
        grid_spec=pltpu.PrefetchScalarGridSpec(
            num_scalar_prefetch=1,
            grid=(count, experts // span),
            in_specs=[
                pl.BlockSpec((stages, 1, BLOCK), lambda p, e, plan: (e, 0, 0)),
                pl.BlockSpec((span, 1, lines, width), lambda p, e, plan: (e, first + p, 0, 0)),
            ],
            out_specs=pl.BlockSpec(memory_space=pltpu.HBM),
            scratch_shapes=[
                pltpu.VMEM((rows, block_rows + STRAIGHT * TILE, width), jnp.bfloat16),
                pltpu.VMEM((256, BLOCK), jnp.bfloat16),
                pltpu.SemaphoreType.DMA((experts // span,)),
            ]
            + [pltpu.VMEM((deep + STRAIGHT * TILE, width), jnp.bfloat16)] * stages,
        ),
        out_shape=jax.ShapeDtypeStruct((rows, count, block_rows, width), jnp.bfloat16),
        compiler_params=pltpu.CompilerParams(vmem_limit_bytes=PACK_LIMIT),
        cost_estimate=pl.CostEstimate(
            flops=2 * count * experts * deep * lines * width,
            bytes_accessed=4 * count * experts * lines * width,
            transcendentals=0,
        ),
        name="pack_lines",
    )(plan, place, expert_lines)


def unpack(arrived, place, plan, piece, shape, deep, slot, previous):
    experts, _, lines, width = shape
    first, count = piece
    span = 2 - experts % 2
    in_specs = [
        pl.BlockSpec((span, 2, lines, LANES), lambda e, plan: (e, 0, 0, 0)),
        pl.BlockSpec(memory_space=pl.ANY),
    ]
    operands = [plan, place, arrived]
    aliases = {}
    if previous is not None:
        in_specs.append(pl.BlockSpec(memory_space=pl.ANY))
        operands.append(previous)
        aliases = {3: 0}
    return pl.pallas_call(
        functools.partial(unpack_kernel, slot, span),
        grid_spec=pltpu.PrefetchScalarGridSpec(
            num_scalar_prefetch=1,
            grid=(experts // span,),
            in_specs=in_specs,
            out_specs=pl.BlockSpec(
                (span, count, lines, width), lambda e, plan: (e, first // count, 0, 0)
            ),
            scratch_shapes=[
                pltpu.VMEM((2, span, count, deep, width), jnp.bfloat16),
                pltpu.SemaphoreType.DMA((2, span)),
            ],
        ),
        out_shape=jax.ShapeDtypeStruct(shape, jnp.bfloat16),
        input_output_aliases=aliases,
        compiler_params=params(),
        cost_estimate=pl.CostEstimate(
            flops=2 * count * experts * deep * lines * width,
            bytes_accessed=4 * count * experts * lines * width,
            transcendentals=0,
        ),
        name="unpack_lines",
    )(*operands)


def after_kernel(*refs):
    del refs


def after(values, signals):
    anywhere = pl.BlockSpec(memory_space=pl.ANY)
    return pl.pallas_call(
        after_kernel,
        in_specs=[anywhere] * (len(values) + len(signals)),
        out_specs=[anywhere] * len(values),
        out_shape=[jax.ShapeDtypeStruct(v.shape, v.dtype) for v in values],
        input_output_aliases={n: n for n in range(len(values))},
        compiler_params=pltpu.CompilerParams(vmem_limit_bytes=PACK_LIMIT),
        name="after",
    )(*values, *signals)


def own_ids(table, lines, width):
    mine = lax.dynamic_slice_in_dim(table, lax.axis_index("row") * lines, lines, 1)
    return jnp.pad(mine, ((0, 0), (0, width - lines)), constant_values=-1)


def from_peer(block, axis, offset):
    size = lax.axis_size(axis)
    return lax.ppermute(block, axis, [(i, i ^ offset) for i in range(size)])


class Migration:
    def __init__(self, expert_lines, old_lines, new_lines):
        rows = lax.axis_size("row")
        experts, parts, lines, width = expert_lines.shape
        padded = up_to(lines, BLOCK)
        blocks = experts * (padded // BLOCK)
        block_rows = up_to(experts * lines // rows, TILE)
        pairs = experts * rows
        compact = up_to(lines + 2 * (TILE - 1) * rows, TILE)
        deep = up_to(min(lines, BLOCK) + 2 * (TILE - 1) * rows, TILE)
        self.slot = min(SLOT, block_rows // TILE)
        self.deep = up_to(max(compact, rows * self.slot * TILE), 256)
        self.shape = expert_lines.shape
        self.pieces = [(parts - 1, 1), (0, parts - 1)]
        out_place, out_plan = call_plan(
            functools.partial(outgoing_kernel, lines, rows), "outgoing_plan",
            new_lines, own_ids(old_lines, lines, padded), blocks * rows,
            jax.ShapeDtypeStruct((blocks, 1, BLOCK), jnp.int32),
        )
        self.in_place, self.in_plan = call_plan(
            functools.partial(incoming_kernel, lines, rows, block_rows // TILE, self.slot),
            "incoming_plan",
            old_lines, own_ids(new_lines, lines, padded), pairs,
            jax.ShapeDtypeStruct((experts, 2, lines, LANES), jnp.bfloat16),
        )
        self.packed = [
            pack(expert_lines, out_place, out_plan, piece, rows, block_rows, deep)
            for piece in self.pieces
        ]
        self.arrived = []
        self.moved = None

    def send(self, signals=()):
        block = self.packed[len(self.arrived)]
        if signals:
            (block,) = after([block], signals)
        self.arrived.append(
            lax.all_to_all(block, "row", split_axis=0, concat_axis=0, tiled=True)
        )

    def receive(self, piece):
        self.moved = unpack(
            self.arrived[piece], self.in_place, self.in_plan, self.pieces[piece], self.shape,
            self.deep, self.slot, self.moved,
        )


def attend(queries, new_kv, prompt_kv, suffix_kv, lengths):
    seq_count = queries.shape[0]
    prompt_rows = prompt_kv.shape[2]
    suffix_rows = suffix_kv.shape[2]
    col_index = lax.axis_index("col")
    query_heads = queries.reshape(seq_count, KVH, REP, HD)
    prompt_keys = prompt_kv[0, 0].reshape(prompt_rows, KVH, HD)
    prompt_values = prompt_kv[0, 1].reshape(prompt_rows, KVH, HD)
    suffix_keys = suffix_kv[:, 0].reshape(seq_count, suffix_rows, KVH, HD)
    suffix_values = suffix_kv[:, 1].reshape(seq_count, suffix_rows, KVH, HD)
    own_keys = new_kv[:, 0].reshape(seq_count, KVH, HD)
    own_values = new_kv[:, 1].reshape(seq_count, KVH, HD)
    score_scale = HD ** (-0.5)
    prompt_scores = (
        jnp.einsum("skgd,pkd->skgp", query_heads, prompt_keys, preferred_element_type=jnp.float32)
        * score_scale
    )
    suffix_scores = (
        jnp.einsum("skgd,spkd->skgp", query_heads, suffix_keys, preferred_element_type=jnp.float32)
        * score_scale
    )
    own_scores = (
        jnp.einsum("skgd,skd->skg", query_heads, own_keys, preferred_element_type=jnp.float32)
        * score_scale
    )
    positions = col_index * suffix_rows + jnp.arange(suffix_rows, dtype=jnp.int32)
    live_slots = (positions[None, :] < lengths[:, None])[:, None, None, :]
    holder = col_index == 0
    suffix_scores = jnp.where(live_slots, suffix_scores, neg_big)
    own_scores = jnp.where(holder, own_scores, neg_big)
    highest = jnp.maximum(
        jnp.maximum(jnp.max(prompt_scores, axis=-1), jnp.max(suffix_scores, axis=-1)), own_scores
    )
    prompt_weights = jnp.exp(prompt_scores - highest[..., None])
    suffix_weights = jnp.where(live_slots, jnp.exp(suffix_scores - highest[..., None]), 0.0)
    own_weights = jnp.where(holder, jnp.exp(own_scores - highest), 0.0)
    totals = jnp.sum(prompt_weights, axis=-1) + jnp.sum(suffix_weights, axis=-1) + own_weights
    mixture = jnp.einsum(
        "skgp,pkd->skgd",
        prompt_weights.astype(jnp.bfloat16),
        prompt_values,
        preferred_element_type=jnp.float32,
    )
    mixture = mixture + jnp.einsum(
        "skgp,spkd->skgd",
        suffix_weights.astype(jnp.bfloat16),
        suffix_values,
        preferred_element_type=jnp.float32,
    )
    own_rounded = lax.optimization_barrier(own_weights.astype(jnp.bfloat16)).astype(jnp.float32)
    mixture = mixture + own_rounded[..., None] * own_values.astype(jnp.float32)[:, :, None, :]
    heads = KVH * REP
    bundle = jnp.concatenate(
        [
            mixture.reshape(seq_count, heads * HD),
            highest.reshape(seq_count, heads),
            totals.reshape(seq_count, heads),
            jnp.zeros((seq_count, LANES - 2 * heads), jnp.float32),
        ],
        axis=1,
    )
    bundles = [bundle] + [from_peer(bundle, "col", o) for o in range(1, lax.axis_size("col"))]
    every = jnp.stack(bundles)
    mixtures = every[:, :, : heads * HD].reshape(-1, seq_count, heads, HD)
    peaks = every[:, :, heads * HD : heads * HD + heads]
    sums = every[:, :, heads * HD + heads : heads * HD + 2 * heads]
    factors = jnp.exp(peaks - jnp.max(peaks, axis=0))
    total = jnp.sum(sums * factors, axis=0)
    mixed = jnp.sum(mixtures * factors[..., None], axis=0)
    return (mixed / total[..., None]).astype(jnp.bfloat16).reshape(seq_count, heads * HD)


def gate_up_kernel(me_ref, h_ref, gain_ref, router_ref, routes_ref, gate_ref, up_ref, out_ref, acc_ref):
    e = pl.program_id(0)
    tokens = h_ref.shape[0]
    lines = gate_ref.shape[2]
    padded = out_ref.shape[3]
    h = h_ref[...].astype(jnp.float32)
    scaled = (h * gain_ref[...].astype(jnp.float32)).astype(jnp.bfloat16)

    @pl.when(e == 0)
    def _():
        acc_ref[...] = jnp.zeros_like(acc_ref)

    against = (((1,), (1,)), ((), ()))
    gate = lax.dot_general(scaled, gate_ref[0, 0], against, preferred_element_type=jnp.float32)
    up = lax.dot_general(scaled, up_ref[0, 0], against, preferred_element_type=jnp.float32)
    for k in range(routes_ref.shape[1]):
        chosen = routes_ref[:, k : k + 1] == e
        acc_ref[2 * k, :, :lines] += jnp.where(chosen, gate, 0.0)
        acc_ref[2 * k + 1, :, :lines] += jnp.where(chosen, up, 0.0)

    @pl.when(e == pl.num_programs(0) - 1)
    def _():
        last = padded - LANES
        shift = lines - last
        experts = pl.num_programs(0)
        extra = jnp.dot(scaled, router_ref[...], preferred_element_type=jnp.float32)
        lane = iota((tokens, LANES), 1)
        square = jnp.sum(h * h, axis=1, keepdims=True)
        extra = jnp.where(lane == shift + experts, square, extra)
        high = extra.astype(jnp.bfloat16).astype(jnp.float32)
        low = extra - high
        acc_ref[0, :, last:] += jnp.where(lane >= shift, high, 0.0)
        acc_ref[1, :, last:] += jnp.where(lane >= shift, low, 0.0)
        peers, _, share, _ = out_ref.shape
        me = me_ref[0]
        for o in range(peers):
            begin = pl.multiple_of((me ^ o) * share, share)
            out_ref[o] = acc_ref[:, pl.ds(begin, share), :].astype(jnp.bfloat16)


def activate_kernel(lines, experts, model_width, routes_ref, *refs):
    out_ref = refs[-1]
    summed = refs[0][...].astype(jnp.float32)
    for ref in refs[1:-1]:
        summed = summed + ref[...].astype(jnp.float32)
    _, share, padded = summed.shape
    last = padded - LANES
    shift = lines - last
    extra = summed[0, :, last:] + summed[1, :, last:]
    lane = iota((share, LANES), 1)
    square = jnp.sum(jnp.where(lane == shift + experts, extra, 0.0), axis=1, keepdims=True)
    inverse_rms = lax.rsqrt(square / model_width + norm_eps)
    logits = []
    for k in range(out_ref.shape[0]):
        wanted = lane == routes_ref[:, k : k + 1] + shift
        logits.append(jnp.sum(jnp.where(wanted, extra, 0.0), axis=1, keepdims=True) * inverse_rms)
    peak = functools.reduce(jnp.maximum, logits)
    shares = [jnp.exp(v - peak) for v in logits]
    total = functools.reduce(jnp.add, shares)
    inside = iota((share, padded), 1) < lines
    for k in range(out_ref.shape[0]):
        gate = summed[2 * k] * inverse_rms
        up = summed[2 * k + 1] * inverse_rms
        act = gate / (1.0 + jnp.exp(-gate)) * up
        out_ref[k] = jnp.where(inside, act * (shares[k] / total), 0.0).astype(jnp.bfloat16)


def down_kernel(me_ref, routes_ref, *refs):
    down_ref, out_ref, act_ref = refs[-3:]
    chunks = refs[:-3]
    e = pl.program_id(0)
    topk, share, _ = chunks[0].shape
    lines = down_ref.shape[2]

    @pl.when(e == 0)
    def _():
        me = me_ref[0]
        out_ref[...] = jnp.zeros_like(out_ref)
        for o, chunk in enumerate(chunks):
            begin = pl.multiple_of((me ^ o) * share, share)
            act_ref[:, pl.ds(begin, share), :] = chunk[...]

    mine = jnp.zeros((act_ref.shape[1], lines), jnp.float32)
    for k in range(topk):
        chosen = routes_ref[:, k : k + 1] == e
        mine = mine + jnp.where(chosen, act_ref[k, :, :lines].astype(jnp.float32), 0.0)
    out_ref[...] += jnp.dot(
        mine.astype(jnp.bfloat16), down_ref[0, 0], preferred_element_type=jnp.float32
    )


def experts_part(h_mid, moe_gain, w_router, expert_lines, routes, migration):
    rows = lax.axis_size("row")
    cols = lax.axis_size("col")
    row_index = lax.axis_index("row")
    col_index = lax.axis_index("col")
    experts, _, lines, width = expert_lines.shape
    own, _ = h_mid.shape
    tokens = own * rows
    topk = routes.shape[1]
    share = tokens // cols
    padded = up_to(lines + experts + 1, LANES)
    shift = lines - (padded - LANES)
    me = col_index.astype(jnp.int32).reshape(1)

    order = row_index ^ jnp.array(sorted(range(rows), key=lambda o: (o % 2, o)), jnp.int32)
    routes = routes.reshape(rows, own, topk)[order].reshape(tokens, topk)
    my_routes = lax.dynamic_slice_in_dim(routes, col_index * share, share, 0)
    router = jnp.pad(w_router, ((0, 0), (shift, LANES - shift - experts)))
    across = [from_peer(h_mid, "row", o) for o in range(2, rows, 2)]
    same_core = jnp.concatenate([h_mid] + across, axis=0)
    every_h = jnp.concatenate([same_core, from_peer(same_core, "row", 1)], axis=0)
    migration.send(across)
    part_spec = lambda part: pl.BlockSpec((1, 1, lines, width), lambda e, me: (e, part, 0, 0))
    whole = lambda a: pl.BlockSpec(a.shape, lambda e, me: (0,) * a.ndim)
    gain = moe_gain.reshape(1, width)
    partial = pl.pallas_call(
        gate_up_kernel,
        grid_spec=pltpu.PrefetchScalarGridSpec(
            num_scalar_prefetch=1,
            grid=(experts,),
            in_specs=[whole(every_h), whole(gain), whole(router), whole(routes)]
            + [part_spec(0), part_spec(1)],
            out_specs=pl.BlockSpec((cols, 2 * topk, share, padded), lambda e, me: (0, 0, 0, 0)),
            scratch_shapes=[pltpu.VMEM((2 * topk, tokens, padded), jnp.float32)],
        ),
        out_shape=jax.ShapeDtypeStruct((cols, 2 * topk, share, padded), jnp.bfloat16),
        compiler_params=params(),
        cost_estimate=pl.CostEstimate(
            flops=4 * experts * tokens * lines * width,
            bytes_accessed=4 * experts * lines * width,
            transcendentals=0,
        ),
        name="gate_up",
    )(me, every_h, gain, router, routes, expert_lines, expert_lines)
    gathered = [partial[0]] + [from_peer(partial[o], "col", o) for o in range(1, cols)]
    activated = pl.pallas_call(
        functools.partial(activate_kernel, lines, experts, width * cols),
        out_shape=jax.ShapeDtypeStruct((topk, share, padded), jnp.bfloat16),
        compiler_params=params(),
        name="activate",
    )(my_routes, *gathered)
    chunks = [activated] + [from_peer(activated, "col", o) for o in range(1, cols)]
    produced = pl.pallas_call(
        down_kernel,
        grid_spec=pltpu.PrefetchScalarGridSpec(
            num_scalar_prefetch=1,
            grid=(experts,),
            in_specs=[whole(routes)] + [whole(c) for c in chunks] + [part_spec(2)],
            out_specs=pl.BlockSpec((tokens, width), lambda e, me: (0, 0)),
            scratch_shapes=[pltpu.VMEM((topk, tokens, padded), jnp.bfloat16)],
        ),
        out_shape=jax.ShapeDtypeStruct((tokens, width), jnp.float32),
        compiler_params=params(),
        cost_estimate=pl.CostEstimate(
            flops=2 * experts * tokens * lines * width,
            bytes_accessed=2 * experts * lines * width,
            transcendentals=0,
        ),
        name="down",
    )(me, routes, *chunks, expert_lines)
    migration.receive(0)
    (produced,) = after([produced], [migration.moved])
    half = tokens // 2
    both_cores = produced[:half] + from_peer(produced[half:], "row", 1)
    blocks = both_cores.reshape(rows // 2, own, width)
    mixed = blocks[0]
    for n in range(1, rows // 2):
        mixed = mixed + from_peer(blocks[n], "row", 2 * n)
    return mixed


def local(
    hidden,
    queries,
    new_kv,
    prompt_kv,
    suffix_kv,
    lengths,
    w_out,
    moe_gain,
    w_router,
    expert_weights,
    old_lines,
    new_lines,
    routes,
):
    expert_lines = jnp.transpose(expert_weights, (0, 2, 1, 3))
    migration = Migration(expert_lines, old_lines, new_lines)
    migration.send()
    attended = attend(queries, new_kv, prompt_kv, suffix_kv, lengths)
    projected = jnp.dot(attended, w_out, preferred_element_type=jnp.float32)
    h_mid = (hidden.astype(jnp.float32) + projected).astype(jnp.bfloat16)
    (h_mid,) = after([h_mid], migration.packed)
    mixed = experts_part(h_mid, moe_gain, w_router, expert_lines, routes, migration)
    migration.receive(1)
    return (h_mid.astype(jnp.float32) + mixed, jnp.transpose(migration.moved, (0, 2, 1, 3)))


def solution(mesh):
    return jax.shard_map(
        local,
        mesh=mesh,
        in_specs=(
            P("row", "col"),
            P("row", None),
            P("row", None, None),
            P("row", None, "col", None),
            P("row", None, "col", None),
            P("row"),
            P(None, "col"),
            P("col"),
            P("col", None),
            P(None, "row", None, "col"),
            P(),
            P(),
            P(),
        ),
        out_specs=(P("row", "col"), P(None, "row", None, "col")),
        check_vma=False,
    )
```

```python
import functools

import jax
import jax.numpy as jnp
from jax import lax
from jax.experimental import pallas as pl
from jax.experimental.pallas import tpu as pltpu
from jax.sharding import PartitionSpec as P

KVH = 16
HD = 128
REP = 2
TILE = 16
LANES = 128

norm_eps = 1e-06
neg_big = -1e30
VMEM_LIMIT = 48 * 1024 * 1024
PACK_LIMIT = 59 * 1024 * 1024


def up_to(value, unit):
    return -(-value // unit) * unit


def iota(shape, axis):
    return lax.broadcasted_iota(jnp.int32, shape, axis)


def ones_where(mask):
    return jnp.where(mask, 1.0, 0.0).astype(jnp.bfloat16)


def params():
    return pltpu.CompilerParams(vmem_limit_bytes=VMEM_LIMIT)


def counting(shape, axis):
    return iota(shape, axis).astype(jnp.float32).astype(jnp.bfloat16)


def as_bf16(values):
    return values.astype(jnp.float32).astype(jnp.bfloat16)


def equal_ones(left, right):
    one = jnp.ones((), jnp.bfloat16)
    return jnp.maximum(one - jnp.abs(left - right), jnp.zeros((), jnp.bfloat16))


def within(place, block):
    place = place - 256 * block
    return as_bf16(jnp.where((place >= 0) & (place < 256), place, -1))


def look_up(table_rows, id_rows, numbers, values):
    full = table_rows[0].shape[1]
    ids = id_rows[0].shape[1]
    high_count = up_to(-(-full // 64), 16)
    zero = jnp.zeros((), jnp.bfloat16)
    highs = [equal_ones(numbers[:high_count], as_bf16(row >> 6)) for row in table_rows]
    lows = []
    for row in table_rows:
        hit = numbers[:64] == as_bf16(row & 63)
        lows += [jnp.where(hit, part, zero) for part in values]
    square = lax.dot_general(
        jnp.concatenate(highs, axis=0),
        jnp.concatenate(lows, axis=0),
        (((1,), (1,)), ((), ())),
        preferred_element_type=jnp.float32,
    )
    wide = 64 * len(values)
    found = []
    for n, row in enumerate(id_rows):
        block = square[n * high_count : (n + 1) * high_count, n * wide : (n + 1) * wide]
        id_high = equal_ones(numbers[:high_count, :ids], as_bf16(row >> 6))
        spread = lax.dot_general(
            block.astype(jnp.bfloat16), id_high, (((0,), (0,)), ((), ())),
            preferred_element_type=jnp.float32,
        )
        wanted = iota((64, ids), 0) == (row & 63)
        found.append(
            [
                jnp.sum(jnp.where(wanted, spread[64 * m : 64 * m + 64], 0.0), axis=0, keepdims=True)
                for m in range(len(values))
            ]
        )
    return found


def look_up_all(table_ref, id_ref, numbers, values):
    experts = table_ref.shape[0]
    group = 4 // len(values)
    found = []
    for first in range(0, experts, group):
        members = range(first, min(first + group, experts))
        found += look_up(
            [table_ref[e : e + 1, :] for e in members],
            [id_ref[e : e + 1, :] for e in members],
            numbers,
            values,
        )
    return found


def numbers_for(full):
    return counting((max(up_to(-(-full // 64), 16), 64), full), 0)


def segment_plan(counts, experts, rows):
    starts = []
    running = jnp.zeros((rows, LANES), jnp.float32)
    for e in range(experts):
        starts.append(running)
        running = running + counts[e * rows : (e + 1) * rows]
    start = jnp.concatenate(starts, axis=0)
    lead = jnp.floor(start * (1.0 / TILE))
    tail = jnp.floor((start + counts + (TILE - 1.0)) * (1.0 / TILE))
    tiles = jnp.where(counts > 0.0, tail - lead, 0.0)
    pairs = experts * rows
    line = iota((pairs, pairs), 0)
    column = iota((pairs, pairs), 1)
    earlier = ones_where((line // rows == column // rows) & (column < line))
    base = jnp.dot(earlier, tiles.astype(jnp.bfloat16), preferred_element_type=jnp.float32)
    return start, lead, tiles, base


def write_plan(plan_ref, parts):
    for n, part in enumerate(parts):
        short = -part.shape[0] % LANES
        if short:
            part = jnp.concatenate([part, jnp.zeros((short, LANES), jnp.float32)], axis=0)
        plan_ref[n : n + 1, :] = jnp.transpose(part)[:1].astype(jnp.int32)


def outgoing_kernel(lines, rows, new_ref, held_ref, stack_ref, plan_ref):
    width = held_ref.shape[1]
    full = new_ref.shape[1]
    numbers = numbers_for(full)
    slot = iota((64, full), 1).astype(jnp.float32)
    values = (jnp.floor((slot + 0.5) * (1.0 / lines)).astype(jnp.bfloat16),)
    hits = []
    reals = []
    for (peer,) in look_up_all(new_ref, held_ref, numbers, values):
        peer = peer.astype(jnp.int32)
        for first in range(0, width, BLOCK):
            real = iota((1, BLOCK), 1) < lines - first
            here = peer[:, first : first + BLOCK]
            hits.append(jnp.where((iota((rows, BLOCK), 0) == here) & real, 1.0, 0.0))
            reals.append(real)
    blocks = len(hits)
    hits = jnp.concatenate(hits, axis=0)
    until = ones_where(iota((BLOCK, BLOCK), 0) <= iota((BLOCK, BLOCK), 1))
    ranks = jnp.dot(hits.astype(jnp.bfloat16), until, preferred_element_type=jnp.float32)
    counts = jnp.broadcast_to(jnp.sum(hits, axis=1, keepdims=True), (blocks * rows, LANES))
    start, lead, tiles, base = segment_plan(counts, blocks, rows)
    write_plan(plan_ref, (lead, tiles, base, start - lead * TILE))
    offset = (base * TILE + start - lead * TILE - 1.0)[:, :1]
    placed = hits * (ranks + offset)
    for n, real in enumerate(reals):
        row = jnp.sum(placed[n * rows : (n + 1) * rows], axis=0, keepdims=True)
        stack_ref[n] = jnp.where(real, row, -1.0).astype(jnp.int32)


def incoming_kernel(lines, rows, block_tiles, slot, old_ref, wanted_ref, stack_ref, plan_ref):
    experts = old_ref.shape[0]
    width = wanted_ref.shape[1]
    real = iota((1, width), 1) < lines
    held_at = []
    hits = []
    full = old_ref.shape[1]
    numbers = numbers_for(full)
    at = iota((64, full), 1)
    values = (as_bf16(at >> 7), as_bf16(at & 127))
    for high, low in look_up_all(old_ref, wanted_ref, numbers, values):
        slots = high * 128.0 + low
        held_at.append(jnp.where(real, slots, 1e9))
        peer = jnp.floor((slots + 0.5) * (1.0 / lines)).astype(jnp.int32)
        hits.append(jnp.where((iota((rows, width), 0) == peer) & real, 1.0, 0.0))
    hits = jnp.concatenate(hits, axis=0)
    counts = jnp.broadcast_to(jnp.sum(hits, axis=1, keepdims=True), (experts * rows, LANES))
    start, lead, tiles, base = segment_plan(counts, experts, rows)
    line = iota((experts * rows, LANES), 0)
    peer = (line % rows).astype(jnp.float32)
    longest = [
        jnp.max(tiles[e * rows : (e + 1) * rows], axis=0, keepdims=True) for e in range(experts)
    ]
    longest = jnp.concatenate(
        [jnp.broadcast_to(most, (rows, LANES)) for most in longest], axis=0
    )
    slotted = longest <= slot
    lead = jnp.where(slotted, jnp.minimum(lead, float(block_tiles - slot)), lead)
    base = jnp.where(slotted, peer * slot, base)
    write_plan(plan_ref, (lead, tiles, base, jnp.where(slotted, 1.0, 0.0)))
    blank = jnp.zeros((LANES - experts, width), jnp.float32)
    columns = jnp.transpose(jnp.concatenate(held_at + [blank], axis=0))
    rows_out = []
    for e in range(experts):
        mine = slice(e * rows, (e + 1) * rows)
        before = jnp.where(columns[:, e : e + 1] < held_at[e], 1.0, 0.0)
        rank = jnp.sum(before, axis=0, keepdims=True)
        ahead = jnp.zeros((1, LANES), jnp.float32)
        firsts = []
        for r in range(rows):
            firsts.append(ahead)
            ahead = ahead + counts[e * rows + r : e * rows + r + 1]
        first = jnp.concatenate(firsts, axis=0)
        offset = (base[mine] * TILE + start[mine] - lead[mine] * TILE - first)[:, :1]
        rows_out.append(jnp.sum(hits[mine] * (rank + offset), axis=0, keepdims=True))
    places = jnp.transpose(jnp.concatenate(rows_out + [blank], axis=0))
    for e in range(experts):
        place = jnp.broadcast_to(places[:lines, e : e + 1], (lines, LANES))
        block = jnp.floor(place * (1.0 / 256.0))
        stack_ref[e, 0] = (place - 256.0 * block).astype(jnp.bfloat16)
        stack_ref[e, 1] = block.astype(jnp.bfloat16)


BLOCK = 256
STRAIGHT = 4
SLOT = 7


def tile_at(index):
    return pl.ds(pl.multiple_of(index * TILE, TILE), TILE)


def pack_kernel(rows, span, steps, plan_ref, place_ref, lines_ref, out_ref, packed_ref, number_ref, sems, *stages):
    part = pl.program_id(0)
    step = pl.program_id(1)
    deep = stages[0].shape[0] - STRAIGHT * TILE
    lines = lines_ref.shape[2]

    @pl.when((part == 0) & (step == 0))
    def _():
        number_ref[...] = counting(number_ref.shape, 0)

    blocks = len(stages) // span

    def entry(n, j, d):
        return plan_ref[n, (step * len(stages) + j) * rows + d]

    def usual(j):
        held = min(BLOCK, lines - j % blocks * BLOCK)
        return min(deep, up_to(held + (rows + 3) * TILE, TILE))

    def move(j, begin, end):
        first = j % blocks * BLOCK
        last = min(first + BLOCK, lines)
        place = place_ref[j][:, : last - first]
        onehot = [
            equal_ones(
                number_ref[: min(256, end - row), : last - first],
                within(place - begin, (row - begin) // 256),
            )
            for row in range(begin, end, 256)
        ]
        stages[j][begin:end] = jnp.dot(
            jnp.concatenate(onehot, axis=0),
            lines_ref[j // blocks, 0, first:last],
            preferred_element_type=jnp.float32,
        ).astype(jnp.bfloat16)

    for j in range(len(stages)):
        move(j, 0, usual(j))
    for j in range(len(stages)):
        if usual(j) < deep:
            used = entry(1, j, rows - 1) + entry(2, j, rows - 1)

            @pl.when(used * TILE > usual(j))
            def _(j=j):
                move(j, usual(j), deep)

    for j, stage_ref in enumerate(stages):

        def one_peer(d, most, j=j, stage_ref=stage_ref):
            lead, tiles, base = entry(0, j, d), entry(1, j, d), entry(2, j, d)
            there = pl.multiple_of(lead * TILE, TILE)
            here = pl.multiple_of(base * TILE, TILE)
            earlier = packed_ref[d, pl.ds(there, TILE), :]
            fresh = stage_ref[pl.ds(here, STRAIGHT * TILE), :]
            packed_ref[d, pl.ds(there + TILE, (STRAIGHT - 1) * TILE), :] = fresh[TILE:]
            kept = jnp.where(entry(3, j, d) > 0, earlier, jnp.zeros_like(earlier))
            added = jnp.where(tiles > 0, fresh[:TILE], jnp.zeros_like(earlier))
            packed_ref[d, pl.ds(there, TILE), :] = kept + added
            return jnp.maximum(most, tiles)

        most = lax.fori_loop(0, rows, one_peer, 0, unroll=rows <= 8)

        @pl.when(most > STRAIGHT)
        def _(j=j, stage_ref=stage_ref):
            def long_peer(d, carry):
                lead, tiles, base = entry(0, j, d), entry(1, j, d), entry(2, j, d)

                def put(t, c):
                    packed_ref[d, tile_at(lead + t), :] = stage_ref[tile_at(base + t), :]
                    return c

                return lax.fori_loop(STRAIGHT, tiles, put, carry)

            lax.fori_loop(0, rows, long_peer, 0)

    block_rows = out_ref.shape[2]
    chunks = []
    begin = 0
    for after_step in range(steps):
        end = block_rows
        if after_step < steps - 1:
            end = max(begin, block_rows * (after_step + 1) // steps // TILE * TILE - 2 * TILE)
        if end > begin:
            chunks.append((after_step, begin, end))
        begin = end

    def chunk_copy(n):
        _, begin, end = chunks[n]
        here = pl.ds(begin, end - begin)
        return pltpu.make_async_copy(
            packed_ref.at[:, here], out_ref.at[:, part, here], sems.at[n]
        )

    def final_by(n):
        after_step, _, end = chunks[n]
        first = (after_step + 1) * len(stages) * rows
        least = functools.reduce(jnp.minimum, [plan_ref[0, first + d] for d in range(rows)])
        return least * TILE >= end

    for n in range(len(chunks) - 1):

        @pl.when((step == chunks[n][0]) & final_by(n))
        def _(n=n):
            chunk_copy(n).start()

    @pl.when(step == steps - 1)
    def _():
        for n in range(len(chunks) - 1):

            @pl.when(jnp.logical_not(final_by(n)))
            def _(n=n):
                chunk_copy(n).start()

        chunk_copy(len(chunks) - 1).start()
        for n in range(len(chunks)):
            chunk_copy(n).wait()


def unpack_kernel(slot, span, plan_ref, place_ref, block_ref, *rest):
    out_ref, stage_ref, sems = rest[-3:]
    step = pl.program_id(0)
    steps = pl.num_programs(0)
    rows, count, _, width = block_ref.shape
    deep = stage_ref.shape[3]
    lines = out_ref.shape[2]
    buffer = step % 2

    def entry(n, e, s):
        return plan_ref[n, e * rows + s]

    def slotted(e):
        return entry(3, e, 0) > 0

    def begin(step, j):
        e = step * span + j

        @pl.when(slotted(e))
        def _():
            for s in range(rows):
                there = pl.ds(pl.multiple_of(entry(0, e, s) * TILE, TILE), slot * TILE)
                here = pl.ds(s * slot * TILE, slot * TILE)
                pltpu.make_async_copy(
                    block_ref.at[s, :, there],
                    stage_ref.at[step % 2, j, :, here],
                    sems.at[step % 2, j],
                ).start()

    @pl.when(step == 0)
    def _():
        for j in range(span):
            begin(step, j)

    lane = counting((lines, LANES), 1)

    def multiply(j, depth):
        within_block, block = place_ref[j, 0], place_ref[j, 1]
        pieces = []
        for first in range(0, depth, LANES):
            away = jnp.abs(block - jnp.asarray(first // 256, jnp.bfloat16))
            place = within_block + away * jnp.asarray(512, jnp.bfloat16)
            pieces.append(equal_ones(lane + jnp.asarray(first % 256, jnp.bfloat16), place))
        onehot = jnp.concatenate(pieces, axis=1)
        for part in range(count):
            out_ref[j, part] = jnp.dot(
                onehot, stage_ref[buffer, j, part, :depth], preferred_element_type=jnp.float32
            ).astype(jnp.bfloat16)

    for j in range(span):
        e = step * span + j
        staged = rows * slot * TILE

        @pl.when(slotted(e))
        def _(j=j):
            all_slots = stage_ref.at[buffer, j, :, pl.ds(0, staged)]
            pltpu.make_async_copy(all_slots, all_slots, sems.at[buffer, j]).wait()

        @pl.when(step + 1 < steps)
        def _(j=j):
            begin(step + 1, j)

        @pl.when(slotted(e))
        def _(j=j):
            if staged % LANES:
                stage_ref[buffer, j, :, staged:] = jnp.zeros(
                    (count, deep - staged, width), jnp.bfloat16
                )
                multiply(j, deep)
            else:
                multiply(j, staged)

        @pl.when(jnp.logical_not(slotted(e)))
        def _(e=e, j=j):
            stage_ref[buffer, j] = jnp.zeros((count, deep, width), jnp.bfloat16)

            def one_peer(s, carry):
                def put(t, c):
                    copy = pltpu.make_async_copy(
                        block_ref.at[s, :, tile_at(entry(0, e, s) + t)],
                        stage_ref.at[buffer, j, :, tile_at(entry(2, e, s) + t)],
                        sems.at[buffer, j],
                    )
                    copy.start()
                    copy.wait()
                    return c

                return lax.fori_loop(0, entry(1, e, s), put, carry)

            lax.fori_loop(0, rows, one_peer, 0)
            multiply(j, deep)


def call_plan(kernel, name, table, ids, pairs, place, limit):
    return pl.pallas_call(
        kernel,
        out_shape=(place, jax.ShapeDtypeStruct((4, up_to(pairs, LANES)), jnp.int32)),
        compiler_params=pltpu.CompilerParams(vmem_limit_bytes=limit),
        cost_estimate=pl.CostEstimate(
            flops=20 * table.size * 256, bytes_accessed=8 * table.size, transcendentals=0
        ),
        name=name,
    )(table, ids)


def pack(expert_lines, place, plan, piece, rows, block_rows, deep):
    experts, _, lines, width = expert_lines.shape
    first, count = piece
    span = 2 - experts % 2
    stages = span * place.shape[0] // experts
    return pl.pallas_call(
        functools.partial(pack_kernel, rows, span, experts // span),
        grid_spec=pltpu.PrefetchScalarGridSpec(
            num_scalar_prefetch=1,
            grid=(count, experts // span),
            in_specs=[
                pl.BlockSpec((stages, 1, BLOCK), lambda p, e, plan: (e, 0, 0)),
                pl.BlockSpec((span, 1, lines, width), lambda p, e, plan: (e, first + p, 0, 0)),
            ],
            out_specs=pl.BlockSpec(memory_space=pltpu.HBM),
            scratch_shapes=[
                pltpu.VMEM((rows, block_rows + STRAIGHT * TILE, width), jnp.bfloat16),
                pltpu.VMEM((256, BLOCK), jnp.bfloat16),
                pltpu.SemaphoreType.DMA((experts // span,)),
            ]
            + [pltpu.VMEM((deep + STRAIGHT * TILE, width), jnp.bfloat16)] * stages,
        ),
        out_shape=jax.ShapeDtypeStruct((rows, count, block_rows, width), jnp.bfloat16),
        compiler_params=pltpu.CompilerParams(vmem_limit_bytes=PACK_LIMIT),
        cost_estimate=pl.CostEstimate(
            flops=2 * count * experts * deep * lines * width,
            bytes_accessed=4 * count * experts * lines * width,
            transcendentals=0,
        ),
        name="pack_lines",
    )(plan, place, expert_lines)


def unpack(arrived, place, plan, piece, shape, deep, slot, previous):
    experts, _, lines, width = shape
    first, count = piece
    span = 2 - experts % 2
    in_specs = [
        pl.BlockSpec((span, 2, lines, LANES), lambda e, plan: (e, 0, 0, 0)),
        pl.BlockSpec(memory_space=pl.ANY),
    ]
    operands = [plan, place, arrived]
    aliases = {}
    if previous is not None:
        in_specs.append(pl.BlockSpec(memory_space=pl.ANY))
        operands.append(previous)
        aliases = {3: 0}
    return pl.pallas_call(
        functools.partial(unpack_kernel, slot, span),
        grid_spec=pltpu.PrefetchScalarGridSpec(
            num_scalar_prefetch=1,
            grid=(experts // span,),
            in_specs=in_specs,
            out_specs=pl.BlockSpec(
                (span, count, lines, width), lambda e, plan: (e, first // count, 0, 0)
            ),
            scratch_shapes=[
                pltpu.VMEM((2, span, count, deep, width), jnp.bfloat16),
                pltpu.SemaphoreType.DMA((2, span)),
            ],
        ),
        out_shape=jax.ShapeDtypeStruct(shape, jnp.bfloat16),
        input_output_aliases=aliases,
        compiler_params=params(),
        cost_estimate=pl.CostEstimate(
            flops=2 * count * experts * deep * lines * width,
            bytes_accessed=4 * count * experts * lines * width,
            transcendentals=0,
        ),
        name="unpack_lines",
    )(*operands)


def after_kernel(*refs):
    del refs


def after(values, signals):
    anywhere = pl.BlockSpec(memory_space=pl.ANY)
    return pl.pallas_call(
        after_kernel,
        in_specs=[anywhere] * (len(values) + len(signals)),
        out_specs=[anywhere] * len(values),
        out_shape=[jax.ShapeDtypeStruct(v.shape, v.dtype) for v in values],
        input_output_aliases={n: n for n in range(len(values))},
        compiler_params=pltpu.CompilerParams(vmem_limit_bytes=PACK_LIMIT),
        name="after",
    )(*values, *signals)


def own_ids(table, lines, width):
    mine = lax.dynamic_slice_in_dim(table, lax.axis_index("row") * lines, lines, 1)
    return jnp.pad(mine, ((0, 0), (0, width - lines)), constant_values=-1)


def from_peer(block, axis, offset):
    size = lax.axis_size(axis)
    return lax.ppermute(block, axis, [(i, i ^ offset) for i in range(size)])


class Migration:
    def __init__(self, expert_lines, old_lines, new_lines):
        rows = lax.axis_size("row")
        experts, parts, lines, width = expert_lines.shape
        padded = up_to(lines, BLOCK)
        blocks = experts * (padded // BLOCK)
        block_rows = up_to(experts * lines // rows, TILE)
        pairs = experts * rows
        compact = up_to(lines + 2 * (TILE - 1) * rows, TILE)
        deep = up_to(min(lines, BLOCK) + 2 * (TILE - 1) * rows, TILE)
        self.slot = min(SLOT, block_rows // TILE)
        self.deep = up_to(max(compact, rows * self.slot * TILE), 256)
        self.shape = expert_lines.shape
        self.pieces = [(parts - 1, 1), (0, parts - 1)]
        out_place, out_plan = call_plan(
            functools.partial(outgoing_kernel, lines, rows), "outgoing_plan",
            new_lines, own_ids(old_lines, lines, padded), blocks * rows,
            jax.ShapeDtypeStruct((blocks, 1, BLOCK), jnp.int32), PACK_LIMIT,
        )
        self.in_place, self.in_plan = call_plan(
            functools.partial(incoming_kernel, lines, rows, block_rows // TILE, self.slot),
            "incoming_plan",
            old_lines, own_ids(new_lines, lines, padded), pairs,
            jax.ShapeDtypeStruct((experts, 2, lines, LANES), jnp.bfloat16), VMEM_LIMIT,
        )
        self.packed = [
            pack(expert_lines, out_place, out_plan, piece, rows, block_rows, deep)
            for piece in self.pieces
        ]
        self.arrived = []
        self.moved = None

    def send(self, signals=()):
        block = self.packed[len(self.arrived)]
        if signals:
            (block,) = after([block], signals)
        self.arrived.append(
            lax.all_to_all(block, "row", split_axis=0, concat_axis=0, tiled=True)
        )

    def receive(self, piece):
        self.moved = unpack(
            self.arrived[piece], self.in_place, self.in_plan, self.pieces[piece], self.shape,
            self.deep, self.slot, self.moved,
        )


def attend(queries, new_kv, prompt_kv, suffix_kv, lengths):
    seq_count = queries.shape[0]
    prompt_rows = prompt_kv.shape[2]
    suffix_rows = suffix_kv.shape[2]
    col_index = lax.axis_index("col")
    query_heads = queries.reshape(seq_count, KVH, REP, HD)
    prompt_keys = prompt_kv[0, 0].reshape(prompt_rows, KVH, HD)
    prompt_values = prompt_kv[0, 1].reshape(prompt_rows, KVH, HD)
    suffix_keys = suffix_kv[:, 0].reshape(seq_count, suffix_rows, KVH, HD)
    suffix_values = suffix_kv[:, 1].reshape(seq_count, suffix_rows, KVH, HD)
    own_keys = new_kv[:, 0].reshape(seq_count, KVH, HD)
    own_values = new_kv[:, 1].reshape(seq_count, KVH, HD)
    score_scale = HD ** (-0.5)
    prompt_scores = (
        jnp.einsum("skgd,pkd->skgp", query_heads, prompt_keys, preferred_element_type=jnp.float32)
        * score_scale
    )
    suffix_scores = (
        jnp.einsum("skgd,spkd->skgp", query_heads, suffix_keys, preferred_element_type=jnp.float32)
        * score_scale
    )
    own_scores = (
        jnp.einsum("skgd,skd->skg", query_heads, own_keys, preferred_element_type=jnp.float32)
        * score_scale
    )
    positions = col_index * suffix_rows + jnp.arange(suffix_rows, dtype=jnp.int32)
    live_slots = (positions[None, :] < lengths[:, None])[:, None, None, :]
    holder = col_index == 0
    suffix_scores = jnp.where(live_slots, suffix_scores, neg_big)
    own_scores = jnp.where(holder, own_scores, neg_big)
    highest = jnp.maximum(
        jnp.maximum(jnp.max(prompt_scores, axis=-1), jnp.max(suffix_scores, axis=-1)), own_scores
    )
    prompt_weights = jnp.exp(prompt_scores - highest[..., None])
    suffix_weights = jnp.where(live_slots, jnp.exp(suffix_scores - highest[..., None]), 0.0)
    own_weights = jnp.where(holder, jnp.exp(own_scores - highest), 0.0)
    totals = jnp.sum(prompt_weights, axis=-1) + jnp.sum(suffix_weights, axis=-1) + own_weights
    mixture = jnp.einsum(
        "skgp,pkd->skgd",
        prompt_weights.astype(jnp.bfloat16),
        prompt_values,
        preferred_element_type=jnp.float32,
    )
    mixture = mixture + jnp.einsum(
        "skgp,spkd->skgd",
        suffix_weights.astype(jnp.bfloat16),
        suffix_values,
        preferred_element_type=jnp.float32,
    )
    own_rounded = lax.optimization_barrier(own_weights.astype(jnp.bfloat16)).astype(jnp.float32)
    mixture = mixture + own_rounded[..., None] * own_values.astype(jnp.float32)[:, :, None, :]
    heads = KVH * REP
    bundle = jnp.concatenate(
        [
            mixture.reshape(seq_count, heads * HD),
            highest.reshape(seq_count, heads),
            totals.reshape(seq_count, heads),
            jnp.zeros((seq_count, LANES - 2 * heads), jnp.float32),
        ],
        axis=1,
    )
    bundles = [bundle] + [from_peer(bundle, "col", o) for o in range(1, lax.axis_size("col"))]
    every = jnp.stack(bundles)
    mixtures = every[:, :, : heads * HD].reshape(-1, seq_count, heads, HD)
    peaks = every[:, :, heads * HD : heads * HD + heads]
    sums = every[:, :, heads * HD + heads : heads * HD + 2 * heads]
    factors = jnp.exp(peaks - jnp.max(peaks, axis=0))
    total = jnp.sum(sums * factors, axis=0)
    mixed = jnp.sum(mixtures * factors[..., None], axis=0)
    return (mixed / total[..., None]).astype(jnp.bfloat16).reshape(seq_count, heads * HD)


def gate_up_kernel(me_ref, h_ref, gain_ref, router_ref, routes_ref, gate_ref, up_ref, out_ref, acc_ref):
    e = pl.program_id(0)
    tokens = h_ref.shape[0]
    lines = gate_ref.shape[2]
    padded = out_ref.shape[3]
    h = h_ref[...].astype(jnp.float32)
    scaled = (h * gain_ref[...].astype(jnp.float32)).astype(jnp.bfloat16)

    @pl.when(e == 0)
    def _():
        acc_ref[...] = jnp.zeros_like(acc_ref)

    against = (((1,), (1,)), ((), ()))
    gate = lax.dot_general(scaled, gate_ref[0, 0], against, preferred_element_type=jnp.float32)
    up = lax.dot_general(scaled, up_ref[0, 0], against, preferred_element_type=jnp.float32)
    for k in range(routes_ref.shape[1]):
        chosen = routes_ref[:, k : k + 1] == e
        acc_ref[2 * k, :, :lines] += jnp.where(chosen, gate, 0.0)
        acc_ref[2 * k + 1, :, :lines] += jnp.where(chosen, up, 0.0)

    @pl.when(e == pl.num_programs(0) - 1)
    def _():
        last = padded - LANES
        shift = lines - last
        experts = pl.num_programs(0)
        extra = jnp.dot(scaled, router_ref[...], preferred_element_type=jnp.float32)
        lane = iota((tokens, LANES), 1)
        square = jnp.sum(h * h, axis=1, keepdims=True)
        extra = jnp.where(lane == shift + experts, square, extra)
        high = extra.astype(jnp.bfloat16).astype(jnp.float32)
        low = extra - high
        acc_ref[0, :, last:] += jnp.where(lane >= shift, high, 0.0)
        acc_ref[1, :, last:] += jnp.where(lane >= shift, low, 0.0)
        peers, _, share, _ = out_ref.shape
        me = me_ref[0]
        for o in range(peers):
            begin = pl.multiple_of((me ^ o) * share, share)
            out_ref[o] = acc_ref[:, pl.ds(begin, share), :].astype(jnp.bfloat16)


def activate_kernel(lines, experts, model_width, routes_ref, *refs):
    out_ref = refs[-1]
    summed = refs[0][...].astype(jnp.float32)
    for ref in refs[1:-1]:
        summed = summed + ref[...].astype(jnp.float32)
    _, share, padded = summed.shape
    last = padded - LANES
    shift = lines - last
    extra = summed[0, :, last:] + summed[1, :, last:]
    lane = iota((share, LANES), 1)
    square = jnp.sum(jnp.where(lane == shift + experts, extra, 0.0), axis=1, keepdims=True)
    inverse_rms = lax.rsqrt(square / model_width + norm_eps)
    logits = []
    for k in range(out_ref.shape[0]):
        wanted = lane == routes_ref[:, k : k + 1] + shift
        logits.append(jnp.sum(jnp.where(wanted, extra, 0.0), axis=1, keepdims=True) * inverse_rms)
    peak = functools.reduce(jnp.maximum, logits)
    shares = [jnp.exp(v - peak) for v in logits]
    total = functools.reduce(jnp.add, shares)
    inside = iota((share, padded), 1) < lines
    for k in range(out_ref.shape[0]):
        gate = summed[2 * k] * inverse_rms
        up = summed[2 * k + 1] * inverse_rms
        act = gate / (1.0 + jnp.exp(-gate)) * up
        out_ref[k] = jnp.where(inside, act * (shares[k] / total), 0.0).astype(jnp.bfloat16)


def down_kernel(me_ref, routes_ref, *refs):
    down_ref, out_ref, act_ref = refs[-3:]
    chunks = refs[:-3]
    e = pl.program_id(0)
    topk, share, _ = chunks[0].shape
    lines = down_ref.shape[2]

    @pl.when(e == 0)
    def _():
        me = me_ref[0]
        out_ref[...] = jnp.zeros_like(out_ref)
        for o, chunk in enumerate(chunks):
            begin = pl.multiple_of((me ^ o) * share, share)
            act_ref[:, pl.ds(begin, share), :] = chunk[...]

    mine = jnp.zeros((act_ref.shape[1], lines), jnp.float32)
    for k in range(topk):
        chosen = routes_ref[:, k : k + 1] == e
        mine = mine + jnp.where(chosen, act_ref[k, :, :lines].astype(jnp.float32), 0.0)
    out_ref[...] += jnp.dot(
        mine.astype(jnp.bfloat16), down_ref[0, 0], preferred_element_type=jnp.float32
    )


def experts_part(h_mid, moe_gain, w_router, expert_lines, routes, migration):
    rows = lax.axis_size("row")
    cols = lax.axis_size("col")
    row_index = lax.axis_index("row")
    col_index = lax.axis_index("col")
    experts, _, lines, width = expert_lines.shape
    own, _ = h_mid.shape
    tokens = own * rows
    topk = routes.shape[1]
    share = tokens // cols
    padded = up_to(lines + experts + 1, LANES)
    shift = lines - (padded - LANES)
    me = col_index.astype(jnp.int32).reshape(1)

    order = row_index ^ jnp.array(sorted(range(rows), key=lambda o: (o % 2, o)), jnp.int32)
    routes = routes.reshape(rows, own, topk)[order].reshape(tokens, topk)
    my_routes = lax.dynamic_slice_in_dim(routes, col_index * share, share, 0)
    router = jnp.pad(w_router, ((0, 0), (shift, LANES - shift - experts)))
    across = [from_peer(h_mid, "row", o) for o in range(2, rows, 2)]
    same_core = jnp.concatenate([h_mid] + across, axis=0)
    every_h = jnp.concatenate([same_core, from_peer(same_core, "row", 1)], axis=0)
    migration.send(across)
    part_spec = lambda part: pl.BlockSpec((1, 1, lines, width), lambda e, me: (e, part, 0, 0))
    whole = lambda a: pl.BlockSpec(a.shape, lambda e, me: (0,) * a.ndim)
    gain = moe_gain.reshape(1, width)
    partial = pl.pallas_call(
        gate_up_kernel,
        grid_spec=pltpu.PrefetchScalarGridSpec(
            num_scalar_prefetch=1,
            grid=(experts,),
            in_specs=[whole(every_h), whole(gain), whole(router), whole(routes)]
            + [part_spec(0), part_spec(1)],
            out_specs=pl.BlockSpec((cols, 2 * topk, share, padded), lambda e, me: (0, 0, 0, 0)),
            scratch_shapes=[pltpu.VMEM((2 * topk, tokens, padded), jnp.float32)],
        ),
        out_shape=jax.ShapeDtypeStruct((cols, 2 * topk, share, padded), jnp.bfloat16),
        compiler_params=params(),
        cost_estimate=pl.CostEstimate(
            flops=4 * experts * tokens * lines * width,
            bytes_accessed=4 * experts * lines * width,
            transcendentals=0,
        ),
        name="gate_up",
    )(me, every_h, gain, router, routes, expert_lines, expert_lines)
    gathered = [partial[0]] + [from_peer(partial[o], "col", o) for o in range(1, cols)]
    activated = pl.pallas_call(
        functools.partial(activate_kernel, lines, experts, width * cols),
        out_shape=jax.ShapeDtypeStruct((topk, share, padded), jnp.bfloat16),
        compiler_params=params(),
        name="activate",
    )(my_routes, *gathered)
    chunks = [activated] + [from_peer(activated, "col", o) for o in range(1, cols)]
    produced = pl.pallas_call(
        down_kernel,
        grid_spec=pltpu.PrefetchScalarGridSpec(
            num_scalar_prefetch=1,
            grid=(experts,),
            in_specs=[whole(routes)] + [whole(c) for c in chunks] + [part_spec(2)],
            out_specs=pl.BlockSpec((tokens, width), lambda e, me: (0, 0)),
            scratch_shapes=[pltpu.VMEM((topk, tokens, padded), jnp.bfloat16)],
        ),
        out_shape=jax.ShapeDtypeStruct((tokens, width), jnp.float32),
        compiler_params=params(),
        cost_estimate=pl.CostEstimate(
            flops=2 * experts * tokens * lines * width,
            bytes_accessed=2 * experts * lines * width,
            transcendentals=0,
        ),
        name="down",
    )(me, routes, *chunks, expert_lines)
    migration.receive(0)
    (produced,) = after([produced], [migration.moved])
    half = tokens // 2
    both_cores = produced[:half] + from_peer(produced[half:], "row", 1)
    blocks = both_cores.reshape(rows // 2, own, width)
    mixed = blocks[0]
    for n in range(1, rows // 2):
        mixed = mixed + from_peer(blocks[n], "row", 2 * n)
    return mixed


def local(
    hidden,
    queries,
    new_kv,
    prompt_kv,
    suffix_kv,
    lengths,
    w_out,
    moe_gain,
    w_router,
    expert_weights,
    old_lines,
    new_lines,
    routes,
):
    expert_lines = jnp.transpose(expert_weights, (0, 2, 1, 3))
    migration = Migration(expert_lines, old_lines, new_lines)
    migration.send()
    attended = attend(queries, new_kv, prompt_kv, suffix_kv, lengths)
    projected = jnp.dot(attended, w_out, preferred_element_type=jnp.float32)
    h_mid = (hidden.astype(jnp.float32) + projected).astype(jnp.bfloat16)
    (h_mid,) = after([h_mid], migration.packed)
    mixed = experts_part(h_mid, moe_gain, w_router, expert_lines, routes, migration)
    migration.receive(1)
    return (h_mid.astype(jnp.float32) + mixed, jnp.transpose(migration.moved, (0, 2, 1, 3)))


def solution(mesh):
    return jax.shard_map(
        local,
        mesh=mesh,
        in_specs=(
            P("row", "col"),
            P("row", None),
            P("row", None, None),
            P("row", None, "col", None),
            P("row", None, "col", None),
            P("row"),
            P(None, "col"),
            P("col"),
            P("col", None),
            P(None, "row", None, "col"),
            P(),
            P(),
            P(),
        ),
        out_specs=(P("row", "col"), P(None, "row", None, "col")),
        check_vma=False,
    )
```
